32 devices in a mesh: vol: 8 (over z, y), seq: 4 (over x, core).
Axes of the slice: x: 2, y: 2, z: 4, core: 2. Of those that a mesh axis runs over, the one named last changes fastest.
Arguments:
- volume_slices: int32 [8], replicated, may hold values from 1 to 4, as said below
- volume_owner: int32 [8], replicated, may hold values from 0 to 7, as said below
- tokens: bfloat16 [32, 1024, 768], P('vol', 'seq'), may hold values from -6 to 6
- cotangent: bfloat16 [32, 1024, 768], P('vol', 'seq'), may hold values from -6 to 6
- attend_gain: bfloat16 [768], replicated, may hold values from 0.5 to 1.5
- attend_shift: bfloat16 [768], replicated, may hold values from -1 to 1
- input_weight: bfloat16 [768, 2304], replicated, may hold values from -0.3125 to 0.3125
- query_bias: bfloat16 [768], replicated, may hold values from -1 to 1
- value_bias: bfloat16 [768], replicated, may hold values from -1 to 1
- output_weight: bfloat16 [768, 768], replicated, may hold values from -0.625 to 0.625
- output_bias: bfloat16 [768], replicated, may hold values from -1 to 1
- mixer_gain: bfloat16 [768], replicated, may hold values from 0.5 to 1.5
- mixer_shift: bfloat16 [768], replicated, may hold values from -1 to 1
- expand_weight: bfloat16 [768, 3072], replicated, may hold values from -0.21875 to 0.21875
- expand_bias: bfloat16 [3072], replicated, may hold values from -1 to 1
- reduce_weight: bfloat16 [3072, 768], replicated, may hold values from -0.109375 to 0.109375
- reduce_bias: bfloat16 [768], replicated, may hold values from -1 to 1
Outputs:
- block_out: bfloat16 [32, 1024, 768], P('vol', 'seq')
- tokens_grad: float32 [32, 1024, 768], P('vol', 'seq')
- attend_gain_grad: float32 [768], P('vol')
- attend_shift_grad: float32 [768], P('vol')
- input_weight_grad: float32 [768, 2304], P('vol')
- query_bias_grad: float32 [768], P('vol')
- value_bias_grad: float32 [768], P('vol')
- output_weight_grad: float32 [768, 768], P('vol')
- output_bias_grad: float32 [768], P('vol')
- mixer_gain_grad: float32 [768], P('vol')
- mixer_shift_grad: float32 [768], P('vol')
- expand_weight_grad: float32 [768, 3072], P('vol')
- expand_bias_grad: float32 [3072], P('vol')
- reduce_weight_grad: float32 [3072, 768], P('vol')
- reduce_bias_grad: float32 [768], P('vol')
The draws below stay inside these ranges and needn't reach their ends.
Inputs may be any that keep to these rules, and one draw needn't show every extreme that they name: `volume_slices`: each volume has 1 to 4 slices in this step. The volumes that one index of vol owns hold at most 4 slices together, and exactly 4 on some index; they fill that index's slots from the first. `volume_owner`: each index of vol owns exactly 1 volume.
All inputs are finite; a program needn't handle non-finite values.
Results may differ from the reference program's by a relative error of at most 0.017.
Values may be sent and summed in bfloat16 or wider, within the bound.
No kernel may reach another device: no remote copies, remote signals or barrier semaphores. Data moves between devices by JAX's collectives and lax.ppermute only.
A program may use at most 256 MiB of HBM per device.

```python
import jax
import jax.numpy as jnp
from jax import lax

D = 768
FF = 3072
HEAD_DIM = 64
TOK_IMG = 1024
MOST = 4
CAPACITY = 4
VOLUMES = 8
SLICES = 32
N_VOL = 8


def shared_volumes(key):
    order = jax.random.permutation(jax.random.fold_in(key, 11), VOLUMES)
    owner = (order % N_VOL).astype(jnp.int32)
    counts = jax.random.randint(jax.random.fold_in(key, 12), (VOLUMES,), 1, MOST + 1)
    fullest = jax.random.randint(jax.random.fold_in(key, 13), (), 0, N_VOL)
    counts = jnp.where(owner == fullest, MOST, counts).astype(jnp.int32)
    return (owner, counts)


def draw_volume_slices(key, part):
    owner, counts = shared_volumes(key)
    return counts


def draw_volume_owner(key, part):
    owner, counts = shared_volumes(key)
    return owner


def levels(own_key, dims, shards, low, top_value):
    def one(dim, parts):
        draws = jax.random.uniform(jax.random.fold_in(jax.random.fold_in(own_key, 6), dim), (parts,), jnp.float32, low / len(shards), top_value / len(shards))
        return jnp.repeat(jnp.exp(draws), dims[dim] // parts).reshape((-1,) + (1,) * (len(dims) - dim - 1))

    level = one(*shards[0])
    for cut in shards[1:]:
        level = level * one(*cut)
    return level


def gaussian(rng, extent, deviation, reach, split=(), dtype=jnp.bfloat16):
    values = deviation * jax.random.normal(rng, extent, jnp.float32)
    if split:
        values = values * levels(rng, extent, split, -0.22, 0.18)
    return jnp.clip(values, -reach, reach).astype(dtype)


def setup_inputs(seed: int = 0) -> dict:
    streams_of = jax.random.split(jax.random.key(seed), 18)
    return {
        "volume_slices": draw_volume_slices(jax.random.fold_in(streams_of[17], 71), 0),
        "volume_owner": draw_volume_owner(jax.random.fold_in(streams_of[17], 71), 0),
        "tokens": gaussian(streams_of[2], (SLICES, TOK_IMG, D), 1.0, 6.0, ((0, 8), (1, 4))),
        "cotangent": gaussian(streams_of[3], (SLICES, TOK_IMG, D), 1.0, 6.0, ((0, 8), (1, 4))),
        "attend_gain": jnp.clip(1.0 + 0.1 * jax.random.normal(streams_of[4], (D,), jnp.float32), 0.5, 1.5).astype(jnp.bfloat16),
        "attend_shift": gaussian(streams_of[5], (D,), 0.2, 1.0),
        "input_weight": gaussian(streams_of[6], (D, 3 * D), (D // 2) ** -0.5, 0.3125),
        "query_bias": gaussian(streams_of[7], (D,), 0.2, 1.0),
        "value_bias": gaussian(streams_of[8], (D,), 0.2, 1.0),
        "output_weight": gaussian(streams_of[9], (D, D), (D // 8) ** -0.5, 0.625),
        "output_bias": gaussian(streams_of[10], (D,), 0.2, 1.0),
        "mixer_gain": jnp.clip(1.0 + 0.1 * jax.random.normal(streams_of[11], (D,), jnp.float32), 0.5, 1.5).astype(jnp.bfloat16),
        "mixer_shift": gaussian(streams_of[12], (D,), 0.2, 1.0),
        "expand_weight": gaussian(streams_of[13], (D, FF), D ** -0.5, 0.21875),
        "expand_bias": gaussian(streams_of[14], (FF,), 0.2, 1.0),
        "reduce_weight": gaussian(streams_of[15], (FF, D), FF ** -0.5, 0.109375),
        "reduce_bias": gaussian(streams_of[16], (D,), 0.2, 1.0),
    }


@jax.custom_vjp
def low(v):
    return lax.optimization_barrier(v.astype(jnp.bfloat16)).astype(jnp.float32)

@jax.custom_vjp
def low_back(v):
    return v

def low_keep(v):
    return (low(v), None)

def low_pass(kept, grad):
    return (grad,)

def back_keep(v):
    return (v, None)

def back_low(kept, grad):
    return (low(grad),)
low.defvjp(low_keep, low_pass)
low_back.defvjp(back_keep, back_low)

def normalize(values, gain, shift):
    centre = lax.optimization_barrier(jnp.mean(values, axis=-1, keepdims=True))
    spread = values - centre
    variance = lax.optimization_barrier(jnp.mean(spread * spread, axis=-1, keepdims=True))
    return spread * lax.rsqrt(variance + 1e-06) * gain + shift

def product(left, right):
    return jnp.einsum('...i,ij->...j', left, right, precision=lax.Precision.HIGHEST)

def forward(params, source):
    attend_gain, attend_shift, input_weight, query_bias, value_bias, output_weight, output_bias, mixer_gain, mixer_shift, expand_weight, expand_bias, reduce_weight, reduce_bias = params
    slice_count, token_count, features = source.shape
    head_count = features // HEAD_DIM
    scaling = HEAD_DIM ** (-0.5)
    first = low(normalize(source, attend_gain, attend_shift))
    biases = jnp.concatenate([query_bias, jnp.zeros_like(query_bias), value_bias])
    packed = low(low_back(product(first, input_weight) + biases))
    packed = packed.reshape(slice_count, token_count, 3, head_count, HEAD_DIM)
    raw_scores = jnp.einsum('cqhd,ckhd->chqk', packed[:, :, 0], packed[:, :, 1], precision=lax.Precision.HIGHEST) * scaling
    scores = low_back(raw_scores)
    highest = lax.optimization_barrier(jnp.max(scores, axis=-1, keepdims=True))
    shifted = jnp.exp(scores - highest)
    weights = low(shifted / lax.optimization_barrier(jnp.sum(shifted, axis=-1, keepdims=True)))
    mixed = jnp.einsum('chqk,ckhd->cqhd', weights, packed[:, :, 2], precision=lax.Precision.HIGHEST)
    mixed = low(low_back(mixed.reshape(slice_count, token_count, features)))
    middle = source + low_back(product(mixed, output_weight) + output_bias)
    second = low(normalize(middle, mixer_gain, mixer_shift))
    hidden = low_back(product(second, expand_weight) + expand_bias)
    activated = low(jax.nn.gelu(hidden, approximate=False))
    return middle + low_back(product(activated, reduce_weight) + reduce_bias)

def reference(volume_slices, volume_owner, tokens, cotangent, attend_gain, attend_shift, input_weight, query_bias, value_bias, output_weight, output_bias, mixer_gain, mixer_shift, expand_weight, expand_bias, reduce_weight, reduce_bias):
    params = tuple((item.astype(jnp.float32) for item in (attend_gain, attend_shift, input_weight, query_bias, value_bias, output_weight, output_bias, mixer_gain, mixer_shift, expand_weight, expand_bias, reduce_weight, reduce_bias)))
    owners = jnp.arange(N_VOL).astype(jnp.int32)
    volume_load = lax.optimization_barrier(jnp.sum(jnp.where(volume_owner[None, :] == owners[:, None], volume_slices[None, :], 0), axis=1))
    slot_index = jnp.arange(CAPACITY).astype(jnp.int32)
    occupied = (slot_index[None, :] < volume_load[:, None]).astype(jnp.float32)[:, :, None, None]
    source = tokens.astype(jnp.float32).reshape(N_VOL, CAPACITY, TOK_IMG, D)
    upstream = cotangent.astype(jnp.float32).reshape(N_VOL, CAPACITY, TOK_IMG, D) * occupied

    def visit(totals, item):
        block, seed_rows = item
        result, pull = jax.vjp(forward, params, block)
        param_grads, block_grad = pull(seed_rows)
        return (tuple((left + right for left, right in zip(totals, param_grads))), (result, block_grad))
    start = tuple((jnp.zeros_like(item) for item in params))
    totals, (results, grads) = lax.scan(visit, start, (source, upstream))
    block_out = (results * occupied).astype(jnp.bfloat16).reshape(SLICES, TOK_IMG, D)
    tokens_grad = grads.reshape(SLICES, TOK_IMG, D)
    return (block_out, tokens_grad, totals[0], totals[1], totals[2], totals[3], totals[4], totals[5], totals[6], totals[7], totals[8], totals[9], totals[10], totals[11], totals[12])
```

```python
import functools

import jax
import jax.numpy as jnp
from jax import lax
from jax.experimental import pallas as pl
from jax.experimental.pallas import tpu as pltpu
from jax.sharding import PartitionSpec as P

HEAD_DIM = 64
PAIR = 2 * HEAD_DIM
LOG2E = 1.4426950408889634
BF = jnp.bfloat16
F32 = jnp.float32
NN = (((1,), (0,)), ((), ()))
NT = (((1,), (1,)), ((), ()))
TAIL = (
    0.11962928008603971,
    0.12075423895539067,
    0.09991176086876633,
    0.12856720585766357,
    -0.05369390237929985,
    0.20636430391507077,
    -0.15720912816414995,
    0.03567616760586865,
)


def dot(a, b, dims):
    return lax.dot_general(a, b, dims, preferred_element_type=F32)


def params():
    return pltpu.CompilerParams(vmem_limit_bytes=60 << 20)


def shape(dims, dtype=BF):
    return jax.ShapeDtypeStruct(dims, dtype)


def normal(h):
    a = jnp.abs(h)
    t = 1.0 / (1.0 + 0.3 * a)
    s = TAIL[7] * t + TAIL[6]
    for c in TAIL[5::-1]:
        s = s * t + c
    e = jnp.exp2(h * h * (-0.5 * LOG2E))
    tail = s * t * e
    return jnp.where(h >= 0, 1.0 - tail, tail), e * 0.3989422804014327


def stats(v):
    spread = v - jnp.mean(v, axis=-1, keepdims=True)
    return spread, lax.rsqrt(jnp.mean(spread * spread, axis=-1, keepdims=True) + 1e-6)


def in_kernel(x_ref, g_ref, b_ref, w_ref, bias_ref, *rest):
    x_out, first_t, packed = rest[-3:]
    x = x_ref[...]
    spread, r = stats(x.astype(F32))
    f = (spread * r * g_ref[...] + b_ref[...]).astype(BF)
    x_out[...] = x
    first_t[...] = f.T
    packed[...] = (dot(f, w_ref[...], NN) + bias_ref[...]).astype(BF)


def project_in(parts, offset, total, before, gain, shift, weight, bias):
    rows, d = parts.shape
    wide = weight.shape[1]
    tm = 256
    first_block = offset // tm

    def full(*s):
        return pl.BlockSpec(s, lambda i: (0, 0))

    in_specs = [pl.BlockSpec((tm, d), lambda i: (i, 0)), full(1, d), full(1, d), full(d, wide), full(1, wide)]
    args = [parts, gain, shift, weight, bias]
    aliases = {}
    if before is not None:
        aliases = {5: 0, 6: 1, 7: 2}
        in_specs += [pl.BlockSpec(memory_space=pl.ANY)] * 3
        args += list(before)
    return pl.pallas_call(
        in_kernel,
        grid=(rows // tm,),
        in_specs=in_specs,
        out_specs=[
            pl.BlockSpec((tm, d), lambda i: (i + first_block, 0)),
            pl.BlockSpec((d, tm), lambda i: (0, i + first_block)),
            pl.BlockSpec((tm, wide), lambda i: (i + first_block, 0)),
        ],
        out_shape=[shape((total, d)), shape((d, total)), shape((total, wide))],
        input_output_aliases=aliases,
        compiler_params=params(),
        cost_estimate=pl.CostEstimate(flops=2 * rows * d * wide, bytes_accessed=2 * (d * wide + rows * (wide + 3 * d)), transcendentals=0),
        name="project_in",
    )(*args)


def attend_kernel(q_ref, k_ref, v_ref, o_ref, inv_ref, p_ref, vx_ref, *, tq):
    n = k_ref.shape[0]
    vx_ref[:, :PAIR] = v_ref[...]
    vx_ref[:, PAIR:] = jnp.ones((n, PAIR), BF)
    low = lax.broadcasted_iota(jnp.int32, (tq, PAIR), 1) < HEAD_DIM
    for t in range(n // tq):
        rows = pl.ds(t * tq, tq)
        q = q_ref[rows, :]
        zero = jnp.zeros_like(q)
        outs = []
        for a in range(2):
            qa = jnp.where(low, q, zero) if a == 0 else jnp.where(low, zero, q)
            s = dot(qa, k_ref[...], NT)
            top = jnp.max(s, axis=-1, keepdims=True)
            p = jnp.exp2((s - top) * (LOG2E * HEAD_DIM**-0.5)).astype(BF)
            p_ref[a, rows, :] = p
            both = dot(p, vx_ref[...], NN)
            inv = 1.0 / both[:, PAIR:]
            outs.append((both[:, :PAIR] * inv, inv))
        o_ref[rows, :] = jnp.where(low, outs[0][0], outs[1][0]).astype(BF)
        inv_ref[rows, :] = jnp.where(low, outs[0][1], outs[1][1])


def attend(packed):
    n, w = packed.shape
    d = w // 3
    hp = d // PAIR

    def cols(off):
        return pl.BlockSpec((n, PAIR), lambda h: (0, h + off))

    return pl.pallas_call(
        functools.partial(attend_kernel, tq=128),
        grid=(hp,),
        in_specs=[cols(0), cols(hp), cols(2 * hp)],
        out_specs=[cols(0), cols(0), pl.BlockSpec((2, n, n), lambda h: (h, 0, 0))],
        out_shape=[shape((n, d)), shape((n, d), F32), shape((2 * hp, n, n))],
        scratch_shapes=[pltpu.VMEM((n, 2 * PAIR), BF)],
        compiler_params=params(),
        cost_estimate=pl.CostEstimate(flops=16 * n * n * d, bytes_accessed=4 * n * n * hp, transcendentals=0),
        name="attend",
    )(packed, packed, packed)


def mlp_kernel(
    c_ref, x_ref, mix_ref, li_ref, up_ref, wo_ref, bo_ref, g2_ref, s2_ref, w1_ref, b1_ref, w2_ref, b2_ref,
    out_ref, dbr_ref, do_ref, dwo_k_ref, dwo_s_ref, dw1_k_ref, dw1_s_ref, dw2_k_ref, dw2_s_ref, vec_ref, db1_ref,
    sec, sec_t, up_t, mid, dsec, acc, act, dh, *, tm, nj,
):
    j = pl.program_id(0)
    n, d = x_ref.shape
    tiles = n // tm
    c = c_ref[0]

    @pl.when(j == 0)
    def _():
        for t in range(tiles):
            rows = pl.ds(t * tm, tm)
            m = x_ref[rows, :].astype(F32) + dot(mix_ref[rows, :], wo_ref[...], NN) + bo_ref[...]
            mid[rows, :] = m
            spread, r = stats(m)
            s = (spread * r * g2_ref[...] + s2_ref[...]).astype(BF)
            sec[rows, :] = s
            sec_t[:, rows] = s.T
            up_t[:, rows] = up_ref[rows, :].T
        vec_ref[...] = jnp.zeros_like(vec_ref)

    db1 = None
    for t in range(tiles):
        rows = pl.ds(t * tm, tm)
        h = dot(sec[rows, :], w1_ref[...], NN) + b1_ref[...]
        da = dot(up_ref[rows, :], w2_ref[...], NT)
        cdf, pdf = normal(h)
        a = (h * cdf).astype(BF)
        dhv = (da * (cdf + h * pdf)).astype(BF)
        act[rows, :] = a
        dh[rows, :] = dhv
        o = dot(a, w2_ref[...], NN)
        ds = dot(dhv, w1_ref[...], NT)
        part = jnp.sum(dhv.astype(F32), axis=0, keepdims=True)
        db1 = part if db1 is None else db1 + part

        @pl.when(j == 0)
        def _():
            acc[rows, :] = o
            dsec[rows, :] = ds

        @pl.when(j > 0)
        def _():
            acc[rows, :] += o
            dsec[rows, :] += ds

    db1_ref[...] = db1
    half = d // 2
    keep = pl.ds(pl.multiple_of(c * half, half), half)
    send = pl.ds(pl.multiple_of((1 - c) * half, half), half)
    pc = dw2_k_ref.shape[2]
    npc = w1_ref.shape[1] // pc
    g = dot(up_t[keep, :], act[...], NN).astype(BF)
    for p in range(npc):
        dw2_k_ref[p] = g[:, p * pc : (p + 1) * pc]
    g = dot(up_t[send, :], act[...], NN).astype(BF)
    for p in range(npc):
        dw2_s_ref[p] = g[:, p * pc : (p + 1) * pc]
    g = dot(sec_t[...], dh[...], NN).astype(BF).reshape(dw1_k_ref.shape)

    @pl.when(j < nj // 2)
    def _():
        dw1_s_ref[...] = g

    @pl.when(j >= nj // 2)
    def _():
        dw1_k_ref[...] = g

    @pl.when(j == nj - 1)
    def _():
        for t in range(tiles):
            rows = pl.ds(t * tm, tm)
            m = mid[rows, :]
            out_ref[rows, :] = (m + acc[rows, :] + b2_ref[...]).astype(BF)
            spread, r = stats(m)
            nv = spread * r
            dy = dsec[rows, :]
            dyg = dy * g2_ref[...]
            up = up_ref[rows, :].astype(F32)
            dm = up + r * (
                dyg
                - jnp.mean(dyg, axis=-1, keepdims=True)
                - nv * jnp.mean(dyg * nv, axis=-1, keepdims=True)
            )
            db = dm.astype(BF)
            dbr_ref[rows, :] = db
            do_ref[rows, :] = (dot(db, wo_ref[...], NT) * li_ref[rows, :]).astype(BF)
            vec_ref[0:1, :] += jnp.sum(db.astype(F32), axis=0, keepdims=True)
            vec_ref[1:2, :] += jnp.sum(dy * nv, axis=0, keepdims=True)
            vec_ref[2:3, :] += jnp.sum(dy, axis=0, keepdims=True)
            vec_ref[3:4, :] += jnp.sum(up, axis=0, keepdims=True)
            sec_t[:, rows] = mix_ref[rows, :].T
        g = dot(sec_t[...], dbr_ref[...], NN).astype(BF)
        left = g[:, :half].reshape(dwo_k_ref.shape)
        right = g[:, half:].reshape(dwo_k_ref.shape)

        @pl.when(c == 0)
        def _():
            dwo_k_ref[...] = left
            dwo_s_ref[...] = right

        @pl.when(c == 1)
        def _():
            dwo_k_ref[...] = right
            dwo_s_ref[...] = left


def mlp(core, x, mix, li, up, wo, bo, g2, s2, w1, b1, w2, b2, nv, fw=768, tm=512):
    n, d = x.shape
    ff = w1.shape[1]
    nj = ff // fw
    pc = ff // nv if ff // nv < fw else fw
    pieces = ff // pc
    h = nj // 2

    def full(*s):
        return pl.BlockSpec(s, lambda j, c: (0,) * len(s), pipeline_mode=pl.Buffered(1))

    def jj(j, c):
        return (j + (1 - c[0]) * h) % nj

    npc = fw // pc
    dr = d // nv
    piece = pl.BlockSpec((npc, d // 2, pc), lambda j, c: (jj(j, c), 0, 0))
    grid_spec = pltpu.PrefetchScalarGridSpec(
        num_scalar_prefetch=1,
        grid=(nj,),
        in_specs=[
            full(n, d), full(n, d), full(n, d), full(n, d), full(d, d), full(1, d), full(1, d), full(1, d),
            pl.BlockSpec((d, fw), lambda j, c: (0, jj(j, c))),
            pl.BlockSpec((1, fw), lambda j, c: (0, jj(j, c))),
            pl.BlockSpec((fw, d), lambda j, c: (jj(j, c), 0)),
            full(1, d),
        ],
        out_specs=[
            full(n, d), full(n, d), full(n, d), full(nv, dr, d // 2), full(nv, dr, d // 2),
            pl.BlockSpec((nv, dr, fw), lambda j, c: (0, 0, jnp.maximum(j - h, 0))),
            pl.BlockSpec((nv, dr, fw), lambda j, c: (0, 0, jnp.minimum(j, h - 1))),
            piece, piece, full(8, d),
            pl.BlockSpec((1, fw), lambda j, c: (0, jj(j, c))),
        ],
        scratch_shapes=[
            pltpu.VMEM((n, d), BF), pltpu.VMEM((d, n), BF), pltpu.VMEM((d, n), BF),
            pltpu.VMEM((n, d), F32), pltpu.VMEM((n, d), F32), pltpu.VMEM((n, d), F32),
            pltpu.VMEM((n, fw), BF), pltpu.VMEM((n, fw), BF),
        ],
    )
    return pl.pallas_call(
        functools.partial(mlp_kernel, tm=tm, nj=nj),
        grid_spec=grid_spec,
        out_shape=[
            shape((n, d)), shape((n, d)), shape((n, d)), shape((nv, dr, d // 2)), shape((nv, dr, d // 2)),
            shape((nv, dr, ff // 2)), shape((nv, dr, ff // 2)), shape((pieces, d // 2, pc)), shape((pieces, d // 2, pc)),
            shape((8, d), F32), shape((1, ff), F32),
        ],
        compiler_params=params(),
        cost_estimate=pl.CostEstimate(flops=24 * n * d * ff, bytes_accessed=8 * d * ff, transcendentals=0),
        name="mlp",
    )(core, x, mix, li, up, wo, bo, g2, s2, w1, b1, w2, b2)


def reflect_kernel(c_ref, q_ref, k_ref, v_ref, o_ref, do_ref, p_ref, ft_ref, dq_ref, dk_ref, dv_ref, gk_ref, gs_ref, ds_ref, *, tq):
    n = k_ref.shape[0]
    low = lax.broadcasted_iota(jnp.int32, (tq, PAIR), 1) < HEAD_DIM
    q_t = q_ref[...].T
    do_t = do_ref[...].T
    scale = HEAD_DIM**-0.5
    dks, dvs = [], []
    for a in range(2):
        for t in range(n // tq):
            rows = pl.ds(t * tq, tq)
            do = do_ref[rows, :]
            zero = jnp.zeros_like(do)
            doa = jnp.where(low, do, zero) if a == 0 else jnp.where(low, zero, do)
            delta = jnp.sum(doa.astype(F32) * o_ref[rows, :].astype(F32), axis=-1, keepdims=True)
            dp = dot(doa, v_ref[...], NT)
            ds = (p_ref[a, rows, :].astype(F32) * (dp - delta)).astype(BF)
            ds_ref[rows, :] = ds
            dq = (dot(ds, k_ref[...], NN) * scale).astype(BF)
            dq_ref[rows, :] = dq if a == 0 else jnp.where(low, dq_ref[rows, :], dq)
        part = slice(HEAD_DIM * a, HEAD_DIM * (a + 1))
        dvs.append(dot(do_t[part], p_ref[a], NN))
        dks.append(dot(q_t[part], ds_ref[...], NN) * scale)
    dv = jnp.concatenate(dvs, axis=0).astype(BF).T
    dk = jnp.concatenate(dks, axis=0).astype(BF).T
    dv_ref[...] = dv
    dk_ref[...] = dk
    g = dot(ft_ref[...], jnp.concatenate([dq_ref[...], dk, dv], axis=1), NN).astype(BF)
    nv, rows, wide = gk_ref.shape
    g = g.reshape(nv, 2, rows, wide)

    @pl.when(c_ref[0] == 0)
    def _():
        gk_ref[...] = g[:, 0]
        gs_ref[...] = g[:, 1]

    @pl.when(c_ref[0] == 1)
    def _():
        gk_ref[...] = g[:, 1]
        gs_ref[...] = g[:, 0]


def reflect(core, packed, o, do, p, first_t, nv, start, count):
    n, w = packed.shape
    d = w // 3
    hp = d // PAIR

    def cols(off):
        return pl.BlockSpec((n, PAIR), lambda h, c: (0, h + off))

    piece = pl.BlockSpec((nv, d // nv // 2, 3 * PAIR), lambda h, c: (0, 0, h))
    return pl.pallas_call(
        functools.partial(reflect_kernel, tq=256),
        grid_spec=pltpu.PrefetchScalarGridSpec(
            num_scalar_prefetch=1,
            grid=(count,),
            in_specs=[
                cols(start), cols(start + hp), cols(start + 2 * hp), cols(start), cols(start),
                pl.BlockSpec((2, n, n), lambda h, c: (h + start, 0, 0)),
                pl.BlockSpec((d, n), lambda h, c: (0, 0)),
            ],
            out_specs=[cols(0)] * 3 + [piece] * 2,
            scratch_shapes=[pltpu.VMEM((n, n), BF)],
        ),
        out_shape=[shape((n, count * PAIR))] * 3 + [shape((nv, d // nv // 2, 3 * PAIR * count))] * 2,
        compiler_params=params(),
        cost_estimate=pl.CostEstimate(flops=80 * n * n * PAIR * count, bytes_accessed=4 * n * n * count, transcendentals=0),
        name="reflect",
    )(core, packed, packed, packed, o, do, p, first_t)


def back_kernel(*refs, chunks):
    x_ref, dbr_ref, w_ref, g_ref = refs[:4]
    parts = refs[4 : 4 + 3 * chunks]
    tg_ref, vec_ref = refs[4 + 3 * chunks :]

    @pl.when(pl.program_id(0) == 0)
    def _():
        vec_ref[...] = jnp.zeros_like(vec_ref)

    d = x_ref.shape[1]
    cw = d // chunks
    dy = None
    for i in range(3 * chunks):
        which, chunk = i % 3, i // 3
        at = which * d + chunk * cw
        part = dot(parts[i][...], w_ref[:, at : at + cw], NT)
        dy = part if dy is None else dy + part
        row = {0: 2, 2: 3}.get(which)
        if row is not None:
            vec_ref[row : row + 1, chunk * cw : (chunk + 1) * cw] += jnp.sum(parts[i][...].astype(F32), axis=0, keepdims=True)
    spread, r = stats(x_ref[...].astype(F32))
    nv = spread * r
    dyg = dy * g_ref[...]
    dx = r * (dyg - jnp.mean(dyg, axis=-1, keepdims=True) - nv * jnp.mean(dyg * nv, axis=-1, keepdims=True))
    tg_ref[...] = (dbr_ref[...].astype(F32) + dx).astype(BF)
    vec_ref[0:1, :] += jnp.sum(dy * nv, axis=0, keepdims=True)
    vec_ref[1:2, :] += jnp.sum(dy, axis=0, keepdims=True)


def project_back(x, dbr, w, g, parts):
    n, d = x.shape
    tm = 256
    row = pl.BlockSpec((tm, d), lambda i: (i, 0))

    def full(*s):
        return pl.BlockSpec(s, lambda i: (0, 0))

    chunks = len(parts) // 3
    return pl.pallas_call(
        functools.partial(back_kernel, chunks=chunks),
        grid=(n // tm,),
        in_specs=[row, row, full(d, 3 * d), full(1, d)] + [pl.BlockSpec((tm, d // chunks), lambda i: (i, 0))] * (3 * chunks),
        out_specs=[row, full(8, d)],
        out_shape=[shape((n, d)), shape((8, d), F32)],
        compiler_params=params(),
        cost_estimate=pl.CostEstimate(flops=6 * n * d * d, bytes_accessed=16 * n * d, transcendentals=0),
        name="project_back",
    )(x, dbr, w, g, *parts)


def exchange(x, axis, by):
    count = lax.axis_size(axis)
    return lax.ppermute(x, axis, [(i, i ^ by) for i in range(count)])


def pick(x, index, axis=0):
    return lax.dynamic_index_in_dim(x, index, axis, keepdims=False)


def total(arrays, dtype=BF):
    s = arrays[0].astype(F32)
    for a in arrays[1:]:
        s = s + a.astype(F32)
    return s.astype(dtype)


def volume_sum(kept, sent, dtype=BF):
    position = lax.axis_index("vol")
    held = [kept, exchange(sent, "seq", 1)]
    count = lax.axis_size("vol")
    bit = 1
    while bit < count:
        split = [a.reshape((a.shape[0] // 2, 2) + a.shape[1:]) for a in held]
        mine = (position // bit) % 2
        received = exchange(total([pick(a, 1 - mine, 1) for a in split], dtype), "vol", bit)
        held = [pick(a, mine, 1) for a in split] + [received]
        bit *= 2
    mine = total([a[0] for a in held], dtype)
    mine = total([mine, exchange(mine, "seq", 2)], dtype)
    return mine, exchange(mine, "seq", 1)


def on_device(
    volume_slices, volume_owner, tokens, cotangent, attend_gain, attend_shift, input_weight, query_bias, value_bias,
    output_weight, output_bias, mixer_gain, mixer_shift, expand_weight, expand_bias, reduce_weight, reduce_bias,
):
    slices, rows, d = tokens.shape
    ff = expand_weight.shape[1]
    nv = lax.axis_size("vol")
    peers = lax.axis_size("seq")
    me = lax.axis_index("seq")
    core_id = me % 2
    core = core_id.astype(jnp.int32).reshape(1)
    load = jnp.sum(jnp.where(volume_owner == lax.axis_index("vol"), volume_slices, 0))
    line = lambda v: v.astype(F32).reshape(1, -1)

    def to_slice(x, k):
        part = pick(x, me ^ k)
        return part if k == 0 else exchange(part, "seq", k)

    live = (jnp.arange(slices) < load).astype(cotangent.dtype)
    near = jnp.concatenate([to_slice(tokens, 0), to_slice(tokens, 1)])
    far_parts = [to_slice(tokens, k) for k in range(2, peers)]
    far = jnp.concatenate(far_parts)
    n = rows * peers
    bias = jnp.concatenate([line(query_bias), jnp.zeros((1, d), F32), line(value_bias)], axis=1)
    gain, shift = line(attend_gain), line(attend_shift)
    made = project_in(near, 0, n, None, gain, shift, input_weight, bias)
    x, first_t, packed = project_in(far, near.shape[0], n, made, gain, shift, input_weight, bias)
    cotangent, _ = lax.optimization_barrier((cotangent, far_parts[-1]))
    upstream = jnp.concatenate([to_slice(cotangent * live[:, None, None], k) for k in range(peers)])

    mixed, inverse, weights = attend(packed)
    (out, d_branch, d_mixed, dwo_k, dwo_s, dw1_k, dw1_s, dw2_k, dw2_s, vec_mid, db1) = mlp(
        core, x, mixed, inverse, upstream, output_weight, line(output_bias), line(mixer_gain), line(mixer_shift),
        expand_weight, line(expand_bias), reduce_weight, line(reduce_bias), nv,
    )
    if dw2_k.shape[0] != nv:
        regroup = lambda a: a.reshape(a.shape[0], d // 2, -1, ff // nv).swapaxes(1, 2).reshape(nv, d // 2, ff // nv)
        dw2_k, dw2_s = regroup(dw2_k), regroup(dw2_s)
    sum_dw2 = volume_sum(dw2_k, dw2_s)
    sum_dw1 = volume_sum(dw1_k, dw1_s)
    sum_dwo = volume_sum(dwo_k, dwo_s)

    pairs = d // PAIR
    chunks = 3
    parts, sum_dwi = [], []
    for i in range(chunks):
        dq, dk, dv, gk, gs = reflect(core, packed, mixed, d_mixed, weights, first_t, nv, i * pairs // chunks, pairs // chunks)
        parts += [dq, dk, dv]
        sum_dwi.append(volume_sum(gk, gs))
    d_tokens, vec_end = project_back(x, d_branch, input_weight, gain, parts)

    def home(x, dtype, mask):
        result = jnp.zeros((slices, rows, d), dtype)
        for k in range(peers):
            part = x[k * rows : (k + 1) * rows]
            if k:
                part = exchange(part, "seq", k)
            if mask:
                part = part * pick(live, me ^ k)
            result = lax.dynamic_update_index_in_dim(result, part.astype(dtype), me ^ k, 0)
        return result

    block_out = home(out, BF, True)
    tokens_grad = home(d_tokens, F32, False)

    rows_of = jnp.concatenate([vec_end[:4], vec_mid[:4], db1.reshape(nv, ff // d, d // nv).swapaxes(0, 1).reshape(ff // d, d)])
    pieces = rows_of.reshape(-1, nv, d // nv).swapaxes(0, 1)
    half = pieces.shape[1] // 2
    small = volume_sum(
        lax.dynamic_slice_in_dim(pieces, core_id * half, half, 1),
        lax.dynamic_slice_in_dim(pieces, (1 - core_id) * half, half, 1), F32,
    )

    def join(pair, axis):
        a, b = pair
        first = jnp.where(core_id == 0, a, b).astype(F32)
        second = jnp.where(core_id == 0, b, a).astype(F32)
        return jnp.concatenate([first, second], axis)

    vectors = join(small, 0)
    reduce_grad = join(sum_dw2, 0).T
    expand_grad = join(sum_dw1, 1)
    output_grad = join(sum_dwo, 1)
    per = pairs // chunks
    input_grad = jnp.concatenate(
        [join(s, 0).reshape(d // nv, per, 3, PAIR).swapaxes(1, 2).reshape(d // nv, 3, per * PAIR) for s in sum_dwi], axis=2
    ).reshape(d // nv, 3 * d)
    return (
        block_out, tokens_grad, vectors[0], vectors[1], input_grad, vectors[2], vectors[3], output_grad, vectors[4],
        vectors[5], vectors[6], expand_grad, vectors[8:].reshape(-1), reduce_grad, vectors[7],
    )


def solution(mesh):
    rows = P("vol", "seq", None)
    return jax.shard_map(
        on_device,
        mesh=mesh,
        in_specs=(P(), P(), rows, rows) + (P(),) * 13,
        out_specs=(rows, rows, P("vol"), P("vol"), P("vol", None), P("vol"), P("vol"), P("vol", None), P("vol"), P("vol"),
                   P("vol"), P("vol", None), P("vol"), P("vol", None), P("vol")),
        check_vma=False,
    )
```

```python
import functools

import jax
import jax.numpy as jnp
from jax import lax
from jax.experimental import pallas as pl
from jax.experimental.pallas import tpu as pltpu
from jax.sharding import PartitionSpec as P

HEAD_DIM = 64
PAIR = 2 * HEAD_DIM
LOG2E = 1.4426950408889634
PIECES = 8
CHUNKS = 3
ROW = {n: i for i, n in enumerate(("ag", "ash", "qb", "zero", "vb", "ob", "mg", "ms", "rb"))}
BF = jnp.bfloat16
F32 = jnp.float32
NN = (((1,), (0,)), ((), ()))
NT = (((1,), (1,)), ((), ()))
TAIL = (
    0.11962928008603971,
    0.12075423895539067,
    0.09991176086876633,
    0.12856720585766357,
    -0.05369390237929985,
    0.20636430391507077,
    -0.15720912816414995,
    0.03567616760586865,
)


def dot(a, b, dims):
    return lax.dot_general(a, b, dims, preferred_element_type=F32)


def params():
    return pltpu.CompilerParams(vmem_limit_bytes=60 << 20)


def line(ref, name):
    return ref[ROW[name] : ROW[name] + 1, :]


def shape(dims, dtype=BF):
    return jax.ShapeDtypeStruct(dims, dtype)


def normal(h):
    a = jnp.abs(h)
    t = 1.0 / (1.0 + 0.3 * a)
    s = TAIL[7] * t + TAIL[6]
    for c in TAIL[5::-1]:
        s = s * t + c
    e = jnp.exp2(h * h * (-0.5 * LOG2E))
    tail = s * t * e
    return jnp.where(h >= 0, 1.0 - tail, tail), e * 0.3989422804014327


def stats(v):
    spread = v - jnp.mean(v, axis=-1, keepdims=True)
    return spread, lax.rsqrt(jnp.mean(spread * spread, axis=-1, keepdims=True) + 1e-6)


def in_kernel(x_ref, vec_ref, w_ref, *rest):
    x_out, first_t, packed = rest[-3:]
    x = x_ref[...]
    d = x.shape[1]
    spread, r = stats(x.astype(F32))
    f = (spread * r * line(vec_ref, "ag") + line(vec_ref, "ash")).astype(BF)
    x_out[...] = x
    for i, bias in enumerate(("qb", "zero", "vb")):
        packed[:, i * d : (i + 1) * d] = (dot(f, w_ref[:, i * d : (i + 1) * d], NN) + line(vec_ref, bias)).astype(BF)
    first_t[...] = f.T


def project_in(part, offset, total, before, vec, weight):
    rows, d = part.shape
    wide = weight.shape[1]
    tm = 256
    first_block = offset // tm

    def full(a):
        return pl.BlockSpec(a.shape, lambda i: (0, 0), pipeline_mode=pl.Buffered(1))

    in_specs = [pl.BlockSpec((tm, d), lambda i: (i, 0)), full(vec), full(weight)]
    args = [part, vec, weight]
    aliases = {}
    if before is not None:
        aliases = {3: 0, 4: 1, 5: 2}
        in_specs += [pl.BlockSpec(memory_space=pl.ANY)] * 3
        args += list(before)
    return pl.pallas_call(
        in_kernel,
        grid=(rows // tm,),
        in_specs=in_specs,
        out_specs=[
            pl.BlockSpec((tm, d), lambda i: (i + first_block, 0)),
            pl.BlockSpec((d, tm), lambda i: (0, i + first_block)),
            pl.BlockSpec((tm, wide), lambda i: (i + first_block, 0)),
        ],
        out_shape=[shape((total, d)), shape((d, total)), shape((total, wide))],
        input_output_aliases=aliases,
        compiler_params=params(),
        cost_estimate=pl.CostEstimate(flops=6 * rows * d * wide, bytes_accessed=2 * (d * wide + rows * (wide + 3 * d)), transcendentals=0),
        name="project_in",
    )(*args)


def attend_kernel(q_ref, k_ref, v_ref, o_ref, inv_ref, p_ref, vx_ref, *, tq):
    n = k_ref.shape[0]
    vx_ref[:, :PAIR] = v_ref[...]
    vx_ref[:, PAIR:] = jnp.ones((n, PAIR), BF)
    low = lax.broadcasted_iota(jnp.int32, (tq, PAIR), 1) < HEAD_DIM
    for t in range(n // tq):
        rows = pl.ds(t * tq, tq)
        q = q_ref[rows, :]
        zero = jnp.zeros_like(q)
        outs = []
        for a in range(2):
            qa = jnp.where(low, q, zero) if a == 0 else jnp.where(low, zero, q)
            s = dot(qa, k_ref[...], NT)
            top = jnp.max(s, axis=-1, keepdims=True)
            p = jnp.exp2((s - top) * (LOG2E * HEAD_DIM**-0.5)).astype(BF)
            p_ref[a, rows, :] = p
            both = dot(p, vx_ref[...], NN)
            inv = 1.0 / both[:, PAIR:]
            outs.append((both[:, :PAIR] * inv, inv))
        o_ref[rows, :] = jnp.where(low, outs[0][0], outs[1][0]).astype(BF)
        inv_ref[rows, :] = jnp.where(low, outs[0][1], outs[1][1])


def attend(packed):
    n, w = packed.shape
    d = w // 3
    hp = d // PAIR

    def cols(off):
        return pl.BlockSpec((n, PAIR), lambda h: (0, h + off))

    return pl.pallas_call(
        functools.partial(attend_kernel, tq=128),
        grid=(hp,),
        in_specs=[cols(0), cols(hp), cols(2 * hp)],
        out_specs=[cols(0), cols(0), pl.BlockSpec((2, n, n), lambda h: (h, 0, 0))],
        out_shape=[shape((n, d)), shape((n, d), F32), shape((2 * hp, n, n))],
        scratch_shapes=[pltpu.VMEM((n, 2 * PAIR), BF)],
        compiler_params=params(),
        cost_estimate=pl.CostEstimate(flops=16 * n * n * d, bytes_accessed=4 * n * n * hp, transcendentals=0),
        name="attend",
    )(packed, packed, packed)


def middle_kernel(x_ref, mix_ref, wo_ref, vec_ref, mid_ref, sec_ref):
    m = x_ref[...].astype(F32) + dot(mix_ref[...], wo_ref[...], NN) + line(vec_ref, "ob")
    mid_ref[...] = m
    spread, r = stats(m)
    sec_ref[...] = (spread * r * line(vec_ref, "mg") + line(vec_ref, "ms")).astype(BF)


def middle_and_second(x, mix, wo, vec, tm=256):
    n, d = x.shape
    row = pl.BlockSpec((tm, d), lambda i: (i, 0))

    def full(a):
        return pl.BlockSpec(a.shape, lambda i: (0, 0), pipeline_mode=pl.Buffered(1))

    return pl.pallas_call(
        middle_kernel,
        grid=(n // tm,),
        in_specs=[row, row, full(wo), full(vec)],
        out_specs=[row, row],
        out_shape=[shape((n, d), F32), shape((n, d))],
        compiler_params=params(),
        cost_estimate=pl.CostEstimate(flops=6 * n * d * d, bytes_accessed=10 * n * d, transcendentals=0),
        name="middle",
    )(x, mix, wo, vec)


def by_piece(g):
    rows = g.shape[0] // PIECES
    return [g[:, i : i + 128].reshape(PIECES, rows, 128) for i in range(0, g.shape[1], 128)]


def hidden_kernel(c_ref, sec_ref, up_ref, w1_ref, w2_ref, b1_ref, act_ref, dh_ref, gk_ref, gs_ref, db1_ref, sec_t, up_t, act, dh, *, sub):
    t = pl.program_id(0)
    tm, d = sec_ref.shape
    wide = act_ref.shape[1]
    rows = pl.ds(pl.multiple_of(t * tm, tm), tm)
    sec = sec_ref[...]
    up = up_ref[...]

    @pl.when(t == 0)
    def _():
        db1_ref[...] = jnp.zeros_like(db1_ref)

    for at in range(0, wide, sub):
        cols = slice(at, at + sub)
        h = dot(sec, w1_ref[:, cols], NN) + b1_ref[:, cols]
        da = dot(up, w2_ref[cols, :], NT)
        cdf, pdf = normal(h)
        a = (h * cdf).astype(BF)
        dhv = (da * (cdf + h * pdf)).astype(BF)
        act_ref[:, cols] = a
        dh_ref[:, cols] = dhv
        act[rows, cols] = a
        dh[rows, cols] = dhv
        db1_ref[:, cols] += jnp.sum(dhv.astype(F32), axis=0, keepdims=True)
    sec_t[:, rows] = sec.T
    up_t[:, rows] = up.T

    @pl.when(t == pl.num_programs(0) - 1)
    def _():
        c = c_ref[0]
        per = d // PIECES
        for ref, mine in ((gs_ref, 1 - c), (gk_ref, c)):
            half = wide // 2
            g = dot(sec_t[...], dh[:, pl.ds(pl.multiple_of(mine * half, half), half)], NN).astype(BF)
            for i, block in enumerate(by_piece(g)):
                ref[:, i * per : (i + 1) * per, :] = block
            at = half // 128 * per
            half = d // 2
            g = dot(up_t[pl.ds(pl.multiple_of(mine * half, half), half), :], act[...], NN).astype(BF)
            for v in range(PIECES):
                ref[v, at:, :] = g[:, v * 128 : (v + 1) * 128]


def hidden_part(core, sec, up, w1, w2, b1, i, tm=256, sub=512):
    n, d = sec.shape
    wide = w1.shape[2]
    assert wide == 128 * PIECES

    def full(*s):
        return pl.BlockSpec(s, lambda t, c: (0,) * len(s), pipeline_mode=pl.Buffered(1))

    def chunk(*s):
        return pl.BlockSpec((None,) + s, lambda t, c: (i,) + (0,) * len(s), pipeline_mode=pl.Buffered(1))

    row = pl.BlockSpec((tm, d), lambda t, c: (t, 0))
    row_wide = pl.BlockSpec((tm, wide), lambda t, c: (t, 0))
    g = (PIECES, d // 2 + wide // 256 * d // PIECES, 128)
    return pl.pallas_call(
        functools.partial(hidden_kernel, sub=sub),
        grid_spec=pltpu.PrefetchScalarGridSpec(
            num_scalar_prefetch=1,
            grid=(n // tm,),
            in_specs=[row, row, chunk(d, wide), chunk(wide, d), chunk(1, wide)],
            out_specs=[row_wide, row_wide, full(*g), full(*g), full(1, wide)],
            scratch_shapes=[pltpu.VMEM((d, n), BF), pltpu.VMEM((d, n), BF), pltpu.VMEM((n, wide), BF), pltpu.VMEM((n, wide), BF)],
        ),
        out_shape=[shape((n, wide)), shape((n, wide)), shape(g), shape(g), shape((1, wide), F32)],
        compiler_params=params(),
        cost_estimate=pl.CostEstimate(flops=12 * n * d * wide, bytes_accessed=8 * d * wide, transcendentals=0),
        name="hidden",
    )(core, sec, up, w1, w2, b1)


def outer_kernel(c_ref, *refs, chunks):
    acts, dhs = refs[:chunks], refs[chunks : 2 * chunks]
    mid_ref, up_ref, mix_ref, li_ref, wo_ref, w1_ref, w2_ref, vec_ref = refs[2 * chunks : 2 * chunks + 8]
    out_ref, dbr_ref, do_ref, gk_ref, gs_ref, sums_ref, mix_t, dbr = refs[2 * chunks + 8 :]
    t = pl.program_id(0)
    tm, d = mid_ref.shape
    rows = pl.ds(pl.multiple_of(t * tm, tm), tm)

    @pl.when(t == 0)
    def _():
        sums_ref[...] = jnp.zeros_like(sums_ref)

    m = mid_ref[...]
    dy = dot(dhs[0][...], w1_ref[0], NT)
    for i in range(1, chunks):
        dy += dot(dhs[i][...], w1_ref[i], NT)
    o = dot(acts[0][...], w2_ref[0], NN)
    for i in range(1, chunks):
        o += dot(acts[i][...], w2_ref[i], NN)
    spread, r = stats(m)
    nv = spread * r
    dyg = dy * line(vec_ref, "mg")
    up = up_ref[...].astype(F32)
    dm = up + r * (dyg - jnp.mean(dyg, axis=-1, keepdims=True) - nv * jnp.mean(dyg * nv, axis=-1, keepdims=True))
    db = dm.astype(BF)
    dbr_ref[...] = db
    dbr[rows, :] = db
    out_ref[...] = (m + o + line(vec_ref, "rb")).astype(BF)
    do_ref[...] = (dot(db, wo_ref[...], NT) * li_ref[...]).astype(BF)
    sums_ref[0:1, :] += jnp.sum(db.astype(F32), axis=0, keepdims=True)
    sums_ref[1:2, :] += jnp.sum(dy * nv, axis=0, keepdims=True)
    sums_ref[2:3, :] += jnp.sum(dy, axis=0, keepdims=True)
    sums_ref[3:4, :] += jnp.sum(up, axis=0, keepdims=True)
    mix_t[:, rows] = mix_ref[...].T

    @pl.when(t == pl.num_programs(0) - 1)
    def _():
        half = d // 2
        per = d // PIECES
        for ref, mine in ((gs_ref, 1 - c_ref[0]), (gk_ref, c_ref[0])):
            g = dot(mix_t[...], dbr[:, pl.ds(pl.multiple_of(mine * half, half), half)], NN).astype(BF)
            for i, block in enumerate(by_piece(g)):
                ref[:, i * per : (i + 1) * per, :] = block


def outer(core, acts, dhs, mid, up, mix, li, wo, w1, w2, vec, tm=256):
    n, d = mid.shape
    wide = acts[0].shape[1]
    chunks = len(acts)

    def full(*s):
        return pl.BlockSpec(s, lambda t, c: (0,) * len(s), pipeline_mode=pl.Buffered(1))

    row = pl.BlockSpec((tm, d), lambda t, c: (t, 0))
    row_wide = pl.BlockSpec((tm, wide), lambda t, c: (t, 0))
    g = (PIECES, d // 256 * d // PIECES, 128)
    return pl.pallas_call(
        functools.partial(outer_kernel, chunks=chunks),
        grid_spec=pltpu.PrefetchScalarGridSpec(
            num_scalar_prefetch=1,
            grid=(n // tm,),
            in_specs=[row_wide] * (2 * chunks) + [row] * 4 + [full(*wo.shape), full(*w1.shape), full(*w2.shape), full(*vec.shape)],
            out_specs=[row, row, row, full(*g), full(*g), full(8, d)],
            scratch_shapes=[pltpu.VMEM((d, n), BF), pltpu.VMEM((n, d), BF)],
        ),
        out_shape=[shape((n, d))] * 3 + [shape(g), shape(g), shape((8, d), F32)],
        compiler_params=params(),
        cost_estimate=pl.CostEstimate(flops=8 * n * d * (wide * chunks + d), bytes_accessed=8 * d * wide * chunks, transcendentals=0),
        name="outer",
    )(core, *acts, *dhs, mid, up, mix, li, wo, w1, w2, vec)


def reflect_kernel(c_ref, q_ref, k_ref, v_ref, o_ref, do_ref, p_ref, ft_ref, dq_ref, dk_ref, dv_ref, gk_ref, gs_ref, ds_ref, *, tq):
    n = k_ref.shape[0]
    low = lax.broadcasted_iota(jnp.int32, (tq, PAIR), 1) < HEAD_DIM
    q_t = q_ref[...].T
    do_t = do_ref[...].T
    scale = HEAD_DIM**-0.5
    dks, dvs = [], []
    for a in range(2):
        for t in range(n // tq):
            rows = pl.ds(t * tq, tq)
            do = do_ref[rows, :]
            zero = jnp.zeros_like(do)
            doa = jnp.where(low, do, zero) if a == 0 else jnp.where(low, zero, do)
            delta = jnp.sum(doa.astype(F32) * o_ref[rows, :].astype(F32), axis=-1, keepdims=True)
            dp = dot(doa, v_ref[...], NT)
            ds = (p_ref[a, rows, :].astype(F32) * (dp - delta)).astype(BF)
            ds_ref[rows, :] = ds
            dq = (dot(ds, k_ref[...], NN) * scale).astype(BF)
            dq_ref[rows, :] = dq if a == 0 else jnp.where(low, dq_ref[rows, :], dq)
        part = slice(HEAD_DIM * a, HEAD_DIM * (a + 1))
        dvs.append(dot(do_t[part], p_ref[a], NN))
        dks.append(dot(q_t[part], ds_ref[...], NN) * scale)
    dv = jnp.concatenate(dvs, axis=0).astype(BF).T
    dk = jnp.concatenate(dks, axis=0).astype(BF).T
    dv_ref[...] = dv
    dk_ref[...] = dk
    g = dot(ft_ref[...], jnp.concatenate([dq_ref[...], dk, dv], axis=1), NN).astype(BF)
    per = g.shape[0] // PIECES
    h = pl.program_id(0)
    for step, ref in enumerate((gs_ref, gk_ref)):

        @pl.when(h == step)
        def _():
            for i, block in enumerate(by_piece(g)):
                ref[:, i * per : (i + 1) * per, :] = block


def reflect(core, packed, o, do, p, first_t, start):
    n, w = packed.shape
    d = w // 3
    hp = d // PAIR

    def which(h, c):
        return (h + 1 - c[0]) % 2

    def cols(off):
        return pl.BlockSpec((n, PAIR), lambda h, c: (0, which(h, c) + off))

    g = (PIECES, 3 * (d // PIECES), 128)
    piece = pl.BlockSpec(g, lambda h, c: (0, 0, 0), pipeline_mode=pl.Buffered(1))
    return pl.pallas_call(
        functools.partial(reflect_kernel, tq=256),
        grid_spec=pltpu.PrefetchScalarGridSpec(
            num_scalar_prefetch=1,
            grid=(2,),
            in_specs=[
                cols(start), cols(start + hp), cols(start + 2 * hp), cols(start), cols(start),
                pl.BlockSpec((2, n, n), lambda h, c: (which(h, c) + start, 0, 0)),
                pl.BlockSpec((d, n), lambda h, c: (0, 0), pipeline_mode=pl.Buffered(1)),
            ],
            out_specs=[cols(0)] * 3 + [piece] * 2,
            scratch_shapes=[pltpu.VMEM((n, n), BF)],
        ),
        out_shape=[shape((n, 2 * PAIR))] * 3 + [shape(g)] * 2,
        compiler_params=params(),
        cost_estimate=pl.CostEstimate(flops=160 * n * n * PAIR, bytes_accessed=8 * n * n, transcendentals=0),
        name="reflect",
    )(core, packed, packed, packed, o, do, p, first_t)


def back_kernel(*refs, chunks):
    x_ref, dbr_ref, w_ref, vec_in = refs[:4]
    parts = refs[4 : 4 + 3 * chunks]
    tg_ref, vec_ref = refs[4 + 3 * chunks :]

    @pl.when(pl.program_id(0) == 0)
    def _():
        vec_ref[...] = jnp.zeros_like(vec_ref)

    d = x_ref.shape[1]
    cw = d // chunks
    dy = None
    for i in range(3 * chunks):
        which, chunk = i % 3, i // 3
        at = which * d + chunk * cw
        part = dot(parts[i][...], w_ref[:, at : at + cw], NT)
        dy = part if dy is None else dy + part
        row = {0: 2, 2: 3}.get(which)
        if row is not None:
            vec_ref[row : row + 1, chunk * cw : (chunk + 1) * cw] += jnp.sum(parts[i][...].astype(F32), axis=0, keepdims=True)
    spread, r = stats(x_ref[...].astype(F32))
    nv = spread * r
    dyg = dy * line(vec_in, "ag")
    dx = r * (dyg - jnp.mean(dyg, axis=-1, keepdims=True) - nv * jnp.mean(dyg * nv, axis=-1, keepdims=True))
    tg_ref[...] = (dbr_ref[...].astype(F32) + dx).astype(BF)
    vec_ref[0:1, :] += jnp.sum(dy * nv, axis=0, keepdims=True)
    vec_ref[1:2, :] += jnp.sum(dy, axis=0, keepdims=True)


def project_back(x, dbr, w, vec, parts):
    n, d = x.shape
    tm = 256
    row = pl.BlockSpec((tm, d), lambda i: (i, 0))

    def full(*s):
        return pl.BlockSpec(s, lambda i: (0, 0))

    chunks = len(parts) // 3
    return pl.pallas_call(
        functools.partial(back_kernel, chunks=chunks),
        grid=(n // tm,),
        in_specs=[row, row, full(d, 3 * d), full(*vec.shape)] + [pl.BlockSpec((tm, d // chunks), lambda i: (i, 0))] * (3 * chunks),
        out_specs=[row, full(8, d)],
        out_shape=[shape((n, d)), shape((8, d), F32)],
        compiler_params=params(),
        cost_estimate=pl.CostEstimate(flops=6 * n * d * d, bytes_accessed=16 * n * d, transcendentals=0),
        name="project_back",
    )(x, dbr, w, vec, *parts)


def exchange(x, axis, by):
    count = lax.axis_size(axis)
    return lax.ppermute(x, axis, [(i, i ^ by) for i in range(count)])


def pick(x, index, axis=0):
    return lax.dynamic_index_in_dim(x, index, axis, keepdims=False)


def add_up(arrays, dtype=BF):
    s = arrays[0].astype(F32)
    for a in arrays[1:]:
        s = s + a.astype(F32)
    return s.astype(dtype)


def after(x, *others):
    return lax.optimization_barrier((x,) + others)[0]


class Sum:
    def __init__(self, order, dtype=BF):
        self.order = list(order)
        self.dtype = dtype
        self.parts = []
        self.split_x = self.order[0] == "x"
        self.gathered = None

    def start(self, *segments):
        self.open = [0, 1, 2]
        self.parts = [[a.reshape((2, 2, 2) + a.shape[1:]) for a in terms] for terms in segments]
        return self

    def sends(self):
        stage = self.order[0]
        position = lax.axis_index("vol")
        unit = lax.axis_size("vol") // PIECES
        if stage == "x" and self.split_x:
            mine = (lax.axis_index("seq") // 2) % 2
            cut = [[a.reshape(a.shape[:-2] + (2, a.shape[-2] // 2, 128)) for a in t] for t in self.parts]
            axis = 3
        elif stage in (0, 1, 2):
            axis = len(self.open) - 1 - self.open.index(stage)
            mine = (position // (unit << stage)) % 2
            cut = self.parts
        else:
            self.keep = [[add_up(t, self.dtype)] for t in self.parts]
            return jnp.concatenate([t[0] for t in self.keep], axis=-2)
        out = [add_up([pick(a, 1 - mine, axis) for a in t], self.dtype) for t in cut]
        self.keep = [[pick(a, mine, axis) for a in t] for t in cut]
        return jnp.concatenate(out, axis=-2) if len(out) > 1 else out[0]

    def carry(self, sent):
        stage = self.order.pop(0)
        unit = lax.axis_size("vol") // PIECES
        if stage == "x":
            received = exchange(sent, "seq", 2)
        elif stage in (0, 1, 2):
            received = exchange(sent, "vol", unit << stage)
            self.open.remove(stage)
        else:
            received = exchange(sent, "vol", stage[1])
        at = 0
        for t in self.keep:
            rows = t[0].shape[-2]
            t.append(received[..., at : at + rows, :])
            at += rows
        self.parts = self.keep

    def step(self):
        sent = self.sends()
        self.carry(sent)
        return sent

    def totals(self):
        return [add_up(t, self.dtype) for t in self.parts]


def on_device(
    volume_slices, volume_owner, tokens, cotangent, attend_gain, attend_shift, input_weight, query_bias, value_bias,
    output_weight, output_bias, mixer_gain, mixer_shift, expand_weight, expand_bias, reduce_weight, reduce_bias,
):
    slices, rows, d = tokens.shape
    ff = expand_weight.shape[1]
    nv = lax.axis_size("vol")
    peers = lax.axis_size("seq")
    me = lax.axis_index("seq")
    core_id = me % 2
    x_id = (me // 2) % 2
    core = core_id.astype(jnp.int32).reshape(1)
    n = rows * peers
    spare = [(("all", 1 << i)) for i in range((nv // PIECES).bit_length() - 1)]

    def from_peers(x, ks):
        parts = [pick(x, me ^ k) for k in ks]
        return [p if k == 0 else exchange(p, "seq", k) for p, k in zip(parts, ks)]

    far_parts = from_peers(tokens, (3, 2))
    near_parts = from_peers(tokens, (0, 1))
    zero = jnp.zeros((d,), BF)
    vec = jnp.concatenate(
        [attend_gain, attend_shift, query_bias, zero, value_bias, output_bias, mixer_gain, mixer_shift, reduce_bias] + [zero] * 7
    ).astype(F32).reshape(16, d)
    wide = ff // CHUNKS
    lanes = wide // PIECES
    w1 = expand_weight.reshape(d, PIECES, CHUNKS, lanes).transpose(2, 0, 1, 3).reshape(CHUNKS, d, wide)
    w2 = reduce_weight.reshape(PIECES, CHUNKS, lanes, d).swapaxes(0, 1).reshape(CHUNKS, wide, d)
    b1 = expand_bias.astype(F32).reshape(PIECES, CHUNKS, lanes).swapaxes(0, 1).reshape(CHUNKS, 1, wide)
    load = jnp.sum(jnp.where(volume_owner == lax.axis_index("vol"), volume_slices, 0))
    live = (jnp.arange(slices) < load).astype(BF)

    made = project_in(jnp.concatenate(near_parts), 0, n, None, vec, input_weight)
    far = jnp.concatenate([after(far_parts[1], made[2], w1, w2, b1), far_parts[0]])
    x, first_t, packed = project_in(far, 2 * rows, n, made, vec, input_weight)
    upstream = jnp.concatenate(from_peers(after(cotangent, far_parts[0], far_parts[1]) * live[:, None, None], (0, 1, 2, 3)))

    mixed, inverse, weights = attend(packed)
    mid, second = middle_and_second(x, mixed, output_weight, vec)

    def to_core(g):
        return exchange(g, "seq", 1)

    acts, dhs, db1 = [], [], []

    def hidden(token, i):
        a, g, gk, gs, b = hidden_part(token, second, upstream, w1, w2, b1, i)
        acts.append(a)
        dhs.append(g)
        db1.append(b)
        return gk, gs

    Y, Z1, Z2 = 0, 1, 2
    k0, s0 = hidden(core, 0)
    r0 = to_core(s0)
    k1, s1 = hidden(after(core, s0), 1)
    r1 = to_core(s1)
    ga = Sum(["x", Y, Z1, Z2] + spare).start([k0, r0])
    sent = ga.step()
    k2, s2 = hidden(after(core, s1, sent), 2)
    r2 = to_core(s2)
    gb = Sum([Z1, Z2, Y] + spare + ["x"]).start([k1, r1])
    sent = gb.step()
    out, d_branch, d_mixed, k3, s3, sums_mid = outer(
        after(core, s2, sent), acts, dhs, mid, upstream, mixed, inverse, output_weight, w1, w2, vec
    )

    def blocks(x):
        return [x[k * rows : (k + 1) * rows] for k in range(peers)]

    r3 = to_core(s3)
    outs = blocks(out)
    outs = [outs[0]] + [exchange(outs[k], "seq", k) for k in (1, 2, 3)]
    sent = ga.step()
    parts = []

    def reflect_part(token, i):
        dq, dk, dv, gk, gs = reflect(token, packed, mixed, d_mixed, weights, first_t, 2 * i)
        parts.extend([dq, dk, dv])
        return gk, gs

    p0, q0 = reflect_part(after(core, s3, sent), 0)
    t0 = to_core(q0)
    gc = Sum([Y, Z1, Z2] + spare + ["x"]).start([k2, r2], [k3, r3])
    sent = [ga.step(), gb.step(), gc.step()]
    p1, q1 = reflect_part(after(core, q0, *sent), 1)
    t1 = to_core(q1)
    sent = [ga.step()]
    p2, q2 = reflect_part(after(core, q1, *sent), 2)
    t2 = to_core(q2)
    gd = Sum(["x", Y, Z1, Z2] + spare).start([p0, t0], [p1, t1])
    ge = Sum([Y, Z1, Z2] + spare + ["x"]).start([p2, t2])
    sent = [gb.step(), gc.step(), gd.step(), ge.step()]
    d_tokens, sums_end = project_back(after(x, *sent), d_branch, input_weight, vec, parts)

    tgs = blocks(d_tokens)
    tgs = [tgs[0]] + [exchange(tgs[k], "seq", k) for k in (1, 2, 3)]
    per = d // PIECES
    small = jnp.concatenate(
        [sums_end[:4], sums_mid[:4]] + [jnp.concatenate([b.reshape(PIECES, lanes) for b in db1], axis=1).reshape(PIECES, ff // d, per).swapaxes(0, 1).reshape(ff // d, d)]
    )
    nsmall = small.shape[0]
    small = small.reshape(nsmall, PIECES, per).swapaxes(0, 1).reshape(PIECES, nsmall * per // 128, 128)
    gv = Sum([Y, Z1, Z2] + spare + ["x"], F32).start([small, to_core(small)])
    for group in (ge, gv, gd, gc, gb):
        if group.order:
            group.step()
    for _ in range(6):
        for group in (ge, gv, gd, gc, gb, ga):
            if group.order:
                group.step()
    waited = ge.parts[0] + gv.parts[0] + gd.parts[0]

    def home(arrays, dtype, mask):
        result = jnp.zeros((slices, rows, d), dtype)
        for k in range(peers):
            part = arrays[k]
            if mask:
                part = part * pick(live, me ^ k)
            result = lax.dynamic_update_index_in_dim(result, part.astype(dtype), me ^ k, 0)
        return result

    block_out = home(outs, BF, True)
    tokens_grad = home([after(t, *waited) for t in tgs], F32, False)

    def gather_core(total, axis=0):
        other = to_core(total)
        first = jnp.where(core_id == 0, total, other)
        second = jnp.where(core_id == 0, other, total)
        return jnp.concatenate([first, second], axis=axis)

    def gather_x(total):
        other = exchange(total, "seq", 2)
        first = jnp.where(x_id == 0, total, other)
        second = jnp.where(x_id == 0, other, total)
        return jnp.concatenate([first, second], axis=-2)

    def squeeze(a):
        return a.reshape(a.shape[-2:])

    half_ff = wide // 256 * per
    chunk_totals = []
    a, = ga.totals()
    b, = gb.totals()
    c, c_o = gc.totals()
    d0, d1 = gd.totals()
    e, = ge.totals()
    a = gather_x(squeeze(a))
    d0, d1 = gather_x(squeeze(d0)), gather_x(squeeze(d1))
    stack = jnp.concatenate([a, squeeze(b), squeeze(c), squeeze(c_o), d0, d1, squeeze(e)], axis=0)
    other = to_core(stack)
    low = jnp.where(core_id == 0, stack, other)
    high = jnp.where(core_id == 0, other, stack)
    size = a.shape[0]
    ex, re = [], []
    for i in range(CHUNKS):
        lo, hi = low[i * size : (i + 1) * size], high[i * size : (i + 1) * size]
        ex.append(jnp.concatenate([lo[:half_ff].reshape(-1, per, 128), hi[:half_ff].reshape(-1, per, 128)], axis=0))
        re.append(jnp.concatenate([lo[half_ff:], hi[half_ff:]], axis=0))
    expand_grad = jnp.stack(ex, axis=1).transpose(2, 0, 1, 3).reshape(per, ff).astype(F32)
    reduce_grad = jnp.concatenate(re, axis=1).T.astype(F32)
    at = CHUNKS * size
    blocks_o = per * (d // 256)
    output_grad = jnp.concatenate([low[at : at + blocks_o], high[at : at + blocks_o]], axis=0).reshape(-1, per, 128).swapaxes(0, 1).reshape(per, d).astype(F32)
    at += blocks_o
    pair_rows = 3 * per
    seq = []
    for i in range(CHUNKS):
        seq += [low[at : at + pair_rows], high[at : at + pair_rows]]
        at += pair_rows
    input_grad = jnp.stack(seq).reshape(2 * CHUNKS, 3, per, 128).transpose(2, 1, 0, 3).reshape(per, 3 * d).astype(F32)
    v, = gv.totals()
    vectors = squeeze(v).reshape(nsmall, per)

    if nv > PIECES:
        unit = nv // PIECES
        sub = lax.axis_index("vol") % unit
        cut = lambda a, axis: lax.dynamic_slice_in_dim(a, sub * (a.shape[axis] // unit), a.shape[axis] // unit, axis)
        expand_grad, reduce_grad, output_grad, input_grad = [cut(a, 0) for a in (expand_grad, reduce_grad, output_grad, input_grad)]
        expand_bias_grad = cut(vectors[8:].reshape(-1), 0)
        vectors = cut(vectors, 1)
    else:
        expand_bias_grad = vectors[8:].reshape(-1)
    return (
        block_out, tokens_grad, vectors[0], vectors[1], input_grad, vectors[2], vectors[3], output_grad, vectors[4],
        vectors[5], vectors[6], expand_grad, expand_bias_grad, reduce_grad, vectors[7],
    )


def solution(mesh):
    rows = P("vol", "seq", None)
    return jax.shard_map(
        on_device,
        mesh=mesh,
        in_specs=(P(), P(), rows, rows) + (P(),) * 13,
        out_specs=(rows, rows, P("vol"), P("vol"), P("vol", None), P("vol"), P("vol"), P("vol", None), P("vol"), P("vol"),
                   P("vol"), P("vol", None), P("vol"), P("vol", None), P("vol")),
        check_vma=False,
    )
```

```python
import functools

import jax
import jax.numpy as jnp
from jax import lax
from jax.experimental import pallas as pl
from jax.experimental.pallas import tpu as pltpu
from jax.sharding import PartitionSpec as P

HEAD_DIM = 64
PAIR = 2 * HEAD_DIM
LOG2E = 1.4426950408889634
PIECES = 8
CHUNKS = 3
ROW = {n: i for i, n in enumerate(("ag", "ash", "qb", "zero", "vb", "ob", "mg", "ms", "rb"))}
BF = jnp.bfloat16
F32 = jnp.float32
NN = (((1,), (0,)), ((), ()))
NT = (((1,), (1,)), ((), ()))
TAIL = (
    0.11962928008603971,
    0.12075423895539067,
    0.09991176086876633,
    0.12856720585766357,
    -0.05369390237929985,
    0.20636430391507077,
    -0.15720912816414995,
    0.03567616760586865,
)


def dot(a, b, dims):
    return lax.dot_general(a, b, dims, preferred_element_type=F32)


def params():
    return pltpu.CompilerParams(vmem_limit_bytes=60 << 20)


def line(ref, name):
    return ref[ROW[name] : ROW[name] + 1, :]


def shape(dims, dtype=BF):
    return jax.ShapeDtypeStruct(dims, dtype)


def normal(h):
    a = jnp.abs(h)
    t = 1.0 / (1.0 + 0.3 * a)
    s = TAIL[7] * t + TAIL[6]
    for c in TAIL[5::-1]:
        s = s * t + c
    e = jnp.exp2(h * h * (-0.5 * LOG2E))
    tail = s * t * e
    return jnp.where(h >= 0, 1.0 - tail, tail), e * 0.3989422804014327


def stats(v):
    spread = v - jnp.mean(v, axis=-1, keepdims=True)
    return spread, lax.rsqrt(jnp.mean(spread * spread, axis=-1, keepdims=True) + 1e-6)


def in_kernel(x_ref, vec_ref, w_ref, *rest):
    x_out, first_t, packed = rest[-3:]
    x = x_ref[...]
    d = x.shape[1]
    spread, r = stats(x.astype(F32))
    f = (spread * r * line(vec_ref, "ag") + line(vec_ref, "ash")).astype(BF)
    x_out[...] = x
    for i, bias in enumerate(("qb", "zero", "vb")):
        packed[:, i * d : (i + 1) * d] = (dot(f, w_ref[:, i * d : (i + 1) * d], NN) + line(vec_ref, bias)).astype(BF)
    first_t[...] = f.T


def project_in(part, offset, total, before, vec, weight):
    rows, d = part.shape
    wide = weight.shape[1]
    tm = 256
    first_block = offset // tm

    def full(a):
        return pl.BlockSpec(a.shape, lambda i: (0, 0), pipeline_mode=pl.Buffered(1))

    in_specs = [pl.BlockSpec((tm, d), lambda i: (i, 0)), full(vec), full(weight)]
    args = [part, vec, weight]
    aliases = {}
    if before is not None:
        aliases = {3: 0, 4: 1, 5: 2}
        in_specs += [pl.BlockSpec(memory_space=pl.ANY)] * 3
        args += list(before)
    return pl.pallas_call(
        in_kernel,
        grid=(rows // tm,),
        in_specs=in_specs,
        out_specs=[
            pl.BlockSpec((tm, d), lambda i: (i + first_block, 0)),
            pl.BlockSpec((d, tm), lambda i: (0, i + first_block)),
            pl.BlockSpec((tm, wide), lambda i: (i + first_block, 0)),
        ],
        out_shape=[shape((total, d)), shape((d, total)), shape((total, wide))],
        input_output_aliases=aliases,
        compiler_params=params(),
        cost_estimate=pl.CostEstimate(flops=6 * rows * d * wide, bytes_accessed=2 * (d * wide + rows * (wide + 3 * d)), transcendentals=0),
        name="project_in",
    )(*args)


def attend_kernel(q_ref, k_ref, v_ref, o_ref, inv_ref, p_ref, vx_ref, *, tq):
    n = k_ref.shape[0]
    vx_ref[:, :PAIR] = v_ref[...]
    vx_ref[:, PAIR:] = jnp.ones((n, PAIR), BF)
    low = lax.broadcasted_iota(jnp.int32, (tq, PAIR), 1) < HEAD_DIM
    for t in range(n // tq):
        rows = pl.ds(t * tq, tq)
        q = q_ref[rows, :]
        zero = jnp.zeros_like(q)
        outs = []
        for a in range(2):
            qa = jnp.where(low, q, zero) if a == 0 else jnp.where(low, zero, q)
            s = dot(qa, k_ref[...], NT)
            top = jnp.max(s, axis=-1, keepdims=True)
            p = jnp.exp2((s - top) * (LOG2E * HEAD_DIM**-0.5)).astype(BF)
            p_ref[a, rows, :] = p
            both = dot(p, vx_ref[...], NN)
            inv = 1.0 / both[:, PAIR:]
            outs.append((both[:, :PAIR] * inv, inv))
        o_ref[rows, :] = jnp.where(low, outs[0][0], outs[1][0]).astype(BF)
        inv_ref[rows, :] = jnp.where(low, outs[0][1], outs[1][1])


def attend(packed):
    n, w = packed.shape
    d = w // 3
    hp = d // PAIR

    def cols(off):
        return pl.BlockSpec((n, PAIR), lambda h: (0, h + off))

    return pl.pallas_call(
        functools.partial(attend_kernel, tq=128),
        grid=(hp,),
        in_specs=[cols(0), cols(hp), cols(2 * hp)],
        out_specs=[cols(0), cols(0), pl.BlockSpec((2, n, n), lambda h: (h, 0, 0))],
        out_shape=[shape((n, d)), shape((n, d), F32), shape((2 * hp, n, n))],
        scratch_shapes=[pltpu.VMEM((n, 2 * PAIR), BF)],
        compiler_params=params(),
        cost_estimate=pl.CostEstimate(flops=16 * n * n * d, bytes_accessed=4 * n * n * hp, transcendentals=0),
        name="attend",
    )(packed, packed, packed)


def by_piece(g):
    rows = g.shape[0] // PIECES
    return [g[:, i : i + 128].reshape(PIECES, rows, 128) for i in range(0, g.shape[1], 128)]


def weight_copies(w1_hbm, w2_hbm, w1, w2, sems, chunks):
    first, second = [], []
    for slot, i in enumerate(chunks):
        for v in range(PIECES):
            at = pl.ds((v * CHUNKS + i) * 128, 128)
            to = pl.ds(v * 128, 128)
            first.append(pltpu.make_async_copy(w1_hbm.at[:, at], w1.at[slot, :, to], sems.at[0, slot, v]))
            second.append(pltpu.make_async_copy(w2_hbm.at[at, :], w2.at[slot, to, :], sems.at[1, slot, v]))
    return first, second


def hidden_kernel(c_ref, *refs, i, sub, head):
    if head:
        x_ref, mix_ref, wo_ref, vec_ref, *refs = refs
    else:
        sec_in, *refs = refs
    up_ref, w1_hbm, w2_hbm, b1_ref, act_ref, dh_ref, gk_ref, gs_ref, db1_ref, *refs = refs
    if head:
        sec_out, *refs = refs
    sec_t, up_t, act, dh, w1, w2, sems = refs
    t = pl.program_id(0)
    tm, d = up_ref.shape
    wide = act_ref.shape[1]
    rows = pl.ds(pl.multiple_of(t * tm, tm), tm)
    first, second = weight_copies(w1_hbm, w2_hbm, w1, w2, sems, [i])

    @pl.when(t == 0)
    def _():
        for copy in first + second:
            copy.start()
        db1_ref[...] = jnp.zeros_like(db1_ref)

    up = up_ref[...]
    if head:
        m = x_ref[...].astype(F32) + dot(mix_ref[...], wo_ref[...], NN) + line(vec_ref, "ob")
        spread, r = stats(m)
        sec = (spread * r * line(vec_ref, "mg") + line(vec_ref, "ms")).astype(BF)
        sec_out[...] = sec
    else:
        sec = sec_in[...]

    @pl.when(t == 0)
    def _():
        for copy in first + second:
            copy.wait()

    for at in range(0, wide, sub):
        cols = slice(at, at + sub)
        bias = jnp.concatenate([b1_ref[v * CHUNKS + i : v * CHUNKS + i + 1, :] for v in range(at // 128, (at + sub) // 128)], axis=1)
        h = dot(sec, w1[0, :, cols], NN) + bias
        da = dot(up, w2[0, cols, :], NT)
        cdf, pdf = normal(h)
        a = (h * cdf).astype(BF)
        dhv = (da * (cdf + h * pdf)).astype(BF)
        act_ref[:, cols] = a
        dh_ref[:, cols] = dhv
        act[rows, cols] = a
        dh[rows, cols] = dhv
        db1_ref[:, cols] += jnp.sum(dhv.astype(F32), axis=0, keepdims=True)
    sec_t[:, rows] = sec.T
    up_t[:, rows] = up.T

    @pl.when(t == pl.num_programs(0) - 1)
    def _():
        c = c_ref[0]
        per = d // PIECES
        for ref, mine in ((gs_ref, 1 - c), (gk_ref, c)):
            half = wide // 2
            g = dot(sec_t[...], dh[:, pl.ds(pl.multiple_of(mine * half, half), half)], NN).astype(BF)
            for k, block in enumerate(by_piece(g)):
                ref[:, k * per : (k + 1) * per, :] = block
            at = half // 128 * per
            half = d // 2
            g = dot(up_t[pl.ds(pl.multiple_of(mine * half, half), half), :], act[...], NN).astype(BF)
            for v in range(PIECES):
                ref[v, at:, :] = g[:, v * 128 : (v + 1) * 128]


def hidden_part(core, head, sec, up, w1, w2, b1, i, tm=256, sub=512):
    n, d = up.shape
    wide = 128 * PIECES
    assert wide * CHUNKS == w1.shape[1]

    def full(*s):
        return pl.BlockSpec(s, lambda t, c: (0,) * len(s), pipeline_mode=pl.Buffered(1))

    row = pl.BlockSpec((tm, d), lambda t, c: (t, 0))
    row_wide = pl.BlockSpec((tm, wide), lambda t, c: (t, 0))
    hbm = pl.BlockSpec(memory_space=pl.ANY)
    g = (PIECES, d // 2 + wide // 256 * d // PIECES, 128)
    if head:
        args, specs = list(head), [row, row, full(*head[2].shape), full(*head[3].shape)]
    else:
        args, specs = [sec], [row]
    return pl.pallas_call(
        functools.partial(hidden_kernel, i=i, sub=sub, head=bool(head)),
        grid_spec=pltpu.PrefetchScalarGridSpec(
            num_scalar_prefetch=1,
            grid=(n // tm,),
            in_specs=specs + [row, hbm, hbm, full(*b1.shape)],
            out_specs=[row_wide, row_wide, full(*g), full(*g), full(1, wide)] + ([row] if head else []),
            scratch_shapes=[
                pltpu.VMEM((d, n), BF), pltpu.VMEM((d, n), BF), pltpu.VMEM((n, wide), BF), pltpu.VMEM((n, wide), BF),
                pltpu.VMEM((1, d, wide), BF), pltpu.VMEM((1, wide, d), BF), pltpu.SemaphoreType.DMA((2, 1, PIECES)),
            ],
        ),
        out_shape=[shape((n, wide)), shape((n, wide)), shape(g), shape(g), shape((1, wide), F32)] + ([shape((n, d))] if head else []),
        compiler_params=params(),
        cost_estimate=pl.CostEstimate(flops=24 * n * d * wide, bytes_accessed=8 * d * wide, transcendentals=0),
        name="hidden",
    )(core, *args, up, w1, w2, b1)


def outer_kernel(c_ref, *refs):
    acts, dhs = refs[:CHUNKS], refs[CHUNKS : 2 * CHUNKS]
    x_ref, up_ref, mix_ref, li_ref, wo_ref, vec_ref, w1_hbm, w2_hbm = refs[2 * CHUNKS : 2 * CHUNKS + 8]
    out_ref, dbr_ref, do_ref, gk_ref, gs_ref, sums_ref, mix_t, dbr, w1, w2, sems = refs[2 * CHUNKS + 8 :]
    t = pl.program_id(0)
    tm, d = x_ref.shape
    rows = pl.ds(pl.multiple_of(t * tm, tm), tm)
    first, second = weight_copies(w1_hbm, w2_hbm, w1, w2, sems, range(CHUNKS))

    @pl.when(t == 0)
    def _():
        for copy in first + second:
            copy.start()
        sums_ref[...] = jnp.zeros_like(sums_ref)

    m = x_ref[...].astype(F32) + dot(mix_ref[...], wo_ref[...], NN) + line(vec_ref, "ob")
    spread, r = stats(m)
    nv = spread * r
    up = up_ref[...].astype(F32)
    mix_t[:, rows] = mix_ref[...].T

    @pl.when(t == 0)
    def _():
        for copy in first + second:
            copy.wait()

    dy = dot(dhs[0][...], w1[0], NT)
    for i in range(1, CHUNKS):
        dy += dot(dhs[i][...], w1[i], NT)
    o = dot(acts[0][...], w2[0], NN)
    for i in range(1, CHUNKS):
        o += dot(acts[i][...], w2[i], NN)
    dyg = dy * line(vec_ref, "mg")
    dm = up + r * (dyg - jnp.mean(dyg, axis=-1, keepdims=True) - nv * jnp.mean(dyg * nv, axis=-1, keepdims=True))
    db = dm.astype(BF)
    dbr_ref[...] = db
    dbr[rows, :] = db
    out_ref[...] = (m + o + line(vec_ref, "rb")).astype(BF)
    do_ref[...] = (dot(db, wo_ref[...], NT) * li_ref[...]).astype(BF)
    sums_ref[0:1, :] += jnp.sum(db.astype(F32), axis=0, keepdims=True)
    sums_ref[1:2, :] += jnp.sum(dy * nv, axis=0, keepdims=True)
    sums_ref[2:3, :] += jnp.sum(dy, axis=0, keepdims=True)
    sums_ref[3:4, :] += jnp.sum(up, axis=0, keepdims=True)

    @pl.when(t == pl.num_programs(0) - 1)
    def _():
        half = d // 2
        per = d // PIECES
        for ref, mine in ((gs_ref, 1 - c_ref[0]), (gk_ref, c_ref[0])):
            g = dot(mix_t[...], dbr[:, pl.ds(pl.multiple_of(mine * half, half), half)], NN).astype(BF)
            for i, block in enumerate(by_piece(g)):
                ref[:, i * per : (i + 1) * per, :] = block


def outer(core, acts, dhs, x, up, mix, li, wo, vec, w1, w2, tm=256):
    n, d = x.shape
    wide = acts[0].shape[1]

    def full(*s):
        return pl.BlockSpec(s, lambda t, c: (0,) * len(s), pipeline_mode=pl.Buffered(1))

    row = pl.BlockSpec((tm, d), lambda t, c: (t, 0))
    row_wide = pl.BlockSpec((tm, wide), lambda t, c: (t, 0))
    hbm = pl.BlockSpec(memory_space=pl.ANY)
    g = (PIECES, d // 256 * d // PIECES, 128)
    return pl.pallas_call(
        outer_kernel,
        grid_spec=pltpu.PrefetchScalarGridSpec(
            num_scalar_prefetch=1,
            grid=(n // tm,),
            in_specs=[row_wide] * (2 * CHUNKS) + [row] * 4 + [full(*wo.shape), full(*vec.shape), hbm, hbm],
            out_specs=[row, row, row, full(*g), full(*g), full(8, d)],
            scratch_shapes=[
                pltpu.VMEM((d, n), BF), pltpu.VMEM((n, d), BF), pltpu.VMEM((CHUNKS, d, wide), BF),
                pltpu.VMEM((CHUNKS, wide, d), BF), pltpu.SemaphoreType.DMA((2, CHUNKS, PIECES)),
            ],
        ),
        out_shape=[shape((n, d))] * 3 + [shape(g), shape(g), shape((8, d), F32)],
        compiler_params=params(),
        cost_estimate=pl.CostEstimate(flops=16 * n * d * (wide * CHUNKS + d), bytes_accessed=8 * d * wide * CHUNKS, transcendentals=0),
        name="outer",
    )(core, *acts, *dhs, x, up, mix, li, wo, vec, w1, w2)


def reflect_kernel(c_ref, q_ref, k_ref, v_ref, o_ref, do_ref, p_ref, ft_ref, dq_ref, dk_ref, dv_ref, gk_ref, gs_ref, ds_ref, *, tq):
    n = k_ref.shape[0]
    low = lax.broadcasted_iota(jnp.int32, (tq, PAIR), 1) < HEAD_DIM
    q_t = q_ref[...].T
    do_t = do_ref[...].T
    scale = HEAD_DIM**-0.5
    dks, dvs = [], []
    for a in range(2):
        for t in range(n // tq):
            rows = pl.ds(t * tq, tq)
            do = do_ref[rows, :]
            zero = jnp.zeros_like(do)
            doa = jnp.where(low, do, zero) if a == 0 else jnp.where(low, zero, do)
            delta = jnp.sum(doa.astype(F32) * o_ref[rows, :].astype(F32), axis=-1, keepdims=True)
            dp = dot(doa, v_ref[...], NT)
            ds = (p_ref[a, rows, :].astype(F32) * (dp - delta)).astype(BF)
            ds_ref[rows, :] = ds
            dq = (dot(ds, k_ref[...], NN) * scale).astype(BF)
            dq_ref[rows, :] = dq if a == 0 else jnp.where(low, dq_ref[rows, :], dq)
        part = slice(HEAD_DIM * a, HEAD_DIM * (a + 1))
        dvs.append(dot(do_t[part], p_ref[a], NN))
        dks.append(dot(q_t[part], ds_ref[...], NN) * scale)
    dv = jnp.concatenate(dvs, axis=0).astype(BF).T
    dk = jnp.concatenate(dks, axis=0).astype(BF).T
    dv_ref[...] = dv
    dk_ref[...] = dk
    g = dot(ft_ref[...], jnp.concatenate([dq_ref[...], dk, dv], axis=1), NN).astype(BF)
    per = g.shape[0] // PIECES
    h = pl.program_id(0)
    for step, ref in enumerate((gs_ref, gk_ref)):

        @pl.when(h == step)
        def _():
            for i, block in enumerate(by_piece(g)):
                ref[:, i * per : (i + 1) * per, :] = block


def reflect(core, packed, o, do, p, first_t, start):
    n, w = packed.shape
    d = w // 3
    hp = d // PAIR

    def which(h, c):
        return (h + 1 - c[0]) % 2

    def cols(off):
        return pl.BlockSpec((n, PAIR), lambda h, c: (0, which(h, c) + off))

    g = (PIECES, 3 * (d // PIECES), 128)
    piece = pl.BlockSpec(g, lambda h, c: (0, 0, 0), pipeline_mode=pl.Buffered(1))
    return pl.pallas_call(
        functools.partial(reflect_kernel, tq=256),
        grid_spec=pltpu.PrefetchScalarGridSpec(
            num_scalar_prefetch=1,
            grid=(2,),
            in_specs=[
                cols(start), cols(start + hp), cols(start + 2 * hp), cols(start), cols(start),
                pl.BlockSpec((2, n, n), lambda h, c: (which(h, c) + start, 0, 0)),
                pl.BlockSpec((d, n), lambda h, c: (0, 0), pipeline_mode=pl.Buffered(1)),
            ],
            out_specs=[cols(0)] * 3 + [piece] * 2,
            scratch_shapes=[pltpu.VMEM((n, n), BF)],
        ),
        out_shape=[shape((n, 2 * PAIR))] * 3 + [shape(g)] * 2,
        compiler_params=params(),
        cost_estimate=pl.CostEstimate(flops=160 * n * n * PAIR, bytes_accessed=8 * n * n, transcendentals=0),
        name="reflect",
    )(core, packed, packed, packed, o, do, p, first_t)


def back_kernel(*refs, chunks):
    x_ref, dbr_ref, w_ref, vec_in = refs[:4]
    parts = refs[4 : 4 + 3 * chunks]
    tg_ref, vec_ref = refs[4 + 3 * chunks :]

    @pl.when(pl.program_id(0) == 0)
    def _():
        vec_ref[...] = jnp.zeros_like(vec_ref)

    d = x_ref.shape[1]
    cw = d // chunks
    dy = None
    for i in range(3 * chunks):
        which, chunk = i % 3, i // 3
        at = which * d + chunk * cw
        part = dot(parts[i][...], w_ref[:, at : at + cw], NT)
        dy = part if dy is None else dy + part
        row = {0: 2, 2: 3}.get(which)
        if row is not None:
            vec_ref[row : row + 1, chunk * cw : (chunk + 1) * cw] += jnp.sum(parts[i][...].astype(F32), axis=0, keepdims=True)
    spread, r = stats(x_ref[...].astype(F32))
    nv = spread * r
    dyg = dy * line(vec_in, "ag")
    dx = r * (dyg - jnp.mean(dyg, axis=-1, keepdims=True) - nv * jnp.mean(dyg * nv, axis=-1, keepdims=True))
    tg_ref[...] = (dbr_ref[...].astype(F32) + dx).astype(BF)
    vec_ref[0:1, :] += jnp.sum(dy * nv, axis=0, keepdims=True)
    vec_ref[1:2, :] += jnp.sum(dy, axis=0, keepdims=True)


def project_back(x, dbr, w, vec, parts):
    n, d = x.shape
    tm = 256
    row = pl.BlockSpec((tm, d), lambda i: (i, 0))

    def full(*s):
        return pl.BlockSpec(s, lambda i: (0, 0))

    chunks = len(parts) // 3
    return pl.pallas_call(
        functools.partial(back_kernel, chunks=chunks),
        grid=(n // tm,),
        in_specs=[row, row, full(d, 3 * d), full(*vec.shape)] + [pl.BlockSpec((tm, d // chunks), lambda i: (i, 0))] * (3 * chunks),
        out_specs=[row, full(8, d)],
        out_shape=[shape((n, d)), shape((8, d), F32)],
        compiler_params=params(),
        cost_estimate=pl.CostEstimate(flops=6 * n * d * d, bytes_accessed=16 * n * d, transcendentals=0),
        name="project_back",
    )(x, dbr, w, vec, *parts)


def exchange(x, axis, by):
    count = lax.axis_size(axis)
    return lax.ppermute(x, axis, [(i, i ^ by) for i in range(count)])


def pick(x, index, axis=0):
    return lax.dynamic_index_in_dim(x, index, axis, keepdims=False)


def add_up(arrays, dtype=BF):
    s = arrays[0].astype(F32)
    for a in arrays[1:]:
        s = s + a.astype(F32)
    return s.astype(dtype)


def after(x, *others):
    return lax.optimization_barrier((x,) + others)[0]


class Sum:
    def __init__(self, *segments):
        self.open = [0, 1, 2]
        self.parts = []
        self.pending = None
        self.join(*segments)

    def join(self, *segments):
        self.parts += [[a.reshape((2, 2, 2) + a.shape[1:]) for a in terms] for terms in segments]

    def land(self, *tokens):
        if self.pending is None:
            return
        received, at = self.pending
        received = after(received, *tokens) if tokens else received
        for terms in self.parts:
            size = terms[0].size // 128
            terms.append(received[at : at + size].reshape(terms[0].shape))
            at += size
        self.pending = None

    def sends(self, stage):
        position = lax.axis_index("vol")
        unit = lax.axis_size("vol") // PIECES
        if stage == "half":
            mine, axis = lax.axis_index("seq") // 2, len(self.open)
            cut = [[a.reshape(a.shape[:-2] + (2, a.shape[-2] // 2, 128)) for a in t] for t in self.parts]
        elif stage in (0, 1, 2):
            axis = len(self.open) - 1 - self.open.index(stage)
            mine = (position // (unit << stage)) % 2
            cut = self.parts
            self.open.remove(stage)
        else:
            self.parts = [[add_up(t)] for t in self.parts]
            return [t[0].reshape(-1, 128) for t in self.parts]
        self.parts = [[pick(a, mine, axis) for a in t] for t in cut]
        return [add_up([pick(a, 1 - mine, axis) for a in t]).reshape(-1, 128) for t in cut]

    def totals(self, *tokens):
        self.land(*tokens)
        return [add_up(t).reshape(-1, 128) for t in self.parts]


def swap(stage, *groups):
    unit = lax.axis_size("vol") // PIECES
    rows, starts = [], []
    at = 0
    for g in groups:
        starts.append(at)
        for r in g.sends(stage):
            rows.append(r)
            at += r.shape[0]
    sent = jnp.concatenate(rows) if len(rows) > 1 else rows[0]
    if stage in ("half", "x"):
        received = exchange(sent, "seq", 2)
    elif stage in (0, 1, 2):
        received = exchange(sent, "vol", unit << stage)
    else:
        received = exchange(sent, "vol", stage[1])
    for g, at in zip(groups, starts):
        g.pending = (received, at)
    return sent, received


def on_device(
    volume_slices, volume_owner, tokens, cotangent, attend_gain, attend_shift, input_weight, query_bias, value_bias,
    output_weight, output_bias, mixer_gain, mixer_shift, expand_weight, expand_bias, reduce_weight, reduce_bias,
):
    slices, rows, d = tokens.shape
    ff = expand_weight.shape[1]
    nv = lax.axis_size("vol")
    peers = lax.axis_size("seq")
    me = lax.axis_index("seq")
    core_id = me % 2
    x_id = (me // 2) % 2
    core = core_id.astype(jnp.int32).reshape(1)
    n = rows * peers
    spare = [(("all", 1 << i)) for i in range((nv // PIECES).bit_length() - 1)]

    def from_peers(x, ks):
        parts = [pick(x, me ^ k) for k in ks]
        return [p if k == 0 else exchange(p, "seq", k) for p, k in zip(parts, ks)]

    far_parts = from_peers(tokens, (3, 2))
    near_parts = from_peers(tokens, (0, 1))
    zero = jnp.zeros((d,), BF)
    vec = jnp.concatenate(
        [attend_gain, attend_shift, query_bias, zero, value_bias, output_bias, mixer_gain, mixer_shift, reduce_bias] + [zero] * 7
    ).astype(F32).reshape(16, d)
    wide = ff // CHUNKS
    lanes = wide // PIECES
    b1 = expand_bias.astype(F32).reshape(ff // 128, 128)
    load = jnp.sum(jnp.where(volume_owner == lax.axis_index("vol"), volume_slices, 0))
    live = (jnp.arange(slices) < load).astype(BF)

    made = project_in(jnp.concatenate(near_parts), 0, n, None, vec, input_weight)
    far = jnp.concatenate([after(far_parts[1], made[2], b1, live), far_parts[0]])
    x, first_t, packed = project_in(far, 2 * rows, n, made, vec, input_weight)
    upstream = jnp.concatenate(from_peers(after(cotangent, far_parts[0], made[2]) * live[:, None, None], (0, 1, 2, 3)))

    mixed, inverse, weights = attend(packed)

    def to_core(g):
        return exchange(g, "seq", 1)

    acts, dhs, db1 = [], [], []
    second = None

    def hidden(token, i):
        head = (x, mixed, output_weight, vec) if i == 0 else None
        a, g, gk, gs, b, *sec = hidden_part(token, head, second, upstream, expand_weight, reduce_weight, b1, i)
        acts.append(a)
        dhs.append(g)
        db1.append(b)
        return gk, gs, sec

    Y, Z1, Z2 = 0, 1, 2
    k0, s0, (second,) = hidden(core, 0)
    r0 = to_core(s0)
    k1, s1, _ = hidden(after(core, s0), 1)
    r1 = to_core(s1)
    ga = Sum([k0, after(r0, s1)])
    sent = [swap("half", ga)[0]]
    k2, s2, _ = hidden(after(core, s1, *sent), 2)
    r2 = to_core(s2)
    gb = Sum([k1, after(r1, s2)])
    sent = [swap(Z1, gb)[0]]
    out, d_branch, d_mixed, k3, s3, sums_mid = outer(
        after(core, s2, *sent), acts, dhs, x, upstream, mixed, inverse, output_weight, vec, expand_weight, reduce_weight
    )

    def blocks(a):
        return [a[k * rows : (k + 1) * rows] for k in range(peers)]

    r3 = to_core(s3)
    out_parts = blocks(out)
    outs = [exchange(out_parts[k], "seq", k) if k else out_parts[0] for k in range(peers)]
    gc = Sum([k2, after(r2, s3)])
    ga.land(s3)
    gb.land(s3)
    sent_c, back_c = swap(Y, gc)
    sent = [sent_c, swap(Z2, gb)[0]] + out_parts[1:]
    parts = []

    def reflect_part(token, i):
        dq, dk, dv, gk, gs = reflect(token, packed, mixed, d_mixed, weights, first_t, 2 * i)
        parts.extend([dq, dk, dv])
        return gk, gs

    p0, q0 = reflect_part(after(core, s3, *sent), 0)
    t0 = to_core(q0)
    for g in (gb, gc):
        g.land(q0)
    sent = [swap(Y, ga, gb)[0]]
    p1, q1 = reflect_part(after(core, q0, back_c, *sent, *outs[1:]), 1)
    t1 = to_core(q1)
    gd = Sum([k3, after(r3, q1)], [p0, after(t0, q1)])
    for g in (ga, gb):
        g.land(q1)
    sent = [swap(Z1, ga, gc)[0], swap("half", gd)[0]]
    p2, q2 = reflect_part(after(core, q1, *sent), 2)
    t2 = to_core(q2)
    ge = Sum([p1, after(t1, q2)], [p2, t2])
    for g in (ga, gc, gd):
        g.land(q2)
    sent = [swap(Y, ge, gd)[0], swap(Z2, ga, gc)[0]]
    late = after(x, *sent)
    d_tokens, sums_end = project_back(late, d_branch, input_weight, vec, parts)

    tg_parts = blocks(d_tokens)
    tgs = [exchange(tg_parts[k], "seq", k) if k else tg_parts[0] for k in range(peers)]
    per = d // PIECES
    lanes = 128
    mids, *db = lax.optimization_barrier((sums_mid, *db1, sums_end))[:-1]
    db = jnp.concatenate([v.reshape(PIECES, lanes) for v in db], axis=1).reshape(PIECES, ff // d, per).swapaxes(0, 1)
    small = jnp.concatenate([sums_end[:4], mids[:4], db.reshape(ff // d, d)])
    nsmall = small.shape[0]
    small = small.reshape(nsmall, PIECES, per).swapaxes(0, 1).reshape(PIECES, nsmall * per // 128, 128)
    gv = Sum([small, to_core(small)])
    for g in (ga, gc, gd, ge):
        g.land(sums_end)
    _, w1 = swap(Y, gv)
    _, w2 = swap("x", ga, gb, gc)
    gv.land()
    swap(Z1, ge, gd, gv)
    for g in (ge, gd, gv):
        g.land(w1, w2)
    _, w1 = swap(Z2, ge, gd, gv)
    for g in (ge, gd, gv):
        g.land(w1, *tgs[2:])
    _, w1 = swap("x", ge, gd, gv)
    for by in spare:
        for g in (ga, gb, gc, gd, ge, gv):
            g.land()
        swap(by, ga, gb, gc, gd, ge, gv)
    waited = [w1]

    def home(arrays, dtype, mask):
        result = jnp.zeros((slices, rows, d), dtype)
        for k in range(peers):
            part = arrays[k]
            if mask:
                part = part * pick(live, me ^ k)
            result = lax.dynamic_update_index_in_dim(result, part.astype(dtype), me ^ k, 0)
        return result

    block_out = home([after(o, sums_end) for o in outs], BF, True)
    tokens_grad = home([after(t, *waited) for t in tgs], F32, False)

    def halves(total):
        other = to_core(total)
        return jnp.where(core_id == 0, total, other), jnp.where(core_id == 0, other, total)

    def gathered(g, *tokens):
        outs = []
        g.land(*tokens)
        for mine, other in g.parts:
            first = jnp.where(x_id == 0, mine, other)
            second = jnp.where(x_id == 0, other, mine)
            outs.append(jnp.concatenate([first.reshape(-1, 128), second.reshape(-1, 128)]))
        return outs

    half_ff = 4 * per
    ex, re = [], []
    for total in (gathered(ga, sums_end)[0], gb.totals(sums_end)[0], gc.totals(sums_end)[0]):
        lo, hi = halves(total)
        ex.append(jnp.concatenate([lo[:half_ff].reshape(-1, per, 128), hi[:half_ff].reshape(-1, per, 128)], axis=0))
        re.append(jnp.concatenate([lo[half_ff:], hi[half_ff:]], axis=0))
    expand_grad = jnp.stack(ex, axis=1).transpose(2, 0, 1, 3).reshape(per, ff).astype(F32)
    reduce_grad = jnp.concatenate(re, axis=1).T.astype(F32)
    lo, hi = halves(jnp.concatenate(gathered(gd, *waited) + ge.totals(*waited)))
    size = 3 * per
    output_grad = jnp.concatenate([lo[:size], hi[:size]], axis=0).reshape(-1, per, 128).swapaxes(0, 1).reshape(per, d).astype(F32)
    seq = []
    for i in range(1, CHUNKS + 1):
        seq += [lo[i * size : (i + 1) * size], hi[i * size : (i + 1) * size]]
    input_grad = jnp.stack(seq).reshape(2 * CHUNKS, 3, per, 128).transpose(2, 1, 0, 3).reshape(per, 3 * d).astype(F32)
    vectors = gv.totals(*waited)[0].astype(F32).reshape(nsmall, per)

    if nv > PIECES:
        unit = nv // PIECES
        sub = lax.axis_index("vol") % unit
        cut = lambda a, axis: lax.dynamic_slice_in_dim(a, sub * (a.shape[axis] // unit), a.shape[axis] // unit, axis)
        expand_grad, reduce_grad, output_grad, input_grad = [cut(a, 0) for a in (expand_grad, reduce_grad, output_grad, input_grad)]
        expand_bias_grad = cut(vectors[8:].reshape(-1), 0)
        vectors = cut(vectors, 1)
    else:
        expand_bias_grad = vectors[8:].reshape(-1)
    return (
        block_out, tokens_grad, vectors[0], vectors[1], input_grad, vectors[2], vectors[3], output_grad, vectors[4],
        vectors[5], vectors[6], expand_grad, expand_bias_grad, reduce_grad, vectors[7],
    )


def solution(mesh):
    rows = P("vol", "seq", None)
    return jax.shard_map(
        on_device,
        mesh=mesh,
        in_specs=(P(), P(), rows, rows) + (P(),) * 13,
        out_specs=(rows, rows, P("vol"), P("vol"), P("vol", None), P("vol"), P("vol"), P("vol", None), P("vol"), P("vol"),
                   P("vol"), P("vol", None), P("vol"), P("vol", None), P("vol")),
        check_vma=False,
    )
```

```python
import functools

import jax
import jax.numpy as jnp
from jax import lax
from jax.experimental import pallas as pl
from jax.experimental.pallas import tpu as pltpu
from jax.sharding import PartitionSpec as P

HEAD_DIM = 64
PAIR = 2 * HEAD_DIM
LOG2E = 1.4426950408889634
PIECES = 8
CHUNKS = 3
ROW = {n: i for i, n in enumerate(("ag", "ash", "qb", "zero", "vb", "ob", "mg", "ms", "rb"))}
BF = jnp.bfloat16
F32 = jnp.float32
NN = (((1,), (0,)), ((), ()))
NT = (((1,), (1,)), ((), ()))
TAIL = (
    0.11962928008603971,
    0.12075423895539067,
    0.09991176086876633,
    0.12856720585766357,
    -0.05369390237929985,
    0.20636430391507077,
    -0.15720912816414995,
    0.03567616760586865,
)


def dot(a, b, dims):
    return lax.dot_general(a, b, dims, preferred_element_type=F32)


def params():
    return pltpu.CompilerParams(vmem_limit_bytes=60 << 20)


def line(ref, name):
    return ref[ROW[name] : ROW[name] + 1, :]


def shape(dims, dtype=BF):
    return jax.ShapeDtypeStruct(dims, dtype)


def normal(h):
    a = jnp.abs(h)
    t = 1.0 / (1.0 + 0.3 * a)
    s = TAIL[7] * t + TAIL[6]
    for c in TAIL[5::-1]:
        s = s * t + c
    e = jnp.exp2(h * h * (-0.5 * LOG2E))
    tail = s * t * e
    return jnp.where(h >= 0, 1.0 - tail, tail), e * 0.3989422804014327


def stats(v):
    spread = v - jnp.mean(v, axis=-1, keepdims=True)
    return spread, lax.rsqrt(jnp.mean(spread * spread, axis=-1, keepdims=True) + 1e-6)


def in_kernel(x_ref, vec_ref, w_ref, *rest):
    x_out, first_t, packed = rest[-3:]
    x = x_ref[...]
    d = x.shape[1]
    spread, r = stats(x.astype(F32))
    f = (spread * r * line(vec_ref, "ag") + line(vec_ref, "ash")).astype(BF)
    x_out[...] = x
    for i, bias in enumerate(("qb", "zero", "vb")):
        packed[:, i * d : (i + 1) * d] = (dot(f, w_ref[:, i * d : (i + 1) * d], NN) + line(vec_ref, bias)).astype(BF)
    first_t[...] = f.T


def project_in(part, offset, total, before, vec, weight):
    rows, d = part.shape
    wide = weight.shape[1]
    tm = 256
    first_block = offset // tm

    def full(a):
        return pl.BlockSpec(a.shape, lambda i: (0, 0), pipeline_mode=pl.Buffered(1))

    in_specs = [pl.BlockSpec((tm, d), lambda i: (i, 0)), full(vec), full(weight)]
    args = [part, vec, weight]
    aliases = {}
    if before is not None:
        aliases = {3: 0, 4: 1, 5: 2}
        in_specs += [pl.BlockSpec(memory_space=pl.ANY)] * 3
        args += list(before)
    return pl.pallas_call(
        in_kernel,
        grid=(rows // tm,),
        in_specs=in_specs,
        out_specs=[
            pl.BlockSpec((tm, d), lambda i: (i + first_block, 0)),
            pl.BlockSpec((d, tm), lambda i: (0, i + first_block)),
            pl.BlockSpec((tm, wide), lambda i: (i + first_block, 0)),
        ],
        out_shape=[shape((total, d)), shape((d, total)), shape((total, wide))],
        input_output_aliases=aliases,
        compiler_params=params(),
        cost_estimate=pl.CostEstimate(flops=6 * rows * d * wide, bytes_accessed=2 * (d * wide + rows * (wide + 3 * d)), transcendentals=0),
        name="project_in",
    )(*args)


def attend_kernel(q_ref, k_ref, v_ref, o_ref, inv_ref, p_ref, vx_ref, *, tq):
    n = k_ref.shape[0]
    vx_ref[:, :PAIR] = v_ref[...]
    vx_ref[:, PAIR:] = jnp.ones((n, PAIR), BF)
    low = lax.broadcasted_iota(jnp.int32, (tq, PAIR), 1) < HEAD_DIM
    for t in range(n // tq):
        rows = pl.ds(t * tq, tq)
        q = q_ref[rows, :]
        zero = jnp.zeros_like(q)
        outs = []
        for a in range(2):
            qa = jnp.where(low, q, zero) if a == 0 else jnp.where(low, zero, q)
            s = dot(qa, k_ref[...], NT)
            top = jnp.max(s, axis=-1, keepdims=True)
            p = jnp.exp2((s - top) * (LOG2E * HEAD_DIM**-0.5)).astype(BF)
            p_ref[a, rows, :] = p
            both = dot(p, vx_ref[...], NN)
            inv = 1.0 / both[:, PAIR:]
            outs.append((both[:, :PAIR] * inv, inv))
        o_ref[rows, :] = jnp.where(low, outs[0][0], outs[1][0]).astype(BF)
        inv_ref[rows, :] = jnp.where(low, outs[0][1], outs[1][1])


def attend(packed):
    n, w = packed.shape
    d = w // 3
    hp = d // PAIR

    def cols(off):
        return pl.BlockSpec((n, PAIR), lambda h: (0, h + off))

    return pl.pallas_call(
        functools.partial(attend_kernel, tq=128),
        grid=(hp,),
        in_specs=[cols(0), cols(hp), cols(2 * hp)],
        out_specs=[cols(0), cols(0), pl.BlockSpec((2, n, n), lambda h: (h, 0, 0))],
        out_shape=[shape((n, d)), shape((n, d), F32), shape((2 * hp, n, n))],
        scratch_shapes=[pltpu.VMEM((n, 2 * PAIR), BF)],
        compiler_params=params(),
        cost_estimate=pl.CostEstimate(flops=16 * n * n * d, bytes_accessed=4 * n * n * hp, transcendentals=0),
        name="attend",
    )(packed, packed, packed)


def by_piece(g):
    rows = g.shape[0] // PIECES
    return [g[:, i : i + 128].reshape(PIECES, rows, 128) for i in range(0, g.shape[1], 128)]


def weight_copies(w1_hbm, w2_hbm, w1, w2, sems, chunks):
    first, second = [], []
    for slot, i in enumerate(chunks):
        for v in range(PIECES):
            at = pl.ds((v * CHUNKS + i) * 128, 128)
            to = pl.ds(v * 128, 128)
            first.append(pltpu.make_async_copy(w1_hbm.at[:, at], w1.at[slot, :, to], sems.at[0, slot, v]))
            second.append(pltpu.make_async_copy(w2_hbm.at[at, :], w2.at[slot, to, :], sems.at[1, slot, v]))
    return first, second


def hidden_kernel(c_ref, *refs, i, sub, head):
    if head:
        x_ref, mix_ref, wo_ref, vec_ref, *refs = refs
    else:
        sec_in, *refs = refs
    up_ref, w1_hbm, w2_hbm, b1_ref, act_ref, dh_ref, gk_ref, gs_ref, db1_ref, *refs = refs
    if head:
        sec_out, *refs = refs
    sec_t, up_t, act, dh, w1, w2, sems = refs
    t = pl.program_id(0)
    tm, d = up_ref.shape
    wide = act_ref.shape[1]
    rows = pl.ds(pl.multiple_of(t * tm, tm), tm)
    first, second = weight_copies(w1_hbm, w2_hbm, w1, w2, sems, [i])

    @pl.when(t == 0)
    def _():
        for copy in first + second:
            copy.start()
        db1_ref[...] = jnp.zeros_like(db1_ref)

    up = up_ref[...]
    if head:
        m = x_ref[...].astype(F32) + dot(mix_ref[...], wo_ref[...], NN) + line(vec_ref, "ob")
        spread, r = stats(m)
        sec = (spread * r * line(vec_ref, "mg") + line(vec_ref, "ms")).astype(BF)
        sec_out[...] = sec
    else:
        sec = sec_in[...]

    @pl.when(t == 0)
    def _():
        for copy in first + second:
            copy.wait()

    for at in range(0, wide, sub):
        cols = slice(at, at + sub)
        bias = jnp.concatenate([b1_ref[v * CHUNKS + i : v * CHUNKS + i + 1, :] for v in range(at // 128, (at + sub) // 128)], axis=1)
        h = dot(sec, w1[0, :, cols], NN) + bias
        da = dot(up, w2[0, cols, :], NT)
        cdf, pdf = normal(h)
        a = (h * cdf).astype(BF)
        dhv = (da * (cdf + h * pdf)).astype(BF)
        act_ref[:, cols] = a
        dh_ref[:, cols] = dhv
        act[rows, cols] = a
        dh[rows, cols] = dhv
        db1_ref[:, cols] += jnp.sum(dhv.astype(F32), axis=0, keepdims=True)
    sec_t[:, rows] = sec.T
    up_t[:, rows] = up.T

    @pl.when(t == pl.num_programs(0) - 1)
    def _():
        c = c_ref[0]
        per = d // PIECES
        for ref, mine in ((gs_ref, 1 - c), (gk_ref, c)):
            half = wide // 2
            g = dot(sec_t[...], dh[:, pl.ds(pl.multiple_of(mine * half, half), half)], NN).astype(BF)
            for k, block in enumerate(by_piece(g)):
                ref[:, k * per : (k + 1) * per, :] = block
            at = half // 128 * per
            half = d // 2
            g = dot(up_t[pl.ds(pl.multiple_of(mine * half, half), half), :], act[...], NN).astype(BF)
            for v in range(PIECES):
                ref[v, at:, :] = g[:, v * 128 : (v + 1) * 128]


def hidden_part(core, head, sec, up, w1, w2, b1, i, tm=256, sub=512):
    n, d = up.shape
    wide = 128 * PIECES
    assert wide * CHUNKS == w1.shape[1]

    def full(*s):
        return pl.BlockSpec(s, lambda t, c: (0,) * len(s), pipeline_mode=pl.Buffered(1))

    row = pl.BlockSpec((tm, d), lambda t, c: (t, 0))
    row_wide = pl.BlockSpec((tm, wide), lambda t, c: (t, 0))
    hbm = pl.BlockSpec(memory_space=pl.ANY)
    g = (PIECES, d // 2 + wide // 256 * d // PIECES, 128)
    if head:
        args, specs = list(head), [row, row, full(*head[2].shape), full(*head[3].shape)]
    else:
        args, specs = [sec], [row]
    return pl.pallas_call(
        functools.partial(hidden_kernel, i=i, sub=sub, head=bool(head)),
        grid_spec=pltpu.PrefetchScalarGridSpec(
            num_scalar_prefetch=1,
            grid=(n // tm,),
            in_specs=specs + [row, hbm, hbm, full(*b1.shape)],
            out_specs=[row_wide, row_wide, full(*g), full(*g), full(1, wide)] + ([row] if head else []),
            scratch_shapes=[
                pltpu.VMEM((d, n), BF), pltpu.VMEM((d, n), BF), pltpu.VMEM((n, wide), BF), pltpu.VMEM((n, wide), BF),
                pltpu.VMEM((1, d, wide), BF), pltpu.VMEM((1, wide, d), BF), pltpu.SemaphoreType.DMA((2, 1, PIECES)),
            ],
        ),
        out_shape=[shape((n, wide)), shape((n, wide)), shape(g), shape(g), shape((1, wide), F32)] + ([shape((n, d))] if head else []),
        compiler_params=params(),
        cost_estimate=pl.CostEstimate(flops=24 * n * d * wide, bytes_accessed=8 * d * wide, transcendentals=0),
        name="hidden",
    )(core, *args, up, w1, w2, b1)


def outer_kernel(c_ref, *refs):
    acts, dhs = refs[:CHUNKS], refs[CHUNKS : 2 * CHUNKS]
    x_ref, up_ref, mix_ref, li_ref, wo_ref, vec_ref, w1_hbm, w2_hbm = refs[2 * CHUNKS : 2 * CHUNKS + 8]
    out_ref, dbr_ref, do_ref, gk_ref, gs_ref, sums_ref, mix_t, dbr, w1, w2, sems = refs[2 * CHUNKS + 8 :]
    t = pl.program_id(0)
    tm, d = x_ref.shape
    rows = pl.ds(pl.multiple_of(t * tm, tm), tm)
    first, second = weight_copies(w1_hbm, w2_hbm, w1, w2, sems, range(CHUNKS))

    @pl.when(t == 0)
    def _():
        for copy in first + second:
            copy.start()
        sums_ref[...] = jnp.zeros_like(sums_ref)

    m = x_ref[...].astype(F32) + dot(mix_ref[...], wo_ref[...], NN) + line(vec_ref, "ob")
    spread, r = stats(m)
    nv = spread * r
    up = up_ref[...].astype(F32)
    mix_t[:, rows] = mix_ref[...].T

    @pl.when(t == 0)
    def _():
        for copy in first + second:
            copy.wait()

    dy = dot(dhs[0][...], w1[0], NT)
    for i in range(1, CHUNKS):
        dy += dot(dhs[i][...], w1[i], NT)
    o = dot(acts[0][...], w2[0], NN)
    for i in range(1, CHUNKS):
        o += dot(acts[i][...], w2[i], NN)
    dyg = dy * line(vec_ref, "mg")
    dm = up + r * (dyg - jnp.mean(dyg, axis=-1, keepdims=True) - nv * jnp.mean(dyg * nv, axis=-1, keepdims=True))
    db = dm.astype(BF)
    dbr_ref[...] = db
    dbr[rows, :] = db
    out_ref[...] = (m + o + line(vec_ref, "rb")).astype(BF)
    do_ref[...] = (dot(db, wo_ref[...], NT) * li_ref[...]).astype(BF)
    sums_ref[0:1, :] += jnp.sum(db.astype(F32), axis=0, keepdims=True)
    sums_ref[1:2, :] += jnp.sum(dy * nv, axis=0, keepdims=True)
    sums_ref[2:3, :] += jnp.sum(dy, axis=0, keepdims=True)
    sums_ref[3:4, :] += jnp.sum(up, axis=0, keepdims=True)

    @pl.when(t == pl.num_programs(0) - 1)
    def _():
        half = d // 2
        per = d // PIECES
        for ref, mine in ((gs_ref, 1 - c_ref[0]), (gk_ref, c_ref[0])):
            g = dot(mix_t[...], dbr[:, pl.ds(pl.multiple_of(mine * half, half), half)], NN).astype(BF)
            for i, block in enumerate(by_piece(g)):
                ref[:, i * per : (i + 1) * per, :] = block


def outer(core, acts, dhs, x, up, mix, li, wo, vec, w1, w2, tm=256):
    n, d = x.shape
    wide = acts[0].shape[1]

    def full(*s):
        return pl.BlockSpec(s, lambda t, c: (0,) * len(s), pipeline_mode=pl.Buffered(1))

    row = pl.BlockSpec((tm, d), lambda t, c: (t, 0))
    row_wide = pl.BlockSpec((tm, wide), lambda t, c: (t, 0))
    hbm = pl.BlockSpec(memory_space=pl.ANY)
    g = (PIECES, d // 256 * d // PIECES, 128)
    return pl.pallas_call(
        outer_kernel,
        grid_spec=pltpu.PrefetchScalarGridSpec(
            num_scalar_prefetch=1,
            grid=(n // tm,),
            in_specs=[row_wide] * (2 * CHUNKS) + [row] * 4 + [full(*wo.shape), full(*vec.shape), hbm, hbm],
            out_specs=[row, row, row, full(*g), full(*g), full(8, d)],
            scratch_shapes=[
                pltpu.VMEM((d, n), BF), pltpu.VMEM((n, d), BF), pltpu.VMEM((CHUNKS, d, wide), BF),
                pltpu.VMEM((CHUNKS, wide, d), BF), pltpu.SemaphoreType.DMA((2, CHUNKS, PIECES)),
            ],
        ),
        out_shape=[shape((n, d))] * 3 + [shape(g), shape(g), shape((8, d), F32)],
        compiler_params=params(),
        cost_estimate=pl.CostEstimate(flops=16 * n * d * (wide * CHUNKS + d), bytes_accessed=8 * d * wide * CHUNKS, transcendentals=0),
        name="outer",
    )(core, *acts, *dhs, x, up, mix, li, wo, vec, w1, w2)


def reflect_kernel(c_ref, q_ref, k_ref, v_ref, o_ref, do_ref, p_ref, ft_ref, dq_ref, dk_ref, dv_ref, gk_ref, gs_ref, ds_ref, *, tq):
    n = k_ref.shape[0]
    low = lax.broadcasted_iota(jnp.int32, (tq, PAIR), 1) < HEAD_DIM
    q_t = q_ref[...].T
    do_t = do_ref[...].T
    scale = HEAD_DIM**-0.5
    dks, dvs = [], []
    for a in range(2):
        for t in range(n // tq):
            rows = pl.ds(t * tq, tq)
            do = do_ref[rows, :]
            zero = jnp.zeros_like(do)
            doa = jnp.where(low, do, zero) if a == 0 else jnp.where(low, zero, do)
            delta = jnp.sum(doa.astype(F32) * o_ref[rows, :].astype(F32), axis=-1, keepdims=True)
            dp = dot(doa, v_ref[...], NT)
            ds = (p_ref[a, rows, :].astype(F32) * (dp - delta)).astype(BF)
            ds_ref[rows, :] = ds
            dq = (dot(ds, k_ref[...], NN) * scale).astype(BF)
            dq_ref[rows, :] = dq if a == 0 else jnp.where(low, dq_ref[rows, :], dq)
        part = slice(HEAD_DIM * a, HEAD_DIM * (a + 1))
        dvs.append(dot(do_t[part], p_ref[a], NN))
        dks.append(dot(q_t[part], ds_ref[...], NN) * scale)
    dv = jnp.concatenate(dvs, axis=0).astype(BF).T
    dk = jnp.concatenate(dks, axis=0).astype(BF).T
    dv_ref[...] = dv
    dk_ref[...] = dk
    g = dot(ft_ref[...], jnp.concatenate([dq_ref[...], dk, dv], axis=1), NN).astype(BF)
    per = g.shape[0] // PIECES
    h = pl.program_id(0)
    for step, ref in enumerate((gs_ref, gk_ref)):

        @pl.when(h == step)
        def _():
            for i, block in enumerate(by_piece(g)):
                ref[:, i * per : (i + 1) * per, :] = block


def reflect(core, packed, o, do, p, first_t, start):
    n, w = packed.shape
    d = w // 3
    hp = d // PAIR

    def which(h, c):
        return (h + 1 - c[0]) % 2

    def cols(off):
        return pl.BlockSpec((n, PAIR), lambda h, c: (0, which(h, c) + off))

    g = (PIECES, 3 * (d // PIECES), 128)
    piece = pl.BlockSpec(g, lambda h, c: (0, 0, 0), pipeline_mode=pl.Buffered(1))
    return pl.pallas_call(
        functools.partial(reflect_kernel, tq=256),
        grid_spec=pltpu.PrefetchScalarGridSpec(
            num_scalar_prefetch=1,
            grid=(2,),
            in_specs=[
                cols(start), cols(start + hp), cols(start + 2 * hp), cols(start), cols(start),
                pl.BlockSpec((2, n, n), lambda h, c: (which(h, c) + start, 0, 0)),
                pl.BlockSpec((d, n), lambda h, c: (0, 0), pipeline_mode=pl.Buffered(1)),
            ],
            out_specs=[cols(0)] * 3 + [piece] * 2,
            scratch_shapes=[pltpu.VMEM((n, n), BF)],
        ),
        out_shape=[shape((n, 2 * PAIR))] * 3 + [shape(g)] * 2,
        compiler_params=params(),
        cost_estimate=pl.CostEstimate(flops=160 * n * n * PAIR, bytes_accessed=8 * n * n, transcendentals=0),
        name="reflect",
    )(core, packed, packed, packed, o, do, p, first_t)


SMALL = 16


def back_kernel(*refs, chunks):
    x_ref, dbr_ref, w_ref, vec_in, mid_ref = refs[:5]
    db1 = refs[5 : 5 + CHUNKS]
    parts = refs[5 + CHUNKS : 5 + CHUNKS + 3 * chunks]
    tg_ref, small_ref, sums = refs[5 + CHUNKS + 3 * chunks :]

    @pl.when(pl.program_id(0) == 0)
    def _():
        sums[...] = jnp.zeros_like(sums)

    d = x_ref.shape[1]
    cw = d // chunks
    dy = None
    for i in range(3 * chunks):
        which, chunk = i % 3, i // 3
        at = which * d + chunk * cw
        part = dot(parts[i][...], w_ref[:, at : at + cw], NT)
        dy = part if dy is None else dy + part
        row = {0: 2, 2: 3}.get(which)
        if row is not None:
            sums[row : row + 1, chunk * cw : (chunk + 1) * cw] += jnp.sum(parts[i][...].astype(F32), axis=0, keepdims=True)
    spread, r = stats(x_ref[...].astype(F32))
    nv = spread * r
    dyg = dy * line(vec_in, "ag")
    dx = r * (dyg - jnp.mean(dyg, axis=-1, keepdims=True) - nv * jnp.mean(dyg * nv, axis=-1, keepdims=True))
    tg_ref[...] = (dbr_ref[...].astype(F32) + dx).astype(BF)
    sums[0:1, :] += jnp.sum(dy * nv, axis=0, keepdims=True)
    sums[1:2, :] += jnp.sum(dy, axis=0, keepdims=True)

    @pl.when(pl.program_id(0) == pl.num_programs(0) - 1)
    def _():
        per = d // PIECES
        sums[4:8, :] = mid_ref[0:4, :]
        rows = sums[...]
        for v in range(PIECES):
            vectors = jnp.concatenate([rows[:, v * per : (v + 1) * per], jnp.zeros((8, 128 - per), F32)], axis=1)
            biases = [b[:, v * 128 : (v + 1) * 128] for b in db1]
            piece = jnp.concatenate([vectors] + biases + [jnp.zeros((SMALL - 8 - CHUNKS, 128), F32)], axis=0)
            small_ref[v * SMALL : (v + 1) * SMALL, :] = piece.astype(BF)


def project_back(x, dbr, w, vec, mids, db1, parts):
    n, d = x.shape
    tm = 256
    row = pl.BlockSpec((tm, d), lambda i: (i, 0))

    def full(*s):
        return pl.BlockSpec(s, lambda i: (0, 0), pipeline_mode=pl.Buffered(1))

    chunks = len(parts) // 3
    return pl.pallas_call(
        functools.partial(back_kernel, chunks=chunks),
        grid=(n // tm,),
        in_specs=[row, row, full(d, 3 * d), full(*vec.shape), full(*mids.shape)]
        + [full(*b.shape) for b in db1]
        + [pl.BlockSpec((tm, d // chunks), lambda i: (i, 0))] * (3 * chunks),
        out_specs=[row, full(PIECES * SMALL, 128)],
        out_shape=[shape((n, d)), shape((PIECES * SMALL, 128))],
        scratch_shapes=[pltpu.VMEM((8, d), F32)],
        compiler_params=params(),
        cost_estimate=pl.CostEstimate(flops=12 * n * d * d, bytes_accessed=16 * n * d, transcendentals=0),
        name="project_back",
    )(x, dbr, w, vec, mids, *db1, *parts)


def exchange(x, axis, by):
    count = lax.axis_size(axis)
    return lax.ppermute(x, axis, [(i, i ^ by) for i in range(count)])


def to_core(g):
    return exchange(g, "seq", 1)


def pick(x, index, axis=0):
    return lax.dynamic_index_in_dim(x, index, axis, keepdims=False)


def after(x, *others):
    return lax.optimization_barrier((x,) + others)[0]


class Part:
    def __init__(self, held, received, rows):
        self.held = (held.reshape(-1, 128), 0)
        self.received = (received.reshape(-1, 128), 0)
        self.rows = rows
        self.open = [0, 1, 2]

    def count(self):
        return self.rows << len(self.open)


def slot_kernel(ids_ref, *refs, items, inputs):
    ins, outs = refs[:inputs], refs[inputs:]

    def read(term, at, count):
        ref, offset = term
        return ins[ref][pl.ds(at + offset, count), :].astype(F32)

    step = 16
    for kind, *rest in items:
        if kind == "split":
            held, received, groups, size, bit, (send, to), keep = rest
            mine = ids_ref[bit]
            for a in range(groups):
                own = pl.multiple_of((2 * a + mine) * size, step)
                other = pl.multiple_of((2 * a + 1 - mine) * size, step)
                outs[send][to + a * size : to + (a + 1) * size, :] = (read(held, other, size) + read(received, other, size)).astype(BF)
                outs[keep][a * size : (a + 1) * size, :] = (read(held, own, size) + read(received, own, size)).astype(BF)
        elif kind == "sum":
            held, received, size, (send, to) = rest
            outs[send][to : to + size, :] = (read(held, 0, size) + read(received, 0, size)).astype(BF)
        else:
            first, second, size, bit, (send, to), keep = rest
            for mine in (0, 1):

                @pl.when(ids_ref[bit] == mine)
                def _():
                    own, other = (first, second) if mine == 0 else (second, first)
                    outs[send][to : to + size, :] = (read(other[0], 0, size) + read(other[1], 0, size)).astype(BF)
                    outs[keep][...] = (read(own[0], 0, size) + read(own[1], 0, size)).astype(BF)


def slot(ids, exchanges, *tokens):
    arrays, items, sizes, moves = [], [], [], []

    def use(term):
        for i, a in enumerate(arrays):
            if a is term[0]:
                return i, term[1]
        arrays.append(term[0])
        return len(arrays) - 1, term[1]

    for stage, parts in exchanges:
        send, to = len(sizes), 0
        sizes.append(0)
        placed = []
        if stage == "pick":
            one, two = parts
            size = one.count()
            items.append(("pick", (use(one.held), use(one.received)), (use(two.held), use(two.received)), size, 1, (send, 0), len(sizes)))
            placed.append((one, len(sizes), 0, 0))
            sizes.append(size)
            to = size
        else:
            for p in parts:
                held, received = use(p.held), use(p.received)
                if stage == "x":
                    items.append(("sum", held, received, p.count(), (send, to)))
                    placed.append((p, send, to, to))
                    to += p.count()
                    continue
                if stage == "half":
                    groups, bit = 1 << len(p.open), 1
                else:
                    groups, bit = 1 << (len(p.open) - 1 - p.open.index(stage)), 2 + stage
                size = p.count() // (2 * groups)
                items.append(("split", held, received, groups, size, bit, (send, to), len(sizes)))
                placed.append((p, len(sizes), 0, to))
                sizes.append(groups * size)
                to += groups * size
                if stage == "half":
                    p.rows //= 2
                else:
                    p.open.remove(stage)
        sizes[send] = to
        moves.append((stage, send, placed))

    if tokens:
        arrays = list(lax.optimization_barrier(tuple(arrays) + tokens)[: len(arrays)])
    whole = pl.BlockSpec(memory_space=pltpu.VMEM)
    outs = pl.pallas_call(
        functools.partial(slot_kernel, items=items, inputs=len(arrays)),
        in_specs=[pl.BlockSpec(memory_space=pltpu.SMEM)] + [whole] * len(arrays),
        out_specs=[whole] * len(sizes),
        out_shape=[shape((size, 128)) for size in sizes],
        compiler_params=params(),
        cost_estimate=pl.CostEstimate(flops=0, bytes_accessed=512 * sum(sizes), transcendentals=0),
        name="slot",
    )(ids, *arrays)
    unit = lax.axis_size("vol") // PIECES
    sent, received = [], []
    for stage, send, placed in moves:
        if stage in ("half", "pick", "x"):
            got = exchange(outs[send], "seq", 2)
        else:
            got = exchange(outs[send], "vol", unit << stage)
        sent.append(outs[send])
        received.append(got)
        for p, keep, at, to in placed:
            p.held = (outs[keep], at)
            p.received = (got, to)
    return sent, received


def home_kernel(ids_ref, live_ref, *refs, mask):
    out_ref = refs[-1]
    for k, ref in enumerate(refs[:-1]):

        @pl.when(pl.program_id(0) == k)
        def _():
            value = ref[...].astype(F32)
            if mask:
                value = value * live_ref[ids_ref[5] ^ k]
            out_ref[...] = value.astype(out_ref.dtype)


def send_home(ids, live, own, others, slices, dtype, mask):
    rows, d = others[0].shape
    return pl.pallas_call(
        functools.partial(home_kernel, mask=mask),
        grid_spec=pltpu.PrefetchScalarGridSpec(
            num_scalar_prefetch=2,
            grid=(slices,),
            in_specs=[pl.BlockSpec((rows, d), lambda k, i, l: (0, 0), pipeline_mode=pl.Buffered(1))] * slices,
            out_specs=pl.BlockSpec((None, rows, d), lambda k, i, l: (k ^ i[5], 0, 0)),
        ),
        out_shape=shape((slices, rows, d), dtype),
        compiler_params=params(),
        cost_estimate=pl.CostEstimate(flops=0, bytes_accessed=6 * slices * rows * d, transcendentals=0),
        name="home",
    )(ids, live, own, *others)


def assemble_ff_kernel(ids_ref, *refs, per):
    ga, gb, gc = refs[:4], refs[4:8], refs[8:12]
    expand_ref, reduce_ref = refs[12:]
    c = ids_ref[0]

    def first_layer(i, core, value):
        for k in range(PIECES // 2):
            at = pl.multiple_of(((core * (PIECES // 2) + k) * CHUNKS + i) * 128, 128)
            expand_ref[:, pl.ds(at, 128)] = value[k * per : (k + 1) * per, :]

    def second_layer(i, core, value):
        d = value.shape[0]
        reduce_ref[i * 128 : (i + 1) * 128, pl.ds(pl.multiple_of(core * d, 128), d)] = value.T

    half = per * (PIECES // 2)
    for core, (mine, other) in ((c, (ga[0], ga[1])), (1 - c, (ga[2], ga[3]))):

        @pl.when(ids_ref[1] == 0)
        def _():
            first_layer(0, core, mine[...].astype(F32))
            second_layer(0, core, other[...].astype(F32))

        @pl.when(ids_ref[1] == 1)
        def _():
            first_layer(0, core, other[...].astype(F32))
            second_layer(0, core, mine[...].astype(F32))

    for i, refs_i in ((1, gb), (2, gc)):
        for core, (one, two) in ((c, refs_i[:2]), (1 - c, refs_i[2:])):
            total = one[...].astype(F32) + two[...].astype(F32)
            first_layer(i, core, total[:half])
            second_layer(i, core, total[half:])


def assemble_end_kernel(ids_ref, *refs, per):
    mine, theirs = refs[:4], refs[4:8]
    small_held, small_received, output_ref, input_ref, vector_ref = refs[8:]
    c = ids_ref[0]
    d = PIECES * per

    def output_part(core, value):
        for k in range(3):
            output_ref[:, pl.ds(pl.multiple_of((core * 3 + k) * 128, 128), 128)] = value[k * per : (k + 1) * per, :]

    def pair_part(i, core, value):
        for k in range(3):
            at = pl.multiple_of(k * d + (2 * i + core) * 128, 128)
            input_ref[:, pl.ds(at, 128)] = value[k * per : (k + 1) * per, :]

    for core, (own, other, one, two) in ((c, mine), (1 - c, theirs)):

        @pl.when(ids_ref[1] == 0)
        def _():
            output_part(core, own[...].astype(F32))
            pair_part(0, core, other[...].astype(F32))

        @pl.when(ids_ref[1] == 1)
        def _():
            output_part(core, other[...].astype(F32))
            pair_part(0, core, own[...].astype(F32))

        total = one[...].astype(F32) + two[...].astype(F32)
        for i in (1, 2):
            pair_part(i, core, total[(i - 1) * 3 * per : i * 3 * per])
    vector_ref[...] = small_held[...].astype(F32) + small_received[...].astype(F32)


def assemble(kernel, ids, per, arrays, outs, name):
    whole = pl.BlockSpec(memory_space=pltpu.VMEM)
    return pl.pallas_call(
        functools.partial(kernel, per=per),
        in_specs=[pl.BlockSpec(memory_space=pltpu.SMEM)] + [whole] * len(arrays),
        out_specs=[whole] * len(outs),
        out_shape=[shape(o, F32) for o in outs],
        compiler_params=params(),
        name=name,
    )(ids, *arrays)


def on_device(
    volume_slices, volume_owner, tokens, cotangent, attend_gain, attend_shift, input_weight, query_bias, value_bias,
    output_weight, output_bias, mixer_gain, mixer_shift, expand_weight, expand_bias, reduce_weight, reduce_bias,
):
    slices, rows, d = tokens.shape
    ff = expand_weight.shape[1]
    nv = lax.axis_size("vol")
    peers = lax.axis_size("seq")
    me = lax.axis_index("seq")
    core_id = me % 2
    x_id = (me // 2) % 2
    core = core_id.astype(jnp.int32).reshape(1)
    n = rows * peers
    vol = lax.axis_index("vol")
    unit = nv // PIECES
    ids = jnp.stack([core_id, x_id, (vol // unit) % 2, (vol // (2 * unit)) % 2, (vol // (4 * unit)) % 2, me]).astype(jnp.int32)

    def from_peers(x, ks):
        parts = [pick(x, me ^ k) for k in ks]
        return [p if k == 0 else exchange(p, "seq", k) for p, k in zip(parts, ks)]

    far_parts = from_peers(tokens, (3, 2))
    near_parts = from_peers(tokens, (0, 1))
    zero = jnp.zeros((d,), BF)
    vec = jnp.concatenate(
        [attend_gain, attend_shift, query_bias, zero, value_bias, output_bias, mixer_gain, mixer_shift, reduce_bias] + [zero] * 7
    ).astype(F32).reshape(16, d)
    wide = ff // CHUNKS
    lanes = wide // PIECES
    b1 = expand_bias.astype(F32).reshape(ff // 128, 128)
    load = jnp.sum(jnp.where(volume_owner == lax.axis_index("vol"), volume_slices, 0))
    live = (jnp.arange(slices) < load).astype(BF)

    made = project_in(jnp.concatenate(near_parts), 0, n, None, vec, input_weight)
    far = jnp.concatenate([after(far_parts[1], made[2], b1, live), far_parts[0]])
    x, first_t, packed = project_in(far, 2 * rows, n, made, vec, input_weight)
    upstream = jnp.concatenate(from_peers(after(cotangent, far_parts[0], made[2]) * live[:, None, None], (0, 1, 2, 3)))

    mixed, inverse, weights = attend(packed)

    acts, dhs, db1 = [], [], []
    second = None

    def hidden(token, i):
        head = (x, mixed, output_weight, vec) if i == 0 else None
        a, g, gk, gs, b, *sec = hidden_part(token, head, second, upstream, expand_weight, reduce_weight, b1, i)
        acts.append(a)
        dhs.append(g)
        db1.append(b)
        return gk, gs, sec

    Y, Z1, Z2 = 0, 1, 2
    piece_rows = d // 2 + d // 2
    pair_rows = 3 * (d // PIECES)
    k0, s0, (second,) = hidden(core, 0)
    r0 = to_core(s0)
    k1, s1, _ = hidden(after(core, s0), 1)
    r1 = to_core(s1)
    ga = Part(k0, r0, piece_rows)
    sent, _ = slot(ids, [("half", [ga])], s1)
    k2, s2, _ = hidden(after(core, s1, *sent), 2)
    r2 = to_core(s2)
    gb = Part(k1, r1, piece_rows)
    sent, _ = slot(ids, [(Z1, [gb])], s2)
    out, d_branch, d_mixed, k3, s3, sums_mid = outer(
        after(core, s2, *sent), acts, dhs, x, upstream, mixed, inverse, output_weight, vec, expand_weight, reduce_weight
    )
    r3 = to_core(s3)

    def homeward(a):
        blocks = [a[k * rows : (k + 1) * rows] for k in range(1, peers)]
        return blocks, [exchange(b, "seq", k + 1) for k, b in enumerate(blocks)]

    out_sent, outs = homeward(out)
    gc = Part(k2, r2, piece_rows)
    sent, got = slot(ids, [(Y, [gc]), (Z2, [gb])], s3)
    parts = []

    def reflect_part(token, i):
        dq, dk, dv, gk, gs = reflect(token, packed, mixed, d_mixed, weights, first_t, 2 * i)
        parts.extend([dq, dk, dv])
        return gk, gs

    p0, q0 = reflect_part(after(core, s3, *sent, *out_sent), 0)
    t0 = to_core(q0)
    wait_c = got[0]
    sent, _ = slot(ids, [(Y, [ga, gb])], q0)
    p1, q1 = reflect_part(after(core, q0, wait_c, *sent, *outs), 1)
    t1 = to_core(q1)
    gd, gd2 = Part(k3, r3, pair_rows), Part(p0, t0, pair_rows)
    sent, _ = slot(ids, [(Z1, [ga, gc]), ("pick", [gd, gd2])], q1)
    p2, q2 = reflect_part(after(core, q1, *sent), 2)
    t2 = to_core(q2)
    ge1, ge2 = Part(p1, t1, pair_rows), Part(p2, t2, pair_rows)
    sent, got_b = slot(ids, [(Y, [ge1, ge2, gd]), (Z2, [ga, gc])], q2)
    d_tokens, small = project_back(after(x, *sent), d_branch, input_weight, vec, sums_mid, db1, parts)

    tg_sent, tgs = homeward(d_tokens)
    gv = Part(small, to_core(small), SMALL)
    sent1, got1 = slot(ids, [(Y, [gv]), ("x", [ga, gb, gc])], small, *tg_sent)
    block_out = send_home(ids, live, out, [after(o, *sent1) for o in outs], slices, BF, True)
    sent2, got2 = slot(ids, [(Z1, [ge1, ge2, gd, gv])], *got1)
    per = d // PIECES

    def both_terms(p, *tokens):
        pieces = [lax.slice_in_dim(a, at, at + p.count()) for a, at in (p.held, p.received)]
        pieces = list(lax.optimization_barrier(tuple(pieces) + tokens)[:2])
        return pieces + [to_core(a) for a in pieces]

    spare = [1 << i for i in range(unit.bit_length() - 1)]
    ff_terms = both_terms(ga, *sent2) + both_terms(gb, *sent2) + both_terms(gc, *sent2)
    sent3, got3 = slot(ids, [(Z2, [ge1, ge2, gd, gv])], *got2)
    expand_grad, reduce_grad = assemble(
        assemble_ff_kernel, ids, per, list(lax.optimization_barrier(tuple(ff_terms) + tuple(sent3))[: len(ff_terms)]), [(per, ff), (ff // PIECES, d)], "assemble_ff"
    )
    sent4, got4 = slot(ids, [("x", [ge1, ge2, gd, gv])], *got3)
    tgs = [after(t, *sent4) for t in tgs]
    tokens_grad = send_home(ids, live, d_tokens, tgs, slices, F32, False)
    at = 2 * pair_rows
    held, received = sent4[0], got4[0]
    ends = [held[at : at + pair_rows], received[at : at + pair_rows], held[:at], received[:at]]
    ends = ends + [to_core(a) for a in ends]
    at += pair_rows
    output_grad, input_grad, vectors = assemble(
        assemble_end_kernel, ids, per, ends + [held[at:], received[at:]], [(per, d), (per, 3 * d), (SMALL, 128)], "assemble_end"
    )
    bias_rows = vectors[8 : 8 + CHUNKS]
    vectors = vectors[:8, :per]
    if unit > 1:
        sub = vol % unit

        def add_rest(a):
            for by in spare:
                a = a + exchange(a, "vol", by)
            return a

        def cut(a, axis):
            size = a.shape[axis] // unit
            return lax.dynamic_slice_in_dim(add_rest(a), sub * size, size, axis)

        expand_grad, reduce_grad, output_grad, input_grad = [cut(a, 0) for a in (expand_grad, reduce_grad, output_grad, input_grad)]
        expand_bias_grad = cut(bias_rows.reshape(-1), 0)
        vectors = cut(vectors, 1)
    else:
        expand_bias_grad = bias_rows.reshape(-1)
    return (
        block_out, tokens_grad, vectors[0], vectors[1], input_grad, vectors[2], vectors[3], output_grad, vectors[4],
        vectors[5], vectors[6], expand_grad, expand_bias_grad, reduce_grad, vectors[7],
    )


def solution(mesh):
    rows = P("vol", "seq", None)
    return jax.shard_map(
        on_device,
        mesh=mesh,
        in_specs=(P(), P(), rows, rows) + (P(),) * 13,
        out_specs=(rows, rows, P("vol"), P("vol"), P("vol", None), P("vol"), P("vol"), P("vol", None), P("vol"), P("vol"),
                   P("vol"), P("vol", None), P("vol"), P("vol", None), P("vol")),
        check_vma=False,
    )
```

```python
import functools

import jax
import jax.numpy as jnp
from jax import lax
from jax.experimental import pallas as pl
from jax.experimental.pallas import tpu as pltpu
from jax.sharding import PartitionSpec as P

HEAD_DIM = 64
PAIR = 2 * HEAD_DIM
LOG2E = 1.4426950408889634
PIECES = 8
CHUNKS = 3
ROW = {n: i for i, n in enumerate(("ag", "ash", "qb", "zero", "vb", "ob", "mg", "ms", "rb"))}
BF = jnp.bfloat16
F32 = jnp.float32
NN = (((1,), (0,)), ((), ()))
NT = (((1,), (1,)), ((), ()))
TAIL = (
    0.11962928008603971,
    0.12075423895539067,
    0.09991176086876633,
    0.12856720585766357,
    -0.05369390237929985,
    0.20636430391507077,
    -0.15720912816414995,
    0.03567616760586865,
)


def dot(a, b, dims):
    return lax.dot_general(a, b, dims, preferred_element_type=F32)


def params():
    return pltpu.CompilerParams(vmem_limit_bytes=24 << 20)


def line(ref, name):
    return ref[ROW[name] : ROW[name] + 1, :]


def shape(dims, dtype=BF):
    return jax.ShapeDtypeStruct(dims, dtype)


def normal(h):
    a = jnp.abs(h)
    t = 1.0 / (1.0 + 0.3 * a)
    s = TAIL[7] * t + TAIL[6]
    for c in TAIL[5::-1]:
        s = s * t + c
    e = jnp.exp2(h * h * (-0.5 * LOG2E))
    tail = s * t * e
    return jnp.where(h >= 0, 1.0 - tail, tail), e * 0.3989422804014327


def stats(v):
    spread = v - jnp.mean(v, axis=-1, keepdims=True)
    return spread, lax.rsqrt(jnp.mean(spread * spread, axis=-1, keepdims=True) + 1e-6)


def in_kernel(x_ref, vec_ref, w_ref, *rest):
    x_out, first_t, packed = rest[-3:]
    x = x_ref[...]
    d = x.shape[1]
    spread, r = stats(x.astype(F32))
    f = (spread * r * line(vec_ref, "ag") + line(vec_ref, "ash")).astype(BF)
    x_out[...] = x
    for i, bias in enumerate(("qb", "zero", "vb")):
        packed[:, i * d : (i + 1) * d] = (dot(f, w_ref[:, i * d : (i + 1) * d], NN) + line(vec_ref, bias)).astype(BF)
    first_t[...] = f.T


def project_in(part, offset, total, before, vec, weight):
    rows, d = part.shape
    wide = weight.shape[1]
    tm = 256
    first_block = offset // tm

    def full(a):
        return pl.BlockSpec(a.shape, lambda i: (0, 0), pipeline_mode=pl.Buffered(1))

    in_specs = [pl.BlockSpec((tm, d), lambda i: (i, 0)), full(vec), full(weight)]
    args = [part, vec, weight]
    aliases = {}
    if before is not None:
        aliases = {3: 0, 4: 1, 5: 2}
        in_specs += [pl.BlockSpec(memory_space=pl.ANY)] * 3
        args += list(before)
    return pl.pallas_call(
        in_kernel,
        grid=(rows // tm,),
        in_specs=in_specs,
        out_specs=[
            pl.BlockSpec((tm, d), lambda i: (i + first_block, 0)),
            pl.BlockSpec((d, tm), lambda i: (0, i + first_block)),
            pl.BlockSpec((tm, wide), lambda i: (i + first_block, 0)),
        ],
        out_shape=[shape((total, d)), shape((d, total)), shape((total, wide))],
        input_output_aliases=aliases,
        compiler_params=params(),
        cost_estimate=pl.CostEstimate(flops=6 * rows * d * wide, bytes_accessed=2 * (d * wide + rows * (wide + 3 * d)), transcendentals=0),
        name="project_in",
    )(*args)


def attend_kernel(q_ref, k_ref, v_ref, o_ref, inv_ref, p_ref, vx_ref, *, tq):
    n = k_ref.shape[0]
    vx_ref[:, :PAIR] = v_ref[...]
    vx_ref[:, PAIR:] = jnp.ones((n, PAIR), BF)
    low = lax.broadcasted_iota(jnp.int32, (tq, PAIR), 1) < HEAD_DIM
    for t in range(n // tq):
        rows = pl.ds(t * tq, tq)
        q = q_ref[rows, :]
        zero = jnp.zeros_like(q)
        outs = []
        for a in range(2):
            qa = jnp.where(low, q, zero) if a == 0 else jnp.where(low, zero, q)
            s = dot(qa, k_ref[...], NT)
            top = jnp.max(s, axis=-1, keepdims=True)
            p = jnp.exp2((s - top) * (LOG2E * HEAD_DIM**-0.5)).astype(BF)
            p_ref[a, rows, :] = p
            both = dot(p, vx_ref[...], NN)
            inv = 1.0 / both[:, PAIR:]
            outs.append((both[:, :PAIR] * inv, inv))
        o_ref[rows, :] = jnp.where(low, outs[0][0], outs[1][0]).astype(BF)
        inv_ref[rows, :] = jnp.where(low, outs[0][1], outs[1][1])


def attend(packed):
    n, w = packed.shape
    d = w // 3
    hp = d // PAIR

    def cols(off):
        return pl.BlockSpec((n, PAIR), lambda h: (0, h + off))

    return pl.pallas_call(
        functools.partial(attend_kernel, tq=128),
        grid=(hp,),
        in_specs=[cols(0), cols(hp), cols(2 * hp)],
        out_specs=[cols(0), cols(0), pl.BlockSpec((2, n, n), lambda h: (h, 0, 0))],
        out_shape=[shape((n, d)), shape((n, d), F32), shape((2 * hp, n, n))],
        scratch_shapes=[pltpu.VMEM((n, 2 * PAIR), BF)],
        compiler_params=params(),
        cost_estimate=pl.CostEstimate(flops=16 * n * n * d, bytes_accessed=4 * n * n * hp, transcendentals=0),
        name="attend",
    )(packed, packed, packed)


def by_piece(g):
    rows = g.shape[0] // PIECES
    return [g[:, i : i + 128].reshape(PIECES, rows, 128) for i in range(0, g.shape[1], 128)]


def weight_copies(w1_hbm, w2_hbm, w1, w2, sems, chunks):
    first, second = [], []
    for slot, i in enumerate(chunks):
        for v in range(PIECES):
            at = pl.ds((v * CHUNKS + i) * 128, 128)
            to = pl.ds(v * 128, 128)
            first.append(pltpu.make_async_copy(w1_hbm.at[:, at], w1.at[slot, :, to], sems.at[0, slot, v]))
            second.append(pltpu.make_async_copy(w2_hbm.at[at, :], w2.at[slot, to, :], sems.at[1, slot, v]))
    return first, second


def hidden_kernel(c_ref, *refs, i, sub, head):
    if head:
        x_ref, mix_ref, wo_ref, vec_ref, *refs = refs
    else:
        sec_in, *refs = refs
    up_ref, w1_hbm, w2_hbm, b1_ref, act_ref, dh_ref, gk_ref, gs_ref, db1_ref, *refs = refs
    if head:
        sec_out, *refs = refs
    sec_t, up_t, act, dh, w1, w2, sems = refs
    t = pl.program_id(0)
    tm, d = up_ref.shape
    wide = act_ref.shape[1]
    rows = pl.ds(pl.multiple_of(t * tm, tm), tm)
    first, second = weight_copies(w1_hbm, w2_hbm, w1, w2, sems, [i])

    @pl.when(t == 0)
    def _():
        for copy in first + second:
            copy.start()
        db1_ref[...] = jnp.zeros_like(db1_ref)

    up = up_ref[...]
    if head:
        m = x_ref[...].astype(F32) + dot(mix_ref[...], wo_ref[...], NN) + line(vec_ref, "ob")
        spread, r = stats(m)
        sec = (spread * r * line(vec_ref, "mg") + line(vec_ref, "ms")).astype(BF)
        sec_out[...] = sec
    else:
        sec = sec_in[...]

    @pl.when(t == 0)
    def _():
        for copy in first + second:
            copy.wait()

    for at in range(0, wide, sub):
        cols = slice(at, at + sub)
        bias = jnp.concatenate([b1_ref[v * CHUNKS + i : v * CHUNKS + i + 1, :] for v in range(at // 128, (at + sub) // 128)], axis=1)
        h = dot(sec, w1[0, :, cols], NN) + bias
        da = dot(up, w2[0, cols, :], NT)
        cdf, pdf = normal(h)
        a = (h * cdf).astype(BF)
        dhv = (da * (cdf + h * pdf)).astype(BF)
        act_ref[:, cols] = a
        dh_ref[:, cols] = dhv
        act[rows, cols] = a
        dh[rows, cols] = dhv
        db1_ref[:, cols] += jnp.sum(dhv.astype(F32), axis=0, keepdims=True)
    sec_t[:, rows] = sec.T
    up_t[:, rows] = up.T

    @pl.when(t == pl.num_programs(0) - 1)
    def _():
        c = c_ref[0]
        per = d // PIECES
        for ref, mine in ((gs_ref, 1 - c), (gk_ref, c)):
            half = wide // 2
            g = dot(sec_t[...], dh[:, pl.ds(pl.multiple_of(mine * half, half), half)], NN).astype(BF)
            for k, block in enumerate(by_piece(g)):
                ref[:, k * per : (k + 1) * per, :] = block
            at = half // 128 * per
            half = d // 2
            g = dot(up_t[pl.ds(pl.multiple_of(mine * half, half), half), :], act[...], NN).astype(BF)
            for v in range(PIECES):
                ref[v, at:, :] = g[:, v * 128 : (v + 1) * 128]


def hidden_part(core, head, sec, up, w1, w2, b1, i, tm=256, sub=512):
    n, d = up.shape
    wide = 128 * PIECES
    assert wide * CHUNKS == w1.shape[1]

    def full(*s):
        return pl.BlockSpec(s, lambda t, c: (0,) * len(s), pipeline_mode=pl.Buffered(1))

    row = pl.BlockSpec((tm, d), lambda t, c: (t, 0))
    row_wide = pl.BlockSpec((tm, wide), lambda t, c: (t, 0))
    hbm = pl.BlockSpec(memory_space=pl.ANY)
    g = (PIECES, d // 2 + wide // 256 * d // PIECES, 128)
    if head:
        args, specs = list(head), [row, row, full(*head[2].shape), full(*head[3].shape)]
    else:
        args, specs = [sec], [row]
    return pl.pallas_call(
        functools.partial(hidden_kernel, i=i, sub=sub, head=bool(head)),
        grid_spec=pltpu.PrefetchScalarGridSpec(
            num_scalar_prefetch=1,
            grid=(n // tm,),
            in_specs=specs + [row, hbm, hbm, full(*b1.shape)],
            out_specs=[row_wide, row_wide, full(*g), full(*g), full(1, wide)] + ([row] if head else []),
            scratch_shapes=[
                pltpu.VMEM((d, n), BF), pltpu.VMEM((d, n), BF), pltpu.VMEM((n, wide), BF), pltpu.VMEM((n, wide), BF),
                pltpu.VMEM((1, d, wide), BF), pltpu.VMEM((1, wide, d), BF), pltpu.SemaphoreType.DMA((2, 1, PIECES)),
            ],
        ),
        out_shape=[shape((n, wide)), shape((n, wide)), shape(g), shape(g), shape((1, wide), F32)] + ([shape((n, d))] if head else []),
        compiler_params=params(),
        cost_estimate=pl.CostEstimate(flops=24 * n * d * wide, bytes_accessed=8 * d * wide, transcendentals=0),
        name="hidden",
    )(core, *args, up, w1, w2, b1)


def outer_kernel(c_ref, *refs):
    acts, dhs = refs[:CHUNKS], refs[CHUNKS : 2 * CHUNKS]
    x_ref, up_ref, mix_ref, li_ref, wo_ref, vec_ref, w1_hbm, w2_hbm = refs[2 * CHUNKS : 2 * CHUNKS + 8]
    out_ref, dbr_ref, do_ref, gk_ref, gs_ref, sums_ref, mix_t, dbr, w1, w2, sems = refs[2 * CHUNKS + 8 :]
    t = pl.program_id(0)
    tm, d = x_ref.shape
    rows = pl.ds(pl.multiple_of(t * tm, tm), tm)
    first, second = weight_copies(w1_hbm, w2_hbm, w1, w2, sems, range(CHUNKS))

    @pl.when(t == 0)
    def _():
        for copy in first + second:
            copy.start()
        sums_ref[...] = jnp.zeros_like(sums_ref)

    m = x_ref[...].astype(F32) + dot(mix_ref[...], wo_ref[...], NN) + line(vec_ref, "ob")
    spread, r = stats(m)
    nv = spread * r
    up = up_ref[...].astype(F32)
    mix_t[:, rows] = mix_ref[...].T

    @pl.when(t == 0)
    def _():
        for copy in first + second:
            copy.wait()

    dy = dot(dhs[0][...], w1[0], NT)
    for i in range(1, CHUNKS):
        dy += dot(dhs[i][...], w1[i], NT)
    o = dot(acts[0][...], w2[0], NN)
    for i in range(1, CHUNKS):
        o += dot(acts[i][...], w2[i], NN)
    dyg = dy * line(vec_ref, "mg")
    dm = up + r * (dyg - jnp.mean(dyg, axis=-1, keepdims=True) - nv * jnp.mean(dyg * nv, axis=-1, keepdims=True))
    db = dm.astype(BF)
    dbr_ref[...] = db
    dbr[rows, :] = db
    out_ref[...] = (m + o + line(vec_ref, "rb")).astype(BF)
    do_ref[...] = (dot(db, wo_ref[...], NT) * li_ref[...]).astype(BF)
    sums_ref[0:1, :] += jnp.sum(db.astype(F32), axis=0, keepdims=True)
    sums_ref[1:2, :] += jnp.sum(dy * nv, axis=0, keepdims=True)
    sums_ref[2:3, :] += jnp.sum(dy, axis=0, keepdims=True)
    sums_ref[3:4, :] += jnp.sum(up, axis=0, keepdims=True)

    @pl.when(t == pl.num_programs(0) - 1)
    def _():
        half = d // 2
        per = d // PIECES
        for ref, mine in ((gs_ref, 1 - c_ref[0]), (gk_ref, c_ref[0])):
            g = dot(mix_t[...], dbr[:, pl.ds(pl.multiple_of(mine * half, half), half)], NN).astype(BF)
            for i, block in enumerate(by_piece(g)):
                ref[:, i * per : (i + 1) * per, :] = block


def outer(core, acts, dhs, x, up, mix, li, wo, vec, w1, w2, tm=256):
    n, d = x.shape
    wide = acts[0].shape[1]

    def full(*s):
        return pl.BlockSpec(s, lambda t, c: (0,) * len(s), pipeline_mode=pl.Buffered(1))

    row = pl.BlockSpec((tm, d), lambda t, c: (t, 0))
    row_wide = pl.BlockSpec((tm, wide), lambda t, c: (t, 0))
    hbm = pl.BlockSpec(memory_space=pl.ANY)
    g = (PIECES, d // 256 * d // PIECES, 128)
    return pl.pallas_call(
        outer_kernel,
        grid_spec=pltpu.PrefetchScalarGridSpec(
            num_scalar_prefetch=1,
            grid=(n // tm,),
            in_specs=[row_wide] * (2 * CHUNKS) + [row] * 4 + [full(*wo.shape), full(*vec.shape), hbm, hbm],
            out_specs=[row, row, row, full(*g), full(*g), full(8, d)],
            scratch_shapes=[
                pltpu.VMEM((d, n), BF), pltpu.VMEM((n, d), BF), pltpu.VMEM((CHUNKS, d, wide), BF),
                pltpu.VMEM((CHUNKS, wide, d), BF), pltpu.SemaphoreType.DMA((2, CHUNKS, PIECES)),
            ],
        ),
        out_shape=[shape((n, d))] * 3 + [shape(g), shape(g), shape((8, d), F32)],
        compiler_params=params(),
        cost_estimate=pl.CostEstimate(flops=16 * n * d * (wide * CHUNKS + d), bytes_accessed=8 * d * wide * CHUNKS, transcendentals=0),
        name="outer",
    )(core, *acts, *dhs, x, up, mix, li, wo, vec, w1, w2)


def reflect_kernel(c_ref, q_ref, k_ref, v_ref, o_ref, do_ref, p_ref, ft_ref, dq_ref, dk_ref, dv_ref, gk_ref, gs_ref, ds_ref, *, tq):
    n = k_ref.shape[0]
    low = lax.broadcasted_iota(jnp.int32, (tq, PAIR), 1) < HEAD_DIM
    q_t = q_ref[...].T
    do_t = do_ref[...].T
    scale = HEAD_DIM**-0.5
    dks, dvs = [], []
    for a in range(2):
        for t in range(n // tq):
            rows = pl.ds(t * tq, tq)
            do = do_ref[rows, :]
            zero = jnp.zeros_like(do)
            doa = jnp.where(low, do, zero) if a == 0 else jnp.where(low, zero, do)
            delta = jnp.sum(doa.astype(F32) * o_ref[rows, :].astype(F32), axis=-1, keepdims=True)
            dp = dot(doa, v_ref[...], NT)
            ds = (p_ref[a, rows, :].astype(F32) * (dp - delta)).astype(BF)
            ds_ref[rows, :] = ds
            dq = (dot(ds, k_ref[...], NN) * scale).astype(BF)
            dq_ref[rows, :] = dq if a == 0 else jnp.where(low, dq_ref[rows, :], dq)
        part = slice(HEAD_DIM * a, HEAD_DIM * (a + 1))
        dvs.append(dot(do_t[part], p_ref[a], NN))
        dks.append(dot(q_t[part], ds_ref[...], NN) * scale)
    dv = jnp.concatenate(dvs, axis=0).astype(BF).T
    dk = jnp.concatenate(dks, axis=0).astype(BF).T
    dv_ref[...] = dv
    dk_ref[...] = dk
    g = dot(ft_ref[...], jnp.concatenate([dq_ref[...], dk, dv], axis=1), NN).astype(BF)
    per = g.shape[0] // PIECES
    h = pl.program_id(0)
    for step, ref in enumerate((gs_ref, gk_ref)):

        @pl.when(h == step)
        def _():
            for i, block in enumerate(by_piece(g)):
                ref[:, i * per : (i + 1) * per, :] = block


def reflect(core, packed, o, do, p, first_t, start):
    n, w = packed.shape
    d = w // 3
    hp = d // PAIR

    def which(h, c):
        return (h + 1 - c[0]) % 2

    def cols(off):
        return pl.BlockSpec((n, PAIR), lambda h, c: (0, which(h, c) + off))

    g = (PIECES, 3 * (d // PIECES), 128)
    piece = pl.BlockSpec(g, lambda h, c: (0, 0, 0), pipeline_mode=pl.Buffered(1))
    return pl.pallas_call(
        functools.partial(reflect_kernel, tq=256),
        grid_spec=pltpu.PrefetchScalarGridSpec(
            num_scalar_prefetch=1,
            grid=(2,),
            in_specs=[
                cols(start), cols(start + hp), cols(start + 2 * hp), cols(start), cols(start),
                pl.BlockSpec((2, n, n), lambda h, c: (which(h, c) + start, 0, 0)),
                pl.BlockSpec((d, n), lambda h, c: (0, 0), pipeline_mode=pl.Buffered(1)),
            ],
            out_specs=[cols(0)] * 3 + [piece] * 2,
            scratch_shapes=[pltpu.VMEM((n, n), BF)],
        ),
        out_shape=[shape((n, 2 * PAIR))] * 3 + [shape(g)] * 2,
        compiler_params=params(),
        cost_estimate=pl.CostEstimate(flops=160 * n * n * PAIR, bytes_accessed=8 * n * n, transcendentals=0),
        name="reflect",
    )(core, packed, packed, packed, o, do, p, first_t)


SMALL = 16


def back_kernel(*refs, chunks):
    x_ref, dbr_ref, w_ref, vec_in, mid_ref = refs[:5]
    db1 = refs[5 : 5 + CHUNKS]
    parts = refs[5 + CHUNKS : 5 + CHUNKS + 3 * chunks]
    tg_ref, small_ref, sums = refs[5 + CHUNKS + 3 * chunks :]

    @pl.when(pl.program_id(0) == 0)
    def _():
        sums[...] = jnp.zeros_like(sums)

    d = x_ref.shape[1]
    cw = d // chunks
    dy = None
    for i in range(3 * chunks):
        which, chunk = i % 3, i // 3
        at = which * d + chunk * cw
        part = dot(parts[i][...], w_ref[:, at : at + cw], NT)
        dy = part if dy is None else dy + part
        row = {0: 2, 2: 3}.get(which)
        if row is not None:
            sums[row : row + 1, chunk * cw : (chunk + 1) * cw] += jnp.sum(parts[i][...].astype(F32), axis=0, keepdims=True)
    spread, r = stats(x_ref[...].astype(F32))
    nv = spread * r
    dyg = dy * line(vec_in, "ag")
    dx = r * (dyg - jnp.mean(dyg, axis=-1, keepdims=True) - nv * jnp.mean(dyg * nv, axis=-1, keepdims=True))
    tg_ref[...] = (dbr_ref[...].astype(F32) + dx).astype(BF)
    sums[0:1, :] += jnp.sum(dy * nv, axis=0, keepdims=True)
    sums[1:2, :] += jnp.sum(dy, axis=0, keepdims=True)

    @pl.when(pl.program_id(0) == pl.num_programs(0) - 1)
    def _():
        per = d // PIECES
        sums[4:8, :] = mid_ref[0:4, :]
        rows = sums[...]
        for v in range(PIECES):
            vectors = jnp.concatenate([rows[:, v * per : (v + 1) * per], jnp.zeros((8, 128 - per), F32)], axis=1)
            biases = [b[:, v * 128 : (v + 1) * 128] for b in db1]
            piece = jnp.concatenate([vectors] + biases + [jnp.zeros((SMALL - 8 - CHUNKS, 128), F32)], axis=0)
            small_ref[v * SMALL : (v + 1) * SMALL, :] = piece.astype(BF)


def project_back(x, dbr, w, vec, mids, db1, parts):
    n, d = x.shape
    tm = 256
    row = pl.BlockSpec((tm, d), lambda i: (i, 0))

    def full(*s):
        return pl.BlockSpec(s, lambda i: (0, 0), pipeline_mode=pl.Buffered(1))

    chunks = len(parts) // 3
    return pl.pallas_call(
        functools.partial(back_kernel, chunks=chunks),
        grid=(n // tm,),
        in_specs=[row, row, full(d, 3 * d), full(*vec.shape), full(*mids.shape)]
        + [full(*b.shape) for b in db1]
        + [pl.BlockSpec((tm, d // chunks), lambda i: (i, 0))] * (3 * chunks),
        out_specs=[row, full(PIECES * SMALL, 128)],
        out_shape=[shape((n, d)), shape((PIECES * SMALL, 128))],
        scratch_shapes=[pltpu.VMEM((8, d), F32)],
        compiler_params=params(),
        cost_estimate=pl.CostEstimate(flops=12 * n * d * d, bytes_accessed=16 * n * d, transcendentals=0),
        name="project_back",
    )(x, dbr, w, vec, mids, *db1, *parts)


def exchange(x, axis, by):
    count = lax.axis_size(axis)
    return lax.ppermute(x, axis, [(i, i ^ by) for i in range(count)])


def to_core(g):
    return exchange(g, "seq", 1)


def pick(x, index, axis=0):
    return lax.dynamic_index_in_dim(x, index, axis, keepdims=False)


def after(x, *others):
    return lax.optimization_barrier((x,) + others)[0]


class Part:
    def __init__(self, held, received, rows):
        self.held = (held.reshape(-1, 128), 0)
        self.received = (received.reshape(-1, 128), 0)
        self.rows = rows
        self.open = [0, 1, 2]

    def count(self):
        return self.rows << len(self.open)


def slot_kernel(ids_ref, *refs, items, inputs):
    ins, outs = refs[:inputs], refs[inputs:]

    def read(term, at, count):
        ref, offset = term
        return ins[ref][pl.ds(at + offset, count), :].astype(F32)

    step = 16
    for kind, *rest in items:
        if kind == "split":
            held, received, groups, size, bit, (send, to), keep = rest
            mine = ids_ref[bit]
            for a in range(groups):
                own = pl.multiple_of((2 * a + mine) * size, step)
                other = pl.multiple_of((2 * a + 1 - mine) * size, step)
                outs[send][to + a * size : to + (a + 1) * size, :] = (read(held, other, size) + read(received, other, size)).astype(BF)
                outs[keep][a * size : (a + 1) * size, :] = (read(held, own, size) + read(received, own, size)).astype(BF)
        elif kind == "sum":
            held, received, size, (send, to) = rest
            outs[send][to : to + size, :] = (read(held, 0, size) + read(received, 0, size)).astype(BF)
        else:
            first, second, size, bit, (send, to), keep = rest
            for mine in (0, 1):

                @pl.when(ids_ref[bit] == mine)
                def _():
                    own, other = (first, second) if mine == 0 else (second, first)
                    outs[send][to : to + size, :] = (read(other[0], 0, size) + read(other[1], 0, size)).astype(BF)
                    outs[keep][...] = (read(own[0], 0, size) + read(own[1], 0, size)).astype(BF)


def slot(ids, exchanges, *tokens):
    arrays, items, sizes, moves = [], [], [], []

    def use(term):
        for i, a in enumerate(arrays):
            if a is term[0]:
                return i, term[1]
        arrays.append(term[0])
        return len(arrays) - 1, term[1]

    for stage, parts in exchanges:
        send, to = len(sizes), 0
        sizes.append(0)
        placed = []
        if stage == "pick":
            one, two = parts
            size = one.count()
            items.append(("pick", (use(one.held), use(one.received)), (use(two.held), use(two.received)), size, 1, (send, 0), len(sizes)))
            placed.append((one, len(sizes), 0, 0))
            sizes.append(size)
            to = size
        else:
            for p in parts:
                held, received = use(p.held), use(p.received)
                if stage == "x":
                    items.append(("sum", held, received, p.count(), (send, to)))
                    placed.append((p, send, to, to))
                    to += p.count()
                    continue
                if stage == "half":
                    groups, bit = 1 << len(p.open), 1
                else:
                    groups, bit = 1 << (len(p.open) - 1 - p.open.index(stage)), 2 + stage
                size = p.count() // (2 * groups)
                items.append(("split", held, received, groups, size, bit, (send, to), len(sizes)))
                placed.append((p, len(sizes), 0, to))
                sizes.append(groups * size)
                to += groups * size
                if stage == "half":
                    p.rows //= 2
                else:
                    p.open.remove(stage)
        sizes[send] = to
        moves.append((stage, send, placed))

    if tokens:
        arrays = list(lax.optimization_barrier(tuple(arrays) + tokens)[: len(arrays)])
    whole = pl.BlockSpec(memory_space=pltpu.VMEM)
    outs = pl.pallas_call(
        functools.partial(slot_kernel, items=items, inputs=len(arrays)),
        in_specs=[pl.BlockSpec(memory_space=pltpu.SMEM)] + [whole] * len(arrays),
        out_specs=[whole] * len(sizes),
        out_shape=[shape((size, 128)) for size in sizes],
        compiler_params=params(),
        cost_estimate=pl.CostEstimate(flops=0, bytes_accessed=512 * sum(sizes), transcendentals=0),
        name="slot",
    )(ids, *arrays)
    unit = lax.axis_size("vol") // PIECES
    sent, received = [], []
    for stage, send, placed in moves:
        if stage in ("half", "pick", "x"):
            got = exchange(outs[send], "seq", 2)
        else:
            got = exchange(outs[send], "vol", unit << stage)
        sent.append(outs[send])
        received.append(got)
        for p, keep, at, to in placed:
            p.held = (outs[keep], at)
            p.received = (got, to)
    return sent, received


def home_kernel(ids_ref, live_ref, *refs, mask):
    out_ref = refs[-1]
    for k, ref in enumerate(refs[:-1]):

        @pl.when(pl.program_id(0) == k)
        def _():
            value = ref[...].astype(F32)
            if mask:
                value = value * live_ref[ids_ref[5] ^ k]
            out_ref[...] = value.astype(out_ref.dtype)


def send_home(ids, live, own, others, slices, dtype, mask):
    rows, d = others[0].shape
    return pl.pallas_call(
        functools.partial(home_kernel, mask=mask),
        grid_spec=pltpu.PrefetchScalarGridSpec(
            num_scalar_prefetch=2,
            grid=(slices,),
            in_specs=[pl.BlockSpec((rows, d), lambda k, i, l: (0, 0), pipeline_mode=pl.Buffered(1))] * slices,
            out_specs=pl.BlockSpec((None, rows, d), lambda k, i, l: (k ^ i[5], 0, 0)),
        ),
        out_shape=shape((slices, rows, d), dtype),
        compiler_params=params(),
        cost_estimate=pl.CostEstimate(flops=0, bytes_accessed=6 * slices * rows * d, transcendentals=0),
        name="home",
    )(ids, live, own, *others)


def assemble_ff_kernel(ids_ref, *refs, per):
    ga, gb, gc = refs[:4], refs[4:8], refs[8:12]
    expand_ref, reduce_ref = refs[12:]
    c = ids_ref[0]

    def first_layer(i, core, value):
        for k in range(PIECES // 2):
            at = pl.multiple_of(((core * (PIECES // 2) + k) * CHUNKS + i) * 128, 128)
            expand_ref[:, pl.ds(at, 128)] = value[k * per : (k + 1) * per, :]

    def second_layer(i, core, value):
        d = value.shape[0]
        reduce_ref[i * 128 : (i + 1) * 128, pl.ds(pl.multiple_of(core * d, 128), d)] = value.T

    half = per * (PIECES // 2)
    for core, (mine, other) in ((c, (ga[0], ga[1])), (1 - c, (ga[2], ga[3]))):

        @pl.when(ids_ref[1] == 0)
        def _():
            first_layer(0, core, mine[...].astype(F32))
            second_layer(0, core, other[...].astype(F32))

        @pl.when(ids_ref[1] == 1)
        def _():
            first_layer(0, core, other[...].astype(F32))
            second_layer(0, core, mine[...].astype(F32))

    for i, refs_i in ((1, gb), (2, gc)):
        for core, (one, two) in ((c, refs_i[:2]), (1 - c, refs_i[2:])):
            total = one[...].astype(F32) + two[...].astype(F32)
            first_layer(i, core, total[:half])
            second_layer(i, core, total[half:])


def assemble_end_kernel(ids_ref, *refs, per):
    mine, theirs = refs[:4], refs[4:8]
    small_held, small_received, output_ref, input_ref, vector_ref = refs[8:]
    c = ids_ref[0]
    d = PIECES * per

    def output_part(core, value):
        for k in range(3):
            output_ref[:, pl.ds(pl.multiple_of((core * 3 + k) * 128, 128), 128)] = value[k * per : (k + 1) * per, :]

    def pair_part(i, core, value):
        for k in range(3):
            at = pl.multiple_of(k * d + (2 * i + core) * 128, 128)
            input_ref[:, pl.ds(at, 128)] = value[k * per : (k + 1) * per, :]

    for core, (own, other, one, two) in ((c, mine), (1 - c, theirs)):

        @pl.when(ids_ref[1] == 0)
        def _():
            output_part(core, own[...].astype(F32))
            pair_part(0, core, other[...].astype(F32))

        @pl.when(ids_ref[1] == 1)
        def _():
            output_part(core, other[...].astype(F32))
            pair_part(0, core, own[...].astype(F32))

        total = one[...].astype(F32) + two[...].astype(F32)
        for i in (1, 2):
            pair_part(i, core, total[(i - 1) * 3 * per : i * 3 * per])
    vector_ref[...] = small_held[...].astype(F32) + small_received[...].astype(F32)


def assemble(kernel, ids, per, arrays, outs, name):
    whole = pl.BlockSpec(memory_space=pltpu.VMEM)
    return pl.pallas_call(
        functools.partial(kernel, per=per),
        in_specs=[pl.BlockSpec(memory_space=pltpu.SMEM)] + [whole] * len(arrays),
        out_specs=[whole] * len(outs),
        out_shape=[shape(o, F32) for o in outs],
        compiler_params=params(),
        name=name,
    )(ids, *arrays)


def on_device(
    volume_slices, volume_owner, tokens, cotangent, attend_gain, attend_shift, input_weight, query_bias, value_bias,
    output_weight, output_bias, mixer_gain, mixer_shift, expand_weight, expand_bias, reduce_weight, reduce_bias,
):
    slices, rows, d = tokens.shape
    ff = expand_weight.shape[1]
    nv = lax.axis_size("vol")
    peers = lax.axis_size("seq")
    me = lax.axis_index("seq")
    core_id = me % 2
    x_id = (me // 2) % 2
    core = core_id.astype(jnp.int32).reshape(1)
    n = rows * peers
    vol = lax.axis_index("vol")
    unit = nv // PIECES
    ids = jnp.stack([core_id, x_id, (vol // unit) % 2, (vol // (2 * unit)) % 2, (vol // (4 * unit)) % 2, me]).astype(jnp.int32)

    def from_peers(x, ks):
        parts = [pick(x, me ^ k) for k in ks]
        return [p if k == 0 else exchange(p, "seq", k) for p, k in zip(parts, ks)]

    far_parts = from_peers(tokens, (3, 2))
    near_parts = from_peers(tokens, (0, 1))
    zero = jnp.zeros((d,), BF)
    vec = jnp.concatenate(
        [attend_gain, attend_shift, query_bias, zero, value_bias, output_bias, mixer_gain, mixer_shift, reduce_bias] + [zero] * 7
    ).astype(F32).reshape(16, d)
    wide = ff // CHUNKS
    lanes = wide // PIECES
    b1 = expand_bias.astype(F32).reshape(ff // 128, 128)
    load = jnp.sum(jnp.where(volume_owner == lax.axis_index("vol"), volume_slices, 0))
    live = (jnp.arange(slices) < load).astype(BF)

    made = project_in(jnp.concatenate(near_parts), 0, n, None, vec, input_weight)
    far = jnp.concatenate([after(far_parts[1], made[2], b1, live), far_parts[0]])
    x, first_t, packed = project_in(far, 2 * rows, n, made, vec, input_weight)
    upstream = jnp.concatenate(from_peers(after(cotangent, far_parts[0], made[2]) * live[:, None, None], (0, 1, 2, 3)))

    mixed, inverse, weights = attend(packed)

    acts, dhs, db1 = [], [], []
    second = None

    def hidden(token, i):
        head = (x, mixed, output_weight, vec) if i == 0 else None
        a, g, gk, gs, b, *sec = hidden_part(token, head, second, upstream, expand_weight, reduce_weight, b1, i)
        acts.append(a)
        dhs.append(g)
        db1.append(b)
        return gk, gs, sec

    Y, Z1, Z2 = 0, 1, 2
    piece_rows = d // 2 + d // 2
    pair_rows = 3 * (d // PIECES)
    k0, s0, (second,) = hidden(core, 0)
    r0 = to_core(s0)
    k1, s1, _ = hidden(after(core, s0), 1)
    r1 = to_core(s1)
    ga = Part(k0, r0, piece_rows)
    sent, _ = slot(ids, [("half", [ga])], s1)
    k2, s2, _ = hidden(after(core, s1, *sent), 2)
    r2 = to_core(s2)
    gb = Part(k1, r1, piece_rows)
    sent, _ = slot(ids, [(Z1, [gb])], s2)
    out, d_branch, d_mixed, k3, s3, sums_mid = outer(
        after(core, s2, *sent), acts, dhs, x, upstream, mixed, inverse, output_weight, vec, expand_weight, reduce_weight
    )
    r3 = to_core(s3)

    def homeward(a):
        blocks = [a[k * rows : (k + 1) * rows] for k in range(1, peers)]
        return blocks, [exchange(b, "seq", k + 1) for k, b in enumerate(blocks)]

    out_sent, outs = homeward(out)
    gc = Part(k2, r2, piece_rows)
    sent, got = slot(ids, [(Y, [gc]), (Z2, [gb])], s3)
    parts = []

    def reflect_part(token, i):
        dq, dk, dv, gk, gs = reflect(token, packed, mixed, d_mixed, weights, first_t, 2 * i)
        parts.extend([dq, dk, dv])
        return gk, gs

    p0, q0 = reflect_part(after(core, s3, *sent, *out_sent), 0)
    t0 = to_core(q0)
    wait_c = got[0]
    sent, _ = slot(ids, [(Y, [ga, gb])], q0)
    p1, q1 = reflect_part(after(core, q0, wait_c, *sent, *outs), 1)
    t1 = to_core(q1)
    gd, gd2 = Part(k3, r3, pair_rows), Part(p0, t0, pair_rows)
    sent, _ = slot(ids, [(Z1, [ga, gc]), ("pick", [gd, gd2])], q1)
    p2, q2 = reflect_part(after(core, q1, *sent), 2)
    t2 = to_core(q2)
    ge1 = Part(p1, t1, pair_rows)
    sent, _ = slot(ids, [(Y, [ge1, gd]), (Z2, [ga, gc])], q2)
    d_tokens, small = project_back(after(x, *sent), d_branch, input_weight, vec, sums_mid, db1, parts)

    tg_sent, tgs = homeward(d_tokens)
    ge2 = Part(p2, t2, pair_rows)
    gv = Part(small, to_core(small), SMALL)
    sent1, got1 = slot(ids, [(Y, [ge2, gv])], small, *tg_sent)
    block_out = send_home(ids, live, out, [after(o, *sent1) for o in outs], slices, BF, True)
    sent2, got2 = slot(ids, [(Z1, [ge1, ge2, gd, gv]), ("x", [ga, gb, gc])], *got1, block_out)
    per = d // PIECES

    def both_terms(p, *tokens):
        pieces = [lax.slice_in_dim(a, at, at + p.count()) for a, at in (p.held, p.received)]
        pieces = list(lax.optimization_barrier(tuple(pieces) + tokens)[:2])
        return pieces + [to_core(a) for a in pieces]

    spare = [1 << i for i in range(unit.bit_length() - 1)]
    sent3, got3 = slot(ids, [(Z2, [ge1, ge2, gd, gv])], *got2)
    tgs = [after(t, *sent3) for t in tgs]
    tokens_grad = send_home(ids, live, d_tokens, tgs, slices, F32, False)
    ff_terms = both_terms(ga, *sent3) + both_terms(gb, *sent3) + both_terms(gc, *sent3)
    sent4, got4 = slot(ids, [("x", [ge1, ge2, gd, gv])], *got3, tokens_grad)
    ff_terms = list(lax.optimization_barrier(tuple(ff_terms) + tuple(sent4))[: len(ff_terms)])
    expand_grad, reduce_grad = assemble(assemble_ff_kernel, ids, per, ff_terms, [(per, ff), (ff // PIECES, d)], "assemble_ff")
    at = 2 * pair_rows
    held, received = sent4[0], got4[0]
    ends = [held[at : at + pair_rows], received[at : at + pair_rows], held[:at], received[:at]]
    ends = ends + [to_core(a) for a in ends]
    at += pair_rows
    output_grad, input_grad, vectors = assemble(
        assemble_end_kernel, ids, per, ends + [held[at:], received[at:]], [(per, d), (per, 3 * d), (SMALL, 128)], "assemble_end"
    )
    bias_rows = vectors[8 : 8 + CHUNKS]
    vectors = vectors[:8, :per]
    if unit > 1:
        sub = vol % unit

        def add_rest(a):
            for by in spare:
                a = a + exchange(a, "vol", by)
            return a

        def cut(a, axis):
            size = a.shape[axis] // unit
            return lax.dynamic_slice_in_dim(add_rest(a), sub * size, size, axis)

        expand_grad, reduce_grad, output_grad, input_grad = [cut(a, 0) for a in (expand_grad, reduce_grad, output_grad, input_grad)]
        expand_bias_grad = cut(bias_rows.reshape(-1), 0)
        vectors = cut(vectors, 1)
    else:
        expand_bias_grad = bias_rows.reshape(-1)
    return (
        block_out, tokens_grad, vectors[0], vectors[1], input_grad, vectors[2], vectors[3], output_grad, vectors[4],
        vectors[5], vectors[6], expand_grad, expand_bias_grad, reduce_grad, vectors[7],
    )


def solution(mesh):
    rows = P("vol", "seq", None)
    return jax.shard_map(
        on_device,
        mesh=mesh,
        in_specs=(P(), P(), rows, rows) + (P(),) * 13,
        out_specs=(rows, rows, P("vol"), P("vol"), P("vol", None), P("vol"), P("vol"), P("vol", None), P("vol"), P("vol"),
                   P("vol"), P("vol", None), P("vol"), P("vol", None), P("vol")),
        check_vma=False,
    )
```

```python
import functools

import jax
import jax.numpy as jnp
from jax import lax
from jax.experimental import pallas as pl
from jax.experimental.pallas import tpu as pltpu
from jax.sharding import PartitionSpec as P

HEAD_DIM = 64
PAIR = 2 * HEAD_DIM
LOG2E = 1.4426950408889634
PIECES = 8
CHUNKS = 3
ROW = {n: i for i, n in enumerate(("ag", "ash", "qb", "zero", "vb", "ob", "mg", "ms", "rb"))}
BF = jnp.bfloat16
F32 = jnp.float32
NN = (((1,), (0,)), ((), ()))
NT = (((1,), (1,)), ((), ()))
TAIL = (
    0.11962928008603971,
    0.12075423895539067,
    0.09991176086876633,
    0.12856720585766357,
    -0.05369390237929985,
    0.20636430391507077,
    -0.15720912816414995,
    0.03567616760586865,
)


def dot(a, b, dims):
    return lax.dot_general(a, b, dims, preferred_element_type=F32)


def params():
    return pltpu.CompilerParams(vmem_limit_bytes=24 << 20)


def line(ref, name):
    return ref[ROW[name] : ROW[name] + 1, :]


def shape(dims, dtype=BF):
    return jax.ShapeDtypeStruct(dims, dtype)


def normal(h):
    a = jnp.abs(h)
    t = 1.0 / (1.0 + 0.3 * a)
    s = TAIL[7] * t + TAIL[6]
    for c in TAIL[5::-1]:
        s = s * t + c
    e = jnp.exp2(h * h * (-0.5 * LOG2E))
    tail = s * t * e
    return jnp.where(h >= 0, 1.0 - tail, tail), e * 0.3989422804014327


def stats(v):
    spread = v - jnp.mean(v, axis=-1, keepdims=True)
    return spread, lax.rsqrt(jnp.mean(spread * spread, axis=-1, keepdims=True) + 1e-6)


def in_kernel(x_ref, vec_ref, w_ref, *rest):
    x_out, first_t, packed = rest[-3:]
    x = x_ref[...]
    d = x.shape[1]
    spread, r = stats(x.astype(F32))
    f = (spread * r * line(vec_ref, "ag") + line(vec_ref, "ash")).astype(BF)
    x_out[...] = x
    for i, bias in enumerate(("qb", "zero", "vb")):
        packed[:, i * d : (i + 1) * d] = (dot(f, w_ref[:, i * d : (i + 1) * d], NN) + line(vec_ref, bias)).astype(BF)
    first_t[...] = f.T


def project_in(part, offset, total, before, vec, weight):
    rows, d = part.shape
    wide = weight.shape[1]
    tm = 256
    first_block = offset // tm

    def full(a):
        return pl.BlockSpec(a.shape, lambda i: (0, 0), pipeline_mode=pl.Buffered(1))

    in_specs = [pl.BlockSpec((tm, d), lambda i: (i, 0)), full(vec), full(weight)]
    args = [part, vec, weight]
    aliases = {}
    if before is not None:
        aliases = {3: 0, 4: 1, 5: 2}
        in_specs += [pl.BlockSpec(memory_space=pl.ANY)] * 3
        args += list(before)
    return pl.pallas_call(
        in_kernel,
        grid=(rows // tm,),
        in_specs=in_specs,
        out_specs=[
            pl.BlockSpec((tm, d), lambda i: (i + first_block, 0)),
            pl.BlockSpec((d, tm), lambda i: (0, i + first_block)),
            pl.BlockSpec((tm, wide), lambda i: (i + first_block, 0)),
        ],
        out_shape=[shape((total, d)), shape((d, total)), shape((total, wide))],
        input_output_aliases=aliases,
        compiler_params=params(),
        cost_estimate=pl.CostEstimate(flops=6 * rows * d * wide, bytes_accessed=2 * (d * wide + rows * (wide + 3 * d)), transcendentals=0),
        name="project_in",
    )(*args)


def attend_kernel(q_ref, k_ref, v_ref, o_ref, inv_ref, p_ref, vx_ref, *, tq):
    n = k_ref.shape[0]
    vx_ref[:, :PAIR] = v_ref[...]
    vx_ref[:, PAIR:] = jnp.ones((n, PAIR), BF)
    low = lax.broadcasted_iota(jnp.int32, (tq, PAIR), 1) < HEAD_DIM
    for t in range(n // tq):
        rows = pl.ds(t * tq, tq)
        q = q_ref[rows, :]
        zero = jnp.zeros_like(q)
        outs = []
        for a in range(2):
            qa = jnp.where(low, q, zero) if a == 0 else jnp.where(low, zero, q)
            s = dot(qa, k_ref[...], NT)
            top = jnp.max(s, axis=-1, keepdims=True)
            p = jnp.exp2((s - top) * (LOG2E * HEAD_DIM**-0.5)).astype(BF)
            p_ref[a, rows, :] = p
            both = dot(p, vx_ref[...], NN)
            inv = 1.0 / both[:, PAIR:]
            outs.append((both[:, :PAIR] * inv, inv))
        o_ref[rows, :] = jnp.where(low, outs[0][0], outs[1][0]).astype(BF)
        inv_ref[rows, :] = jnp.where(low, outs[0][1], outs[1][1])


def attend(packed):
    n, w = packed.shape
    d = w // 3
    hp = d // PAIR

    def cols(off):
        return pl.BlockSpec((n, PAIR), lambda h: (0, h + off))

    return pl.pallas_call(
        functools.partial(attend_kernel, tq=128),
        grid=(hp,),
        in_specs=[cols(0), cols(hp), cols(2 * hp)],
        out_specs=[cols(0), cols(0), pl.BlockSpec((2, n, n), lambda h: (h, 0, 0))],
        out_shape=[shape((n, d)), shape((n, d), F32), shape((2 * hp, n, n))],
        scratch_shapes=[pltpu.VMEM((n, 2 * PAIR), BF)],
        compiler_params=params(),
        cost_estimate=pl.CostEstimate(flops=16 * n * n * d, bytes_accessed=4 * n * n * hp, transcendentals=0),
        name="attend",
    )(packed, packed, packed)


WHOLE = pl.BlockSpec(memory_space=pltpu.VMEM)
FAR = pl.BlockSpec(memory_space=pltpu.HBM)


def transpose_rows(block, out, cols):
    t = block.T
    d = t.shape[0]
    half = d // PIECES // 2
    for h in range(2):
        for v in range(PIECES):
            at = (2 * v + h) * half
            to = (h * PIECES + v) * half
            out[to : to + half, cols] = t[at : at + half]


def core_rows(ref, which):
    half = ref.shape[0] // 2
    return ref[pl.ds(pl.multiple_of(which * half, half), half), :]


def piece_blocks(g, ref, first):
    rows = g.shape[0] // PIECES
    for k in range(g.shape[1] // 128):
        at = (first + k) * rows
        ref[:, at : at + rows, :] = g[:, k * 128 : (k + 1) * 128].reshape(PIECES, rows, 128)


def middle_of(x_ref, mix_ref, wo_ref, vec_ref, rows):
    return x_ref[rows, :].astype(F32) + dot(mix_ref[rows, :], wo_ref[...], NN) + line(vec_ref, "ob")


def hidden_kernel(c_ref, *refs, i, head, tm, sub):
    if head:
        x_ref, mix_ref, wo_ref, vec_ref, up_ref, w1_hbm, w2_hbm, b1_ref, *refs = refs
        gk_ref, gs_ref, db1_ref, o_ref, ds_ref, sec_ref, sec_t, up_t, act, dh, w1, w2, sems = refs
    else:
        sec_ref, sec_t, up_t, o_in, ds_in, up_ref, w1_hbm, w2_hbm, b1_ref, *refs = refs
        gk_ref, gs_ref, db1_ref, o_ref, ds_ref, act, dh, w1, w2, sems = refs
    n, d = up_ref.shape
    wide = act.shape[1]
    first, second = [], []
    for v in range(PIECES):
        at = pl.ds((v * CHUNKS + i) * 128, 128)
        to = pl.ds(v * 128, 128)
        first.append(pltpu.make_async_copy(w1_hbm.at[:, at], w1.at[:, to], sems.at[0, v]))
        second.append(pltpu.make_async_copy(w2_hbm.at[at, :], w2.at[to, :], sems.at[1, v]))
        first[-1].start()
        second[-1].start()
    if head:
        for t in range(n // tm):
            rows = slice(t * tm, (t + 1) * tm)
            spread, r = stats(middle_of(x_ref, mix_ref, wo_ref, vec_ref, rows))
            sec = (spread * r * line(vec_ref, "mg") + line(vec_ref, "ms")).astype(BF)
            sec_ref[rows, :] = sec
            transpose_rows(sec, sec_t, rows)
            up_t[:, rows] = up_ref[rows, :].T

    def products(at):
        for v in range(at // 128, (at + sub) // 128):
            first[v].wait()
            second[v].wait()
        cols = slice(at, at + sub)
        return dot(sec_ref[...], w1[:, cols], NN), dot(up_ref[...], w2[cols, :], NT)

    c = c_ref[0]
    now = products(0)
    for at in range(0, wide, sub):
        later = products(at + sub) if at + sub < wide else None
        cols = slice(at, at + sub)
        bias = jnp.concatenate([b1_ref[v * CHUNKS + i : v * CHUNKS + i + 1, :] for v in range(at // 128, (at + sub) // 128)], axis=1)
        h, da = now
        h = h + bias
        cdf, pdf = normal(h)
        act[:, cols] = (h * cdf).astype(BF)
        dhv = (da * (cdf + h * pdf)).astype(BF)
        dh[:, cols] = dhv
        db1_ref[:, cols] = jnp.sum(dhv.astype(F32), axis=0, keepdims=True)
        block = at // 128
        base = PIECES * (d // PIECES // 2)
        for ref, mine in ((gs_ref, 1 - c), (gk_ref, c)):
            piece_blocks(dot(core_rows(sec_t, mine), dh[:, cols], NN).astype(BF), ref, block)
            g = dot(core_rows(up_t, mine), act[:, cols], NN).astype(BF)
            for k in range(sub // 128):
                ref[block + k, base:, :] = g[:, k * 128 : (k + 1) * 128]
        now = later
    for t in range(n // tm):
        rows = slice(t * tm, (t + 1) * tm)
        o = dot(act[rows, :], w2[...], NN)
        ds = dot(dh[rows, :], w1[...], NT)
        o_ref[rows, :] = o if head else o_in[rows, :] + o
        ds_ref[rows, :] = ds if head else ds_in[rows, :] + ds


def hidden_part(core, head, carried, up, w1, w2, b1, i, tm=256, sub=256):
    n, d = up.shape
    wide = 128 * PIECES
    assert wide * CHUNKS == w1.shape[1]
    g = (PIECES, PIECES * (d // PIECES // 2) + d // 2, 128)
    args = list(head) if head else list(carried)
    made = [shape(g), shape(g), shape((1, wide), F32), shape((n, d), F32), shape((n, d), F32)]
    if head:
        made += [shape((n, d)), shape((d, n)), shape((d, n))]
    return pl.pallas_call(
        functools.partial(hidden_kernel, i=i, head=bool(head), tm=tm, sub=sub),
        in_specs=[pl.BlockSpec(memory_space=pltpu.SMEM)] + [WHOLE] * (len(args) + 1) + [FAR, FAR, WHOLE],
        out_specs=[WHOLE] * len(made),
        out_shape=made,
        input_output_aliases={} if head else {4: 3, 5: 4},
        scratch_shapes=[
            pltpu.VMEM((n, wide), BF), pltpu.VMEM((n, wide), BF), pltpu.VMEM((d, wide), BF), pltpu.VMEM((wide, d), BF),
            pltpu.SemaphoreType.DMA((2, PIECES)),
        ],
        compiler_params=params(),
        cost_estimate=pl.CostEstimate(flops=24 * n * d * wide, bytes_accessed=8 * d * wide, transcendentals=0),
        name="hidden",
    )(core, *args, up, w1, w2, b1)


def outer_kernel(c_ref, x_ref, up_ref, mix_ref, li_ref, wo_ref, vec_ref, o_ref, ds_ref, out_ref, dbr_ref, do_ref, gk_ref, gs_ref, sums_ref, mix_t, *, tm):
    n, d = x_ref.shape
    sums = None
    for t in range(n // tm):
        rows = slice(t * tm, (t + 1) * tm)
        m = middle_of(x_ref, mix_ref, wo_ref, vec_ref, rows)
        spread, r = stats(m)
        nv = spread * r
        up = up_ref[rows, :].astype(F32)
        transpose_rows(mix_ref[rows, :], mix_t, rows)
        dy = ds_ref[rows, :]
        dyg = dy * line(vec_ref, "mg")
        dm = up + r * (dyg - jnp.mean(dyg, axis=-1, keepdims=True) - nv * jnp.mean(dyg * nv, axis=-1, keepdims=True))
        db = dm.astype(BF)
        dbr_ref[rows, :] = db
        out_ref[rows, :] = (m + o_ref[rows, :] + line(vec_ref, "rb")).astype(BF)
        do_ref[rows, :] = (dot(db, wo_ref[...], NT) * li_ref[rows, :]).astype(BF)
        part = [jnp.sum(v, axis=0, keepdims=True) for v in (db.astype(F32), dy * nv, dy, up)]
        sums = part if sums is None else [a + b for a, b in zip(sums, part)]
    sums_ref[...] = jnp.concatenate(sums + [jnp.zeros((4, d), F32)], axis=0)
    for ref, mine in ((gs_ref, 1 - c_ref[0]), (gk_ref, c_ref[0])):
        piece_blocks(dot(core_rows(mix_t, mine), dbr_ref[...], NN).astype(BF), ref, 0)


def outer(core, x, up, mix, li, wo, vec, o, ds, tm=256):
    n, d = x.shape
    g = (PIECES, d // 128 * (d // PIECES // 2), 128)
    return pl.pallas_call(
        functools.partial(outer_kernel, tm=tm),
        in_specs=[pl.BlockSpec(memory_space=pltpu.SMEM)] + [WHOLE] * 8,
        out_specs=[WHOLE] * 6,
        out_shape=[shape((n, d))] * 3 + [shape(g), shape(g), shape((8, d), F32)],
        scratch_shapes=[pltpu.VMEM((d, n), BF)],
        compiler_params=params(),
        cost_estimate=pl.CostEstimate(flops=24 * n * d * d, bytes_accessed=20 * n * d, transcendentals=0),
        name="outer",
    )(core, x, up, mix, li, wo, vec, o, ds)


def by_piece(g):
    rows = g.shape[0] // PIECES
    return [g[:, i : i + 128].reshape(PIECES, rows, 128) for i in range(0, g.shape[1], 128)]


def reflect_kernel(c_ref, q_ref, k_ref, v_ref, o_ref, do_ref, p_ref, ft_ref, dq_ref, dk_ref, dv_ref, gk_ref, gs_ref, ds_ref, *, tq):
    n = k_ref.shape[0]
    low = lax.broadcasted_iota(jnp.int32, (tq, PAIR), 1) < HEAD_DIM
    q_t = q_ref[...].T
    do_t = do_ref[...].T
    scale = HEAD_DIM**-0.5
    dks, dvs = [], []
    for a in range(2):
        for t in range(n // tq):
            rows = pl.ds(t * tq, tq)
            do = do_ref[rows, :]
            zero = jnp.zeros_like(do)
            doa = jnp.where(low, do, zero) if a == 0 else jnp.where(low, zero, do)
            delta = jnp.sum(doa.astype(F32) * o_ref[rows, :].astype(F32), axis=-1, keepdims=True)
            dp = dot(doa, v_ref[...], NT)
            ds = (p_ref[a, rows, :].astype(F32) * (dp - delta)).astype(BF)
            ds_ref[rows, :] = ds
            dq = (dot(ds, k_ref[...], NN) * scale).astype(BF)
            dq_ref[rows, :] = dq if a == 0 else jnp.where(low, dq_ref[rows, :], dq)
        part = slice(HEAD_DIM * a, HEAD_DIM * (a + 1))
        dvs.append(dot(do_t[part], p_ref[a], NN))
        dks.append(dot(q_t[part], ds_ref[...], NN) * scale)
    dv = jnp.concatenate(dvs, axis=0).astype(BF).T
    dk = jnp.concatenate(dks, axis=0).astype(BF).T
    dv_ref[...] = dv
    dk_ref[...] = dk
    g = dot(ft_ref[...], jnp.concatenate([dq_ref[...], dk, dv], axis=1), NN).astype(BF)
    per = g.shape[0] // PIECES
    h = pl.program_id(0)
    for step, ref in enumerate((gs_ref, gk_ref)):

        @pl.when(h == step)
        def _():
            for i, block in enumerate(by_piece(g)):
                ref[:, i * per : (i + 1) * per, :] = block


def reflect(core, packed, o, do, p, first_t, start):
    n, w = packed.shape
    d = w // 3
    hp = d // PAIR

    def which(h, c):
        return (h + 1 - c[0]) % 2

    def cols(off):
        return pl.BlockSpec((n, PAIR), lambda h, c: (0, which(h, c) + off))

    g = (PIECES, 3 * (d // PIECES), 128)
    piece = pl.BlockSpec(g, lambda h, c: (0, 0, 0), pipeline_mode=pl.Buffered(1))
    return pl.pallas_call(
        functools.partial(reflect_kernel, tq=256),
        grid_spec=pltpu.PrefetchScalarGridSpec(
            num_scalar_prefetch=1,
            grid=(2,),
            in_specs=[
                cols(start), cols(start + hp), cols(start + 2 * hp), cols(start), cols(start),
                pl.BlockSpec((2, n, n), lambda h, c: (which(h, c) + start, 0, 0)),
                pl.BlockSpec((d, n), lambda h, c: (0, 0), pipeline_mode=pl.Buffered(1)),
            ],
            out_specs=[cols(0)] * 3 + [piece] * 2,
            scratch_shapes=[pltpu.VMEM((n, n), BF)],
        ),
        out_shape=[shape((n, 2 * PAIR))] * 3 + [shape(g)] * 2,
        compiler_params=params(),
        cost_estimate=pl.CostEstimate(flops=160 * n * n * PAIR, bytes_accessed=8 * n * n, transcendentals=0),
        name="reflect",
    )(core, packed, packed, packed, o, do, p, first_t)


SMALL = 16


def back_kernel(*refs, chunks):
    x_ref, dbr_ref, w_ref, vec_in, mid_ref = refs[:5]
    db1 = refs[5 : 5 + CHUNKS]
    parts = refs[5 + CHUNKS : 5 + CHUNKS + 3 * chunks]
    tg_ref, small_ref, sums = refs[5 + CHUNKS + 3 * chunks :]

    @pl.when(pl.program_id(0) == 0)
    def _():
        sums[...] = jnp.zeros_like(sums)

    d = x_ref.shape[1]
    cw = d // chunks
    dy = None
    for i in range(3 * chunks):
        which, chunk = i % 3, i // 3
        at = which * d + chunk * cw
        part = dot(parts[i][...], w_ref[:, at : at + cw], NT)
        dy = part if dy is None else dy + part
        row = {0: 2, 2: 3}.get(which)
        if row is not None:
            sums[row : row + 1, chunk * cw : (chunk + 1) * cw] += jnp.sum(parts[i][...].astype(F32), axis=0, keepdims=True)
    spread, r = stats(x_ref[...].astype(F32))
    nv = spread * r
    dyg = dy * line(vec_in, "ag")
    dx = r * (dyg - jnp.mean(dyg, axis=-1, keepdims=True) - nv * jnp.mean(dyg * nv, axis=-1, keepdims=True))
    tg_ref[...] = (dbr_ref[...].astype(F32) + dx).astype(BF)
    sums[0:1, :] += jnp.sum(dy * nv, axis=0, keepdims=True)
    sums[1:2, :] += jnp.sum(dy, axis=0, keepdims=True)

    @pl.when(pl.program_id(0) == pl.num_programs(0) - 1)
    def _():
        per = d // PIECES
        sums[4:8, :] = mid_ref[0:4, :]
        rows = sums[...]
        for v in range(PIECES):
            vectors = jnp.concatenate([rows[:, v * per : (v + 1) * per], jnp.zeros((8, 128 - per), F32)], axis=1)
            biases = [b[:, v * 128 : (v + 1) * 128] for b in db1]
            piece = jnp.concatenate([vectors] + biases + [jnp.zeros((SMALL - 8 - CHUNKS, 128), F32)], axis=0)
            small_ref[v * SMALL : (v + 1) * SMALL, :] = piece.astype(BF)


def project_back(x, dbr, w, vec, mids, db1, parts):
    n, d = x.shape
    tm = 256
    row = pl.BlockSpec((tm, d), lambda i: (i, 0))

    def full(*s):
        return pl.BlockSpec(s, lambda i: (0, 0), pipeline_mode=pl.Buffered(1))

    chunks = len(parts) // 3
    return pl.pallas_call(
        functools.partial(back_kernel, chunks=chunks),
        grid=(n // tm,),
        in_specs=[row, row, full(d, 3 * d), full(*vec.shape), full(*mids.shape)]
        + [full(*b.shape) for b in db1]
        + [pl.BlockSpec((tm, d // chunks), lambda i: (i, 0))] * (3 * chunks),
        out_specs=[row, full(PIECES * SMALL, 128)],
        out_shape=[shape((n, d)), shape((PIECES * SMALL, 128))],
        scratch_shapes=[pltpu.VMEM((8, d), F32)],
        compiler_params=params(),
        cost_estimate=pl.CostEstimate(flops=12 * n * d * d, bytes_accessed=16 * n * d, transcendentals=0),
        name="project_back",
    )(x, dbr, w, vec, mids, *db1, *parts)


def exchange(x, axis, by):
    count = lax.axis_size(axis)
    return lax.ppermute(x, axis, [(i, i ^ by) for i in range(count)])


def to_core(g):
    return exchange(g, "seq", 1)


def pick(x, index, axis=0):
    return lax.dynamic_index_in_dim(x, index, axis, keepdims=False)


def after(x, *others):
    return lax.optimization_barrier((x,) + others)[0]


class Part:
    def __init__(self, held, received, rows):
        self.held = (held.reshape(-1, 128), 0)
        self.received = (received.reshape(-1, 128), 0)
        self.rows = rows
        self.open = [0, 1, 2]

    def count(self):
        return self.rows << len(self.open)


def slot_kernel(ids_ref, *refs, items, inputs):
    ins, outs = refs[:inputs], refs[inputs:]

    def read(term, at, count):
        ref, offset = term
        return ins[ref][pl.ds(at + offset, count), :].astype(F32)

    step = 16
    for kind, *rest in items:
        if kind == "split":
            held, received, groups, size, bit, (send, to), keep = rest
            mine = ids_ref[bit]
            for a in range(groups):
                own = pl.multiple_of((2 * a + mine) * size, step)
                other = pl.multiple_of((2 * a + 1 - mine) * size, step)
                outs[send][to + a * size : to + (a + 1) * size, :] = (read(held, other, size) + read(received, other, size)).astype(BF)
                outs[keep][a * size : (a + 1) * size, :] = (read(held, own, size) + read(received, own, size)).astype(BF)
        elif kind == "sum":
            held, received, size, (send, to) = rest
            outs[send][to : to + size, :] = (read(held, 0, size) + read(received, 0, size)).astype(BF)
        else:
            first, second, size, bit, (send, to), keep = rest
            for mine in (0, 1):

                @pl.when(ids_ref[bit] == mine)
                def _():
                    own, other = (first, second) if mine == 0 else (second, first)
                    outs[send][to : to + size, :] = (read(other[0], 0, size) + read(other[1], 0, size)).astype(BF)
                    outs[keep][...] = (read(own[0], 0, size) + read(own[1], 0, size)).astype(BF)


def slot(ids, exchanges, *tokens):
    arrays, items, sizes, moves = [], [], [], []

    def use(term):
        for i, a in enumerate(arrays):
            if a is term[0]:
                return i, term[1]
        arrays.append(term[0])
        return len(arrays) - 1, term[1]

    for stage, parts in exchanges:
        send, to = len(sizes), 0
        sizes.append(0)
        placed = []
        if stage == "pick":
            one, two = parts
            size = one.count()
            items.append(("pick", (use(one.held), use(one.received)), (use(two.held), use(two.received)), size, 1, (send, 0), len(sizes)))
            placed.append((one, len(sizes), 0, 0))
            sizes.append(size)
            to = size
        else:
            for p in parts:
                held, received = use(p.held), use(p.received)
                if stage == "x":
                    items.append(("sum", held, received, p.count(), (send, to)))
                    placed.append((p, send, to, to))
                    to += p.count()
                    continue
                if stage == "half":
                    groups, bit = 1 << len(p.open), 1
                else:
                    groups, bit = 1 << (len(p.open) - 1 - p.open.index(stage)), 2 + stage
                size = p.count() // (2 * groups)
                items.append(("split", held, received, groups, size, bit, (send, to), len(sizes)))
                placed.append((p, len(sizes), 0, to))
                sizes.append(groups * size)
                to += groups * size
                if stage == "half":
                    p.rows //= 2
                else:
                    p.open.remove(stage)
        sizes[send] = to
        moves.append((stage, send, placed))

    if tokens:
        arrays = list(lax.optimization_barrier(tuple(arrays) + tokens)[: len(arrays)])
    whole = pl.BlockSpec(memory_space=pltpu.VMEM)
    outs = pl.pallas_call(
        functools.partial(slot_kernel, items=items, inputs=len(arrays)),
        in_specs=[pl.BlockSpec(memory_space=pltpu.SMEM)] + [whole] * len(arrays),
        out_specs=[whole] * len(sizes),
        out_shape=[shape((size, 128)) for size in sizes],
        compiler_params=params(),
        cost_estimate=pl.CostEstimate(flops=0, bytes_accessed=512 * sum(sizes), transcendentals=0),
        name="slot",
    )(ids, *arrays)
    unit = lax.axis_size("vol") // PIECES
    sent, received = [], []
    for stage, send, placed in moves:
        if stage in ("half", "pick", "x"):
            got = exchange(outs[send], "seq", 2)
        else:
            got = exchange(outs[send], "vol", unit << stage)
        sent.append(outs[send])
        received.append(got)
        for p, keep, at, to in placed:
            p.held = (outs[keep], at)
            p.received = (got, to)
    return sent, received


def home_kernel(ids_ref, live_ref, *refs, mask):
    out_ref = refs[-1]
    for k, ref in enumerate(refs[:-1]):

        @pl.when(pl.program_id(0) == k)
        def _():
            value = ref[...].astype(F32)
            if mask:
                value = value * live_ref[ids_ref[5] ^ k]
            out_ref[...] = value.astype(out_ref.dtype)


def send_home(ids, live, own, others, slices, dtype, mask):
    rows, d = others[0].shape
    return pl.pallas_call(
        functools.partial(home_kernel, mask=mask),
        grid_spec=pltpu.PrefetchScalarGridSpec(
            num_scalar_prefetch=2,
            grid=(slices,),
            in_specs=[pl.BlockSpec((rows, d), lambda k, i, l: (0, 0), pipeline_mode=pl.Buffered(1))] * slices,
            out_specs=pl.BlockSpec((None, rows, d), lambda k, i, l: (k ^ i[5], 0, 0)),
        ),
        out_shape=shape((slices, rows, d), dtype),
        compiler_params=params(),
        cost_estimate=pl.CostEstimate(flops=0, bytes_accessed=6 * slices * rows * d, transcendentals=0),
        name="home",
    )(ids, live, own, *others)


def assemble_ff_kernel(ids_ref, *refs, per):
    ga, gb, gc = refs[:4], refs[4:8], refs[8:12]
    expand_ref, reduce_ref = refs[12:]
    c = ids_ref[0]

    def first_layer(i, core, value):
        size = per // 2
        for k in range(PIECES):
            at = (k * CHUNKS + i) * 128
            expand_ref[pl.ds(pl.multiple_of(core * size, size), size), at : at + 128] = value[k * size : (k + 1) * size, :]

    def second_layer(i, core, value):
        d = value.shape[0]
        reduce_ref[i * 128 : (i + 1) * 128, pl.ds(pl.multiple_of(core * d, 128), d)] = value.T

    half = per * (PIECES // 2)
    for core, (mine, other) in ((c, (ga[0], ga[1])), (1 - c, (ga[2], ga[3]))):

        @pl.when(ids_ref[1] == 0)
        def _():
            first_layer(0, core, mine[...].astype(F32))
            second_layer(0, core, other[...].astype(F32))

        @pl.when(ids_ref[1] == 1)
        def _():
            first_layer(0, core, other[...].astype(F32))
            second_layer(0, core, mine[...].astype(F32))

    for i, refs_i in ((1, gb), (2, gc)):
        for core, (one, two) in ((c, refs_i[:2]), (1 - c, refs_i[2:])):
            total = one[...].astype(F32) + two[...].astype(F32)
            first_layer(i, core, total[:half])
            second_layer(i, core, total[half:])


def assemble_end_kernel(ids_ref, *refs, per):
    mine, theirs = refs[:4], refs[4:8]
    small_held, small_received, output_ref, input_ref, vector_ref = refs[8:]
    c = ids_ref[0]
    d = PIECES * per

    def output_part(core, value):
        size = per // 2
        for k in range(d // 128):
            rows = pl.ds(pl.multiple_of(core * size, size), size)
            output_ref[rows, k * 128 : (k + 1) * 128] = value[k * size : (k + 1) * size, :]

    def pair_part(i, core, value):
        for k in range(3):
            at = pl.multiple_of(k * d + (2 * i + core) * 128, 128)
            input_ref[:, pl.ds(at, 128)] = value[k * per : (k + 1) * per, :]

    for core, (own, other, one, two) in ((c, mine), (1 - c, theirs)):

        @pl.when(ids_ref[1] == 0)
        def _():
            output_part(core, own[...].astype(F32))
            pair_part(0, core, other[...].astype(F32))

        @pl.when(ids_ref[1] == 1)
        def _():
            output_part(core, other[...].astype(F32))
            pair_part(0, core, own[...].astype(F32))

        total = one[...].astype(F32) + two[...].astype(F32)
        for i in (1, 2):
            pair_part(i, core, total[(i - 1) * 3 * per : i * 3 * per])
    vector_ref[...] = small_held[...].astype(F32) + small_received[...].astype(F32)


def assemble(kernel, ids, per, arrays, outs, name):
    whole = pl.BlockSpec(memory_space=pltpu.VMEM)
    return pl.pallas_call(
        functools.partial(kernel, per=per),
        in_specs=[pl.BlockSpec(memory_space=pltpu.SMEM)] + [whole] * len(arrays),
        out_specs=[whole] * len(outs),
        out_shape=[shape(o, F32) for o in outs],
        compiler_params=params(),
        name=name,
    )(ids, *arrays)


def on_device(
    volume_slices, volume_owner, tokens, cotangent, attend_gain, attend_shift, input_weight, query_bias, value_bias,
    output_weight, output_bias, mixer_gain, mixer_shift, expand_weight, expand_bias, reduce_weight, reduce_bias,
):
    slices, rows, d = tokens.shape
    ff = expand_weight.shape[1]
    nv = lax.axis_size("vol")
    peers = lax.axis_size("seq")
    me = lax.axis_index("seq")
    core_id = me % 2
    x_id = (me // 2) % 2
    core = core_id.astype(jnp.int32).reshape(1)
    n = rows * peers
    vol = lax.axis_index("vol")
    unit = nv // PIECES
    ids = jnp.stack([core_id, x_id, (vol // unit) % 2, (vol // (2 * unit)) % 2, (vol // (4 * unit)) % 2, me]).astype(jnp.int32)

    def from_peers(x, ks):
        parts = [pick(x, me ^ k) for k in ks]
        return [p if k == 0 else exchange(p, "seq", k) for p, k in zip(parts, ks)]

    far_parts = from_peers(tokens, (3, 2))
    near_parts = from_peers(tokens, (0, 1))
    zero = jnp.zeros((d,), BF)
    vec = jnp.concatenate(
        [attend_gain, attend_shift, query_bias, zero, value_bias, output_bias, mixer_gain, mixer_shift, reduce_bias] + [zero] * 7
    ).astype(F32).reshape(16, d)
    wide = ff // CHUNKS
    lanes = wide // PIECES
    b1 = expand_bias.astype(F32).reshape(ff // 128, 128)
    load = jnp.sum(jnp.where(volume_owner == lax.axis_index("vol"), volume_slices, 0))
    live = (jnp.arange(slices) < load).astype(BF)

    made = project_in(jnp.concatenate(near_parts), 0, n, None, vec, input_weight)
    far = jnp.concatenate([after(far_parts[1], made[2], b1, live), far_parts[0]])
    x, first_t, packed = project_in(far, 2 * rows, n, made, vec, input_weight)
    upstream = jnp.concatenate(from_peers(after(cotangent, far_parts[0], made[2]) * live[:, None, None], (0, 1, 2, 3)))

    mixed, inverse, weights = attend(packed)

    db1 = []

    def hidden(token, head, carried, i):
        gk, gs, b, *made = hidden_part(token, head, carried, upstream, expand_weight, reduce_weight, b1, i)
        db1.append(b)
        return gk, gs, made

    Y, Z1, Z2 = 0, 1, 2
    piece_rows = d // 2 + d // 2
    pair_rows = 3 * (d // PIECES)
    k0, s0, (o, ds, *kept) = hidden(core, (x, mixed, output_weight, vec), None, 0)
    r0 = to_core(s0)
    k1, s1, (o, ds) = hidden(after(core, s0), None, (*kept, o, ds), 1)
    r1 = to_core(s1)
    ga = Part(k0, r0, piece_rows)
    sent, _ = slot(ids, [("half", [ga])], s1)
    k2, s2, (o, ds) = hidden(after(core, s1, *sent), None, (*kept, o, ds), 2)
    r2 = to_core(s2)
    gb = Part(k1, r1, piece_rows)
    sent, _ = slot(ids, [(Z1, [gb])], s2)
    out, d_branch, d_mixed, k3, s3, sums_mid = outer(
        after(core, s2, *sent), x, upstream, mixed, inverse, output_weight, vec, o, ds
    )
    r3 = to_core(s3)

    def homeward(a):
        blocks = [a[k * rows : (k + 1) * rows] for k in range(1, peers)]
        return blocks, [exchange(b, "seq", k + 1) for k, b in enumerate(blocks)]

    out_sent, outs = homeward(out)
    gc = Part(k2, r2, piece_rows)
    sent, got = slot(ids, [(Y, [gc]), (Z2, [gb])], s3)
    parts = []

    def reflect_part(token, i):
        dq, dk, dv, gk, gs = reflect(token, packed, mixed, d_mixed, weights, first_t, 2 * i)
        parts.extend([dq, dk, dv])
        return gk, gs

    p0, q0 = reflect_part(after(core, s3, *sent, *out_sent), 0)
    t0 = to_core(q0)
    wait_c = got[0]
    sent, _ = slot(ids, [(Y, [ga, gb])], q0)
    p1, q1 = reflect_part(after(core, q0, wait_c, *sent, *outs), 1)
    t1 = to_core(q1)
    gd, gd2 = Part(k3, r3, pair_rows), Part(p0, t0, pair_rows)
    sent, _ = slot(ids, [(Z1, [ga, gc]), ("pick", [gd, gd2])], q1)
    p2, q2 = reflect_part(after(core, q1, *sent), 2)
    t2 = to_core(q2)
    ge1 = Part(p1, t1, pair_rows)
    sent, _ = slot(ids, [(Y, [ge1, gd]), (Z2, [ga, gc])], q2)
    d_tokens, small = project_back(after(x, *sent), d_branch, input_weight, vec, sums_mid, db1, parts)

    tg_sent, tgs = homeward(d_tokens)
    ge2 = Part(p2, t2, pair_rows)
    gv = Part(small, to_core(small), SMALL)
    sent1, got1 = slot(ids, [(Y, [ge2, gv])], small, *tg_sent)
    block_out = send_home(ids, live, out, [after(o, *sent1) for o in outs], slices, BF, True)
    sent2, got2 = slot(ids, [(Z1, [ge1, ge2, gd, gv]), ("x", [ga, gb, gc])], *got1, block_out)
    per = d // PIECES

    def both_terms(p, *tokens):
        pieces = [lax.slice_in_dim(a, at, at + p.count()) for a, at in (p.held, p.received)]
        pieces = list(lax.optimization_barrier(tuple(pieces) + tokens)[:2])
        return pieces + [to_core(a) for a in pieces]

    spare = [1 << i for i in range(unit.bit_length() - 1)]
    sent3, got3 = slot(ids, [(Z2, [ge1, ge2, gd, gv])], *got2)
    tgs = [after(t, *sent3) for t in tgs]
    tokens_grad = send_home(ids, live, d_tokens, tgs, slices, F32, False)
    ff_terms = both_terms(ga, *sent3) + both_terms(gb, *sent3) + both_terms(gc, *sent3)
    sent4, got4 = slot(ids, [("x", [ge1, ge2, gd, gv])], *got3, tokens_grad)
    ff_terms = list(lax.optimization_barrier(tuple(ff_terms) + tuple(sent4))[: len(ff_terms)])
    expand_grad, reduce_grad = assemble(assemble_ff_kernel, ids, per, ff_terms, [(per, ff), (ff // PIECES, d)], "assemble_ff")
    at = 2 * pair_rows
    held, received = sent4[0], got4[0]
    ends = [held[at : at + pair_rows], received[at : at + pair_rows], held[:at], received[:at]]
    ends = ends + [to_core(a) for a in ends]
    at += pair_rows
    output_grad, input_grad, vectors = assemble(
        assemble_end_kernel, ids, per, ends + [held[at:], received[at:]], [(per, d), (per, 3 * d), (SMALL, 128)], "assemble_end"
    )
    bias_rows = vectors[8 : 8 + CHUNKS]
    vectors = vectors[:8, :per]
    if unit > 1:
        sub = vol % unit

        def add_rest(a):
            for by in spare:
                a = a + exchange(a, "vol", by)
            return a

        def cut(a, axis):
            size = a.shape[axis] // unit
            return lax.dynamic_slice_in_dim(add_rest(a), sub * size, size, axis)

        expand_grad, reduce_grad, output_grad, input_grad = [cut(a, 0) for a in (expand_grad, reduce_grad, output_grad, input_grad)]
        expand_bias_grad = cut(bias_rows.reshape(-1), 0)
        vectors = cut(vectors, 1)
    else:
        expand_bias_grad = bias_rows.reshape(-1)
    return (
        block_out, tokens_grad, vectors[0], vectors[1], input_grad, vectors[2], vectors[3], output_grad, vectors[4],
        vectors[5], vectors[6], expand_grad, expand_bias_grad, reduce_grad, vectors[7],
    )


def solution(mesh):
    rows = P("vol", "seq", None)
    return jax.shard_map(
        on_device,
        mesh=mesh,
        in_specs=(P(), P(), rows, rows) + (P(),) * 13,
        out_specs=(rows, rows, P("vol"), P("vol"), P("vol", None), P("vol"), P("vol"), P("vol", None), P("vol"), P("vol"),
                   P("vol"), P("vol", None), P("vol"), P("vol", None), P("vol")),
        check_vma=False,
    )
```

```python
import functools

import jax
import jax.numpy as jnp
from jax import lax
from jax.experimental import pallas as pl
from jax.experimental.pallas import tpu as pltpu
from jax.sharding import PartitionSpec as P

HEAD_DIM = 64
PAIR = 2 * HEAD_DIM
LOG2E = 1.4426950408889634
PIECES = 8
CHUNKS = 3
ROW = {n: i for i, n in enumerate(("ag", "ash", "qb", "zero", "vb", "ob", "mg", "ms", "rb"))}
BF = jnp.bfloat16
F32 = jnp.float32
NN = (((1,), (0,)), ((), ()))
NT = (((1,), (1,)), ((), ()))
TAIL = (
    0.11962928008603971,
    0.12075423895539067,
    0.09991176086876633,
    0.12856720585766357,
    -0.05369390237929985,
    0.20636430391507077,
    -0.15720912816414995,
    0.03567616760586865,
)


def dot(a, b, dims):
    return lax.dot_general(a, b, dims, preferred_element_type=F32)


def params(mib=24):
    return pltpu.CompilerParams(vmem_limit_bytes=mib << 20)


def line(ref, name):
    return ref[ROW[name] : ROW[name] + 1, :]


def shape(dims, dtype=BF):
    return jax.ShapeDtypeStruct(dims, dtype)


def normal(h):
    a = jnp.abs(h)
    t = 1.0 / (1.0 + 0.3 * a)
    s = TAIL[7] * t + TAIL[6]
    for c in TAIL[5::-1]:
        s = s * t + c
    e = jnp.exp2(h * h * (-0.5 * LOG2E))
    tail = s * t * e
    return jnp.where(h >= 0, 1.0 - tail, tail), e * 0.3989422804014327


def stats(v):
    spread = v - jnp.mean(v, axis=-1, keepdims=True)
    return spread, lax.rsqrt(jnp.mean(spread * spread, axis=-1, keepdims=True) + 1e-6)


def in_kernel(x_ref, vec_ref, w_ref, *rest):
    x_out, first_t, packed = rest[-3:]
    x = x_ref[...]
    d = x.shape[1]
    spread, r = stats(x.astype(F32))
    f = (spread * r * line(vec_ref, "ag") + line(vec_ref, "ash")).astype(BF)
    x_out[...] = x
    for i, bias in enumerate(("qb", "zero", "vb")):
        packed[:, i * d : (i + 1) * d] = (dot(f, w_ref[:, i * d : (i + 1) * d], NN) + line(vec_ref, bias)).astype(BF)
    first_t[...] = f.T


def project_in(part, offset, total, before, vec, weight):
    rows, d = part.shape
    wide = weight.shape[1]
    tm = 256
    first_block = offset // tm

    def full(a):
        return pl.BlockSpec(a.shape, lambda i: (0, 0), pipeline_mode=pl.Buffered(1))

    in_specs = [pl.BlockSpec((tm, d), lambda i: (i, 0)), full(vec), full(weight)]
    args = [part, vec, weight]
    aliases = {}
    if before is not None:
        aliases = {3: 0, 4: 1, 5: 2}
        in_specs += [pl.BlockSpec(memory_space=pl.ANY)] * 3
        args += list(before)
    return pl.pallas_call(
        in_kernel,
        grid=(rows // tm,),
        in_specs=in_specs,
        out_specs=[
            pl.BlockSpec((tm, d), lambda i: (i + first_block, 0)),
            pl.BlockSpec((d, tm), lambda i: (0, i + first_block)),
            pl.BlockSpec((tm, wide), lambda i: (i + first_block, 0)),
        ],
        out_shape=[shape((total, d)), shape((d, total)), shape((total, wide))],
        input_output_aliases=aliases,
        compiler_params=params(),
        cost_estimate=pl.CostEstimate(flops=6 * rows * d * wide, bytes_accessed=2 * (d * wide + rows * (wide + 3 * d)), transcendentals=0),
        name="project_in",
    )(*args)


def attend_kernel(q_ref, k_ref, v_ref, o_ref, inv_ref, p_ref, vx_ref, *, tq):
    n = k_ref.shape[0]
    head = 2 * pl.program_id(0)
    lane = lax.broadcasted_iota(jnp.int32, (tq, PAIR), 1)
    vx_ref[:, :PAIR] = v_ref[...]
    vx_ref[:, PAIR:] = jnp.ones((n, PAIR), BF)
    low = lax.broadcasted_iota(jnp.int32, (tq, PAIR), 1) < HEAD_DIM
    for t in range(n // tq):
        rows = pl.ds(t * tq, tq)
        q = q_ref[rows, :]
        zero = jnp.zeros_like(q)
        outs = []
        for a in range(2):
            qa = jnp.where(low, q, zero) if a == 0 else jnp.where(low, zero, q)
            s = dot(qa, k_ref[...], NT)
            top = jnp.max(s, axis=-1, keepdims=True)
            p = jnp.exp2((s - top) * (LOG2E * HEAD_DIM**-0.5)).astype(BF)
            p_ref[a, rows, :] = p
            both = dot(p, vx_ref[...], NN)
            inv = 1.0 / both[:, PAIR:]
            outs.append((both[:, :PAIR] * inv, inv))
        o_ref[rows, :] = jnp.where(low, outs[0][0], outs[1][0]).astype(BF)
        inv_ref[rows, :] = jnp.where(lane == head, outs[0][1], jnp.where(lane == head + 1, outs[1][1], inv_ref[rows, :]))


def attend(packed):
    n, w = packed.shape
    d = w // 3
    hp = d // PAIR

    def cols(off):
        return pl.BlockSpec((n, PAIR), lambda h: (0, h + off))

    return pl.pallas_call(
        functools.partial(attend_kernel, tq=128),
        grid=(hp,),
        in_specs=[cols(0), cols(hp), cols(2 * hp)],
        out_specs=[cols(0), pl.BlockSpec((n, PAIR), lambda h: (0, 0)), pl.BlockSpec((2, n, n), lambda h: (h, 0, 0))],
        out_shape=[shape((n, d)), shape((n, PAIR), F32), shape((2 * hp, n, n))],
        scratch_shapes=[pltpu.VMEM((n, 2 * PAIR), BF)],
        compiler_params=params(),
        cost_estimate=pl.CostEstimate(flops=16 * n * n * d, bytes_accessed=4 * n * n * hp, transcendentals=0),
        name="attend",
    )(packed, packed, packed)


WHOLE = pl.BlockSpec(memory_space=pltpu.VMEM)
FAR = pl.BlockSpec(memory_space=pltpu.HBM)


def transpose_rows(block, out, cols):
    t = block.T
    d = t.shape[0]
    half = d // PIECES // 2
    for h in range(2):
        for v in range(PIECES):
            at = (2 * v + h) * half
            to = (h * PIECES + v) * half
            out[to : to + half, cols] = t[at : at + half]


def core_rows(ref, which):
    half = ref.shape[0] // 2
    return ref[pl.ds(pl.multiple_of(which * half, half), half), :]


def piece_blocks(g, ref, first):
    rows = g.shape[0] // PIECES
    for k in range(g.shape[1] // 128):
        at = (first + k) * rows
        ref[:, at : at + rows, :] = g[:, k * 128 : (k + 1) * 128].reshape(PIECES, rows, 128)


def middle_of(x_ref, mix_ref, wo_ref, vec_ref, rows):
    return x_ref[rows, :].astype(F32) + dot(mix_ref[rows, :], wo_ref[...], NN) + line(vec_ref, "ob")


def chunk_copies(w1_hbm, w2_hbm, w1, w2, sems, i):
    copies = []
    for v in range(PIECES):
        at = pl.ds((v * CHUNKS + i) * 128, 128)
        to = pl.ds(v * 128, 128)
        copies.append(pltpu.make_async_copy(w1_hbm.at[:, at], w1.at[:, to], sems.at[0, v]))
        copies.append(pltpu.make_async_copy(w2_hbm.at[at, :], w2.at[to, :], sems.at[1, v]))
    for copy in copies:
        copy.start()
    return copies


def hidden_kernel(c_ref, *refs, i, head, tail, tm, sub):
    refs = list(refs)
    take = lambda k: [refs.pop(0) for _ in range(k)]
    if head:
        x_ref, mix_ref, wo_ref, vec_ref = take(4)
    else:
        sec_ref, sec_t, up_t, o_in, ds_in, w1, w2 = take(7)
    up_ref, w1_hbm, w2_hbm, b1_ref, gk_ref, gs_ref, db1_ref, o_ref, ds_ref = take(9)
    if head:
        sec_ref, sec_t, up_t = take(3)
    if not tail:
        w1_next, w2_next = take(2)
    act, dh = take(2)
    own, coming = [], []
    if head:
        w1, w2, sems = take(3)
        own = chunk_copies(w1_hbm, w2_hbm, w1, w2, sems, i)
    n, d = up_ref.shape
    wide = act.shape[1]
    if not tail:
        coming = chunk_copies(w1_hbm, w2_hbm, w1_next, w2_next, take(1)[0], i + 1)
    if head:
        for t in range(n // tm):
            rows = slice(t * tm, (t + 1) * tm)
            spread, r = stats(middle_of(x_ref, mix_ref, wo_ref, vec_ref, rows))
            sec = (spread * r * line(vec_ref, "mg") + line(vec_ref, "ms")).astype(BF)
            sec_ref[rows, :] = sec
            transpose_rows(sec, sec_t, rows)
            up_t[:, rows] = up_ref[rows, :].T

    for copy in own:
        copy.wait()
    c = c_ref[0]
    for at in range(0, wide, sub):
        cols = slice(at, at + sub)
        bias = jnp.concatenate([b1_ref[v * CHUNKS + i : v * CHUNKS + i + 1, :] for v in range(at // 128, (at + sub) // 128)], axis=1)
        for t in range(n // tm):
            rows = slice(t * tm, (t + 1) * tm)
            h = dot(sec_ref[rows, :], w1[:, cols], NN) + bias
            da = dot(up_ref[rows, :], w2[cols, :], NT)
            cdf, pdf = normal(h)
            act[rows, cols] = (h * cdf).astype(BF)
            dhv = da * (cdf + h * pdf)
            dh[rows, cols] = dhv.astype(BF)
            part = jnp.sum(dhv, axis=0, keepdims=True)
            db1_ref[:, cols] = part if t == 0 else db1_ref[:, cols] + part
    base = PIECES * (d // PIECES // 2)
    for ref, mine in ((gs_ref, 1 - c), (gk_ref, c)):
        piece_blocks(dot(core_rows(sec_t, mine), dh[...], NN).astype(BF), ref, 0)
        g = dot(core_rows(up_t, mine), act[...], NN).astype(BF)
        for k in range(wide // 128):
            ref[k, base:, :] = g[:, k * 128 : (k + 1) * 128]
    o = dot(act[...], w2[...], NN)
    o_ref[...] = o if head else o_in[...] + o
    ds = dot(dh[...], w1[...], NT)
    ds_ref[...] = ds if head else ds_in[...] + ds
    for copy in coming:
        copy.wait()


def hidden_part(core, head, carried, up, w1, w2, b1, i, tm=512, sub=512):
    n, d = up.shape
    wide = 128 * PIECES
    assert wide * CHUNKS == w1.shape[1]
    g = (PIECES, PIECES * (d // PIECES // 2) + d // 2, 128)
    tail = i == CHUNKS - 1
    args = list(head) if head else list(carried)
    made = [shape(g), shape(g), shape((1, wide), F32), shape((n, d), F32), shape((n, d), F32)]
    scratch = [pltpu.VMEM((n, wide), BF), pltpu.VMEM((n, wide), BF)]
    sems = pltpu.SemaphoreType.DMA((2, PIECES))
    if head:
        made += [shape((n, d)), shape((d, n)), shape((d, n))]
        scratch += [pltpu.VMEM((d, wide), BF), pltpu.VMEM((wide, d), BF), sems]
    if not tail:
        made += [shape((d, wide)), shape((wide, d))]
        scratch += [sems]
    return pl.pallas_call(
        functools.partial(hidden_kernel, i=i, head=bool(head), tail=tail, tm=tm, sub=sub),
        in_specs=[pl.BlockSpec(memory_space=pltpu.SMEM)] + [WHOLE] * (len(args) + 1) + [FAR, FAR, WHOLE],
        out_specs=[WHOLE] * len(made),
        out_shape=made,
        input_output_aliases={} if head else {4: 3, 5: 4},
        scratch_shapes=scratch,
        compiler_params=params(),
        cost_estimate=pl.CostEstimate(flops=24 * n * d * wide, bytes_accessed=8 * d * wide, transcendentals=0),
        name="hidden",
    )(core, *args, up, w1, w2, b1)


def outer_kernel(c_ref, x_ref, up_ref, mix_ref, li_ref, wo_ref, vec_ref, o_ref, ds_ref, out_ref, dbr_ref, do_ref, gk_ref, gs_ref, sums_ref, mix_t, *, tm):
    n, d = x_ref.shape
    sums = None
    lanes = lax.broadcasted_iota(jnp.int32, (PAIR, d), 1) // HEAD_DIM
    spread_heads = (lanes == lax.broadcasted_iota(jnp.int32, (PAIR, d), 0)).astype(BF)
    for t in range(n // tm):
        rows = slice(t * tm, (t + 1) * tm)
        m = middle_of(x_ref, mix_ref, wo_ref, vec_ref, rows)
        spread, r = stats(m)
        nv = spread * r
        up = up_ref[rows, :].astype(F32)
        transpose_rows(mix_ref[rows, :], mix_t, rows)
        dy = ds_ref[rows, :]
        dyg = dy * line(vec_ref, "mg")
        dm = up + r * (dyg - jnp.mean(dyg, axis=-1, keepdims=True) - nv * jnp.mean(dyg * nv, axis=-1, keepdims=True))
        db = dm.astype(BF)
        dbr_ref[rows, :] = db
        out_ref[rows, :] = (m + o_ref[rows, :] + line(vec_ref, "rb")).astype(BF)
        li = li_ref[rows, :]
        coarse = li.astype(BF)
        fine = (li - coarse.astype(F32)).astype(BF)
        scale = dot(coarse, spread_heads, NN) + dot(fine, spread_heads, NN)
        do_ref[rows, :] = (dot(db, wo_ref[...], NT) * scale).astype(BF)
        part = [jnp.sum(v, axis=0, keepdims=True) for v in (db.astype(F32), dy * nv, dy, up)]
        sums = part if sums is None else [a + b for a, b in zip(sums, part)]
    sums_ref[...] = jnp.concatenate(sums + [jnp.zeros((4, d), F32)], axis=0)
    for ref, mine in ((gs_ref, 1 - c_ref[0]), (gk_ref, c_ref[0])):
        piece_blocks(dot(core_rows(mix_t, mine), dbr_ref[...], NN).astype(BF), ref, 0)


def outer(core, x, up, mix, li, wo, vec, o, ds, tm=256):
    n, d = x.shape
    g = (PIECES, d // 128 * (d // PIECES // 2), 128)
    return pl.pallas_call(
        functools.partial(outer_kernel, tm=tm),
        in_specs=[pl.BlockSpec(memory_space=pltpu.SMEM)] + [WHOLE] * 8,
        out_specs=[WHOLE] * 6,
        out_shape=[shape((n, d))] * 3 + [shape(g), shape(g), shape((8, d), F32)],
        scratch_shapes=[pltpu.VMEM((d, n), BF)],
        compiler_params=params(),
        cost_estimate=pl.CostEstimate(flops=24 * n * d * d, bytes_accessed=20 * n * d, transcendentals=0),
        name="outer",
    )(core, x, up, mix, li, wo, vec, o, ds)


def by_piece(g):
    rows = g.shape[0] // PIECES
    return [g[:, i : i + 128].reshape(PIECES, rows, 128) for i in range(0, g.shape[1], 128)]


def reflect_kernel(c_ref, q_ref, k_ref, v_ref, o_ref, do_ref, p_ref, ft_ref, dq_ref, dk_ref, dv_ref, gk_ref, gs_ref, ds_ref, *, tq):
    n = k_ref.shape[0]
    low = lax.broadcasted_iota(jnp.int32, (tq, PAIR), 1) < HEAD_DIM
    q_t = q_ref[...].T
    do_t = do_ref[...].T
    scale = HEAD_DIM**-0.5
    dks, dvs = [], []
    for a in range(2):
        for t in range(n // tq):
            rows = pl.ds(t * tq, tq)
            do = do_ref[rows, :]
            zero = jnp.zeros_like(do)
            doa = jnp.where(low, do, zero) if a == 0 else jnp.where(low, zero, do)
            delta = jnp.sum(doa.astype(F32) * o_ref[rows, :].astype(F32), axis=-1, keepdims=True)
            dp = dot(doa, v_ref[...], NT)
            ds = (p_ref[a, rows, :].astype(F32) * (dp - delta)).astype(BF)
            ds_ref[rows, :] = ds
            dq = (dot(ds, k_ref[...], NN) * scale).astype(BF)
            dq_ref[rows, :] = dq if a == 0 else jnp.where(low, dq_ref[rows, :], dq)
        part = slice(HEAD_DIM * a, HEAD_DIM * (a + 1))
        dvs.append(dot(do_t[part], p_ref[a], NN))
        dks.append(dot(q_t[part], ds_ref[...], NN) * scale)
    dv = jnp.concatenate(dvs, axis=0).astype(BF).T
    dk = jnp.concatenate(dks, axis=0).astype(BF).T
    dv_ref[...] = dv
    dk_ref[...] = dk
    g = dot(ft_ref[...], jnp.concatenate([dq_ref[...], dk, dv], axis=1), NN).astype(BF)
    per = g.shape[0] // PIECES
    h = pl.program_id(0)
    for step, ref in enumerate((gs_ref, gk_ref)):

        @pl.when(h == step)
        def _():
            for i, block in enumerate(by_piece(g)):
                ref[:, i * per : (i + 1) * per, :] = block


def reflect(core, packed, o, do, p, first_t, start):
    n, w = packed.shape
    d = w // 3
    hp = d // PAIR

    def which(h, c):
        return (h + 1 - c[0]) % 2

    def cols(off):
        return pl.BlockSpec((n, PAIR), lambda h, c: (0, which(h, c) + off))

    g = (PIECES, 3 * (d // PIECES), 128)
    piece = pl.BlockSpec(g, lambda h, c: (0, 0, 0), pipeline_mode=pl.Buffered(1))
    return pl.pallas_call(
        functools.partial(reflect_kernel, tq=256),
        grid_spec=pltpu.PrefetchScalarGridSpec(
            num_scalar_prefetch=1,
            grid=(2,),
            in_specs=[
                cols(start), cols(start + hp), cols(start + 2 * hp), cols(start), cols(start),
                pl.BlockSpec((2, n, n), lambda h, c: (which(h, c) + start, 0, 0)),
                pl.BlockSpec((d, n), lambda h, c: (0, 0), pipeline_mode=pl.Buffered(1)),
            ],
            out_specs=[cols(0)] * 3 + [piece] * 2,
            scratch_shapes=[pltpu.VMEM((n, n), BF)],
        ),
        out_shape=[shape((n, 2 * PAIR))] * 3 + [shape(g)] * 2,
        compiler_params=params(),
        cost_estimate=pl.CostEstimate(flops=160 * n * n * PAIR, bytes_accessed=8 * n * n, transcendentals=0),
        name="reflect",
    )(core, packed, packed, packed, o, do, p, first_t)


SMALL = 16


def back_kernel(*refs, chunks):
    x_ref, dbr_ref, w_ref, vec_in, mid_ref = refs[:5]
    db1 = refs[5 : 5 + CHUNKS]
    parts = refs[5 + CHUNKS : 5 + CHUNKS + 3 * chunks]
    tg_ref, small_ref, sums = refs[5 + CHUNKS + 3 * chunks :]

    @pl.when(pl.program_id(0) == 0)
    def _():
        sums[...] = jnp.zeros_like(sums)

    d = x_ref.shape[1]
    cw = d // chunks
    dy = None
    for i in range(3 * chunks):
        which, chunk = i % 3, i // 3
        at = which * d + chunk * cw
        part = dot(parts[i][...], w_ref[:, at : at + cw], NT)
        dy = part if dy is None else dy + part
        row = {0: 2, 2: 3}.get(which)
        if row is not None:
            sums[row : row + 1, chunk * cw : (chunk + 1) * cw] += jnp.sum(parts[i][...].astype(F32), axis=0, keepdims=True)
    spread, r = stats(x_ref[...].astype(F32))
    nv = spread * r
    dyg = dy * line(vec_in, "ag")
    dx = r * (dyg - jnp.mean(dyg, axis=-1, keepdims=True) - nv * jnp.mean(dyg * nv, axis=-1, keepdims=True))
    tg_ref[...] = (dbr_ref[...].astype(F32) + dx).astype(BF)
    sums[0:1, :] += jnp.sum(dy * nv, axis=0, keepdims=True)
    sums[1:2, :] += jnp.sum(dy, axis=0, keepdims=True)

    @pl.when(pl.program_id(0) == pl.num_programs(0) - 1)
    def _():
        per = d // PIECES
        sums[4:8, :] = mid_ref[0:4, :]
        rows = sums[...]
        for v in range(PIECES):
            vectors = jnp.concatenate([rows[:, v * per : (v + 1) * per], jnp.zeros((8, 128 - per), F32)], axis=1)
            biases = [b[:, v * 128 : (v + 1) * 128] for b in db1]
            piece = jnp.concatenate([vectors] + biases + [jnp.zeros((SMALL - 8 - CHUNKS, 128), F32)], axis=0)
            small_ref[v * SMALL : (v + 1) * SMALL, :] = piece.astype(BF)


def project_back(x, dbr, w, vec, mids, db1, parts):
    n, d = x.shape
    tm = 256
    row = pl.BlockSpec((tm, d), lambda i: (i, 0))

    def full(*s):
        return pl.BlockSpec(s, lambda i: (0, 0), pipeline_mode=pl.Buffered(1))

    chunks = len(parts) // 3
    return pl.pallas_call(
        functools.partial(back_kernel, chunks=chunks),
        grid=(n // tm,),
        in_specs=[row, row, full(d, 3 * d), full(*vec.shape), full(*mids.shape)]
        + [full(*b.shape) for b in db1]
        + [pl.BlockSpec((tm, d // chunks), lambda i: (i, 0))] * (3 * chunks),
        out_specs=[row, full(PIECES * SMALL, 128)],
        out_shape=[shape((n, d)), shape((PIECES * SMALL, 128))],
        scratch_shapes=[pltpu.VMEM((8, d), F32)],
        compiler_params=params(),
        cost_estimate=pl.CostEstimate(flops=12 * n * d * d, bytes_accessed=16 * n * d, transcendentals=0),
        name="project_back",
    )(x, dbr, w, vec, mids, *db1, *parts)


def exchange(x, axis, by):
    count = lax.axis_size(axis)
    return lax.ppermute(x, axis, [(i, i ^ by) for i in range(count)])


def to_core(g):
    return exchange(g, "seq", 1)


def pick(x, index, axis=0):
    return lax.dynamic_index_in_dim(x, index, axis, keepdims=False)


def after(x, *others):
    return lax.optimization_barrier((x,) + others)[0]


class Part:
    def __init__(self, held, received, rows):
        self.held = (held.reshape(-1, 128), 0)
        self.received = (received.reshape(-1, 128), 0)
        self.rows = rows
        self.open = [0, 1, 2]

    def count(self):
        return self.rows << len(self.open)


def slot_kernel(ids_ref, *refs, items, inputs):
    ins, outs = refs[:inputs], refs[inputs:]

    def read(term, at, count):
        ref, offset = term
        return ins[ref][pl.ds(at + offset, count), :].astype(F32)

    step = 16
    for kind, *rest in items:
        if kind == "split":
            held, received, groups, size, bit, (send, to), keep = rest
            mine = ids_ref[bit]
            for a in range(groups):
                own = pl.multiple_of((2 * a + mine) * size, step)
                other = pl.multiple_of((2 * a + 1 - mine) * size, step)
                outs[send][to + a * size : to + (a + 1) * size, :] = (read(held, other, size) + read(received, other, size)).astype(BF)
                outs[keep][a * size : (a + 1) * size, :] = (read(held, own, size) + read(received, own, size)).astype(BF)
        elif kind == "sum":
            held, received, size, (send, to) = rest
            outs[send][to : to + size, :] = (read(held, 0, size) + read(received, 0, size)).astype(BF)
        else:
            first, second, size, bit, (send, to), keep = rest
            for mine in (0, 1):

                @pl.when(ids_ref[bit] == mine)
                def _():
                    own, other = (first, second) if mine == 0 else (second, first)
                    outs[send][to : to + size, :] = (read(other[0], 0, size) + read(other[1], 0, size)).astype(BF)
                    outs[keep][...] = (read(own[0], 0, size) + read(own[1], 0, size)).astype(BF)


def slot(ids, exchanges, *tokens):
    arrays, items, sizes, moves = [], [], [], []

    def use(term):
        for i, a in enumerate(arrays):
            if a is term[0]:
                return i, term[1]
        arrays.append(term[0])
        return len(arrays) - 1, term[1]

    for stage, parts in exchanges:
        send, to = len(sizes), 0
        sizes.append(0)
        placed = []
        if stage == "pick":
            one, two = parts
            size = one.count()
            items.append(("pick", (use(one.held), use(one.received)), (use(two.held), use(two.received)), size, 1, (send, 0), len(sizes)))
            placed.append((one, len(sizes), 0, 0))
            sizes.append(size)
            to = size
        else:
            for p in parts:
                held, received = use(p.held), use(p.received)
                if stage == "x":
                    items.append(("sum", held, received, p.count(), (send, to)))
                    placed.append((p, send, to, to))
                    to += p.count()
                    continue
                if stage == "half":
                    groups, bit = 1 << len(p.open), 1
                else:
                    groups, bit = 1 << (len(p.open) - 1 - p.open.index(stage)), 2 + stage
                size = p.count() // (2 * groups)
                items.append(("split", held, received, groups, size, bit, (send, to), len(sizes)))
                placed.append((p, len(sizes), 0, to))
                sizes.append(groups * size)
                to += groups * size
                if stage == "half":
                    p.rows //= 2
                else:
                    p.open.remove(stage)
        sizes[send] = to
        moves.append((stage, send, placed))

    if tokens:
        arrays = list(lax.optimization_barrier(tuple(arrays) + tokens)[: len(arrays)])
    whole = pl.BlockSpec(memory_space=pltpu.VMEM)
    outs = pl.pallas_call(
        functools.partial(slot_kernel, items=items, inputs=len(arrays)),
        in_specs=[pl.BlockSpec(memory_space=pltpu.SMEM)] + [whole] * len(arrays),
        out_specs=[whole] * len(sizes),
        out_shape=[shape((size, 128)) for size in sizes],
        compiler_params=params(),
        cost_estimate=pl.CostEstimate(flops=0, bytes_accessed=512 * sum(sizes), transcendentals=0),
        name="slot",
    )(ids, *arrays)
    unit = lax.axis_size("vol") // PIECES
    sent, received = [], []
    for stage, send, placed in moves:
        if stage in ("half", "pick", "x"):
            got = exchange(outs[send], "seq", 2)
        else:
            got = exchange(outs[send], "vol", unit << stage)
        sent.append(outs[send])
        received.append(got)
        for p, keep, at, to in placed:
            p.held = (outs[keep], at)
            p.received = (got, to)
    return sent, received


def home_kernel(ids_ref, live_ref, *refs, mask):
    out_ref = refs[-1]
    for k, ref in enumerate(refs[:-1]):

        @pl.when(pl.program_id(0) == k)
        def _():
            value = ref[...].astype(F32)
            if mask:
                value = value * live_ref[ids_ref[5] ^ k]
            out_ref[...] = value.astype(out_ref.dtype)


def send_home(ids, live, own, others, slices, dtype, mask):
    rows, d = others[0].shape
    return pl.pallas_call(
        functools.partial(home_kernel, mask=mask),
        grid_spec=pltpu.PrefetchScalarGridSpec(
            num_scalar_prefetch=2,
            grid=(slices,),
            in_specs=[pl.BlockSpec((rows, d), lambda k, i, l: (0, 0), pipeline_mode=pl.Buffered(1))] * slices,
            out_specs=pl.BlockSpec((None, rows, d), lambda k, i, l: (k ^ i[5], 0, 0)),
        ),
        out_shape=shape((slices, rows, d), dtype),
        compiler_params=params(),
        cost_estimate=pl.CostEstimate(flops=0, bytes_accessed=6 * slices * rows * d, transcendentals=0),
        name="home",
    )(ids, live, own, *others)


def assemble_ff_kernel(ids_ref, *refs, per):
    ga, gb, gc = refs[:4], refs[4:8], refs[8:12]
    expand_ref, reduce_ref = refs[12:]
    c = ids_ref[0]

    def first_layer(i, core, value):
        size = per // 2
        for k in range(PIECES):
            at = (k * CHUNKS + i) * 128
            expand_ref[pl.ds(pl.multiple_of(core * size, size), size), at : at + 128] = value[k * size : (k + 1) * size, :]

    def second_layer(i, core, value):
        d = value.shape[0]
        reduce_ref[i * 128 : (i + 1) * 128, pl.ds(pl.multiple_of(core * d, 128), d)] = value.T

    half = per * (PIECES // 2)
    for core, (mine, other) in ((c, (ga[0], ga[1])), (1 - c, (ga[2], ga[3]))):

        @pl.when(ids_ref[1] == 0)
        def _():
            first_layer(0, core, mine[...].astype(F32))
            second_layer(0, core, other[...].astype(F32))

        @pl.when(ids_ref[1] == 1)
        def _():
            first_layer(0, core, other[...].astype(F32))
            second_layer(0, core, mine[...].astype(F32))

    for i, refs_i in ((1, gb), (2, gc)):
        for core, (one, two) in ((c, refs_i[:2]), (1 - c, refs_i[2:])):
            total = one[...].astype(F32) + two[...].astype(F32)
            first_layer(i, core, total[:half])
            second_layer(i, core, total[half:])


def assemble_end_kernel(ids_ref, *refs, per):
    mine, theirs = refs[:4], refs[4:8]
    small_held, small_received, output_ref, input_ref, vector_ref = refs[8:]
    c = ids_ref[0]
    d = PIECES * per

    def output_part(core, value):
        size = per // 2
        for k in range(d // 128):
            rows = pl.ds(pl.multiple_of(core * size, size), size)
            output_ref[rows, k * 128 : (k + 1) * 128] = value[k * size : (k + 1) * size, :]

    def pair_part(i, core, value):
        for k in range(3):
            at = pl.multiple_of(k * d + (2 * i + core) * 128, 128)
            input_ref[:, pl.ds(at, 128)] = value[k * per : (k + 1) * per, :]

    for core, (own, other, one, two) in ((c, mine), (1 - c, theirs)):

        @pl.when(ids_ref[1] == 0)
        def _():
            output_part(core, own[...].astype(F32))
            pair_part(0, core, other[...].astype(F32))

        @pl.when(ids_ref[1] == 1)
        def _():
            output_part(core, other[...].astype(F32))
            pair_part(0, core, own[...].astype(F32))

        total = one[...].astype(F32) + two[...].astype(F32)
        for i in (1, 2):
            pair_part(i, core, total[(i - 1) * 3 * per : i * 3 * per])
    vector_ref[...] = small_held[...].astype(F32) + small_received[...].astype(F32)


def assemble(kernel, ids, per, arrays, outs, name):
    whole = pl.BlockSpec(memory_space=pltpu.VMEM)
    return pl.pallas_call(
        functools.partial(kernel, per=per),
        in_specs=[pl.BlockSpec(memory_space=pltpu.SMEM)] + [whole] * len(arrays),
        out_specs=[whole] * len(outs),
        out_shape=[shape(o, F32) for o in outs],
        compiler_params=params(),
        name=name,
    )(ids, *arrays)


def on_device(
    volume_slices, volume_owner, tokens, cotangent, attend_gain, attend_shift, input_weight, query_bias, value_bias,
    output_weight, output_bias, mixer_gain, mixer_shift, expand_weight, expand_bias, reduce_weight, reduce_bias,
):
    slices, rows, d = tokens.shape
    ff = expand_weight.shape[1]
    nv = lax.axis_size("vol")
    peers = lax.axis_size("seq")
    me = lax.axis_index("seq")
    core_id = me % 2
    x_id = (me // 2) % 2
    core = core_id.astype(jnp.int32).reshape(1)
    n = rows * peers
    vol = lax.axis_index("vol")
    unit = nv // PIECES
    ids = jnp.stack([core_id, x_id, (vol // unit) % 2, (vol // (2 * unit)) % 2, (vol // (4 * unit)) % 2, me]).astype(jnp.int32)

    def from_peers(x, ks):
        parts = [pick(x, me ^ k) for k in ks]
        return [p if k == 0 else exchange(p, "seq", k) for p, k in zip(parts, ks)]

    far_parts = from_peers(tokens, (3, 2))
    near_parts = from_peers(tokens, (0, 1))
    zero = jnp.zeros((d,), BF)
    vec = jnp.concatenate(
        [attend_gain, attend_shift, query_bias, zero, value_bias, output_bias, mixer_gain, mixer_shift, reduce_bias] + [zero] * 7
    ).astype(F32).reshape(16, d)
    wide = ff // CHUNKS
    lanes = wide // PIECES
    b1 = expand_bias.astype(F32).reshape(ff // 128, 128)
    load = jnp.sum(jnp.where(volume_owner == lax.axis_index("vol"), volume_slices, 0))
    live = (jnp.arange(slices) < load).astype(BF)

    made = project_in(jnp.concatenate(near_parts), 0, n, None, vec, input_weight)
    far = jnp.concatenate([after(far_parts[1], made[2], b1, live), far_parts[0]])
    x, first_t, packed = project_in(far, 2 * rows, n, made, vec, input_weight)
    upstream = jnp.concatenate(from_peers(after(cotangent, far_parts[0], made[2]) * live[:, None, None], (0, 1, 2, 3)))

    mixed, inverse, weights = attend(packed)

    db1 = []

    def hidden(token, head, carried, i):
        gk, gs, b, *made = hidden_part(token, head, carried, upstream, expand_weight, reduce_weight, b1, i)
        db1.append(b)
        return gk, gs, made

    Y, Z1, Z2 = 0, 1, 2
    piece_rows = d // 2 + d // 2
    pair_rows = 3 * (d // PIECES)
    k0, s0, (o, ds, second, second_t, upstream_t, *weights_next) = hidden(core, (x, mixed, output_weight, vec), None, 0)
    kept = (second, second_t, upstream_t)
    r0 = to_core(s0)
    k1, s1, (o, ds, *weights_next) = hidden(after(core, s0), None, (*kept, o, ds, *weights_next), 1)
    r1 = to_core(s1)
    ga = Part(k0, r0, piece_rows)
    sent, _ = slot(ids, [("half", [ga])], s1)
    k2, s2, (o, ds) = hidden(after(core, s1, *sent), None, (*kept, o, ds, *weights_next), 2)
    r2 = to_core(s2)
    gb = Part(k1, r1, piece_rows)
    sent, _ = slot(ids, [(Z1, [gb])], s2)
    out, d_branch, d_mixed, k3, s3, sums_mid = outer(
        after(core, s2, *sent), x, upstream, mixed, inverse, output_weight, vec, o, ds
    )
    r3 = to_core(s3)

    def homeward(a):
        blocks = [a[k * rows : (k + 1) * rows] for k in range(1, peers)]
        return blocks, [exchange(b, "seq", k + 1) for k, b in enumerate(blocks)]

    out_sent, outs = homeward(out)
    gc = Part(k2, r2, piece_rows)
    sent, got = slot(ids, [(Y, [gc]), (Z2, [gb])], s3)
    parts = []

    def reflect_part(token, i):
        dq, dk, dv, gk, gs = reflect(token, packed, mixed, d_mixed, weights, first_t, 2 * i)
        parts.extend([dq, dk, dv])
        return gk, gs

    p0, q0 = reflect_part(after(core, s3, *sent, *out_sent), 0)
    t0 = to_core(q0)
    wait_c = got[0]
    sent, _ = slot(ids, [(Y, [ga, gb])], q0)
    p1, q1 = reflect_part(after(core, q0, wait_c, *sent, *outs), 1)
    t1 = to_core(q1)
    gd, gd2 = Part(k3, r3, pair_rows), Part(p0, t0, pair_rows)
    sent, _ = slot(ids, [(Z1, [ga, gc]), ("pick", [gd, gd2])], q1)
    p2, q2 = reflect_part(after(core, q1, *sent), 2)
    t2 = to_core(q2)
    ge1 = Part(p1, t1, pair_rows)
    sent, late_got = slot(ids, [(Y, [ge1, gd]), (Z2, [ga, gc])], q2)
    d_tokens, small = project_back(after(x, *sent), d_branch, input_weight, vec, sums_mid, db1, parts)

    tg_sent, tgs = homeward(d_tokens)
    ge2 = Part(p2, t2, pair_rows)
    gv = Part(small, to_core(small), SMALL)
    sent1, got1 = slot(ids, [(Y, [ge2, gv])], small, *tg_sent, late_got[1])
    block_out = send_home(ids, live, out, [after(o, *sent1) for o in outs], slices, BF, True)
    sent2, got2 = slot(ids, [(Z1, [ge1, ge2, gd, gv])], *got1, block_out, tgs[1])
    per = d // PIECES

    def both_terms(p, *tokens):
        pieces = [lax.slice_in_dim(a, at, at + p.count()) for a, at in (p.held, p.received)]
        pieces = list(lax.optimization_barrier(tuple(pieces) + tokens)[:2])
        return pieces + [to_core(a) for a in pieces]

    spare = [1 << i for i in range(unit.bit_length() - 1)]
    sent3, got3 = slot(ids, [(Z2, [ge1, ge2, gd, gv]), ("x", [ga, gb, gc])], *got2, *tgs)
    tgs = [after(t, *sent3) for t in tgs]
    tokens_grad = send_home(ids, live, d_tokens, tgs, slices, F32, False)
    sent4, got4 = slot(ids, [("x", [ge1, ge2, gd, gv])], *got3, tokens_grad)
    ff_terms = both_terms(ga, *sent4) + both_terms(gb, *sent4) + both_terms(gc, *sent4)
    expand_grad, reduce_grad = assemble(assemble_ff_kernel, ids, per, ff_terms, [(per, ff), (ff // PIECES, d)], "assemble_ff")
    at = 2 * pair_rows
    held, received = sent4[0], got4[0]
    ends = [held[at : at + pair_rows], received[at : at + pair_rows], held[:at], received[:at]]
    ends = ends + [to_core(a) for a in ends]
    at += pair_rows
    output_grad, input_grad, vectors = assemble(
        assemble_end_kernel, ids, per, ends + [held[at:], received[at:]], [(per, d), (per, 3 * d), (SMALL, 128)], "assemble_end"
    )
    bias_rows = vectors[8 : 8 + CHUNKS]
    vectors = vectors[:8, :per]
    if unit > 1:
        sub = vol % unit

        def add_rest(a):
            for by in spare:
                a = a + exchange(a, "vol", by)
            return a

        def cut(a, axis):
            size = a.shape[axis] // unit
            return lax.dynamic_slice_in_dim(add_rest(a), sub * size, size, axis)

        expand_grad, reduce_grad, output_grad, input_grad = [cut(a, 0) for a in (expand_grad, reduce_grad, output_grad, input_grad)]
        expand_bias_grad = cut(bias_rows.reshape(-1), 0)
        vectors = cut(vectors, 1)
    else:
        expand_bias_grad = bias_rows.reshape(-1)
    return (
        block_out, tokens_grad, vectors[0], vectors[1], input_grad, vectors[2], vectors[3], output_grad, vectors[4],
        vectors[5], vectors[6], expand_grad, expand_bias_grad, reduce_grad, vectors[7],
    )


def solution(mesh):
    rows = P("vol", "seq", None)
    return jax.shard_map(
        on_device,
        mesh=mesh,
        in_specs=(P(), P(), rows, rows) + (P(),) * 13,
        out_specs=(rows, rows, P("vol"), P("vol"), P("vol", None), P("vol"), P("vol"), P("vol", None), P("vol"), P("vol"),
                   P("vol"), P("vol", None), P("vol"), P("vol", None), P("vol")),
        check_vma=False,
    )
```

```python
import functools

import jax
import jax.numpy as jnp
from jax import lax
from jax.experimental import pallas as pl
from jax.experimental.pallas import tpu as pltpu
from jax.sharding import PartitionSpec as P

HEAD_DIM = 64
PAIR = 2 * HEAD_DIM
LOG2E = 1.4426950408889634
PIECES = 8
CHUNKS = 3
ROW = {n: i for i, n in enumerate(("ag", "ash", "qb", "zero", "vb", "ob", "mg", "ms", "rb"))}
BF = jnp.bfloat16
F32 = jnp.float32
NN = (((1,), (0,)), ((), ()))
NT = (((1,), (1,)), ((), ()))
TAIL = (
    0.11962928008603971,
    0.12075423895539067,
    0.09991176086876633,
    0.12856720585766357,
    -0.05369390237929985,
    0.20636430391507077,
    -0.15720912816414995,
    0.03567616760586865,
)


def dot(a, b, dims):
    return lax.dot_general(a, b, dims, preferred_element_type=F32)


def params(mib=24):
    return pltpu.CompilerParams(vmem_limit_bytes=mib << 20)


def line(ref, name):
    return ref[ROW[name] : ROW[name] + 1, :]


def shape(dims, dtype=BF):
    return jax.ShapeDtypeStruct(dims, dtype)


def normal(h):
    a = jnp.abs(h)
    t = 1.0 / (1.0 + 0.3 * a)
    s = TAIL[7] * t + TAIL[6]
    for c in TAIL[5::-1]:
        s = s * t + c
    e = jnp.exp2(h * h * (-0.5 * LOG2E))
    tail = s * t * e
    return jnp.where(h >= 0, 1.0 - tail, tail), e * 0.3989422804014327


def stats(v):
    spread = v - jnp.mean(v, axis=-1, keepdims=True)
    return spread, lax.rsqrt(jnp.mean(spread * spread, axis=-1, keepdims=True) + 1e-6)


def in_kernel(x_ref, vec_ref, w_ref, *rest):
    x_out, first_t, packed = rest[-3:]
    x = x_ref[...]
    d = x.shape[1]
    spread, r = stats(x.astype(F32))
    f = (spread * r * line(vec_ref, "ag") + line(vec_ref, "ash")).astype(BF)
    x_out[...] = x
    for i, bias in enumerate(("qb", "zero", "vb")):
        packed[:, i * d : (i + 1) * d] = (dot(f, w_ref[:, i * d : (i + 1) * d], NN) + line(vec_ref, bias)).astype(BF)
    first_t[...] = f.T


def project_in(part, offset, total, before, vec, weight):
    rows, d = part.shape
    wide = weight.shape[1]
    tm = 256
    first_block = offset // tm

    def full(a):
        return pl.BlockSpec(a.shape, lambda i: (0, 0), pipeline_mode=pl.Buffered(1))

    in_specs = [pl.BlockSpec((tm, d), lambda i: (i, 0)), full(vec), full(weight)]
    args = [part, vec, weight]
    aliases = {}
    if before is not None:
        aliases = {3: 0, 4: 1, 5: 2}
        in_specs += [pl.BlockSpec(memory_space=pl.ANY)] * 3
        args += list(before)
    return pl.pallas_call(
        in_kernel,
        grid=(rows // tm,),
        in_specs=in_specs,
        out_specs=[
            pl.BlockSpec((tm, d), lambda i: (i + first_block, 0)),
            pl.BlockSpec((d, tm), lambda i: (0, i + first_block)),
            pl.BlockSpec((tm, wide), lambda i: (i + first_block, 0)),
        ],
        out_shape=[shape((total, d)), shape((d, total)), shape((total, wide))],
        input_output_aliases=aliases,
        compiler_params=params(),
        cost_estimate=pl.CostEstimate(flops=6 * rows * d * wide, bytes_accessed=2 * (d * wide + rows * (wide + 3 * d)), transcendentals=0),
        name="project_in",
    )(*args)


def attend_kernel(q_ref, k_ref, v_ref, o_ref, inv_ref, p_ref, vx_ref, *, tq):
    n = k_ref.shape[0]
    head = 2 * pl.program_id(0)
    lane = lax.broadcasted_iota(jnp.int32, (tq, PAIR), 1)
    vx_ref[:, :PAIR] = v_ref[...]
    vx_ref[:, PAIR:] = jnp.ones((n, PAIR), BF)
    low = lax.broadcasted_iota(jnp.int32, (tq, PAIR), 1) < HEAD_DIM
    for t in range(n // tq):
        rows = pl.ds(t * tq, tq)
        q = q_ref[rows, :]
        zero = jnp.zeros_like(q)
        outs = []
        for a in range(2):
            qa = jnp.where(low, q, zero) if a == 0 else jnp.where(low, zero, q)
            s = dot(qa, k_ref[...], NT)
            top = jnp.max(s, axis=-1, keepdims=True)
            p = jnp.exp2((s - top) * (LOG2E * HEAD_DIM**-0.5)).astype(BF)
            p_ref[a, rows, :] = p
            both = dot(p, vx_ref[...], NN)
            inv = 1.0 / both[:, PAIR:]
            outs.append((both[:, :PAIR] * inv, inv))
        o_ref[rows, :] = jnp.where(low, outs[0][0], outs[1][0]).astype(BF)
        inv_ref[rows, :] = jnp.where(lane == head, outs[0][1], jnp.where(lane == head + 1, outs[1][1], inv_ref[rows, :]))


def attend(packed):
    n, w = packed.shape
    d = w // 3
    hp = d // PAIR

    def cols(off):
        return pl.BlockSpec((n, PAIR), lambda h: (0, h + off))

    return pl.pallas_call(
        functools.partial(attend_kernel, tq=128),
        grid=(hp,),
        in_specs=[cols(0), cols(hp), cols(2 * hp)],
        out_specs=[cols(0), pl.BlockSpec((n, PAIR), lambda h: (0, 0)), pl.BlockSpec((2, n, n), lambda h: (h, 0, 0))],
        out_shape=[shape((n, d)), shape((n, PAIR), F32), shape((2 * hp, n, n))],
        scratch_shapes=[pltpu.VMEM((n, 2 * PAIR), BF)],
        compiler_params=params(),
        cost_estimate=pl.CostEstimate(flops=16 * n * n * d, bytes_accessed=4 * n * n * hp, transcendentals=0),
        name="attend",
    )(packed, packed, packed)


WHOLE = pl.BlockSpec(memory_space=pltpu.VMEM)
FAR = pl.BlockSpec(memory_space=pltpu.HBM)


def transpose_rows(block, out, cols):
    t = block.T
    d = t.shape[0]
    half = d // PIECES // 2
    for h in range(2):
        for v in range(PIECES):
            at = (2 * v + h) * half
            to = (h * PIECES + v) * half
            out[to : to + half, cols] = t[at : at + half]


def core_rows(ref, which):
    half = ref.shape[0] // 2
    return ref[pl.ds(pl.multiple_of(which * half, half), half), :]


def piece_blocks(g, ref, first):
    rows = g.shape[0] // PIECES
    for k in range(g.shape[1] // 128):
        at = (first + k) * rows
        ref[:, at : at + rows, :] = g[:, k * 128 : (k + 1) * 128].reshape(PIECES, rows, 128)


def middle_of(x_ref, mix_ref, wo_ref, vec_ref, rows):
    return x_ref[rows, :].astype(F32) + dot(mix_ref[rows, :], wo_ref[...], NN) + line(vec_ref, "ob")


def hidden_kernel(c_ref, *refs, i, head, tm, sub):
    refs = list(refs)
    take = lambda k: [refs.pop(0) for _ in range(k)]
    if head:
        x_ref, mix_ref, wo_ref, vec_ref = take(4)
    else:
        sec_ref, sec_t, up_t, o_in, ds_in = take(5)
    up_ref, w1_ref, w2_ref, b1_ref, gk_ref, gs_ref, db1_ref, o_ref, ds_ref = take(9)
    if head:
        sec_ref, sec_t, up_t = take(3)
    act, dh = take(2)
    n, d = up_ref.shape
    wide = act.shape[1]

    def shares(first, last):
        return [slice((v * CHUNKS + i) * 128, (v * CHUNKS + i + 1) * 128) for v in range(first // 128, last // 128)]

    def columns(first, last):
        return jnp.concatenate([w1_ref[:, at] for at in shares(first, last)], axis=1)

    def lines(first, last):
        return jnp.concatenate([w2_ref[at, :] for at in shares(first, last)], axis=0)

    if head:
        for t in range(n // 256):
            rows = slice(t * 256, (t + 1) * 256)
            spread, r = stats(middle_of(x_ref, mix_ref, wo_ref, vec_ref, rows))
            sec = (spread * r * line(vec_ref, "mg") + line(vec_ref, "ms")).astype(BF)
            sec_ref[rows, :] = sec
            transpose_rows(sec, sec_t, rows)
            up_t[:, rows] = up_ref[rows, :].T
    db1_ref[...] = jnp.zeros_like(db1_ref)
    for first in range(0, wide, sub):
        cols = slice(first, first + sub)
        bias = jnp.concatenate([b1_ref[v * CHUNKS + i : v * CHUNKS + i + 1, :] for v in range(first // 128, (first + sub) // 128)], axis=1)

        def tile(t, _):
            rows = pl.ds(pl.multiple_of(t * tm, tm), tm)
            h = dot(sec_ref[rows, :], columns(first, first + sub), NN) + bias
            da = dot(up_ref[rows, :], lines(first, first + sub), NT)
            cdf, pdf = normal(h)
            act[rows, cols] = (h * cdf).astype(BF)
            dhv = da * (cdf + h * pdf)
            dh[rows, cols] = dhv.astype(BF)
            db1_ref[:, cols] += jnp.sum(dhv, axis=0, keepdims=True)
            return 0

        lax.fori_loop(0, n // tm, tile, 0)
    base = PIECES * (d // PIECES // 2)
    c = c_ref[0]
    for ref, mine in ((gs_ref, 1 - c), (gk_ref, c)):
        piece_blocks(dot(core_rows(sec_t, mine), dh[...], NN).astype(BF), ref, 0)
        g = dot(core_rows(up_t, mine), act[...], NN).astype(BF)
        for k in range(wide // 128):
            ref[k, base:, :] = g[:, k * 128 : (k + 1) * 128]

    def gather(t, _):
        rows = pl.ds(pl.multiple_of(t * tm, tm), tm)
        o = dot(act[rows, :], lines(0, wide), NN)
        o_ref[rows, :] = o if head else o_in[rows, :] + o
        ds = dot(dh[rows, :], columns(0, wide), NT)
        ds_ref[rows, :] = ds if head else ds_in[rows, :] + ds
        return 0

    lax.fori_loop(0, n // tm, gather, 0)


def hidden_part(core, head, carried, up, w1, w2, b1, i, tm=512, sub=512):
    n, d = up.shape
    wide = 128 * PIECES
    assert wide * CHUNKS == w1.shape[1]
    g = (PIECES, PIECES * (d // PIECES // 2) + d // 2, 128)
    args = list(head) if head else list(carried)
    made = [shape(g), shape(g), shape((1, wide), F32), shape((n, d), F32), shape((n, d), F32)]
    if head:
        made += [shape((n, d)), shape((d, n)), shape((d, n))]
    return pl.pallas_call(
        functools.partial(hidden_kernel, i=i, head=bool(head), tm=tm, sub=sub),
        in_specs=[pl.BlockSpec(memory_space=pltpu.SMEM)] + [WHOLE] * (len(args) + 4),
        out_specs=[WHOLE] * len(made),
        out_shape=made,
        input_output_aliases={} if head else {4: 3, 5: 4},
        scratch_shapes=[pltpu.VMEM((n, wide), BF), pltpu.VMEM((n, wide), BF)],
        compiler_params=params(14),
        cost_estimate=pl.CostEstimate(flops=24 * n * d * wide, bytes_accessed=8 * d * wide, transcendentals=0),
        name="hidden",
    )(core, *args, up, w1, w2, b1)


def outer_kernel(c_ref, x_ref, up_ref, mix_ref, li_ref, wo_ref, vec_ref, o_ref, ds_ref, out_ref, dbr_ref, do_ref, gk_ref, gs_ref, sums_ref, mix_t, *, tm):
    n, d = x_ref.shape
    sums = None
    lanes = lax.broadcasted_iota(jnp.int32, (PAIR, d), 1) // HEAD_DIM
    spread_heads = (lanes == lax.broadcasted_iota(jnp.int32, (PAIR, d), 0)).astype(BF)
    for t in range(n // tm):
        rows = slice(t * tm, (t + 1) * tm)
        m = middle_of(x_ref, mix_ref, wo_ref, vec_ref, rows)
        spread, r = stats(m)
        nv = spread * r
        up = up_ref[rows, :].astype(F32)
        transpose_rows(mix_ref[rows, :], mix_t, rows)
        dy = ds_ref[rows, :]
        dyg = dy * line(vec_ref, "mg")
        dm = up + r * (dyg - jnp.mean(dyg, axis=-1, keepdims=True) - nv * jnp.mean(dyg * nv, axis=-1, keepdims=True))
        db = dm.astype(BF)
        dbr_ref[rows, :] = db
        out_ref[rows, :] = (m + o_ref[rows, :] + line(vec_ref, "rb")).astype(BF)
        li = li_ref[rows, :]
        coarse = li.astype(BF)
        fine = (li - coarse.astype(F32)).astype(BF)
        scale = dot(coarse, spread_heads, NN) + dot(fine, spread_heads, NN)
        do_ref[rows, :] = (dot(db, wo_ref[...], NT) * scale).astype(BF)
        part = [jnp.sum(v, axis=0, keepdims=True) for v in (db.astype(F32), dy * nv, dy, up)]
        sums = part if sums is None else [a + b for a, b in zip(sums, part)]
    sums_ref[...] = jnp.concatenate(sums + [jnp.zeros((4, d), F32)], axis=0)
    for ref, mine in ((gs_ref, 1 - c_ref[0]), (gk_ref, c_ref[0])):
        piece_blocks(dot(core_rows(mix_t, mine), dbr_ref[...], NN).astype(BF), ref, 0)


def outer(core, x, up, mix, li, wo, vec, o, ds, tm=256):
    n, d = x.shape
    g = (PIECES, d // 128 * (d // PIECES // 2), 128)
    return pl.pallas_call(
        functools.partial(outer_kernel, tm=tm),
        in_specs=[pl.BlockSpec(memory_space=pltpu.SMEM)] + [WHOLE] * 8,
        out_specs=[WHOLE] * 6,
        out_shape=[shape((n, d))] * 3 + [shape(g), shape(g), shape((8, d), F32)],
        scratch_shapes=[pltpu.VMEM((d, n), BF)],
        compiler_params=params(),
        cost_estimate=pl.CostEstimate(flops=24 * n * d * d, bytes_accessed=20 * n * d, transcendentals=0),
        name="outer",
    )(core, x, up, mix, li, wo, vec, o, ds)


def by_piece(g):
    rows = g.shape[0] // PIECES
    return [g[:, i : i + 128].reshape(PIECES, rows, 128) for i in range(0, g.shape[1], 128)]


def reflect_kernel(c_ref, q_ref, k_ref, v_ref, o_ref, do_ref, p_ref, ft_ref, dq_ref, dk_ref, dv_ref, gk_ref, gs_ref, ds_ref, *, tq):
    n = k_ref.shape[0]
    low = lax.broadcasted_iota(jnp.int32, (tq, PAIR), 1) < HEAD_DIM
    q_t = q_ref[...].T
    do_t = do_ref[...].T
    scale = HEAD_DIM**-0.5
    dks, dvs = [], []
    for a in range(2):
        for t in range(n // tq):
            rows = pl.ds(t * tq, tq)
            do = do_ref[rows, :]
            zero = jnp.zeros_like(do)
            doa = jnp.where(low, do, zero) if a == 0 else jnp.where(low, zero, do)
            delta = jnp.sum(doa.astype(F32) * o_ref[rows, :].astype(F32), axis=-1, keepdims=True)
            dp = dot(doa, v_ref[...], NT)
            ds = (p_ref[a, rows, :].astype(F32) * (dp - delta)).astype(BF)
            ds_ref[rows, :] = ds
            dq = (dot(ds, k_ref[...], NN) * scale).astype(BF)
            dq_ref[rows, :] = dq if a == 0 else jnp.where(low, dq_ref[rows, :], dq)
        part = slice(HEAD_DIM * a, HEAD_DIM * (a + 1))
        dvs.append(dot(do_t[part], p_ref[a], NN))
        dks.append(dot(q_t[part], ds_ref[...], NN) * scale)
    dv = jnp.concatenate(dvs, axis=0).astype(BF).T
    dk = jnp.concatenate(dks, axis=0).astype(BF).T
    dv_ref[...] = dv
    dk_ref[...] = dk
    g = dot(ft_ref[...], jnp.concatenate([dq_ref[...], dk, dv], axis=1), NN).astype(BF)
    per = g.shape[0] // PIECES
    h = pl.program_id(0)
    for step, ref in enumerate((gs_ref, gk_ref)):

        @pl.when(h == step)
        def _():
            for i, block in enumerate(by_piece(g)):
                ref[:, i * per : (i + 1) * per, :] = block


def reflect(core, packed, o, do, p, first_t, start):
    n, w = packed.shape
    d = w // 3
    hp = d // PAIR

    def which(h, c):
        return (h + 1 - c[0]) % 2

    def cols(off):
        return pl.BlockSpec((n, PAIR), lambda h, c: (0, which(h, c) + off))

    g = (PIECES, 3 * (d // PIECES), 128)
    piece = pl.BlockSpec(g, lambda h, c: (0, 0, 0), pipeline_mode=pl.Buffered(1))
    return pl.pallas_call(
        functools.partial(reflect_kernel, tq=256),
        grid_spec=pltpu.PrefetchScalarGridSpec(
            num_scalar_prefetch=1,
            grid=(2,),
            in_specs=[
                cols(start), cols(start + hp), cols(start + 2 * hp), cols(start), cols(start),
                pl.BlockSpec((2, n, n), lambda h, c: (which(h, c) + start, 0, 0)),
                pl.BlockSpec((d, n), lambda h, c: (0, 0), pipeline_mode=pl.Buffered(1)),
            ],
            out_specs=[cols(0)] * 3 + [piece] * 2,
            scratch_shapes=[pltpu.VMEM((n, n), BF)],
        ),
        out_shape=[shape((n, 2 * PAIR))] * 3 + [shape(g)] * 2,
        compiler_params=params(),
        cost_estimate=pl.CostEstimate(flops=160 * n * n * PAIR, bytes_accessed=8 * n * n, transcendentals=0),
        name="reflect",
    )(core, packed, packed, packed, o, do, p, first_t)


SMALL = 16


def back_kernel(*refs, chunks):
    x_ref, dbr_ref, w_ref, vec_in, mid_ref = refs[:5]
    db1 = refs[5 : 5 + CHUNKS]
    parts = refs[5 + CHUNKS : 5 + CHUNKS + 3 * chunks]
    tg_ref, small_ref, sums = refs[5 + CHUNKS + 3 * chunks :]

    @pl.when(pl.program_id(0) == 0)
    def _():
        sums[...] = jnp.zeros_like(sums)

    d = x_ref.shape[1]
    cw = d // chunks
    dy = None
    for i in range(3 * chunks):
        which, chunk = i % 3, i // 3
        at = which * d + chunk * cw
        part = dot(parts[i][...], w_ref[:, at : at + cw], NT)
        dy = part if dy is None else dy + part
        row = {0: 2, 2: 3}.get(which)
        if row is not None:
            sums[row : row + 1, chunk * cw : (chunk + 1) * cw] += jnp.sum(parts[i][...].astype(F32), axis=0, keepdims=True)
    spread, r = stats(x_ref[...].astype(F32))
    nv = spread * r
    dyg = dy * line(vec_in, "ag")
    dx = r * (dyg - jnp.mean(dyg, axis=-1, keepdims=True) - nv * jnp.mean(dyg * nv, axis=-1, keepdims=True))
    tg_ref[...] = (dbr_ref[...].astype(F32) + dx).astype(BF)
    sums[0:1, :] += jnp.sum(dy * nv, axis=0, keepdims=True)
    sums[1:2, :] += jnp.sum(dy, axis=0, keepdims=True)

    @pl.when(pl.program_id(0) == pl.num_programs(0) - 1)
    def _():
        per = d // PIECES
        sums[4:8, :] = mid_ref[0:4, :]
        rows = sums[...]
        for v in range(PIECES):
            vectors = jnp.concatenate([rows[:, v * per : (v + 1) * per], jnp.zeros((8, 128 - per), F32)], axis=1)
            biases = [b[:, v * 128 : (v + 1) * 128] for b in db1]
            piece = jnp.concatenate([vectors] + biases + [jnp.zeros((SMALL - 8 - CHUNKS, 128), F32)], axis=0)
            small_ref[v * SMALL : (v + 1) * SMALL, :] = piece.astype(BF)


def project_back(x, dbr, w, vec, mids, db1, parts):
    n, d = x.shape
    tm = 256
    row = pl.BlockSpec((tm, d), lambda i: (i, 0))

    def full(*s):
        return pl.BlockSpec(s, lambda i: (0, 0), pipeline_mode=pl.Buffered(1))

    chunks = len(parts) // 3
    return pl.pallas_call(
        functools.partial(back_kernel, chunks=chunks),
        grid=(n // tm,),
        in_specs=[row, row, full(d, 3 * d), full(*vec.shape), full(*mids.shape)]
        + [full(*b.shape) for b in db1]
        + [pl.BlockSpec((tm, d // chunks), lambda i: (i, 0))] * (3 * chunks),
        out_specs=[row, full(PIECES * SMALL, 128)],
        out_shape=[shape((n, d)), shape((PIECES * SMALL, 128))],
        scratch_shapes=[pltpu.VMEM((8, d), F32)],
        compiler_params=params(),
        cost_estimate=pl.CostEstimate(flops=12 * n * d * d, bytes_accessed=16 * n * d, transcendentals=0),
        name="project_back",
    )(x, dbr, w, vec, mids, *db1, *parts)


def exchange(x, axis, by):
    count = lax.axis_size(axis)
    return lax.ppermute(x, axis, [(i, i ^ by) for i in range(count)])


def to_core(g):
    return exchange(g, "seq", 1)


def pick(x, index, axis=0):
    return lax.dynamic_index_in_dim(x, index, axis, keepdims=False)


def after(x, *others):
    return lax.optimization_barrier((x,) + others)[0]


class Part:
    def __init__(self, held, received, rows):
        self.held = (held.reshape(-1, 128), 0)
        self.received = (received.reshape(-1, 128), 0)
        self.rows = rows
        self.open = [0, 1, 2]

    def count(self):
        return self.rows << len(self.open)


def slot_kernel(ids_ref, *refs, items, inputs):
    ins, outs = refs[:inputs], refs[inputs:]

    def read(term, at, count):
        ref, offset = term
        return ins[ref][pl.ds(at + offset, count), :].astype(F32)

    step = 16
    for kind, *rest in items:
        if kind == "split":
            held, received, groups, size, bit, (send, to), keep = rest
            mine = ids_ref[bit]
            for a in range(groups):
                own = pl.multiple_of((2 * a + mine) * size, step)
                other = pl.multiple_of((2 * a + 1 - mine) * size, step)
                outs[send][to + a * size : to + (a + 1) * size, :] = (read(held, other, size) + read(received, other, size)).astype(BF)
                outs[keep][a * size : (a + 1) * size, :] = (read(held, own, size) + read(received, own, size)).astype(BF)
        elif kind == "sum":
            held, received, size, (send, to) = rest
            outs[send][to : to + size, :] = (read(held, 0, size) + read(received, 0, size)).astype(BF)
        else:
            first, second, size, bit, (send, to), keep = rest
            for mine in (0, 1):

                @pl.when(ids_ref[bit] == mine)
                def _():
                    own, other = (first, second) if mine == 0 else (second, first)
                    outs[send][to : to + size, :] = (read(other[0], 0, size) + read(other[1], 0, size)).astype(BF)
                    outs[keep][...] = (read(own[0], 0, size) + read(own[1], 0, size)).astype(BF)


def slot(ids, exchanges, *tokens):
    arrays, items, sizes, moves = [], [], [], []

    def use(term):
        for i, a in enumerate(arrays):
            if a is term[0]:
                return i, term[1]
        arrays.append(term[0])
        return len(arrays) - 1, term[1]

    for stage, parts in exchanges:
        send, to = len(sizes), 0
        sizes.append(0)
        placed = []
        if stage == "pick":
            one, two = parts
            size = one.count()
            items.append(("pick", (use(one.held), use(one.received)), (use(two.held), use(two.received)), size, 1, (send, 0), len(sizes)))
            placed.append((one, len(sizes), 0, 0))
            sizes.append(size)
            to = size
        else:
            for p in parts:
                held, received = use(p.held), use(p.received)
                if stage == "x":
                    items.append(("sum", held, received, p.count(), (send, to)))
                    placed.append((p, send, to, to))
                    to += p.count()
                    continue
                if stage == "half":
                    groups, bit = 1 << len(p.open), 1
                else:
                    groups, bit = 1 << (len(p.open) - 1 - p.open.index(stage)), 2 + stage
                size = p.count() // (2 * groups)
                items.append(("split", held, received, groups, size, bit, (send, to), len(sizes)))
                placed.append((p, len(sizes), 0, to))
                sizes.append(groups * size)
                to += groups * size
                if stage == "half":
                    p.rows //= 2
                else:
                    p.open.remove(stage)
        sizes[send] = to
        moves.append((stage, send, placed))

    if tokens:
        arrays = list(lax.optimization_barrier(tuple(arrays) + tokens)[: len(arrays)])
    whole = pl.BlockSpec(memory_space=pltpu.VMEM)
    outs = pl.pallas_call(
        functools.partial(slot_kernel, items=items, inputs=len(arrays)),
        in_specs=[pl.BlockSpec(memory_space=pltpu.SMEM)] + [whole] * len(arrays),
        out_specs=[whole] * len(sizes),
        out_shape=[shape((size, 128)) for size in sizes],
        compiler_params=params(),
        cost_estimate=pl.CostEstimate(flops=0, bytes_accessed=512 * sum(sizes), transcendentals=0),
        name="slot",
    )(ids, *arrays)
    unit = lax.axis_size("vol") // PIECES
    sent, received = [], []
    for stage, send, placed in moves:
        if stage in ("half", "pick", "x"):
            got = exchange(outs[send], "seq", 2)
        else:
            got = exchange(outs[send], "vol", unit << stage)
        sent.append(outs[send])
        received.append(got)
        for p, keep, at, to in placed:
            p.held = (outs[keep], at)
            p.received = (got, to)
    return sent, received


def home_kernel(ids_ref, live_ref, *refs, mask):
    out_ref = refs[-1]
    for k, ref in enumerate(refs[:-1]):

        @pl.when(pl.program_id(0) == k)
        def _():
            value = ref[...].astype(F32)
            if mask:
                value = value * live_ref[ids_ref[5] ^ k]
            out_ref[...] = value.astype(out_ref.dtype)


def send_home(ids, live, own, others, slices, dtype, mask):
    rows, d = others[0].shape
    return pl.pallas_call(
        functools.partial(home_kernel, mask=mask),
        grid_spec=pltpu.PrefetchScalarGridSpec(
            num_scalar_prefetch=2,
            grid=(slices,),
            in_specs=[pl.BlockSpec((rows, d), lambda k, i, l: (0, 0), pipeline_mode=pl.Buffered(1))] * slices,
            out_specs=pl.BlockSpec((None, rows, d), lambda k, i, l: (k ^ i[5], 0, 0)),
        ),
        out_shape=shape((slices, rows, d), dtype),
        compiler_params=params(),
        cost_estimate=pl.CostEstimate(flops=0, bytes_accessed=6 * slices * rows * d, transcendentals=0),
        name="home",
    )(ids, live, own, *others)


def assemble_ff_kernel(ids_ref, *refs, per):
    ga, gb, gc = refs[:4], refs[4:8], refs[8:12]
    expand_ref, reduce_ref = refs[12:]
    c = ids_ref[0]

    def first_layer(i, core, value):
        size = per // 2
        for k in range(PIECES):
            at = (k * CHUNKS + i) * 128
            expand_ref[pl.ds(pl.multiple_of(core * size, size), size), at : at + 128] = value[k * size : (k + 1) * size, :]

    def second_layer(i, core, value):
        d = value.shape[0]
        reduce_ref[i * 128 : (i + 1) * 128, pl.ds(pl.multiple_of(core * d, 128), d)] = value.T

    half = per * (PIECES // 2)
    for core, (mine, other) in ((c, (ga[0], ga[1])), (1 - c, (ga[2], ga[3]))):

        @pl.when(ids_ref[1] == 0)
        def _():
            first_layer(0, core, mine[...].astype(F32))
            second_layer(0, core, other[...].astype(F32))

        @pl.when(ids_ref[1] == 1)
        def _():
            first_layer(0, core, other[...].astype(F32))
            second_layer(0, core, mine[...].astype(F32))

    for i, refs_i in ((1, gb), (2, gc)):
        for core, (one, two) in ((c, refs_i[:2]), (1 - c, refs_i[2:])):
            total = one[...].astype(F32) + two[...].astype(F32)
            first_layer(i, core, total[:half])
            second_layer(i, core, total[half:])


def assemble_end_kernel(ids_ref, *refs, per):
    mine, theirs = refs[:4], refs[4:8]
    small_held, small_received, output_ref, input_ref, vector_ref = refs[8:]
    c = ids_ref[0]
    d = PIECES * per

    def output_part(core, value):
        size = per // 2
        for k in range(d // 128):
            rows = pl.ds(pl.multiple_of(core * size, size), size)
            output_ref[rows, k * 128 : (k + 1) * 128] = value[k * size : (k + 1) * size, :]

    def pair_part(i, core, value):
        for k in range(3):
            at = pl.multiple_of(k * d + (2 * i + core) * 128, 128)
            input_ref[:, pl.ds(at, 128)] = value[k * per : (k + 1) * per, :]

    for core, (own, other, one, two) in ((c, mine), (1 - c, theirs)):

        @pl.when(ids_ref[1] == 0)
        def _():
            output_part(core, own[...].astype(F32))
            pair_part(0, core, other[...].astype(F32))

        @pl.when(ids_ref[1] == 1)
        def _():
            output_part(core, other[...].astype(F32))
            pair_part(0, core, own[...].astype(F32))

        total = one[...].astype(F32) + two[...].astype(F32)
        for i in (1, 2):
            pair_part(i, core, total[(i - 1) * 3 * per : i * 3 * per])
    vector_ref[...] = small_held[...].astype(F32) + small_received[...].astype(F32)


def assemble(kernel, ids, per, arrays, outs, name):
    whole = pl.BlockSpec(memory_space=pltpu.VMEM)
    return pl.pallas_call(
        functools.partial(kernel, per=per),
        in_specs=[pl.BlockSpec(memory_space=pltpu.SMEM)] + [whole] * len(arrays),
        out_specs=[whole] * len(outs),
        out_shape=[shape(o, F32) for o in outs],
        compiler_params=params(),
        name=name,
    )(ids, *arrays)


def on_device(
    volume_slices, volume_owner, tokens, cotangent, attend_gain, attend_shift, input_weight, query_bias, value_bias,
    output_weight, output_bias, mixer_gain, mixer_shift, expand_weight, expand_bias, reduce_weight, reduce_bias,
):
    slices, rows, d = tokens.shape
    ff = expand_weight.shape[1]
    nv = lax.axis_size("vol")
    peers = lax.axis_size("seq")
    me = lax.axis_index("seq")
    core_id = me % 2
    x_id = (me // 2) % 2
    core = core_id.astype(jnp.int32).reshape(1)
    n = rows * peers
    vol = lax.axis_index("vol")
    unit = nv // PIECES
    ids = jnp.stack([core_id, x_id, (vol // unit) % 2, (vol // (2 * unit)) % 2, (vol // (4 * unit)) % 2, me]).astype(jnp.int32)

    def from_peers(x, ks):
        parts = [pick(x, me ^ k) for k in ks]
        return [p if k == 0 else exchange(p, "seq", k) for p, k in zip(parts, ks)]

    far_parts = from_peers(tokens, (3, 2))
    near_parts = from_peers(tokens, (0, 1))
    zero = jnp.zeros((d,), BF)
    vec = jnp.concatenate(
        [attend_gain, attend_shift, query_bias, zero, value_bias, output_bias, mixer_gain, mixer_shift, reduce_bias] + [zero] * 7
    ).astype(F32).reshape(16, d)
    wide = ff // CHUNKS
    lanes = wide // PIECES
    b1 = expand_bias.astype(F32).reshape(ff // 128, 128)
    load = jnp.sum(jnp.where(volume_owner == lax.axis_index("vol"), volume_slices, 0))
    live = (jnp.arange(slices) < load).astype(BF)

    made = project_in(jnp.concatenate(near_parts), 0, n, None, vec, input_weight)
    far = jnp.concatenate([after(far_parts[1], made[2], b1, live), far_parts[0]])
    x, first_t, packed = project_in(far, 2 * rows, n, made, vec, input_weight)
    upstream = jnp.concatenate(from_peers(after(cotangent, far_parts[0], made[2]) * live[:, None, None], (0, 1, 2, 3)))

    mixed, inverse, weights = attend(packed)

    db1 = []

    def hidden(token, head, carried, i):
        gk, gs, b, *made = hidden_part(token, head, carried, upstream, expand_weight, reduce_weight, b1, i)
        db1.append(b)
        return gk, gs, made

    Y, Z1, Z2 = 0, 1, 2
    piece_rows = d // 2 + d // 2
    pair_rows = 3 * (d // PIECES)
    k0, s0, (o, ds, *kept) = hidden(core, (x, mixed, output_weight, vec), None, 0)
    r0 = to_core(s0)
    k1, s1, (o, ds) = hidden(after(core, s0), None, (*kept, o, ds), 1)
    r1 = to_core(s1)
    ga = Part(k0, r0, piece_rows)
    sent, _ = slot(ids, [("half", [ga])], s1)
    k2, s2, (o, ds) = hidden(after(core, s1, *sent), None, (*kept, o, ds), 2)
    r2 = to_core(s2)
    gb = Part(k1, r1, piece_rows)
    sent, _ = slot(ids, [(Z1, [gb])], s2)
    out, d_branch, d_mixed, k3, s3, sums_mid = outer(
        after(core, s2, *sent), x, upstream, mixed, inverse, output_weight, vec, o, ds
    )
    r3 = to_core(s3)

    def homeward(a):
        blocks = [a[k * rows : (k + 1) * rows] for k in range(1, peers)]
        return blocks, [exchange(b, "seq", k + 1) for k, b in enumerate(blocks)]

    out_sent, outs = homeward(out)
    gc = Part(k2, r2, piece_rows)
    sent, got = slot(ids, [(Y, [gc]), (Z2, [gb])], s3)
    parts = []

    def reflect_part(token, i):
        dq, dk, dv, gk, gs = reflect(token, packed, mixed, d_mixed, weights, first_t, 2 * i)
        parts.extend([dq, dk, dv])
        return gk, gs

    p0, q0 = reflect_part(after(core, s3, *sent, *out_sent), 0)
    t0 = to_core(q0)
    wait_c = got[0]
    sent, _ = slot(ids, [(Y, [ga, gb])], q0)
    p1, q1 = reflect_part(after(core, q0, wait_c, *sent, *outs), 1)
    t1 = to_core(q1)
    gd, gd2 = Part(k3, r3, pair_rows), Part(p0, t0, pair_rows)
    sent, _ = slot(ids, [(Z1, [ga, gc]), ("pick", [gd, gd2])], q1)
    p2, q2 = reflect_part(after(core, q1, *sent), 2)
    t2 = to_core(q2)
    ge1 = Part(p1, t1, pair_rows)
    sent, late_got = slot(ids, [(Y, [ge1, gd]), (Z2, [ga, gc])], q2)
    d_tokens, small = project_back(after(x, *sent), d_branch, input_weight, vec, sums_mid, db1, parts)

    tg_sent, tgs = homeward(d_tokens)
    ge2 = Part(p2, t2, pair_rows)
    gv = Part(small, to_core(small), SMALL)
    sent1, got1 = slot(ids, [(Y, [ge2, gv])], small, *tg_sent, late_got[1])
    block_out = send_home(ids, live, out, [after(o, *sent1) for o in outs], slices, BF, True)
    sent2, got2 = slot(ids, [(Z1, [ge1, ge2, gd, gv])], *got1, block_out, tgs[1])
    per = d // PIECES

    def both_terms(p, *tokens):
        pieces = [lax.slice_in_dim(a, at, at + p.count()) for a, at in (p.held, p.received)]
        pieces = list(lax.optimization_barrier(tuple(pieces) + tokens)[:2])
        return pieces + [to_core(a) for a in pieces]

    spare = [1 << i for i in range(unit.bit_length() - 1)]
    sent3, got3 = slot(ids, [(Z2, [ge1, ge2, gd, gv]), ("x", [ga, gb, gc])], *got2, *tgs)
    tgs = [after(t, *sent3) for t in tgs]
    tokens_grad = send_home(ids, live, d_tokens, tgs, slices, F32, False)
    sent4, got4 = slot(ids, [("x", [ge1, ge2, gd, gv])], *got3, tokens_grad)
    ff_terms = both_terms(ga, *sent4) + both_terms(gb, *sent4) + both_terms(gc, *sent4)
    expand_grad, reduce_grad = assemble(assemble_ff_kernel, ids, per, ff_terms, [(per, ff), (ff // PIECES, d)], "assemble_ff")
    at = 2 * pair_rows
    held, received = sent4[0], got4[0]
    ends = [held[at : at + pair_rows], received[at : at + pair_rows], held[:at], received[:at]]
    ends = ends + [to_core(a) for a in ends]
    at += pair_rows
    output_grad, input_grad, vectors = assemble(
        assemble_end_kernel, ids, per, ends + [held[at:], received[at:]], [(per, d), (per, 3 * d), (SMALL, 128)], "assemble_end"
    )
    bias_rows = vectors[8 : 8 + CHUNKS]
    vectors = vectors[:8, :per]
    if unit > 1:
        sub = vol % unit

        def add_rest(a):
            for by in spare:
                a = a + exchange(a, "vol", by)
            return a

        def cut(a, axis):
            size = a.shape[axis] // unit
            return lax.dynamic_slice_in_dim(add_rest(a), sub * size, size, axis)

        expand_grad, reduce_grad, output_grad, input_grad = [cut(a, 0) for a in (expand_grad, reduce_grad, output_grad, input_grad)]
        expand_bias_grad = cut(bias_rows.reshape(-1), 0)
        vectors = cut(vectors, 1)
    else:
        expand_bias_grad = bias_rows.reshape(-1)
    return (
        block_out, tokens_grad, vectors[0], vectors[1], input_grad, vectors[2], vectors[3], output_grad, vectors[4],
        vectors[5], vectors[6], expand_grad, expand_bias_grad, reduce_grad, vectors[7],
    )


def solution(mesh):
    rows = P("vol", "seq", None)
    return jax.shard_map(
        on_device,
        mesh=mesh,
        in_specs=(P(), P(), rows, rows) + (P(),) * 13,
        out_specs=(rows, rows, P("vol"), P("vol"), P("vol", None), P("vol"), P("vol"), P("vol", None), P("vol"), P("vol"),
                   P("vol"), P("vol", None), P("vol"), P("vol", None), P("vol")),
        check_vma=False,
    )
```

```python
import functools

import jax
import jax.numpy as jnp
from jax import lax
from jax.experimental import pallas as pl
from jax.experimental.pallas import tpu as pltpu
from jax.sharding import PartitionSpec as P

HEAD_DIM = 64
PAIR = 2 * HEAD_DIM
LOG2E = 1.4426950408889634
PIECES = 8
CHUNKS = 3
ROW = {n: i for i, n in enumerate(("ag", "ash", "qb", "zero", "vb", "ob", "mg", "ms", "rb"))}
BF = jnp.bfloat16
F32 = jnp.float32
NN = (((1,), (0,)), ((), ()))
NT = (((1,), (1,)), ((), ()))

def dot(a, b, dims):
    return lax.dot_general(a, b, dims, preferred_element_type=F32)


def params(mib=24):
    return pltpu.CompilerParams(vmem_limit_bytes=mib << 20)


def line(ref, name):
    return ref[ROW[name] : ROW[name] + 1, :]


def shape(dims, dtype=BF):
    return jax.ShapeDtypeStruct(dims, dtype)


def normal(h):
    return 0.5 + 0.5 * lax.erf(h * 0.5**0.5), jnp.exp2(h * h * (-0.5 * LOG2E)) * 0.3989422804014327


def stats(v):
    spread = v - jnp.mean(v, axis=-1, keepdims=True)
    return spread, lax.rsqrt(jnp.mean(spread * spread, axis=-1, keepdims=True) + 1e-6)


def in_kernel(x_ref, vec_ref, w_ref, *rest):
    x_out, first_t, packed = rest[-3:]
    x = x_ref[...]
    d = x.shape[1]
    spread, r = stats(x.astype(F32))
    f = (spread * r * line(vec_ref, "ag") + line(vec_ref, "ash")).astype(BF)
    x_out[...] = x
    for i, bias in enumerate(("qb", "zero", "vb")):
        packed[:, i * d : (i + 1) * d] = (dot(f, w_ref[:, i * d : (i + 1) * d], NN) + line(vec_ref, bias)).astype(BF)
    first_t[...] = f.T


def project_in(part, offset, total, before, vec, weight):
    rows, d = part.shape
    wide = weight.shape[1]
    tm = 256
    first_block = offset // tm

    def full(a):
        return pl.BlockSpec(a.shape, lambda i: (0, 0), pipeline_mode=pl.Buffered(1))

    in_specs = [pl.BlockSpec((tm, d), lambda i: (i, 0)), full(vec), full(weight)]
    args = [part, vec, weight]
    aliases = {}
    if before is not None:
        aliases = {3: 0, 4: 1, 5: 2}
        in_specs += [pl.BlockSpec(memory_space=pl.ANY)] * 3
        args += list(before)
    return pl.pallas_call(
        in_kernel,
        grid=(rows // tm,),
        in_specs=in_specs,
        out_specs=[
            pl.BlockSpec((tm, d), lambda i: (i + first_block, 0)),
            pl.BlockSpec((d, tm), lambda i: (0, i + first_block)),
            pl.BlockSpec((tm, wide), lambda i: (i + first_block, 0)),
        ],
        out_shape=[shape((total, d)), shape((d, total)), shape((total, wide))],
        input_output_aliases=aliases,
        compiler_params=params(24),
        cost_estimate=pl.CostEstimate(flops=6 * rows * d * wide, bytes_accessed=2 * (d * wide + rows * (wide + 3 * d)), transcendentals=0),
        name="project_in",
    )(*args)


def attend_kernel(q_ref, k_ref, v_ref, o_ref, inv_ref, p_ref, vx_ref, *, tq):
    n = k_ref.shape[0]
    head = 2 * pl.program_id(0)
    lane = lax.broadcasted_iota(jnp.int32, (tq, PAIR), 1)
    vx_ref[:, :PAIR] = v_ref[...]
    vx_ref[:, PAIR:] = jnp.ones((n, PAIR), BF)
    low = lax.broadcasted_iota(jnp.int32, (tq, PAIR), 1) < HEAD_DIM
    for t in range(n // tq):
        rows = pl.ds(t * tq, tq)
        q = q_ref[rows, :]
        zero = jnp.zeros_like(q)
        outs = []
        for a in range(2):
            qa = jnp.where(low, q, zero) if a == 0 else jnp.where(low, zero, q)
            s = dot(qa, k_ref[...], NT)
            top = jnp.max(s, axis=-1, keepdims=True)
            p = jnp.exp2((s - top) * (LOG2E * HEAD_DIM**-0.5)).astype(BF)
            p_ref[a, rows, :] = p
            both = dot(p, vx_ref[...], NN)
            inv = 1.0 / both[:, PAIR:]
            outs.append((both[:, :PAIR] * inv, inv))
        o_ref[rows, :] = jnp.where(low, outs[0][0], outs[1][0]).astype(BF)
        inv_ref[rows, :] = jnp.where(lane == head, outs[0][1], jnp.where(lane == head + 1, outs[1][1], inv_ref[rows, :]))


def attend(packed):
    n, w = packed.shape
    d = w // 3
    hp = d // PAIR

    def cols(off):
        return pl.BlockSpec((n, PAIR), lambda h: (0, h + off))

    return pl.pallas_call(
        functools.partial(attend_kernel, tq=128),
        grid=(hp,),
        in_specs=[cols(0), cols(hp), cols(2 * hp)],
        out_specs=[cols(0), pl.BlockSpec((n, PAIR), lambda h: (0, 0)), pl.BlockSpec((2, n, n), lambda h: (h, 0, 0))],
        out_shape=[shape((n, d)), shape((n, PAIR), F32), shape((2 * hp, n, n))],
        scratch_shapes=[pltpu.VMEM((n, 2 * PAIR), BF)],
        compiler_params=params(40),
        cost_estimate=pl.CostEstimate(flops=16 * n * n * d, bytes_accessed=4 * n * n * hp, transcendentals=0),
        name="attend",
    )(packed, packed, packed)


WHOLE = pl.BlockSpec(memory_space=pltpu.VMEM)
FAR = pl.BlockSpec(memory_space=pltpu.HBM)


def transpose_rows(block, out, cols):
    t = block.T
    d = t.shape[0]
    half = d // PIECES // 2
    for h in range(2):
        for v in range(PIECES):
            at = (2 * v + h) * half
            to = (h * PIECES + v) * half
            out[to : to + half, cols] = t[at : at + half]


def core_rows(ref, which):
    half = ref.shape[0] // 2
    return ref[pl.ds(pl.multiple_of(which * half, half), half), :]


def piece_blocks(g, ref, first):
    rows = g.shape[0] // PIECES
    for k in range(g.shape[1] // 128):
        at = (first + k) * rows
        ref[:, at : at + rows, :] = g[:, k * 128 : (k + 1) * 128].reshape(PIECES, rows, 128)


def middle_of(x_ref, mix_ref, wo_ref, vec_ref, rows):
    return x_ref[rows, :].astype(F32) + dot(mix_ref[rows, :], wo_ref[...], NN) + line(vec_ref, "ob")


def hidden_kernel(c_ref, *refs, i, head, tm, sub):
    refs = list(refs)
    take = lambda k: [refs.pop(0) for _ in range(k)]
    if head:
        x_ref, mix_ref, wo_ref, vec_ref = take(4)
    else:
        sec_ref, sec_t, up_t, o_in, ds_in = take(5)
    up_ref, w1_ref, w2_ref, b1_ref, gk_ref, gs_ref, db1_ref, o_ref, ds_ref = take(9)
    if head:
        sec_ref, sec_t, up_t = take(3)
    act, dh = take(2)
    n, d = up_ref.shape
    wide = act.shape[1]

    def shares(first, last):
        return [slice((v * CHUNKS + i) * 128, (v * CHUNKS + i + 1) * 128) for v in range(first // 128, last // 128)]

    def columns(first, last):
        return jnp.concatenate([w1_ref[:, at] for at in shares(first, last)], axis=1)

    def lines(first, last):
        return jnp.concatenate([w2_ref[at, :] for at in shares(first, last)], axis=0)

    if head:
        for t in range(n // 256):
            rows = slice(t * 256, (t + 1) * 256)
            spread, r = stats(middle_of(x_ref, mix_ref, wo_ref, vec_ref, rows))
            sec = (spread * r * line(vec_ref, "mg") + line(vec_ref, "ms")).astype(BF)
            sec_ref[rows, :] = sec
            transpose_rows(sec, sec_t, rows)
            up_t[:, rows] = up_ref[rows, :].T
    db1_ref[...] = jnp.zeros_like(db1_ref)
    for first in range(0, wide, sub):
        cols = slice(first, first + sub)
        bias = jnp.concatenate([b1_ref[v * CHUNKS + i : v * CHUNKS + i + 1, :] for v in range(first // 128, (first + sub) // 128)], axis=1)

        def tile(t, _):
            rows = pl.ds(pl.multiple_of(t * tm, tm), tm)
            h = dot(sec_ref[rows, :], columns(first, first + sub), NN) + bias
            da = dot(up_ref[rows, :], lines(first, first + sub), NT)
            cdf, pdf = normal(h)
            act[rows, cols] = (h * cdf).astype(BF)
            dhv = da * (cdf + h * pdf)
            dh[rows, cols] = dhv.astype(BF)
            db1_ref[:, cols] += jnp.sum(dhv, axis=0, keepdims=True)
            return 0

        lax.fori_loop(0, n // tm, tile, 0)
    base = PIECES * (d // PIECES // 2)
    c = c_ref[0]
    for ref, mine in ((gs_ref, 1 - c), (gk_ref, c)):
        piece_blocks(dot(core_rows(sec_t, mine), dh[...], NN).astype(BF), ref, 0)
        g = dot(core_rows(up_t, mine), act[...], NN).astype(BF)
        for k in range(wide // 128):
            ref[k, base:, :] = g[:, k * 128 : (k + 1) * 128]

    def gather(t, _):
        rows = pl.ds(pl.multiple_of(t * tm, tm), tm)
        o = dot(act[rows, :], lines(0, wide), NN)
        o_ref[rows, :] = o if head else o_in[rows, :] + o
        ds = dot(dh[rows, :], columns(0, wide), NT)
        ds_ref[rows, :] = ds if head else ds_in[rows, :] + ds
        return 0

    lax.fori_loop(0, n // tm, gather, 0)


def hidden_part(core, head, carried, up, w1, w2, b1, i, tm=512, sub=512):
    n, d = up.shape
    wide = 128 * PIECES
    assert wide * CHUNKS == w1.shape[1]
    g = (PIECES, PIECES * (d // PIECES // 2) + d // 2, 128)
    args = list(head) if head else list(carried)
    made = [shape(g), shape(g), shape((1, wide), F32), shape((n, d), F32), shape((n, d), F32)]
    if head:
        made += [shape((n, d)), shape((d, n)), shape((d, n))]
    return pl.pallas_call(
        functools.partial(hidden_kernel, i=i, head=bool(head), tm=tm, sub=sub),
        in_specs=[pl.BlockSpec(memory_space=pltpu.SMEM)] + [WHOLE] * (len(args) + 4),
        out_specs=[WHOLE] * len(made),
        out_shape=made,
        input_output_aliases={} if head else {4: 3, 5: 4},
        scratch_shapes=[pltpu.VMEM((n, wide), BF), pltpu.VMEM((n, wide), BF)],
        compiler_params=params(12),
        cost_estimate=pl.CostEstimate(flops=24 * n * d * wide, bytes_accessed=8 * d * wide, transcendentals=0),
        name="hidden",
    )(core, *args, up, w1, w2, b1)


def outer_kernel(c_ref, x_ref, up_ref, mix_ref, li_ref, wo_ref, vec_ref, o_ref, ds_ref, out_ref, dbr_ref, do_ref, gk_ref, gs_ref, sums_ref, mix_t, *, tm):
    n, d = x_ref.shape
    sums = None
    lanes = lax.broadcasted_iota(jnp.int32, (PAIR, d), 1) // HEAD_DIM
    spread_heads = (lanes == lax.broadcasted_iota(jnp.int32, (PAIR, d), 0)).astype(BF)
    for t in range(n // tm):
        rows = slice(t * tm, (t + 1) * tm)
        m = middle_of(x_ref, mix_ref, wo_ref, vec_ref, rows)
        spread, r = stats(m)
        nv = spread * r
        up = up_ref[rows, :].astype(F32)
        transpose_rows(mix_ref[rows, :], mix_t, rows)
        dy = ds_ref[rows, :]
        dyg = dy * line(vec_ref, "mg")
        dm = up + r * (dyg - jnp.mean(dyg, axis=-1, keepdims=True) - nv * jnp.mean(dyg * nv, axis=-1, keepdims=True))
        db = dm.astype(BF)
        dbr_ref[rows, :] = db
        out_ref[rows, :] = (m + o_ref[rows, :] + line(vec_ref, "rb")).astype(BF)
        li = li_ref[rows, :]
        coarse = li.astype(BF)
        fine = (li - coarse.astype(F32)).astype(BF)
        scale = dot(coarse, spread_heads, NN) + dot(fine, spread_heads, NN)
        do_ref[rows, :] = (dot(db, wo_ref[...], NT) * scale).astype(BF)
        part = [jnp.sum(v, axis=0, keepdims=True) for v in (db.astype(F32), dy * nv, dy, up)]
        sums = part if sums is None else [a + b for a, b in zip(sums, part)]
    sums_ref[...] = jnp.concatenate(sums + [jnp.zeros((4, d), F32)], axis=0)
    for ref, mine in ((gs_ref, 1 - c_ref[0]), (gk_ref, c_ref[0])):
        piece_blocks(dot(core_rows(mix_t, mine), dbr_ref[...], NN).astype(BF), ref, 0)


def outer(core, x, up, mix, li, wo, vec, o, ds, tm=256):
    n, d = x.shape
    g = (PIECES, d // 128 * (d // PIECES // 2), 128)
    return pl.pallas_call(
        functools.partial(outer_kernel, tm=tm),
        in_specs=[pl.BlockSpec(memory_space=pltpu.SMEM)] + [WHOLE] * 8,
        out_specs=[WHOLE] * 6,
        out_shape=[shape((n, d))] * 3 + [shape(g), shape(g), shape((8, d), F32)],
        scratch_shapes=[pltpu.VMEM((d, n), BF)],
        compiler_params=params(8),
        cost_estimate=pl.CostEstimate(flops=24 * n * d * d, bytes_accessed=20 * n * d, transcendentals=0),
        name="outer",
    )(core, x, up, mix, li, wo, vec, o, ds)


def by_piece(g):
    rows = g.shape[0] // PIECES
    return [g[:, i : i + 128].reshape(PIECES, rows, 128) for i in range(0, g.shape[1], 128)]


def reflect_kernel(c_ref, q_ref, k_ref, v_ref, o_ref, do_ref, p_ref, ft_ref, dq_ref, dk_ref, dv_ref, gk_ref, gs_ref, ds_ref, *, tq):
    n = k_ref.shape[0]
    low = lax.broadcasted_iota(jnp.int32, (tq, PAIR), 1) < HEAD_DIM
    q_t = q_ref[...].T
    do_t = do_ref[...].T
    scale = HEAD_DIM**-0.5
    dks, dvs = [], []
    for a in range(2):
        for t in range(n // tq):
            rows = pl.ds(t * tq, tq)
            do = do_ref[rows, :]
            zero = jnp.zeros_like(do)
            doa = jnp.where(low, do, zero) if a == 0 else jnp.where(low, zero, do)
            delta = jnp.sum(doa.astype(F32) * o_ref[rows, :].astype(F32), axis=-1, keepdims=True)
            dp = dot(doa, v_ref[...], NT)
            ds = (p_ref[a, rows, :].astype(F32) * (dp - delta)).astype(BF)
            ds_ref[rows, :] = ds
            dq = (dot(ds, k_ref[...], NN) * scale).astype(BF)
            dq_ref[rows, :] = dq if a == 0 else jnp.where(low, dq_ref[rows, :], dq)
        part = slice(HEAD_DIM * a, HEAD_DIM * (a + 1))
        dvs.append(dot(do_t[part], p_ref[a], NN))
        dks.append(dot(q_t[part], ds_ref[...], NN) * scale)
    dv = jnp.concatenate(dvs, axis=0).astype(BF).T
    dk = jnp.concatenate(dks, axis=0).astype(BF).T
    dv_ref[...] = dv
    dk_ref[...] = dk
    g = dot(ft_ref[...], jnp.concatenate([dq_ref[...], dk, dv], axis=1), NN).astype(BF)
    per = g.shape[0] // PIECES
    h = pl.program_id(0)
    for step, ref in enumerate((gs_ref, gk_ref)):

        @pl.when(h == step)
        def _():
            for i, block in enumerate(by_piece(g)):
                ref[:, i * per : (i + 1) * per, :] = block


def reflect(core, packed, o, do, p, first_t, start):
    n, w = packed.shape
    d = w // 3
    hp = d // PAIR

    def which(h, c):
        return (h + 1 - c[0]) % 2

    def cols(off):
        return pl.BlockSpec((n, PAIR), lambda h, c: (0, which(h, c) + off))

    g = (PIECES, 3 * (d // PIECES), 128)
    piece = pl.BlockSpec(g, lambda h, c: (0, 0, 0), pipeline_mode=pl.Buffered(1))
    return pl.pallas_call(
        functools.partial(reflect_kernel, tq=256),
        grid_spec=pltpu.PrefetchScalarGridSpec(
            num_scalar_prefetch=1,
            grid=(2,),
            in_specs=[
                cols(start), cols(start + hp), cols(start + 2 * hp), cols(start), cols(start),
                pl.BlockSpec((2, n, n), lambda h, c: (which(h, c) + start, 0, 0)),
                pl.BlockSpec((d, n), lambda h, c: (0, 0), pipeline_mode=pl.Buffered(1)),
            ],
            out_specs=[cols(0)] * 3 + [piece] * 2,
            scratch_shapes=[pltpu.VMEM((n, n), BF)],
        ),
        out_shape=[shape((n, 2 * PAIR))] * 3 + [shape(g)] * 2,
        compiler_params=params(30),
        cost_estimate=pl.CostEstimate(flops=160 * n * n * PAIR, bytes_accessed=8 * n * n, transcendentals=0),
        name="reflect",
    )(core, packed, packed, packed, o, do, p, first_t)


SMALL = 16


def back_kernel(*refs, chunks):
    x_ref, dbr_ref, w_ref, vec_in, mid_ref = refs[:5]
    db1 = refs[5 : 5 + CHUNKS]
    parts = refs[5 + CHUNKS : 5 + CHUNKS + 3 * chunks]
    tg_ref, small_ref, sums = refs[5 + CHUNKS + 3 * chunks :]

    @pl.when(pl.program_id(0) == 0)
    def _():
        sums[...] = jnp.zeros_like(sums)

    d = x_ref.shape[1]
    cw = d // chunks
    dy = None
    for i in range(3 * chunks):
        which, chunk = i % 3, i // 3
        at = which * d + chunk * cw
        part = dot(parts[i][...], w_ref[:, at : at + cw], NT)
        dy = part if dy is None else dy + part
        row = {0: 2, 2: 3}.get(which)
        if row is not None:
            sums[row : row + 1, chunk * cw : (chunk + 1) * cw] += jnp.sum(parts[i][...].astype(F32), axis=0, keepdims=True)
    spread, r = stats(x_ref[...].astype(F32))
    nv = spread * r
    dyg = dy * line(vec_in, "ag")
    dx = r * (dyg - jnp.mean(dyg, axis=-1, keepdims=True) - nv * jnp.mean(dyg * nv, axis=-1, keepdims=True))
    tg_ref[...] = (dbr_ref[...].astype(F32) + dx).astype(BF)
    sums[0:1, :] += jnp.sum(dy * nv, axis=0, keepdims=True)
    sums[1:2, :] += jnp.sum(dy, axis=0, keepdims=True)

    @pl.when(pl.program_id(0) == pl.num_programs(0) - 1)
    def _():
        per = d // PIECES
        sums[4:8, :] = mid_ref[0:4, :]
        rows = sums[...]
        for v in range(PIECES):
            vectors = jnp.concatenate([rows[:, v * per : (v + 1) * per], jnp.zeros((8, 128 - per), F32)], axis=1)
            biases = [b[:, v * 128 : (v + 1) * 128] for b in db1]
            piece = jnp.concatenate([vectors] + biases + [jnp.zeros((SMALL - 8 - CHUNKS, 128), F32)], axis=0)
            small_ref[v * SMALL : (v + 1) * SMALL, :] = piece.astype(BF)


def project_back(x, dbr, w, vec, mids, db1, parts):
    n, d = x.shape
    tm = 256
    row = pl.BlockSpec((tm, d), lambda i: (i, 0))

    def full(*s):
        return pl.BlockSpec(s, lambda i: (0, 0), pipeline_mode=pl.Buffered(1))

    chunks = len(parts) // 3
    return pl.pallas_call(
        functools.partial(back_kernel, chunks=chunks),
        grid=(n // tm,),
        in_specs=[row, row, full(d, 3 * d), full(*vec.shape), full(*mids.shape)]
        + [full(*b.shape) for b in db1]
        + [pl.BlockSpec((tm, d // chunks), lambda i: (i, 0))] * (3 * chunks),
        out_specs=[row, full(PIECES * SMALL, 128)],
        out_shape=[shape((n, d)), shape((PIECES * SMALL, 128))],
        scratch_shapes=[pltpu.VMEM((8, d), F32)],
        compiler_params=params(24),
        cost_estimate=pl.CostEstimate(flops=12 * n * d * d, bytes_accessed=16 * n * d, transcendentals=0),
        name="project_back",
    )(x, dbr, w, vec, mids, *db1, *parts)


def exchange(x, axis, by):
    count = lax.axis_size(axis)
    return lax.ppermute(x, axis, [(i, i ^ by) for i in range(count)])


def to_core(g):
    return exchange(g, "seq", 1)


def pick(x, index, axis=0):
    return lax.dynamic_index_in_dim(x, index, axis, keepdims=False)


def after(x, *others):
    return lax.optimization_barrier((x,) + others)[0]


class Part:
    def __init__(self, held, received, rows):
        self.held = (held.reshape(-1, 128), 0)
        self.received = (received.reshape(-1, 128), 0)
        self.rows = rows
        self.open = [0, 1, 2]

    def count(self):
        return self.rows << len(self.open)


def slot_kernel(ids_ref, *refs, items, inputs):
    ins, outs = refs[:inputs], refs[inputs:]

    def read(term, at, count):
        ref, offset = term
        return ins[ref][pl.ds(at + offset, count), :].astype(F32)

    step = 16
    for kind, *rest in items:
        if kind == "split":
            held, received, groups, size, bit, (send, to), keep = rest
            mine = ids_ref[bit]
            for a in range(groups):
                own = pl.multiple_of((2 * a + mine) * size, step)
                other = pl.multiple_of((2 * a + 1 - mine) * size, step)
                outs[send][to + a * size : to + (a + 1) * size, :] = (read(held, other, size) + read(received, other, size)).astype(BF)
                outs[keep][a * size : (a + 1) * size, :] = (read(held, own, size) + read(received, own, size)).astype(BF)
        elif kind == "sum":
            held, received, size, (send, to) = rest
            outs[send][to : to + size, :] = (read(held, 0, size) + read(received, 0, size)).astype(BF)
        else:
            first, second, size, bit, (send, to), keep = rest
            for mine in (0, 1):

                @pl.when(ids_ref[bit] == mine)
                def _():
                    own, other = (first, second) if mine == 0 else (second, first)
                    outs[send][to : to + size, :] = (read(other[0], 0, size) + read(other[1], 0, size)).astype(BF)
                    outs[keep][...] = (read(own[0], 0, size) + read(own[1], 0, size)).astype(BF)


def slot(ids, exchanges, *tokens):
    arrays, items, sizes, moves = [], [], [], []

    def use(term):
        for i, a in enumerate(arrays):
            if a is term[0]:
                return i, term[1]
        arrays.append(term[0])
        return len(arrays) - 1, term[1]

    for stage, parts in exchanges:
        send, to = len(sizes), 0
        sizes.append(0)
        placed = []
        if stage == "pick":
            one, two = parts
            size = one.count()
            items.append(("pick", (use(one.held), use(one.received)), (use(two.held), use(two.received)), size, 1, (send, 0), len(sizes)))
            placed.append((one, len(sizes), 0, 0))
            sizes.append(size)
            to = size
        else:
            for p in parts:
                held, received = use(p.held), use(p.received)
                if stage == "x":
                    items.append(("sum", held, received, p.count(), (send, to)))
                    placed.append((p, send, to, to))
                    to += p.count()
                    continue
                if stage == "half":
                    groups, bit = 1 << len(p.open), 1
                else:
                    groups, bit = 1 << (len(p.open) - 1 - p.open.index(stage)), 2 + stage
                size = p.count() // (2 * groups)
                items.append(("split", held, received, groups, size, bit, (send, to), len(sizes)))
                placed.append((p, len(sizes), 0, to))
                sizes.append(groups * size)
                to += groups * size
                if stage == "half":
                    p.rows //= 2
                else:
                    p.open.remove(stage)
        sizes[send] = to
        moves.append((stage, send, placed))

    if tokens:
        arrays = list(lax.optimization_barrier(tuple(arrays) + tokens)[: len(arrays)])
    whole = pl.BlockSpec(memory_space=pltpu.VMEM)
    outs = pl.pallas_call(
        functools.partial(slot_kernel, items=items, inputs=len(arrays)),
        in_specs=[pl.BlockSpec(memory_space=pltpu.SMEM)] + [whole] * len(arrays),
        out_specs=[whole] * len(sizes),
        out_shape=[shape((size, 128)) for size in sizes],
        compiler_params=params(2),
        cost_estimate=pl.CostEstimate(flops=0, bytes_accessed=512 * sum(sizes), transcendentals=0),
        name="slot",
    )(ids, *arrays)
    unit = lax.axis_size("vol") // PIECES
    sent, received = [], []
    for stage, send, placed in moves:
        if stage in ("half", "pick", "x"):
            got = exchange(outs[send], "seq", 2)
        else:
            got = exchange(outs[send], "vol", unit << stage)
        sent.append(outs[send])
        received.append(got)
        for p, keep, at, to in placed:
            p.held = (outs[keep], at)
            p.received = (got, to)
    return sent, received


def home_kernel(ids_ref, live_ref, *refs, mask):
    out_ref = refs[-1]
    for k, ref in enumerate(refs[:-1]):

        @pl.when(pl.program_id(0) == k)
        def _():
            value = ref[...].astype(F32)
            if mask:
                value = value * live_ref[ids_ref[5] ^ k]
            out_ref[...] = value.astype(out_ref.dtype)


def send_home(ids, live, own, others, slices, dtype, mask):
    rows, d = others[0].shape
    return pl.pallas_call(
        functools.partial(home_kernel, mask=mask),
        grid_spec=pltpu.PrefetchScalarGridSpec(
            num_scalar_prefetch=2,
            grid=(slices,),
            in_specs=[pl.BlockSpec((rows, d), lambda k, i, l: (0, 0), pipeline_mode=pl.Buffered(1))] * slices,
            out_specs=pl.BlockSpec((None, rows, d), lambda k, i, l: (k ^ i[5], 0, 0)),
        ),
        out_shape=shape((slices, rows, d), dtype),
        compiler_params=params(8),
        cost_estimate=pl.CostEstimate(flops=0, bytes_accessed=6 * slices * rows * d, transcendentals=0),
        name="home",
    )(ids, live, own, *others)


def assemble_ff_kernel(ids_ref, *refs, per, sizes):
    terms = refs[:4]
    expand_ref, reduce_ref = refs[4:]
    c = ids_ref[0]

    def first_layer(i, core, value):
        size = per // 2
        for k in range(PIECES):
            at = (k * CHUNKS + i) * 128
            expand_ref[pl.ds(pl.multiple_of(core * size, size), size), at : at + 128] = value[k * size : (k + 1) * size, :]

    def second_layer(i, core, value):
        d = value.shape[0]
        reduce_ref[i * 128 : (i + 1) * 128, pl.ds(pl.multiple_of(core * d, 128), d)] = value.T

    half = per // 2 * PIECES
    for core, (own, partner) in ((c, terms[:2]), (1 - c, terms[2:])):
        for x in (0, 1):

            @pl.when(ids_ref[1] == x)
            def _():
                one, two = (own, partner) if x == 0 else (partner, own)
                first_layer(0, core, one[: sizes[0], :].astype(F32))
                second_layer(0, core, two[: sizes[0], :].astype(F32))

        at = sizes[0]
        for i in (1, 2):
            rows = slice(at, at + sizes[i])
            value = own[rows, :].astype(F32) + partner[rows, :].astype(F32)
            first_layer(i, core, value[:half])
            second_layer(i, core, value[half:])
            at += sizes[i]


def assemble_end_kernel(ids_ref, *refs, per, size):
    terms = refs[:4]
    output_ref, input_ref, vector_ref = refs[4:]
    c = ids_ref[0]
    d = PIECES * per

    def output_part(core, value):
        part = per // 2
        for k in range(d // 128):
            rows = pl.ds(pl.multiple_of(core * part, part), part)
            output_ref[rows, k * 128 : (k + 1) * 128] = value[k * part : (k + 1) * part, :]

    def pair_part(i, core, value):
        for k in range(3):
            at = pl.multiple_of(k * d + (2 * i + core) * 128, 128)
            input_ref[:, pl.ds(at, 128)] = value[k * per : (k + 1) * per, :]

    for core, (own, partner) in ((c, terms[:2]), (1 - c, terms[2:])):
        for i in (1, 2):
            rows = slice((i - 1) * size, i * size)
            pair_part(i, core, own[rows, :].astype(F32) + partner[rows, :].astype(F32))
        for x in (0, 1):

            @pl.when(ids_ref[1] == x)
            def _():
                one, two = (own, partner) if x == 0 else (partner, own)
                output_part(core, one[2 * size : 3 * size, :].astype(F32))
                pair_part(0, core, two[2 * size : 3 * size, :].astype(F32))

    vector_ref[...] = terms[0][3 * size :, :].astype(F32) + terms[1][3 * size :, :].astype(F32)


def assemble(kernel, ids, per, arrays, outs, name):
    whole = pl.BlockSpec(memory_space=pltpu.VMEM)
    return pl.pallas_call(
        functools.partial(kernel, per=per),
        in_specs=[pl.BlockSpec(memory_space=pltpu.SMEM)] + [whole] * len(arrays),
        out_specs=[whole] * len(outs),
        out_shape=[shape(o, F32) for o in outs],
        compiler_params=params(8),
        name=name,
    )(ids, *arrays)


def on_device(
    volume_slices, volume_owner, tokens, cotangent, attend_gain, attend_shift, input_weight, query_bias, value_bias,
    output_weight, output_bias, mixer_gain, mixer_shift, expand_weight, expand_bias, reduce_weight, reduce_bias,
):
    slices, rows, d = tokens.shape
    ff = expand_weight.shape[1]
    nv = lax.axis_size("vol")
    peers = lax.axis_size("seq")
    me = lax.axis_index("seq")
    core_id = me % 2
    x_id = (me // 2) % 2
    core = core_id.astype(jnp.int32).reshape(1)
    n = rows * peers
    vol = lax.axis_index("vol")
    unit = nv // PIECES
    ids = jnp.stack([core_id, x_id, (vol // unit) % 2, (vol // (2 * unit)) % 2, (vol // (4 * unit)) % 2, me]).astype(jnp.int32)

    def from_peers(x, ks):
        parts = [pick(x, me ^ k) for k in ks]
        return [p if k == 0 else exchange(p, "seq", k) for p, k in zip(parts, ks)]

    far_parts = from_peers(tokens, (3, 2))
    near_parts = from_peers(tokens, (0, 1))
    zero = jnp.zeros((d,), BF)
    vec = jnp.concatenate(
        [attend_gain, attend_shift, query_bias, zero, value_bias, output_bias, mixer_gain, mixer_shift, reduce_bias] + [zero] * 7
    ).astype(F32).reshape(16, d)
    wide = ff // CHUNKS
    lanes = wide // PIECES
    b1 = expand_bias.astype(F32).reshape(ff // 128, 128)
    load = jnp.sum(jnp.where(volume_owner == lax.axis_index("vol"), volume_slices, 0))
    live = (jnp.arange(slices) < load).astype(BF)

    made = project_in(jnp.concatenate(near_parts), 0, n, None, vec, input_weight)
    far = jnp.concatenate([after(far_parts[1], made[2], b1, live), far_parts[0]])
    x, first_t, packed = project_in(far, 2 * rows, n, made, vec, input_weight)
    upstream = jnp.concatenate(from_peers(after(cotangent, far_parts[0], made[2]) * live[:, None, None], (0, 1, 2, 3)))

    mixed, inverse, weights = attend(packed)

    db1 = []

    def hidden(token, head, carried, i):
        gk, gs, b, *made = hidden_part(token, head, carried, upstream, expand_weight, reduce_weight, b1, i)
        db1.append(b)
        return gk, gs, made

    Y, Z1, Z2 = 0, 1, 2
    piece_rows = d // 2 + d // 2
    pair_rows = 3 * (d // PIECES)
    k0, s0, (o, ds, *kept) = hidden(core, (x, mixed, output_weight, vec), None, 0)
    r0 = to_core(s0)
    k1, s1, (o, ds) = hidden(after(core, s0), None, (*kept, o, ds), 1)
    r1 = to_core(s1)
    ga = Part(k0, r0, piece_rows)
    sent, _ = slot(ids, [("half", [ga])], s1)
    k2, s2, (o, ds) = hidden(after(core, s1, *sent), None, (*kept, o, ds), 2)
    r2 = to_core(s2)
    gb = Part(k1, r1, piece_rows)
    sent, _ = slot(ids, [(Z1, [gb])], s2)
    out, d_branch, d_mixed, k3, s3, sums_mid = outer(
        after(core, s2, *sent), x, upstream, mixed, inverse, output_weight, vec, o, ds
    )
    r3 = to_core(s3)

    def homeward(a):
        blocks = [a[k * rows : (k + 1) * rows] for k in range(1, peers)]
        return blocks, [exchange(b, "seq", k + 1) for k, b in enumerate(blocks)]

    out_sent, outs = homeward(out)
    gc = Part(k2, r2, piece_rows)
    sent, got = slot(ids, [(Y, [gc]), (Z2, [gb])], s3)
    parts = []

    def reflect_part(token, i):
        dq, dk, dv, gk, gs = reflect(token, packed, mixed, d_mixed, weights, first_t, 2 * i)
        parts.extend([dq, dk, dv])
        return gk, gs

    p0, q0 = reflect_part(after(core, s3, *sent, *out_sent), 0)
    t0 = to_core(q0)
    wait_c = got[0]
    sent, _ = slot(ids, [(Y, [ga, gb])], q0)
    p1, q1 = reflect_part(after(core, q0, wait_c, *sent, *outs), 1)
    t1 = to_core(q1)
    gd, gd2 = Part(k3, r3, pair_rows), Part(p0, t0, pair_rows)
    sent, _ = slot(ids, [(Z1, [ga, gc]), ("pick", [gd, gd2])], q1)
    p2, q2 = reflect_part(after(core, q1, *sent), 2)
    t2 = to_core(q2)
    ge1 = Part(p1, t1, pair_rows)
    sent, late_got = slot(ids, [(Y, [ge1, gd]), (Z2, [ga, gc])], q2)
    d_tokens, small = project_back(after(x, *sent), d_branch, input_weight, vec, sums_mid, db1, parts)

    tg_sent, tgs = homeward(d_tokens)
    ge2 = Part(p2, t2, pair_rows)
    gv = Part(small, to_core(small), SMALL)
    sent1, got1 = slot(ids, [(Y, [ge2, gv])], small, *tg_sent, late_got[1])
    block_out = send_home(ids, live, out, [after(o, *sent1) for o in outs], slices, BF, True)
    sent2, got2 = slot(ids, [(Z1, [ge1, ge2, gd, gv]), ("x", [ga, gb, gc])], *got1, block_out, tgs[1])
    per = d // PIECES
    spare = [1 << i for i in range(unit.bit_length() - 1)]
    sent3, got3 = slot(ids, [(Z2, [ge1, ge2, gd, gv])], *got2)
    ff_terms = [after(a, *sent3) for a in (sent2[1], got2[1])]
    ff_terms += [to_core(a) for a in ff_terms]
    expand_grad, reduce_grad = assemble(
        functools.partial(assemble_ff_kernel, sizes=[p.count() for p in (ga, gb, gc)]), ids, per, ff_terms, [(per, ff), (ff // PIECES, d)], "assemble_ff"
    )
    sent4, got4 = slot(ids, [("x", [ge1, ge2, gd, gv])], *got3, expand_grad, *tgs[1:])
    tgs = [after(t, *sent4) for t in tgs]
    tokens_grad = send_home(ids, live, d_tokens, tgs, slices, F32, False)
    ends = [sent4[0], got4[0]]
    ends += [to_core(a) for a in ends]
    output_grad, input_grad, vectors = assemble(
        functools.partial(assemble_end_kernel, size=pair_rows), ids, per, ends, [(per, d), (per, 3 * d), (SMALL, 128)], "assemble_end"
    )
    bias_rows = vectors[8 : 8 + CHUNKS]
    vectors = vectors[:8, :per]
    if unit > 1:
        sub = vol % unit

        def add_rest(a):
            for by in spare:
                a = a + exchange(a, "vol", by)
            return a

        def cut(a, axis):
            size = a.shape[axis] // unit
            return lax.dynamic_slice_in_dim(add_rest(a), sub * size, size, axis)

        expand_grad, reduce_grad, output_grad, input_grad = [cut(a, 0) for a in (expand_grad, reduce_grad, output_grad, input_grad)]
        expand_bias_grad = cut(bias_rows.reshape(-1), 0)
        vectors = cut(vectors, 1)
    else:
        expand_bias_grad = bias_rows.reshape(-1)
    return (
        block_out, tokens_grad, vectors[0], vectors[1], input_grad, vectors[2], vectors[3], output_grad, vectors[4],
        vectors[5], vectors[6], expand_grad, expand_bias_grad, reduce_grad, vectors[7],
    )


def solution(mesh):
    rows = P("vol", "seq", None)
    return jax.shard_map(
        on_device,
        mesh=mesh,
        in_specs=(P(), P(), rows, rows) + (P(),) * 13,
        out_specs=(rows, rows, P("vol"), P("vol"), P("vol", None), P("vol"), P("vol"), P("vol", None), P("vol"), P("vol"),
                   P("vol"), P("vol", None), P("vol"), P("vol", None), P("vol")),
        check_vma=False,
    )
```

```python
import functools

import jax
import jax.numpy as jnp
from jax import lax
from jax.experimental import pallas as pl
from jax.experimental.pallas import tpu as pltpu
from jax.sharding import PartitionSpec as P

HEAD_DIM = 64
PAIR = 2 * HEAD_DIM
LOG2E = 1.4426950408889634
PIECES = 8
CHUNKS = 3
ROW = {n: i for i, n in enumerate(("ag", "ash", "qb", "zero", "vb", "ob", "mg", "ms", "rb"))}
BF = jnp.bfloat16
F32 = jnp.float32
NN = (((1,), (0,)), ((), ()))
NT = (((1,), (1,)), ((), ()))

def dot(a, b, dims):
    return lax.dot_general(a, b, dims, preferred_element_type=F32)


def params(mib=24):
    return pltpu.CompilerParams(vmem_limit_bytes=mib << 20)


def line(ref, name):
    return ref[ROW[name] : ROW[name] + 1, :]


def shape(dims, dtype=BF):
    return jax.ShapeDtypeStruct(dims, dtype)


def normal(h):
    return 0.5 + 0.5 * lax.erf(h * 0.5**0.5), jnp.exp2(h * h * (-0.5 * LOG2E)) * 0.3989422804014327


def stats(v):
    spread = v - jnp.mean(v, axis=-1, keepdims=True)
    return spread, lax.rsqrt(jnp.mean(spread * spread, axis=-1, keepdims=True) + 1e-6)


def in_kernel(x_ref, vec_ref, w_ref, *rest):
    x_out, first_t, packed = rest[-3:]
    x = x_ref[...]
    d = x.shape[1]
    spread, r = stats(x.astype(F32))
    f = (spread * r * line(vec_ref, "ag") + line(vec_ref, "ash")).astype(BF)
    x_out[...] = x
    for i, bias in enumerate(("qb", "zero", "vb")):
        packed[:, i * d : (i + 1) * d] = (dot(f, w_ref[:, i * d : (i + 1) * d], NN) + line(vec_ref, bias)).astype(BF)
    first_t[...] = f.T


def project_in(part, offset, total, before, vec, weight):
    rows, d = part.shape
    wide = weight.shape[1]
    tm = 256
    first_block = offset // tm

    def full(a):
        return pl.BlockSpec(a.shape, lambda i: (0, 0), pipeline_mode=pl.Buffered(1))

    in_specs = [pl.BlockSpec((tm, d), lambda i: (i, 0)), full(vec), full(weight)]
    args = [part, vec, weight]
    aliases = {}
    if before is not None:
        aliases = {3: 0, 4: 1, 5: 2}
        in_specs += [pl.BlockSpec(memory_space=pl.ANY)] * 3
        args += list(before)
    return pl.pallas_call(
        in_kernel,
        grid=(rows // tm,),
        in_specs=in_specs,
        out_specs=[
            pl.BlockSpec((tm, d), lambda i: (i + first_block, 0)),
            pl.BlockSpec((d, tm), lambda i: (0, i + first_block)),
            pl.BlockSpec((tm, wide), lambda i: (i + first_block, 0)),
        ],
        out_shape=[shape((total, d)), shape((d, total)), shape((total, wide))],
        input_output_aliases=aliases,
        compiler_params=params(24),
        cost_estimate=pl.CostEstimate(flops=6 * rows * d * wide, bytes_accessed=2 * (d * wide + rows * (wide + 3 * d)), transcendentals=0),
        name="project_in",
    )(*args)


def attend_kernel(q_ref, k_ref, v_ref, o_ref, inv_ref, p_ref, vx_ref, *, tq):
    n = k_ref.shape[0]
    head = 2 * pl.program_id(0)
    lane = lax.broadcasted_iota(jnp.int32, (tq, PAIR), 1)
    vx_ref[:, :PAIR] = v_ref[...]
    vx_ref[:, PAIR:] = jnp.ones((n, PAIR), BF)
    low = lax.broadcasted_iota(jnp.int32, (tq, PAIR), 1) < HEAD_DIM
    for t in range(n // tq):
        rows = pl.ds(t * tq, tq)
        q = q_ref[rows, :]
        zero = jnp.zeros_like(q)
        outs = []
        for a in range(2):
            qa = jnp.where(low, q, zero) if a == 0 else jnp.where(low, zero, q)
            s = dot(qa, k_ref[...], NT)
            top = jnp.max(s, axis=-1, keepdims=True)
            p = jnp.exp2((s - top) * (LOG2E * HEAD_DIM**-0.5)).astype(BF)
            p_ref[a, rows, :] = p
            both = dot(p, vx_ref[...], NN)
            inv = 1.0 / both[:, PAIR:]
            outs.append((both[:, :PAIR] * inv, inv))
        o_ref[rows, :] = jnp.where(low, outs[0][0], outs[1][0]).astype(BF)
        inv_ref[rows, :] = jnp.where(lane == head, outs[0][1], jnp.where(lane == head + 1, outs[1][1], inv_ref[rows, :]))


def attend(packed):
    n, w = packed.shape
    d = w // 3
    hp = d // PAIR

    def cols(off):
        return pl.BlockSpec((n, PAIR), lambda h: (0, h + off))

    return pl.pallas_call(
        functools.partial(attend_kernel, tq=128),
        grid=(hp,),
        in_specs=[cols(0), cols(hp), cols(2 * hp)],
        out_specs=[cols(0), pl.BlockSpec((n, PAIR), lambda h: (0, 0)), pl.BlockSpec((2, n, n), lambda h: (h, 0, 0))],
        out_shape=[shape((n, d)), shape((n, PAIR), F32), shape((2 * hp, n, n))],
        scratch_shapes=[pltpu.VMEM((n, 2 * PAIR), BF)],
        compiler_params=params(40),
        cost_estimate=pl.CostEstimate(flops=16 * n * n * d, bytes_accessed=4 * n * n * hp, transcendentals=0),
        name="attend",
    )(packed, packed, packed)


WHOLE = pl.BlockSpec(memory_space=pltpu.VMEM)
FAR = pl.BlockSpec(memory_space=pltpu.HBM)


def transpose_rows(block, out, cols):
    t = block.T
    d = t.shape[0]
    half = d // PIECES // 2
    for h in range(2):
        for v in range(PIECES):
            at = (2 * v + h) * half
            to = (h * PIECES + v) * half
            out[to : to + half, cols] = t[at : at + half]


def core_rows(ref, which):
    half = ref.shape[0] // 2
    return ref[pl.ds(pl.multiple_of(which * half, half), half), :]


def piece_blocks(g, ref, first):
    rows = g.shape[0] // PIECES
    for k in range(g.shape[1] // 128):
        at = (first + k) * rows
        ref[:, at : at + rows, :] = g[:, k * 128 : (k + 1) * 128].reshape(PIECES, rows, 128)


def middle_of(x_ref, mix_ref, wo_ref, vec_ref, rows):
    return x_ref[rows, :].astype(F32) + dot(mix_ref[rows, :], wo_ref[...], NN) + line(vec_ref, "ob")


def hidden_kernel(c_ref, *refs, i, head, tm, sub):
    refs = list(refs)
    take = lambda k: [refs.pop(0) for _ in range(k)]
    if head:
        x_ref, mix_ref, wo_ref, vec_ref = take(4)
    else:
        sec_ref, sec_t, up_t, o_in, ds_in = take(5)
    up_ref, w1_ref, w2_ref, b1_ref, gk_ref, gs_ref, db1_ref, o_ref, ds_ref = take(9)
    if head:
        sec_ref, sec_t, up_t = take(3)
    act, dh = take(2)
    n, d = up_ref.shape
    wide = act.shape[1]

    def shares(first, last):
        return [slice((v * CHUNKS + i) * 128, (v * CHUNKS + i + 1) * 128) for v in range(first // 128, last // 128)]

    def columns(first, last):
        return jnp.concatenate([w1_ref[:, at] for at in shares(first, last)], axis=1)

    def lines(first, last):
        return jnp.concatenate([w2_ref[at, :] for at in shares(first, last)], axis=0)

    if head:
        for t in range(n // 256):
            rows = slice(t * 256, (t + 1) * 256)
            spread, r = stats(middle_of(x_ref, mix_ref, wo_ref, vec_ref, rows))
            sec = (spread * r * line(vec_ref, "mg") + line(vec_ref, "ms")).astype(BF)
            sec_ref[rows, :] = sec
            transpose_rows(sec, sec_t, rows)
            up_t[:, rows] = up_ref[rows, :].T
    db1_ref[...] = jnp.zeros_like(db1_ref)
    for first in range(0, wide, sub):
        cols = slice(first, first + sub)
        bias = jnp.concatenate([b1_ref[v * CHUNKS + i : v * CHUNKS + i + 1, :] for v in range(first // 128, (first + sub) // 128)], axis=1)

        def tile(t, _):
            rows = pl.ds(pl.multiple_of(t * tm, tm), tm)
            h = dot(sec_ref[rows, :], columns(first, first + sub), NN) + bias
            da = dot(up_ref[rows, :], lines(first, first + sub), NT)
            cdf, pdf = normal(h)
            act[rows, cols] = (h * cdf).astype(BF)
            dhv = da * (cdf + h * pdf)
            dh[rows, cols] = dhv.astype(BF)
            db1_ref[:, cols] += jnp.sum(dhv, axis=0, keepdims=True)
            return 0

        lax.fori_loop(0, n // tm, tile, 0)
    base = PIECES * (d // PIECES // 2)
    c = c_ref[0]
    for ref, mine in ((gs_ref, 1 - c), (gk_ref, c)):
        piece_blocks(dot(core_rows(sec_t, mine), dh[...], NN).astype(BF), ref, 0)
        g = dot(core_rows(up_t, mine), act[...], NN).astype(BF)
        for k in range(wide // 128):
            ref[k, base:, :] = g[:, k * 128 : (k + 1) * 128]

    def gather(t, _):
        rows = pl.ds(pl.multiple_of(t * tm, tm), tm)
        o = dot(act[rows, :], lines(0, wide), NN)
        o_ref[rows, :] = o if head else o_in[rows, :] + o
        ds = dot(dh[rows, :], columns(0, wide), NT)
        ds_ref[rows, :] = ds if head else ds_in[rows, :] + ds
        return 0

    lax.fori_loop(0, n // tm, gather, 0)


def hidden_part(core, head, carried, up, w1, w2, b1, i, tm=512, sub=512):
    n, d = up.shape
    wide = 128 * PIECES
    assert wide * CHUNKS == w1.shape[1]
    g = (PIECES, PIECES * (d // PIECES // 2) + d // 2, 128)
    args = list(head) if head else list(carried)
    made = [shape(g), shape(g), shape((1, wide), F32), shape((n, d), F32), shape((n, d), F32)]
    if head:
        made += [shape((n, d)), shape((d, n)), shape((d, n))]
    return pl.pallas_call(
        functools.partial(hidden_kernel, i=i, head=bool(head), tm=tm, sub=sub),
        in_specs=[pl.BlockSpec(memory_space=pltpu.SMEM)] + [WHOLE] * (len(args) + 4),
        out_specs=[WHOLE] * len(made),
        out_shape=made,
        input_output_aliases={} if head else {4: 3, 5: 4},
        scratch_shapes=[pltpu.VMEM((n, wide), BF), pltpu.VMEM((n, wide), BF)],
        compiler_params=params(10),
        cost_estimate=pl.CostEstimate(flops=24 * n * d * wide, bytes_accessed=8 * d * wide, transcendentals=0),
        name="hidden",
    )(core, *args, up, w1, w2, b1)


def outer_kernel(c_ref, x_ref, up_ref, mix_ref, li_ref, wo_ref, vec_ref, o_ref, ds_ref, out_ref, dbr_ref, do_ref, gk_ref, gs_ref, sums_ref, mix_t, *, tm):
    n, d = x_ref.shape
    sums = None
    lanes = lax.broadcasted_iota(jnp.int32, (PAIR, d), 1) // HEAD_DIM
    spread_heads = (lanes == lax.broadcasted_iota(jnp.int32, (PAIR, d), 0)).astype(BF)
    for t in range(n // tm):
        rows = slice(t * tm, (t + 1) * tm)
        m = middle_of(x_ref, mix_ref, wo_ref, vec_ref, rows)
        spread, r = stats(m)
        nv = spread * r
        up = up_ref[rows, :].astype(F32)
        transpose_rows(mix_ref[rows, :], mix_t, rows)
        dy = ds_ref[rows, :]
        dyg = dy * line(vec_ref, "mg")
        dm = up + r * (dyg - jnp.mean(dyg, axis=-1, keepdims=True) - nv * jnp.mean(dyg * nv, axis=-1, keepdims=True))
        db = dm.astype(BF)
        dbr_ref[rows, :] = db
        out_ref[rows, :] = (m + o_ref[rows, :] + line(vec_ref, "rb")).astype(BF)
        li = li_ref[rows, :]
        coarse = li.astype(BF)
        fine = (li - coarse.astype(F32)).astype(BF)
        scale = dot(coarse, spread_heads, NN) + dot(fine, spread_heads, NN)
        do_ref[rows, :] = (dot(db, wo_ref[...], NT) * scale).astype(BF)
        part = [jnp.sum(v, axis=0, keepdims=True) for v in (db.astype(F32), dy * nv, dy, up)]
        sums = part if sums is None else [a + b for a, b in zip(sums, part)]
    sums_ref[...] = jnp.concatenate(sums + [jnp.zeros((4, d), F32)], axis=0)
    for ref, mine in ((gs_ref, 1 - c_ref[0]), (gk_ref, c_ref[0])):
        piece_blocks(dot(core_rows(mix_t, mine), dbr_ref[...], NN).astype(BF), ref, 0)


def outer(core, x, up, mix, li, wo, vec, o, ds, tm=256):
    n, d = x.shape
    g = (PIECES, d // 128 * (d // PIECES // 2), 128)
    return pl.pallas_call(
        functools.partial(outer_kernel, tm=tm),
        in_specs=[pl.BlockSpec(memory_space=pltpu.SMEM)] + [WHOLE] * 8,
        out_specs=[WHOLE] * 6,
        out_shape=[shape((n, d))] * 3 + [shape(g), shape(g), shape((8, d), F32)],
        scratch_shapes=[pltpu.VMEM((d, n), BF)],
        compiler_params=params(8),
        cost_estimate=pl.CostEstimate(flops=24 * n * d * d, bytes_accessed=20 * n * d, transcendentals=0),
        name="outer",
    )(core, x, up, mix, li, wo, vec, o, ds)


def by_piece(g):
    rows = g.shape[0] // PIECES
    return [g[:, i : i + 128].reshape(PIECES, rows, 128) for i in range(0, g.shape[1], 128)]


def reflect_kernel(c_ref, q_ref, k_ref, v_ref, o_ref, do_ref, p_ref, ft_ref, dq_ref, dk_ref, dv_ref, gk_ref, gs_ref, ds_ref, *, tq):
    n = k_ref.shape[0]
    low = lax.broadcasted_iota(jnp.int32, (tq, PAIR), 1) < HEAD_DIM
    q_t = q_ref[...].T
    do_t = do_ref[...].T
    scale = HEAD_DIM**-0.5
    dks, dvs = [], []
    for a in range(2):
        for t in range(n // tq):
            rows = pl.ds(t * tq, tq)
            do = do_ref[rows, :]
            zero = jnp.zeros_like(do)
            doa = jnp.where(low, do, zero) if a == 0 else jnp.where(low, zero, do)
            delta = jnp.sum(doa.astype(F32) * o_ref[rows, :].astype(F32), axis=-1, keepdims=True)
            dp = dot(doa, v_ref[...], NT)
            ds = (p_ref[a, rows, :].astype(F32) * (dp - delta)).astype(BF)
            ds_ref[rows, :] = ds
            dq = (dot(ds, k_ref[...], NN) * scale).astype(BF)
            dq_ref[rows, :] = dq if a == 0 else jnp.where(low, dq_ref[rows, :], dq)
        part = slice(HEAD_DIM * a, HEAD_DIM * (a + 1))
        dvs.append(dot(do_t[part], p_ref[a], NN))
        dks.append(dot(q_t[part], ds_ref[...], NN) * scale)
    dv = jnp.concatenate(dvs, axis=0).astype(BF).T
    dk = jnp.concatenate(dks, axis=0).astype(BF).T
    dv_ref[...] = dv
    dk_ref[...] = dk
    g = dot(ft_ref[...], jnp.concatenate([dq_ref[...], dk, dv], axis=1), NN).astype(BF)
    per = g.shape[0] // PIECES
    h = pl.program_id(0)
    for step, ref in enumerate((gs_ref, gk_ref)):

        @pl.when(h == step)
        def _():
            for i, block in enumerate(by_piece(g)):
                ref[:, i * per : (i + 1) * per, :] = block


def reflect(core, packed, o, do, p, first_t, start):
    n, w = packed.shape
    d = w // 3
    hp = d // PAIR

    def which(h, c):
        return (h + 1 - c[0]) % 2

    def cols(off):
        return pl.BlockSpec((n, PAIR), lambda h, c: (0, which(h, c) + off))

    g = (PIECES, 3 * (d // PIECES), 128)
    piece = pl.BlockSpec(g, lambda h, c: (0, 0, 0), pipeline_mode=pl.Buffered(1))
    return pl.pallas_call(
        functools.partial(reflect_kernel, tq=256),
        grid_spec=pltpu.PrefetchScalarGridSpec(
            num_scalar_prefetch=1,
            grid=(2,),
            in_specs=[
                cols(start), cols(start + hp), cols(start + 2 * hp), cols(start), cols(start),
                pl.BlockSpec((2, n, n), lambda h, c: (which(h, c) + start, 0, 0)),
                pl.BlockSpec((d, n), lambda h, c: (0, 0), pipeline_mode=pl.Buffered(1)),
            ],
            out_specs=[cols(0)] * 3 + [piece] * 2,
            scratch_shapes=[pltpu.VMEM((n, n), BF)],
        ),
        out_shape=[shape((n, 2 * PAIR))] * 3 + [shape(g)] * 2,
        compiler_params=params(30),
        cost_estimate=pl.CostEstimate(flops=160 * n * n * PAIR, bytes_accessed=8 * n * n, transcendentals=0),
        name="reflect",
    )(core, packed, packed, packed, o, do, p, first_t)


SMALL = 16


def back_kernel(*refs, chunks):
    x_ref, dbr_ref, w_ref, vec_in, mid_ref = refs[:5]
    db1 = refs[5 : 5 + CHUNKS]
    parts = refs[5 + CHUNKS : 5 + CHUNKS + 3 * chunks]
    tg_ref, small_ref, sums = refs[5 + CHUNKS + 3 * chunks :]

    @pl.when(pl.program_id(0) == 0)
    def _():
        sums[...] = jnp.zeros_like(sums)

    d = x_ref.shape[1]
    cw = d // chunks
    dy = None
    for i in range(3 * chunks):
        which, chunk = i % 3, i // 3
        at = which * d + chunk * cw
        part = dot(parts[i][...], w_ref[:, at : at + cw], NT)
        dy = part if dy is None else dy + part
        row = {0: 2, 2: 3}.get(which)
        if row is not None:
            sums[row : row + 1, chunk * cw : (chunk + 1) * cw] += jnp.sum(parts[i][...].astype(F32), axis=0, keepdims=True)
    spread, r = stats(x_ref[...].astype(F32))
    nv = spread * r
    dyg = dy * line(vec_in, "ag")
    dx = r * (dyg - jnp.mean(dyg, axis=-1, keepdims=True) - nv * jnp.mean(dyg * nv, axis=-1, keepdims=True))
    tg_ref[...] = (dbr_ref[...].astype(F32) + dx).astype(BF)
    sums[0:1, :] += jnp.sum(dy * nv, axis=0, keepdims=True)
    sums[1:2, :] += jnp.sum(dy, axis=0, keepdims=True)

    @pl.when(pl.program_id(0) == pl.num_programs(0) - 1)
    def _():
        per = d // PIECES
        sums[4:8, :] = mid_ref[0:4, :]
        rows = sums[...]
        for v in range(PIECES):
            vectors = jnp.concatenate([rows[:, v * per : (v + 1) * per], jnp.zeros((8, 128 - per), F32)], axis=1)
            biases = [b[:, v * 128 : (v + 1) * 128] for b in db1]
            piece = jnp.concatenate([vectors] + biases + [jnp.zeros((SMALL - 8 - CHUNKS, 128), F32)], axis=0)
            small_ref[v * SMALL : (v + 1) * SMALL, :] = piece.astype(BF)


def project_back(x, dbr, w, vec, mids, db1, parts):
    n, d = x.shape
    tm = 256
    row = pl.BlockSpec((tm, d), lambda i: (i, 0))

    def full(*s):
        return pl.BlockSpec(s, lambda i: (0, 0), pipeline_mode=pl.Buffered(1))

    chunks = len(parts) // 3
    return pl.pallas_call(
        functools.partial(back_kernel, chunks=chunks),
        grid=(n // tm,),
        in_specs=[row, row, full(d, 3 * d), full(*vec.shape), full(*mids.shape)]
        + [full(*b.shape) for b in db1]
        + [pl.BlockSpec((tm, d // chunks), lambda i: (i, 0))] * (3 * chunks),
        out_specs=[row, full(PIECES * SMALL, 128)],
        out_shape=[shape((n, d)), shape((PIECES * SMALL, 128))],
        scratch_shapes=[pltpu.VMEM((8, d), F32)],
        compiler_params=params(24),
        cost_estimate=pl.CostEstimate(flops=12 * n * d * d, bytes_accessed=16 * n * d, transcendentals=0),
        name="project_back",
    )(x, dbr, w, vec, mids, *db1, *parts)


def exchange(x, axis, by):
    count = lax.axis_size(axis)
    return lax.ppermute(x, axis, [(i, i ^ by) for i in range(count)])


def to_core(g):
    return exchange(g, "seq", 1)


def pick(x, index, axis=0):
    return lax.dynamic_index_in_dim(x, index, axis, keepdims=False)


def after(x, *others):
    return lax.optimization_barrier((x,) + others)[0]


class Part:
    def __init__(self, held, received, rows):
        self.held = (held.reshape(-1, 128), 0)
        self.received = (received.reshape(-1, 128), 0)
        self.rows = rows
        self.open = [0, 1, 2]

    def count(self):
        return self.rows << len(self.open)


def slot_kernel(ids_ref, *refs, items, inputs):
    ins, outs = refs[:inputs], refs[inputs:]

    def read(term, at, count):
        ref, offset = term
        return ins[ref][pl.ds(at + offset, count), :].astype(F32)

    step = 16
    for kind, *rest in items:
        if kind == "split":
            held, received, groups, size, bit, (send, to), keep = rest
            mine = ids_ref[bit]
            for a in range(groups):
                own = pl.multiple_of((2 * a + mine) * size, step)
                other = pl.multiple_of((2 * a + 1 - mine) * size, step)
                outs[send][to + a * size : to + (a + 1) * size, :] = (read(held, other, size) + read(received, other, size)).astype(BF)
                outs[keep][a * size : (a + 1) * size, :] = (read(held, own, size) + read(received, own, size)).astype(BF)
        elif kind == "sum":
            held, received, size, (send, to) = rest
            outs[send][to : to + size, :] = (read(held, 0, size) + read(received, 0, size)).astype(BF)
        else:
            first, second, size, bit, (send, to), keep = rest
            for mine in (0, 1):

                @pl.when(ids_ref[bit] == mine)
                def _():
                    own, other = (first, second) if mine == 0 else (second, first)
                    outs[send][to : to + size, :] = (read(other[0], 0, size) + read(other[1], 0, size)).astype(BF)
                    outs[keep][...] = (read(own[0], 0, size) + read(own[1], 0, size)).astype(BF)


def slot(ids, exchanges, *tokens):
    arrays, items, sizes, moves = [], [], [], []

    def use(term):
        for i, a in enumerate(arrays):
            if a is term[0]:
                return i, term[1]
        arrays.append(term[0])
        return len(arrays) - 1, term[1]

    for stage, parts in exchanges:
        send, to = len(sizes), 0
        sizes.append(0)
        placed = []
        if stage == "pick":
            one, two = parts
            size = one.count()
            items.append(("pick", (use(one.held), use(one.received)), (use(two.held), use(two.received)), size, 1, (send, 0), len(sizes)))
            placed.append((one, len(sizes), 0, 0))
            sizes.append(size)
            to = size
        else:
            for p in parts:
                held, received = use(p.held), use(p.received)
                if stage == "x":
                    items.append(("sum", held, received, p.count(), (send, to)))
                    placed.append((p, send, to, to))
                    to += p.count()
                    continue
                if stage == "half":
                    groups, bit = 1 << len(p.open), 1
                else:
                    groups, bit = 1 << (len(p.open) - 1 - p.open.index(stage)), 2 + stage
                size = p.count() // (2 * groups)
                items.append(("split", held, received, groups, size, bit, (send, to), len(sizes)))
                placed.append((p, len(sizes), 0, to))
                sizes.append(groups * size)
                to += groups * size
                if stage == "half":
                    p.rows //= 2
                else:
                    p.open.remove(stage)
        sizes[send] = to
        moves.append((stage, send, placed))

    if tokens:
        arrays = list(lax.optimization_barrier(tuple(arrays) + tokens)[: len(arrays)])
    whole = pl.BlockSpec(memory_space=pltpu.VMEM)
    outs = pl.pallas_call(
        functools.partial(slot_kernel, items=items, inputs=len(arrays)),
        in_specs=[pl.BlockSpec(memory_space=pltpu.SMEM)] + [whole] * len(arrays),
        out_specs=[whole] * len(sizes),
        out_shape=[shape((size, 128)) for size in sizes],
        compiler_params=params(2),
        cost_estimate=pl.CostEstimate(flops=0, bytes_accessed=512 * sum(sizes), transcendentals=0),
        name="slot",
    )(ids, *arrays)
    unit = lax.axis_size("vol") // PIECES
    sent, received = [], []
    for stage, send, placed in moves:
        if stage in ("half", "pick", "x"):
            got = exchange(outs[send], "seq", 2)
        else:
            got = exchange(outs[send], "vol", unit << stage)
        sent.append(outs[send])
        received.append(got)
        for p, keep, at, to in placed:
            p.held = (outs[keep], at)
            p.received = (got, to)
    return sent, received


def home_kernel(ids_ref, live_ref, *refs, mask):
    out_ref = refs[-1]
    for k, ref in enumerate(refs[:-1]):

        @pl.when(pl.program_id(0) == k)
        def _():
            value = ref[...].astype(F32)
            if mask:
                value = value * live_ref[ids_ref[5] ^ k]
            out_ref[...] = value.astype(out_ref.dtype)


def send_home(ids, live, own, others, slices, dtype, mask):
    rows, d = others[0].shape
    return pl.pallas_call(
        functools.partial(home_kernel, mask=mask),
        grid_spec=pltpu.PrefetchScalarGridSpec(
            num_scalar_prefetch=2,
            grid=(slices,),
            in_specs=[pl.BlockSpec((rows, d), lambda k, i, l: (0, 0), pipeline_mode=pl.Buffered(1))] * slices,
            out_specs=pl.BlockSpec((None, rows, d), lambda k, i, l: (k ^ i[5], 0, 0)),
        ),
        out_shape=shape((slices, rows, d), dtype),
        compiler_params=params(8),
        cost_estimate=pl.CostEstimate(flops=0, bytes_accessed=6 * slices * rows * d, transcendentals=0),
        name="home",
    )(ids, live, own, *others)


def assemble_ff_kernel(ids_ref, *refs, per, sizes):
    terms = refs[:4]
    expand_ref, reduce_ref = refs[4:]
    c = ids_ref[0]

    def first_layer(i, core, value):
        size = per // 2
        for k in range(PIECES):
            at = (k * CHUNKS + i) * 128
            expand_ref[pl.ds(pl.multiple_of(core * size, size), size), at : at + 128] = value[k * size : (k + 1) * size, :]

    def second_layer(i, core, value):
        d = value.shape[0]
        reduce_ref[i * 128 : (i + 1) * 128, pl.ds(pl.multiple_of(core * d, 128), d)] = value.T

    half = per // 2 * PIECES
    for core, (own, partner) in ((c, terms[:2]), (1 - c, terms[2:])):
        for x in (0, 1):

            @pl.when(ids_ref[1] == x)
            def _():
                one, two = (own, partner) if x == 0 else (partner, own)
                first_layer(0, core, one[: sizes[0], :].astype(F32))
                second_layer(0, core, two[: sizes[0], :].astype(F32))

        at = sizes[0]
        for i in (1, 2):
            rows = slice(at, at + sizes[i])
            value = own[rows, :].astype(F32) + partner[rows, :].astype(F32)
            first_layer(i, core, value[:half])
            second_layer(i, core, value[half:])
            at += sizes[i]


def assemble_end_kernel(ids_ref, *refs, per, size):
    terms = refs[:4]
    output_ref, input_ref, vector_ref = refs[4:]
    c = ids_ref[0]
    d = PIECES * per

    def output_part(core, value):
        part = per // 2
        for k in range(d // 128):
            rows = pl.ds(pl.multiple_of(core * part, part), part)
            output_ref[rows, k * 128 : (k + 1) * 128] = value[k * part : (k + 1) * part, :]

    def pair_part(i, core, value):
        for k in range(3):
            at = pl.multiple_of(k * d + (2 * i + core) * 128, 128)
            input_ref[:, pl.ds(at, 128)] = value[k * per : (k + 1) * per, :]

    for core, (own, partner) in ((c, terms[:2]), (1 - c, terms[2:])):
        for i in (1, 2):
            rows = slice((i - 1) * size, i * size)
            pair_part(i, core, own[rows, :].astype(F32) + partner[rows, :].astype(F32))
        for x in (0, 1):

            @pl.when(ids_ref[1] == x)
            def _():
                one, two = (own, partner) if x == 0 else (partner, own)
                output_part(core, one[2 * size : 3 * size, :].astype(F32))
                pair_part(0, core, two[2 * size : 3 * size, :].astype(F32))

    vector_ref[...] = terms[0][3 * size :, :].astype(F32) + terms[1][3 * size :, :].astype(F32)


def assemble(kernel, ids, per, arrays, outs, name):
    whole = pl.BlockSpec(memory_space=pltpu.VMEM)
    return pl.pallas_call(
        functools.partial(kernel, per=per),
        in_specs=[pl.BlockSpec(memory_space=pltpu.SMEM)] + [whole] * len(arrays),
        out_specs=[whole] * len(outs),
        out_shape=[shape(o, F32) for o in outs],
        compiler_params=params(8),
        name=name,
    )(ids, *arrays)


def on_device(
    volume_slices, volume_owner, tokens, cotangent, attend_gain, attend_shift, input_weight, query_bias, value_bias,
    output_weight, output_bias, mixer_gain, mixer_shift, expand_weight, expand_bias, reduce_weight, reduce_bias,
):
    slices, rows, d = tokens.shape
    ff = expand_weight.shape[1]
    nv = lax.axis_size("vol")
    peers = lax.axis_size("seq")
    me = lax.axis_index("seq")
    core_id = me % 2
    x_id = (me // 2) % 2
    core = core_id.astype(jnp.int32).reshape(1)
    n = rows * peers
    vol = lax.axis_index("vol")
    unit = nv // PIECES
    ids = jnp.stack([core_id, x_id, (vol // unit) % 2, (vol // (2 * unit)) % 2, (vol // (4 * unit)) % 2, me]).astype(jnp.int32)

    def from_peers(x, ks):
        parts = [pick(x, me ^ k) for k in ks]
        return [p if k == 0 else exchange(p, "seq", k) for p, k in zip(parts, ks)]

    far_parts = from_peers(tokens, (3, 2))
    near_parts = from_peers(tokens, (0, 1))
    zero = jnp.zeros((d,), BF)
    vec = jnp.concatenate(
        [attend_gain, attend_shift, query_bias, zero, value_bias, output_bias, mixer_gain, mixer_shift, reduce_bias] + [zero] * 7
    ).astype(F32).reshape(16, d)
    wide = ff // CHUNKS
    lanes = wide // PIECES
    b1 = expand_bias.astype(F32).reshape(ff // 128, 128)
    load = jnp.sum(jnp.where(volume_owner == lax.axis_index("vol"), volume_slices, 0))
    live = (jnp.arange(slices) < load).astype(BF)

    made = project_in(jnp.concatenate(near_parts), 0, n, None, vec, input_weight)
    far = jnp.concatenate([after(far_parts[1], made[2], b1, live), far_parts[0]])
    x, first_t, packed = project_in(far, 2 * rows, n, made, vec, input_weight)
    upstream = jnp.concatenate(from_peers(after(cotangent, far_parts[0], made[2]) * live[:, None, None], (0, 1, 2, 3)))

    mixed, inverse, weights = attend(packed)

    db1 = []

    def hidden(token, head, carried, i):
        gk, gs, b, *made = hidden_part(token, head, carried, upstream, expand_weight, reduce_weight, b1, i)
        db1.append(b)
        return gk, gs, made

    Y, Z1, Z2 = 0, 1, 2
    piece_rows = d // 2 + d // 2
    pair_rows = 3 * (d // PIECES)
    k0, s0, (o, ds, *kept) = hidden(core, (x, mixed, output_weight, vec), None, 0)
    r0 = to_core(s0)
    k1, s1, (o, ds) = hidden(after(core, s0), None, (*kept, o, ds), 1)
    r1 = to_core(s1)
    ga = Part(k0, r0, piece_rows)
    sent, _ = slot(ids, [("half", [ga])], s1)
    k2, s2, (o, ds) = hidden(after(core, s1, *sent), None, (*kept, o, ds), 2)
    r2 = to_core(s2)
    gb = Part(k1, r1, piece_rows)
    sent, _ = slot(ids, [(Z1, [gb])], s2)
    out, d_branch, d_mixed, k3, s3, sums_mid = outer(
        after(core, s2, *sent), x, upstream, mixed, inverse, output_weight, vec, o, ds
    )
    r3 = to_core(s3)

    def homeward(a):
        blocks = [a[k * rows : (k + 1) * rows] for k in range(1, peers)]
        return blocks, [exchange(b, "seq", k + 1) for k, b in enumerate(blocks)]

    out_sent, outs = homeward(out)
    gc = Part(k2, r2, piece_rows)
    sent, got = slot(ids, [(Y, [gc])], s3)
    parts = []

    def reflect_part(token, i):
        dq, dk, dv, gk, gs = reflect(token, packed, mixed, d_mixed, weights, first_t, 2 * i)
        parts.extend([dq, dk, dv])
        return gk, gs

    p0, q0 = reflect_part(after(core, s3, *sent, *out_sent), 0)
    t0 = to_core(q0)
    wait_c = got[0]
    sent, _ = slot(ids, [(Y, [ga]), (Z2, [gb])], q0)
    p1, q1 = reflect_part(after(core, q0, wait_c, *sent, *outs), 1)
    t1 = to_core(q1)
    gd, gd2 = Part(k3, r3, pair_rows), Part(p0, t0, pair_rows)
    sent, _ = slot(ids, [(Z1, [ga, gc]), ("pick", [gd, gd2])], q1)
    p2, q2 = reflect_part(after(core, q1, *sent), 2)
    t2 = to_core(q2)
    ge1 = Part(p1, t1, pair_rows)
    sent, late_got = slot(ids, [(Y, [ge1, gd]), (Z2, [ga, gc])], q2)
    d_tokens, small = project_back(after(x, *sent), d_branch, input_weight, vec, sums_mid, db1, parts)

    tg_sent, tgs = homeward(d_tokens)
    ge2 = Part(p2, t2, pair_rows)
    gv = Part(small, to_core(small), SMALL)
    sent1, got1 = slot(ids, [(Y, [ge2, gv]), (Z1, [ge1, gd])], small, *tg_sent, late_got[1])
    block_out = send_home(ids, live, out, [after(o, *sent1) for o in outs], slices, BF, True)
    sent2, got2 = slot(ids, [(Z1, [ge2, gv]), (Z2, [ge1, gd]), (Y, [gb])], *got1, block_out, tgs[1])
    per = d // PIECES
    spare = [1 << i for i in range(unit.bit_length() - 1)]
    sent3, got3 = slot(ids, [(Z2, [ge2, gv]), ("x", [ga, gb, gc])], *got2)
    tgs = [after(t, *sent3) for t in tgs]
    tokens_grad = send_home(ids, live, d_tokens, tgs, slices, F32, False)
    sent4, got4 = slot(ids, [("x", [ge1, ge2, gd, gv])], got3[0], tokens_grad)
    ff_terms = [after(a, *sent4) for a in (sent3[-1], got3[-1])]
    ff_terms += [to_core(a) for a in ff_terms]
    expand_grad, reduce_grad = assemble(
        functools.partial(assemble_ff_kernel, sizes=[p.count() for p in (ga, gb, gc)]), ids, per, ff_terms, [(per, ff), (ff // PIECES, d)], "assemble_ff"
    )
    ends = [sent4[0], got4[0]]
    ends += [to_core(a) for a in ends]
    output_grad, input_grad, vectors = assemble(
        functools.partial(assemble_end_kernel, size=pair_rows), ids, per, ends, [(per, d), (per, 3 * d), (SMALL, 128)], "assemble_end"
    )
    bias_rows = vectors[8 : 8 + CHUNKS]
    vectors = vectors[:8, :per]
    if unit > 1:
        sub = vol % unit

        def add_rest(a):
            for by in spare:
                a = a + exchange(a, "vol", by)
            return a

        def cut(a, axis):
            size = a.shape[axis] // unit
            return lax.dynamic_slice_in_dim(add_rest(a), sub * size, size, axis)

        expand_grad, reduce_grad, output_grad, input_grad = [cut(a, 0) for a in (expand_grad, reduce_grad, output_grad, input_grad)]
        expand_bias_grad = cut(bias_rows.reshape(-1), 0)
        vectors = cut(vectors, 1)
    else:
        expand_bias_grad = bias_rows.reshape(-1)
    return (
        block_out, tokens_grad, vectors[0], vectors[1], input_grad, vectors[2], vectors[3], output_grad, vectors[4],
        vectors[5], vectors[6], expand_grad, expand_bias_grad, reduce_grad, vectors[7],
    )


def solution(mesh):
    rows = P("vol", "seq", None)
    return jax.shard_map(
        on_device,
        mesh=mesh,
        in_specs=(P(), P(), rows, rows) + (P(),) * 13,
        out_specs=(rows, rows, P("vol"), P("vol"), P("vol", None), P("vol"), P("vol"), P("vol", None), P("vol"), P("vol"),
                   P("vol"), P("vol", None), P("vol"), P("vol", None), P("vol")),
        check_vma=False,
    )
```

```python
import functools

import jax
import jax.numpy as jnp
from jax import lax
from jax.experimental import pallas as pl
from jax.experimental.pallas import tpu as pltpu
from jax.sharding import PartitionSpec as P

HEAD_DIM = 64
PAIR = 2 * HEAD_DIM
LOG2E = 1.4426950408889634
PIECES = 8
CHUNKS = 3
ROW = {n: i for i, n in enumerate(("ag", "ash", "qb", "zero", "vb", "ob", "mg", "ms", "rb"))}
BF = jnp.bfloat16
F32 = jnp.float32
NN = (((1,), (0,)), ((), ()))
NT = (((1,), (1,)), ((), ()))

def dot(a, b, dims):
    return lax.dot_general(a, b, dims, preferred_element_type=F32)


def params(mib=24):
    return pltpu.CompilerParams(vmem_limit_bytes=mib << 20)


def line(ref, name):
    return ref[ROW[name] : ROW[name] + 1, :]


def shape(dims, dtype=BF):
    return jax.ShapeDtypeStruct(dims, dtype)


def normal(h):
    return 0.5 + 0.5 * lax.erf(h * 0.5**0.5), jnp.exp2(h * h * (-0.5 * LOG2E)) * 0.3989422804014327


def stats(v):
    spread = v - jnp.mean(v, axis=-1, keepdims=True)
    return spread, lax.rsqrt(jnp.mean(spread * spread, axis=-1, keepdims=True) + 1e-6)


def in_kernel(x_ref, vec_ref, w_ref, *rest):
    x_out, first_t, packed = rest[-3:]
    x = x_ref[...]
    d = x.shape[1]
    spread, r = stats(x.astype(F32))
    f = (spread * r * line(vec_ref, "ag") + line(vec_ref, "ash")).astype(BF)
    x_out[...] = x
    for i, bias in enumerate(("qb", "zero", "vb")):
        packed[:, i * d : (i + 1) * d] = (dot(f, w_ref[:, i * d : (i + 1) * d], NN) + line(vec_ref, bias)).astype(BF)
    first_t[...] = f.T


def project_in(part, offset, total, before, vec, weight):
    rows, d = part.shape
    wide = weight.shape[1]
    tm = 256
    first_block = offset // tm

    def full(a):
        return pl.BlockSpec(a.shape, lambda i: (0, 0), pipeline_mode=pl.Buffered(1))

    in_specs = [pl.BlockSpec((tm, d), lambda i: (i, 0)), full(vec), full(weight)]
    args = [part, vec, weight]
    aliases = {}
    if before is not None:
        aliases = {3: 0, 4: 1, 5: 2}
        in_specs += [pl.BlockSpec(memory_space=pl.ANY)] * 3
        args += list(before)
    return pl.pallas_call(
        in_kernel,
        grid=(rows // tm,),
        in_specs=in_specs,
        out_specs=[
            pl.BlockSpec((tm, d), lambda i: (i + first_block, 0)),
            pl.BlockSpec((d, tm), lambda i: (0, i + first_block)),
            pl.BlockSpec((tm, wide), lambda i: (i + first_block, 0)),
        ],
        out_shape=[shape((total, d)), shape((d, total)), shape((total, wide))],
        input_output_aliases=aliases,
        compiler_params=params(24),
        cost_estimate=pl.CostEstimate(flops=6 * rows * d * wide, bytes_accessed=2 * (d * wide + rows * (wide + 3 * d)), transcendentals=0),
        name="project_in",
    )(*args)


def attend_kernel(q_ref, k_ref, v_ref, o_ref, inv_ref, p_ref, vx_ref, *, tq):
    n = k_ref.shape[0]
    head = 2 * pl.program_id(0)
    lane = lax.broadcasted_iota(jnp.int32, (tq, PAIR), 1)
    vx_ref[:, :PAIR] = v_ref[...]
    vx_ref[:, PAIR:] = jnp.ones((n, PAIR), BF)
    low = lax.broadcasted_iota(jnp.int32, (tq, PAIR), 1) < HEAD_DIM
    for t in range(n // tq):
        rows = pl.ds(t * tq, tq)
        q = q_ref[rows, :]
        zero = jnp.zeros_like(q)
        outs = []
        for a in range(2):
            qa = jnp.where(low, q, zero) if a == 0 else jnp.where(low, zero, q)
            s = dot(qa, k_ref[...], NT)
            top = jnp.max(s, axis=-1, keepdims=True)
            p = jnp.exp2((s - top) * (LOG2E * HEAD_DIM**-0.5)).astype(BF)
            p_ref[a, rows, :] = p
            both = dot(p, vx_ref[...], NN)
            inv = 1.0 / both[:, PAIR:]
            outs.append((both[:, :PAIR] * inv, inv))
        o_ref[rows, :] = jnp.where(low, outs[0][0], outs[1][0]).astype(BF)
        inv_ref[rows, :] = jnp.where(lane == head, outs[0][1], jnp.where(lane == head + 1, outs[1][1], inv_ref[rows, :]))


def attend(packed):
    n, w = packed.shape
    d = w // 3
    hp = d // PAIR

    def cols(off):
        return pl.BlockSpec((n, PAIR), lambda h: (0, h + off))

    return pl.pallas_call(
        functools.partial(attend_kernel, tq=128),
        grid=(hp,),
        in_specs=[cols(0), cols(hp), cols(2 * hp)],
        out_specs=[cols(0), pl.BlockSpec((n, PAIR), lambda h: (0, 0)), pl.BlockSpec((2, n, n), lambda h: (h, 0, 0))],
        out_shape=[shape((n, d)), shape((n, PAIR), F32), shape((2 * hp, n, n))],
        scratch_shapes=[pltpu.VMEM((n, 2 * PAIR), BF)],
        compiler_params=params(40),
        cost_estimate=pl.CostEstimate(flops=16 * n * n * d, bytes_accessed=4 * n * n * hp, transcendentals=0),
        name="attend",
    )(packed, packed, packed)


WHOLE = pl.BlockSpec(memory_space=pltpu.VMEM)
FAR = pl.BlockSpec(memory_space=pltpu.HBM)


def transpose_rows(block, out, cols):
    t = block.T
    d = t.shape[0]
    half = d // PIECES // 2
    for h in range(2):
        for v in range(PIECES):
            at = (2 * v + h) * half
            to = (h * PIECES + v) * half
            out[to : to + half, cols] = t[at : at + half]


def core_rows(ref, which):
    half = ref.shape[0] // 2
    return ref[pl.ds(pl.multiple_of(which * half, half), half), :]


def piece_blocks(g, ref, first):
    rows = g.shape[0] // PIECES
    for k in range(g.shape[1] // 128):
        at = (first + k) * rows
        ref[:, at : at + rows, :] = g[:, k * 128 : (k + 1) * 128].reshape(PIECES, rows, 128)


def middle_of(x_ref, mix_ref, wo_ref, vec_ref, rows):
    return x_ref[rows, :].astype(F32) + dot(mix_ref[rows, :], wo_ref[...], NN) + line(vec_ref, "ob")


def hidden_kernel(c_ref, *refs, i, head, tm, sub):
    refs = list(refs)
    take = lambda k: [refs.pop(0) for _ in range(k)]
    if head:
        x_ref, mix_ref, wo_ref, vec_ref = take(4)
    else:
        sec_ref, sec_t, up_t, o_in, ds_in = take(5)
    up_ref, w1_ref, w2_ref, b1_ref, gk_ref, gs_ref, db1_ref, o_ref, ds_ref = take(9)
    if head:
        sec_ref, sec_t, up_t = take(3)
    act, dh = take(2)
    n, d = up_ref.shape
    wide = act.shape[1]

    def shares(first, last):
        return [slice((v * CHUNKS + i) * 128, (v * CHUNKS + i + 1) * 128) for v in range(first // 128, last // 128)]

    def columns(first, last):
        return jnp.concatenate([w1_ref[:, at] for at in shares(first, last)], axis=1)

    def lines(first, last):
        return jnp.concatenate([w2_ref[at, :] for at in shares(first, last)], axis=0)

    if head:
        for t in range(n // 256):
            rows = slice(t * 256, (t + 1) * 256)
            spread, r = stats(middle_of(x_ref, mix_ref, wo_ref, vec_ref, rows))
            sec = (spread * r * line(vec_ref, "mg") + line(vec_ref, "ms")).astype(BF)
            sec_ref[rows, :] = sec
            transpose_rows(sec, sec_t, rows)
            up_t[:, rows] = up_ref[rows, :].T
    db1_ref[...] = jnp.zeros_like(db1_ref)
    for first in range(0, wide, sub):
        cols = slice(first, first + sub)
        bias = jnp.concatenate([b1_ref[v * CHUNKS + i : v * CHUNKS + i + 1, :] for v in range(first // 128, (first + sub) // 128)], axis=1)

        def tile(t, _):
            rows = pl.ds(pl.multiple_of(t * tm, tm), tm)
            h = dot(sec_ref[rows, :], columns(first, first + sub), NN) + bias
            da = dot(up_ref[rows, :], lines(first, first + sub), NT)
            cdf, pdf = normal(h)
            act[rows, cols] = (h * cdf).astype(BF)
            dhv = da * (cdf + h * pdf)
            dh[rows, cols] = dhv.astype(BF)
            db1_ref[:, cols] += jnp.sum(dhv, axis=0, keepdims=True)
            return 0

        lax.fori_loop(0, n // tm, tile, 0)
    base = PIECES * (d // PIECES // 2)
    c = c_ref[0]
    for ref, mine in ((gs_ref, 1 - c), (gk_ref, c)):
        piece_blocks(dot(core_rows(sec_t, mine), dh[...], NN).astype(BF), ref, 0)
        g = dot(core_rows(up_t, mine), act[...], NN).astype(BF)
        for k in range(wide // 128):
            ref[k, base:, :] = g[:, k * 128 : (k + 1) * 128]

    def gather(t, _):
        rows = pl.ds(pl.multiple_of(t * tm, tm), tm)
        o = dot(act[rows, :], lines(0, wide), NN)
        o_ref[rows, :] = o if head else o_in[rows, :] + o
        ds = dot(dh[rows, :], columns(0, wide), NT)
        ds_ref[rows, :] = ds if head else ds_in[rows, :] + ds
        return 0

    lax.fori_loop(0, n // tm, gather, 0)


def hidden_part(core, head, carried, up, w1, w2, b1, i, tm=512, sub=512):
    n, d = up.shape
    wide = 128 * PIECES
    assert wide * CHUNKS == w1.shape[1]
    g = (PIECES, PIECES * (d // PIECES // 2) + d // 2, 128)
    args = list(head) if head else list(carried)
    made = [shape(g), shape(g), shape((1, wide), F32), shape((n, d), F32), shape((n, d), F32)]
    if head:
        made += [shape((n, d)), shape((d, n)), shape((d, n))]
    return pl.pallas_call(
        functools.partial(hidden_kernel, i=i, head=bool(head), tm=tm, sub=sub),
        in_specs=[pl.BlockSpec(memory_space=pltpu.SMEM)] + [WHOLE] * (len(args) + 4),
        out_specs=[WHOLE] * len(made),
        out_shape=made,
        input_output_aliases={} if head else {4: 3, 5: 4},
        scratch_shapes=[pltpu.VMEM((n, wide), BF), pltpu.VMEM((n, wide), BF)],
        compiler_params=params(10),
        cost_estimate=pl.CostEstimate(flops=24 * n * d * wide, bytes_accessed=8 * d * wide, transcendentals=0),
        name="hidden",
    )(core, *args, up, w1, w2, b1)


def outer_kernel(c_ref, x_ref, up_ref, mix_ref, li_ref, wo_ref, vec_ref, o_ref, ds_ref, out_ref, dbr_ref, do_ref, gk_ref, gs_ref, sums_ref, mix_t, *, tm):
    n, d = x_ref.shape
    sums = None
    lanes = lax.broadcasted_iota(jnp.int32, (PAIR, d), 1) // HEAD_DIM
    spread_heads = (lanes == lax.broadcasted_iota(jnp.int32, (PAIR, d), 0)).astype(BF)
    for t in range(n // tm):
        rows = slice(t * tm, (t + 1) * tm)
        m = middle_of(x_ref, mix_ref, wo_ref, vec_ref, rows)
        spread, r = stats(m)
        nv = spread * r
        up = up_ref[rows, :].astype(F32)
        transpose_rows(mix_ref[rows, :], mix_t, rows)
        dy = ds_ref[rows, :]
        dyg = dy * line(vec_ref, "mg")
        dm = up + r * (dyg - jnp.mean(dyg, axis=-1, keepdims=True) - nv * jnp.mean(dyg * nv, axis=-1, keepdims=True))
        db = dm.astype(BF)
        dbr_ref[rows, :] = db
        out_ref[rows, :] = (m + o_ref[rows, :] + line(vec_ref, "rb")).astype(BF)
        li = li_ref[rows, :]
        coarse = li.astype(BF)
        fine = (li - coarse.astype(F32)).astype(BF)
        scale = dot(coarse, spread_heads, NN) + dot(fine, spread_heads, NN)
        do_ref[rows, :] = (dot(db, wo_ref[...], NT) * scale).astype(BF)
        part = [jnp.sum(v, axis=0, keepdims=True) for v in (db.astype(F32), dy * nv, dy, up)]
        sums = part if sums is None else [a + b for a, b in zip(sums, part)]
    sums_ref[...] = jnp.concatenate(sums + [jnp.zeros((4, d), F32)], axis=0)
    for ref, mine in ((gs_ref, 1 - c_ref[0]), (gk_ref, c_ref[0])):
        piece_blocks(dot(core_rows(mix_t, mine), dbr_ref[...], NN).astype(BF), ref, 0)


def outer(core, x, up, mix, li, wo, vec, o, ds, tm=256):
    n, d = x.shape
    g = (PIECES, d // 128 * (d // PIECES // 2), 128)
    return pl.pallas_call(
        functools.partial(outer_kernel, tm=tm),
        in_specs=[pl.BlockSpec(memory_space=pltpu.SMEM)] + [WHOLE] * 8,
        out_specs=[WHOLE] * 6,
        out_shape=[shape((n, d))] * 3 + [shape(g), shape(g), shape((8, d), F32)],
        scratch_shapes=[pltpu.VMEM((d, n), BF)],
        compiler_params=params(8),
        cost_estimate=pl.CostEstimate(flops=24 * n * d * d, bytes_accessed=20 * n * d, transcendentals=0),
        name="outer",
    )(core, x, up, mix, li, wo, vec, o, ds)


def by_piece(g):
    rows = g.shape[0] // PIECES
    return [g[:, i : i + 128].reshape(PIECES, rows, 128) for i in range(0, g.shape[1], 128)]


def reflect_kernel(c_ref, q_ref, k_ref, v_ref, o_ref, do_ref, p_ref, ft_ref, dq_ref, dk_ref, dv_ref, gk_ref, gs_ref, ds_ref, *, tq):
    n = k_ref.shape[0]
    low = lax.broadcasted_iota(jnp.int32, (tq, PAIR), 1) < HEAD_DIM
    q_t = q_ref[...].T
    do_t = do_ref[...].T
    scale = HEAD_DIM**-0.5
    dks, dvs = [], []
    for a in range(2):
        for t in range(n // tq):
            rows = pl.ds(t * tq, tq)
            do = do_ref[rows, :]
            zero = jnp.zeros_like(do)
            doa = jnp.where(low, do, zero) if a == 0 else jnp.where(low, zero, do)
            delta = jnp.sum(doa.astype(F32) * o_ref[rows, :].astype(F32), axis=-1, keepdims=True)
            dp = dot(doa, v_ref[...], NT)
            ds = (p_ref[a, rows, :].astype(F32) * (dp - delta)).astype(BF)
            ds_ref[rows, :] = ds
            dq = (dot(ds, k_ref[...], NN) * scale).astype(BF)
            dq_ref[rows, :] = dq if a == 0 else jnp.where(low, dq_ref[rows, :], dq)
        part = slice(HEAD_DIM * a, HEAD_DIM * (a + 1))
        dvs.append(dot(do_t[part], p_ref[a], NN))
        dks.append(dot(q_t[part], ds_ref[...], NN) * scale)
    dv = jnp.concatenate(dvs, axis=0).astype(BF).T
    dk = jnp.concatenate(dks, axis=0).astype(BF).T
    dv_ref[...] = dv
    dk_ref[...] = dk
    g = dot(ft_ref[...], jnp.concatenate([dq_ref[...], dk, dv], axis=1), NN).astype(BF)
    per = g.shape[0] // PIECES
    h = pl.program_id(0)
    for step, ref in enumerate((gs_ref, gk_ref)):

        @pl.when(h == step)
        def _():
            for i, block in enumerate(by_piece(g)):
                ref[:, i * per : (i + 1) * per, :] = block


def reflect(core, packed, o, do, p, first_t, start):
    n, w = packed.shape
    d = w // 3
    hp = d // PAIR

    def which(h, c):
        return (h + 1 - c[0]) % 2

    def cols(off):
        return pl.BlockSpec((n, PAIR), lambda h, c: (0, which(h, c) + off))

    g = (PIECES, 3 * (d // PIECES), 128)
    piece = pl.BlockSpec(g, lambda h, c: (0, 0, 0), pipeline_mode=pl.Buffered(1))
    return pl.pallas_call(
        functools.partial(reflect_kernel, tq=256),
        grid_spec=pltpu.PrefetchScalarGridSpec(
            num_scalar_prefetch=1,
            grid=(2,),
            in_specs=[
                cols(start), cols(start + hp), cols(start + 2 * hp), cols(start), cols(start),
                pl.BlockSpec((2, n, n), lambda h, c: (which(h, c) + start, 0, 0)),
                pl.BlockSpec((d, n), lambda h, c: (0, 0), pipeline_mode=pl.Buffered(1)),
            ],
            out_specs=[cols(0)] * 3 + [piece] * 2,
            scratch_shapes=[pltpu.VMEM((n, n), BF)],
        ),
        out_shape=[shape((n, 2 * PAIR))] * 3 + [shape(g)] * 2,
        compiler_params=params(29),
        cost_estimate=pl.CostEstimate(flops=160 * n * n * PAIR, bytes_accessed=8 * n * n, transcendentals=0),
        name="reflect",
    )(core, packed, packed, packed, o, do, p, first_t)


SMALL = 16


def back_kernel(*refs, chunks):
    x_ref, dbr_ref, w_ref, vec_in, mid_ref = refs[:5]
    db1 = refs[5 : 5 + CHUNKS]
    parts = refs[5 + CHUNKS : 5 + CHUNKS + 3 * chunks]
    tg_ref, small_ref, sums = refs[5 + CHUNKS + 3 * chunks :]

    @pl.when(pl.program_id(0) == 0)
    def _():
        sums[...] = jnp.zeros_like(sums)

    d = x_ref.shape[1]
    cw = d // chunks
    dy = None
    for i in range(3 * chunks):
        which, chunk = i % 3, i // 3
        at = which * d + chunk * cw
        part = dot(parts[i][...], w_ref[:, at : at + cw], NT)
        dy = part if dy is None else dy + part
        row = {0: 2, 2: 3}.get(which)
        if row is not None:
            sums[row : row + 1, chunk * cw : (chunk + 1) * cw] += jnp.sum(parts[i][...].astype(F32), axis=0, keepdims=True)
    spread, r = stats(x_ref[...].astype(F32))
    nv = spread * r
    dyg = dy * line(vec_in, "ag")
    dx = r * (dyg - jnp.mean(dyg, axis=-1, keepdims=True) - nv * jnp.mean(dyg * nv, axis=-1, keepdims=True))
    tg_ref[...] = (dbr_ref[...].astype(F32) + dx).astype(BF)
    sums[0:1, :] += jnp.sum(dy * nv, axis=0, keepdims=True)
    sums[1:2, :] += jnp.sum(dy, axis=0, keepdims=True)

    @pl.when(pl.program_id(0) == pl.num_programs(0) - 1)
    def _():
        per = d // PIECES
        sums[4:8, :] = mid_ref[0:4, :]
        rows = sums[...]
        for v in range(PIECES):
            vectors = jnp.concatenate([rows[:, v * per : (v + 1) * per], jnp.zeros((8, 128 - per), F32)], axis=1)
            biases = [b[:, v * 128 : (v + 1) * 128] for b in db1]
            piece = jnp.concatenate([vectors] + biases + [jnp.zeros((SMALL - 8 - CHUNKS, 128), F32)], axis=0)
            small_ref[v * SMALL : (v + 1) * SMALL, :] = piece.astype(BF)


def project_back(x, dbr, w, vec, mids, db1, parts):
    n, d = x.shape
    tm = 256
    row = pl.BlockSpec((tm, d), lambda i: (i, 0))

    def full(*s):
        return pl.BlockSpec(s, lambda i: (0, 0), pipeline_mode=pl.Buffered(1))

    chunks = len(parts) // 3
    return pl.pallas_call(
        functools.partial(back_kernel, chunks=chunks),
        grid=(n // tm,),
        in_specs=[row, row, full(d, 3 * d), full(*vec.shape), full(*mids.shape)]
        + [full(*b.shape) for b in db1]
        + [pl.BlockSpec((tm, d // chunks), lambda i: (i, 0))] * (3 * chunks),
        out_specs=[row, full(PIECES * SMALL, 128)],
        out_shape=[shape((n, d)), shape((PIECES * SMALL, 128))],
        scratch_shapes=[pltpu.VMEM((8, d), F32)],
        compiler_params=params(24),
        cost_estimate=pl.CostEstimate(flops=12 * n * d * d, bytes_accessed=16 * n * d, transcendentals=0),
        name="project_back",
    )(x, dbr, w, vec, mids, *db1, *parts)


def exchange(x, axis, by):
    count = lax.axis_size(axis)
    return lax.ppermute(x, axis, [(i, i ^ by) for i in range(count)])


def to_core(g):
    return exchange(g, "seq", 1)


def pick(x, index, axis=0):
    return lax.dynamic_index_in_dim(x, index, axis, keepdims=False)


def after(x, *others):
    return lax.optimization_barrier((x,) + others)[0]


class Part:
    def __init__(self, held, received, rows):
        self.held = (held.reshape(-1, 128), 0)
        self.received = (received.reshape(-1, 128), 0)
        self.rows = rows
        self.open = [0, 1, 2]

    def count(self):
        return self.rows << len(self.open)


def slot_kernel(ids_ref, *refs, items, inputs):
    ins, outs = refs[:inputs], refs[inputs:]

    def read(term, at, count):
        ref, offset = term
        return ins[ref][pl.ds(at + offset, count), :].astype(F32)

    step = 16
    for kind, *rest in items:
        if kind == "split":
            held, received, groups, size, bit, (send, to), keep = rest
            mine = ids_ref[bit]
            for a in range(groups):
                own = pl.multiple_of((2 * a + mine) * size, step)
                other = pl.multiple_of((2 * a + 1 - mine) * size, step)
                outs[send][to + a * size : to + (a + 1) * size, :] = (read(held, other, size) + read(received, other, size)).astype(BF)
                outs[keep][a * size : (a + 1) * size, :] = (read(held, own, size) + read(received, own, size)).astype(BF)
        elif kind == "sum":
            held, received, size, (send, to) = rest
            outs[send][to : to + size, :] = (read(held, 0, size) + read(received, 0, size)).astype(BF)
        else:
            first, second, size, bit, (send, to), keep = rest
            for mine in (0, 1):

                @pl.when(ids_ref[bit] == mine)
                def _():
                    own, other = (first, second) if mine == 0 else (second, first)
                    outs[send][to : to + size, :] = (read(other[0], 0, size) + read(other[1], 0, size)).astype(BF)
                    outs[keep][...] = (read(own[0], 0, size) + read(own[1], 0, size)).astype(BF)


def slot(ids, exchanges, *tokens):
    arrays, items, sizes, moves = [], [], [], []

    def use(term):
        for i, a in enumerate(arrays):
            if a is term[0]:
                return i, term[1]
        arrays.append(term[0])
        return len(arrays) - 1, term[1]

    for stage, parts in exchanges:
        send, to = len(sizes), 0
        sizes.append(0)
        placed = []
        if stage == "pick":
            one, two = parts
            size = one.count()
            items.append(("pick", (use(one.held), use(one.received)), (use(two.held), use(two.received)), size, 1, (send, 0), len(sizes)))
            placed.append((one, len(sizes), 0, 0))
            sizes.append(size)
            to = size
        else:
            for p in parts:
                held, received = use(p.held), use(p.received)
                if stage == "x":
                    items.append(("sum", held, received, p.count(), (send, to)))
                    placed.append((p, send, to, to))
                    to += p.count()
                    continue
                if stage == "half":
                    groups, bit = 1 << len(p.open), 1
                else:
                    groups, bit = 1 << (len(p.open) - 1 - p.open.index(stage)), 2 + stage
                size = p.count() // (2 * groups)
                items.append(("split", held, received, groups, size, bit, (send, to), len(sizes)))
                placed.append((p, len(sizes), 0, to))
                sizes.append(groups * size)
                to += groups * size
                if stage == "half":
                    p.rows //= 2
                else:
                    p.open.remove(stage)
        sizes[send] = to
        moves.append((stage, send, placed))

    if tokens:
        arrays = list(lax.optimization_barrier(tuple(arrays) + tokens)[: len(arrays)])
    whole = pl.BlockSpec(memory_space=pltpu.VMEM)
    outs = pl.pallas_call(
        functools.partial(slot_kernel, items=items, inputs=len(arrays)),
        in_specs=[pl.BlockSpec(memory_space=pltpu.SMEM)] + [whole] * len(arrays),
        out_specs=[whole] * len(sizes),
        out_shape=[shape((size, 128)) for size in sizes],
        compiler_params=params(2),
        cost_estimate=pl.CostEstimate(flops=0, bytes_accessed=512 * sum(sizes), transcendentals=0),
        name="slot",
    )(ids, *arrays)
    unit = lax.axis_size("vol") // PIECES
    sent, received = [], []
    for stage, send, placed in moves:
        if stage in ("half", "pick", "x"):
            got = exchange(outs[send], "seq", 2)
        else:
            got = exchange(outs[send], "vol", unit << stage)
        sent.append(outs[send])
        received.append(got)
        for p, keep, at, to in placed:
            p.held = (outs[keep], at)
            p.received = (got, to)
    return sent, received


def home_kernel(ids_ref, live_ref, *refs, mask):
    out_ref = refs[-1]
    for k, ref in enumerate(refs[:-1]):

        @pl.when(pl.program_id(0) == k)
        def _():
            value = ref[...].astype(F32)
            if mask:
                value = value * live_ref[ids_ref[5] ^ k]
            out_ref[...] = value.astype(out_ref.dtype)


def send_home(ids, live, own, others, slices, dtype, mask):
    rows, d = others[0].shape
    return pl.pallas_call(
        functools.partial(home_kernel, mask=mask),
        grid_spec=pltpu.PrefetchScalarGridSpec(
            num_scalar_prefetch=2,
            grid=(slices,),
            in_specs=[pl.BlockSpec((rows, d), lambda k, i, l: (0, 0), pipeline_mode=pl.Buffered(1))] * slices,
            out_specs=pl.BlockSpec((None, rows, d), lambda k, i, l: (k ^ i[5], 0, 0)),
        ),
        out_shape=shape((slices, rows, d), dtype),
        compiler_params=params(8),
        cost_estimate=pl.CostEstimate(flops=0, bytes_accessed=6 * slices * rows * d, transcendentals=0),
        name="home",
    )(ids, live, own, *others)


def assemble_ff_kernel(ids_ref, *refs, per, sizes):
    terms = refs[:4]
    expand_ref, reduce_ref = refs[4:]
    c = ids_ref[0]

    def first_layer(i, core, value):
        size = per // 2
        for k in range(PIECES):
            at = (k * CHUNKS + i) * 128
            expand_ref[pl.ds(pl.multiple_of(core * size, size), size), at : at + 128] = value[k * size : (k + 1) * size, :]

    def second_layer(i, core, value):
        d = value.shape[0]
        reduce_ref[i * 128 : (i + 1) * 128, pl.ds(pl.multiple_of(core * d, 128), d)] = value.T

    half = per // 2 * PIECES
    for core, (own, partner) in ((c, terms[:2]), (1 - c, terms[2:])):
        for x in (0, 1):

            @pl.when(ids_ref[1] == x)
            def _():
                one, two = (own, partner) if x == 0 else (partner, own)
                first_layer(0, core, one[: sizes[0], :].astype(F32))
                second_layer(0, core, two[: sizes[0], :].astype(F32))

        at = sizes[0]
        for i in (1, 2):
            rows = slice(at, at + sizes[i])
            value = own[rows, :].astype(F32) + partner[rows, :].astype(F32)
            first_layer(i, core, value[:half])
            second_layer(i, core, value[half:])
            at += sizes[i]


def assemble_end_kernel(ids_ref, *refs, per, size):
    terms = refs[:4]
    output_ref, input_ref, vector_ref = refs[4:]
    c = ids_ref[0]
    d = PIECES * per

    def output_part(core, value):
        part = per // 2
        for k in range(d // 128):
            rows = pl.ds(pl.multiple_of(core * part, part), part)
            output_ref[rows, k * 128 : (k + 1) * 128] = value[k * part : (k + 1) * part, :]

    def pair_part(i, core, value):
        for k in range(3):
            at = pl.multiple_of(k * d + (2 * i + core) * 128, 128)
            input_ref[:, pl.ds(at, 128)] = value[k * per : (k + 1) * per, :]

    for core, (own, partner) in ((c, terms[:2]), (1 - c, terms[2:])):
        for i in (1, 2):
            rows = slice((i - 1) * size, i * size)
            pair_part(i, core, own[rows, :].astype(F32) + partner[rows, :].astype(F32))
        for x in (0, 1):

            @pl.when(ids_ref[1] == x)
            def _():
                one, two = (own, partner) if x == 0 else (partner, own)
                output_part(core, one[2 * size : 3 * size, :].astype(F32))
                pair_part(0, core, two[2 * size : 3 * size, :].astype(F32))

    vector_ref[...] = terms[0][3 * size :, :].astype(F32) + terms[1][3 * size :, :].astype(F32)


def assemble(kernel, ids, per, arrays, outs, name):
    whole = pl.BlockSpec(memory_space=pltpu.VMEM)
    return pl.pallas_call(
        functools.partial(kernel, per=per),
        in_specs=[pl.BlockSpec(memory_space=pltpu.SMEM)] + [whole] * len(arrays),
        out_specs=[whole] * len(outs),
        out_shape=[shape(o, F32) for o in outs],
        compiler_params=params(8),
        name=name,
    )(ids, *arrays)


def on_device(
    volume_slices, volume_owner, tokens, cotangent, attend_gain, attend_shift, input_weight, query_bias, value_bias,
    output_weight, output_bias, mixer_gain, mixer_shift, expand_weight, expand_bias, reduce_weight, reduce_bias,
):
    slices, rows, d = tokens.shape
    ff = expand_weight.shape[1]
    nv = lax.axis_size("vol")
    peers = lax.axis_size("seq")
    me = lax.axis_index("seq")
    core_id = me % 2
    x_id = (me // 2) % 2
    core = core_id.astype(jnp.int32).reshape(1)
    n = rows * peers
    vol = lax.axis_index("vol")
    unit = nv // PIECES
    ids = jnp.stack([core_id, x_id, (vol // unit) % 2, (vol // (2 * unit)) % 2, (vol // (4 * unit)) % 2, me]).astype(jnp.int32)

    def from_peers(x, ks):
        parts = [pick(x, me ^ k) for k in ks]
        return [p if k == 0 else exchange(p, "seq", k) for p, k in zip(parts, ks)]

    far_parts = from_peers(tokens, (3, 2))
    near_parts = from_peers(tokens, (0, 1))
    zero = jnp.zeros((d,), BF)
    vec = jnp.concatenate(
        [attend_gain, attend_shift, query_bias, zero, value_bias, output_bias, mixer_gain, mixer_shift, reduce_bias] + [zero] * 7
    ).astype(F32).reshape(16, d)
    wide = ff // CHUNKS
    lanes = wide // PIECES
    b1 = expand_bias.astype(F32).reshape(ff // 128, 128)
    load = jnp.sum(jnp.where(volume_owner == lax.axis_index("vol"), volume_slices, 0))
    live = (jnp.arange(slices) < load).astype(BF)

    made = project_in(jnp.concatenate(near_parts), 0, n, None, vec, input_weight)
    far = jnp.concatenate([after(far_parts[1], made[2], b1, live), far_parts[0]])
    x, first_t, packed = project_in(far, 2 * rows, n, made, vec, input_weight)
    upstream = jnp.concatenate(from_peers(after(cotangent, far_parts[0], made[2]) * live[:, None, None], (0, 1, 2, 3)))

    mixed, inverse, weights = attend(packed)

    db1 = []

    def hidden(token, head, carried, i):
        gk, gs, b, *made = hidden_part(token, head, carried, upstream, expand_weight, reduce_weight, b1, i)
        db1.append(b)
        return gk, gs, made

    Y, Z1, Z2 = 0, 1, 2
    piece_rows = d // 2 + d // 2
    pair_rows = 3 * (d // PIECES)
    k0, s0, (o, ds, *kept) = hidden(core, (x, mixed, output_weight, vec), None, 0)
    r0 = to_core(s0)
    k1, s1, (o, ds) = hidden(after(core, s0), None, (*kept, o, ds), 1)
    r1 = to_core(s1)
    ga = Part(k0, r0, piece_rows)
    sent, _ = slot(ids, [("half", [ga])], s1)
    k2, s2, (o, ds) = hidden(after(core, s1, *sent), None, (*kept, o, ds), 2)
    r2 = to_core(s2)
    gb = Part(k1, r1, piece_rows)
    sent, _ = slot(ids, [(Z1, [gb])], s2)
    out, d_branch, d_mixed, k3, s3, sums_mid = outer(
        after(core, s2, *sent), x, upstream, mixed, inverse, output_weight, vec, o, ds
    )
    r3 = to_core(s3)

    def homeward(a):
        blocks = [a[k * rows : (k + 1) * rows] for k in range(1, peers)]
        return blocks, [exchange(b, "seq", k + 1) for k, b in enumerate(blocks)]

    out_sent, outs = homeward(out)
    gc = Part(k2, r2, piece_rows)
    sent, got = slot(ids, [(Y, [gc])], s3)
    parts = []

    def reflect_part(token, i):
        dq, dk, dv, gk, gs = reflect(token, packed, mixed, d_mixed, weights, first_t, 2 * i)
        parts.extend([dq, dk, dv])
        return gk, gs

    p0, q0 = reflect_part(after(core, s3, *sent, *out_sent), 0)
    t0 = to_core(q0)
    wait_c = got[0]
    sent, _ = slot(ids, [(Y, [ga]), (Z2, [gb])], q0)
    p1, q1 = reflect_part(after(core, q0, wait_c, *sent, *outs), 1)
    t1 = to_core(q1)
    gd, gd2 = Part(k3, r3, pair_rows), Part(p0, t0, pair_rows)
    sent, _ = slot(ids, [(Z1, [ga, gc]), ("pick", [gd, gd2])], q1)
    p2, q2 = reflect_part(after(core, q1, *sent), 2)
    t2 = to_core(q2)
    ge1 = Part(p1, t1, pair_rows)
    sent, late_got = slot(ids, [(Y, [ge1, gd]), (Z2, [ga, gc]), (Y, [gb])], q2)
    d_tokens, small = project_back(after(x, *sent), d_branch, input_weight, vec, sums_mid, db1, parts)

    tg_sent, tgs = homeward(d_tokens)
    ge2 = Part(p2, t2, pair_rows)
    gv = Part(small, to_core(small), SMALL)
    sent1, got1 = slot(ids, [(Y, [ge2, gv]), (Z1, [ge1, gd])], small, *tg_sent, late_got[1])
    block_out = send_home(ids, live, out, [after(o, *sent1) for o in outs], slices, BF, True)
    sent2, got2 = slot(ids, [(Z1, [ge2, gv]), (Z2, [ge1, gd]), ("x", [ga, gb, gc])], *got1, block_out, *tgs[1:])
    per = d // PIECES
    spare = [1 << i for i in range(unit.bit_length() - 1)]
    tgs = [after(t, *sent2) for t in tgs]
    tokens_grad = send_home(ids, live, d_tokens, tgs, slices, F32, False)
    sent3, got3 = slot(ids, [(Z2, [ge2, gv])], *got2[:2], tokens_grad)
    ff_terms = [after(a, *sent3) for a in (sent2[2], got2[2])]
    ff_terms += [to_core(a) for a in ff_terms]
    sent4, got4 = slot(ids, [("x", [ge1, ge2, gd, gv])], *got3, *ff_terms[2:])
    ff_terms[0] = after(ff_terms[0], *sent4)
    expand_grad, reduce_grad = assemble(
        functools.partial(assemble_ff_kernel, sizes=[p.count() for p in (ga, gb, gc)]), ids, per, ff_terms, [(per, ff), (ff // PIECES, d)], "assemble_ff"
    )
    ends = [sent4[0], after(got4[0], expand_grad)]
    ends += [to_core(a) for a in ends]
    output_grad, input_grad, vectors = assemble(
        functools.partial(assemble_end_kernel, size=pair_rows), ids, per, ends, [(per, d), (per, 3 * d), (SMALL, 128)], "assemble_end"
    )
    bias_rows = vectors[8 : 8 + CHUNKS]
    vectors = vectors[:8, :per]
    if unit > 1:
        sub = vol % unit

        def add_rest(a):
            for by in spare:
                a = a + exchange(a, "vol", by)
            return a

        def cut(a, axis):
            size = a.shape[axis] // unit
            return lax.dynamic_slice_in_dim(add_rest(a), sub * size, size, axis)

        expand_grad, reduce_grad, output_grad, input_grad = [cut(a, 0) for a in (expand_grad, reduce_grad, output_grad, input_grad)]
        expand_bias_grad = cut(bias_rows.reshape(-1), 0)
        vectors = cut(vectors, 1)
    else:
        expand_bias_grad = bias_rows.reshape(-1)
    return (
        block_out, tokens_grad, vectors[0], vectors[1], input_grad, vectors[2], vectors[3], output_grad, vectors[4],
        vectors[5], vectors[6], expand_grad, expand_bias_grad, reduce_grad, vectors[7],
    )


def solution(mesh):
    rows = P("vol", "seq", None)
    return jax.shard_map(
        on_device,
        mesh=mesh,
        in_specs=(P(), P(), rows, rows) + (P(),) * 13,
        out_specs=(rows, rows, P("vol"), P("vol"), P("vol", None), P("vol"), P("vol"), P("vol", None), P("vol"), P("vol"),
                   P("vol"), P("vol", None), P("vol"), P("vol", None), P("vol")),
        check_vma=False,
    )
```

```python
import functools

import jax
import jax.numpy as jnp
from jax import lax
from jax.experimental import pallas as pl
from jax.experimental.pallas import tpu as pltpu
from jax.sharding import PartitionSpec as P

HEAD_DIM = 64
PAIR = 2 * HEAD_DIM
LOG2E = 1.4426950408889634
PIECES = 8
CHUNKS = 3
ROW = {n: i for i, n in enumerate(("ag", "ash", "qb", "zero", "vb", "ob", "mg", "ms", "rb"))}
BF = jnp.bfloat16
F32 = jnp.float32
NN = (((1,), (0,)), ((), ()))
NT = (((1,), (1,)), ((), ()))

def dot(a, b, dims):
    return lax.dot_general(a, b, dims, preferred_element_type=F32)


def params(mib=24):
    return pltpu.CompilerParams(vmem_limit_bytes=mib << 20)


def line(ref, name):
    return ref[ROW[name] : ROW[name] + 1, :]


def shape(dims, dtype=BF):
    return jax.ShapeDtypeStruct(dims, dtype)


def normal(h):
    return 0.5 + 0.5 * lax.erf(h * 0.5**0.5), jnp.exp2(h * h * (-0.5 * LOG2E)) * 0.3989422804014327


def stats(v):
    spread = v - jnp.mean(v, axis=-1, keepdims=True)
    return spread, lax.rsqrt(jnp.mean(spread * spread, axis=-1, keepdims=True) + 1e-6)


def in_kernel(x_ref, vec_ref, w_ref, *rest):
    x_out, first_t, packed = rest[-3:]
    x = x_ref[...]
    d = x.shape[1]
    spread, r = stats(x.astype(F32))
    f = (spread * r * line(vec_ref, "ag") + line(vec_ref, "ash")).astype(BF)
    x_out[...] = x
    for i, bias in enumerate(("qb", "zero", "vb")):
        packed[:, i * d : (i + 1) * d] = (dot(f, w_ref[:, i * d : (i + 1) * d], NN) + line(vec_ref, bias)).astype(BF)
    first_t[...] = f.T


def project_in(part, offset, total, before, vec, weight):
    rows, d = part.shape
    wide = weight.shape[1]
    tm = 256
    first_block = offset // tm

    def full(a):
        return pl.BlockSpec(a.shape, lambda i: (0, 0), pipeline_mode=pl.Buffered(1))

    in_specs = [pl.BlockSpec((tm, d), lambda i: (i, 0)), full(vec), full(weight)]
    args = [part, vec, weight]
    aliases = {}
    if before is not None:
        aliases = {3: 0, 4: 1, 5: 2}
        in_specs += [pl.BlockSpec(memory_space=pl.ANY)] * 3
        args += list(before)
    return pl.pallas_call(
        in_kernel,
        grid=(rows // tm,),
        in_specs=in_specs,
        out_specs=[
            pl.BlockSpec((tm, d), lambda i: (i + first_block, 0)),
            pl.BlockSpec((d, tm), lambda i: (0, i + first_block)),
            pl.BlockSpec((tm, wide), lambda i: (i + first_block, 0)),
        ],
        out_shape=[shape((total, d)), shape((d, total)), shape((total, wide))],
        input_output_aliases=aliases,
        compiler_params=params(24),
        cost_estimate=pl.CostEstimate(flops=6 * rows * d * wide, bytes_accessed=2 * (d * wide + rows * (wide + 3 * d)), transcendentals=0),
        name="project_in",
    )(*args)


def attend_kernel(q_ref, k_ref, v_ref, o_ref, inv_ref, p_ref, vx_ref, *, tq):
    n = k_ref.shape[0]
    head = 2 * pl.program_id(0)
    lane = lax.broadcasted_iota(jnp.int32, (tq, PAIR), 1)
    vx_ref[:, :PAIR] = v_ref[...]
    vx_ref[:, PAIR:] = jnp.ones((n, PAIR), BF)
    low = lax.broadcasted_iota(jnp.int32, (tq, PAIR), 1) < HEAD_DIM
    for t in range(n // tq):
        rows = pl.ds(t * tq, tq)
        q = q_ref[rows, :]
        zero = jnp.zeros_like(q)
        outs = []
        for a in range(2):
            qa = jnp.where(low, q, zero) if a == 0 else jnp.where(low, zero, q)
            s = dot(qa, k_ref[...], NT)
            top = jnp.max(s, axis=-1, keepdims=True)
            p = jnp.exp2((s - top) * (LOG2E * HEAD_DIM**-0.5)).astype(BF)
            p_ref[a, rows, :] = p
            both = dot(p, vx_ref[...], NN)
            inv = 1.0 / both[:, PAIR:]
            outs.append((both[:, :PAIR] * inv, inv))
        o_ref[rows, :] = jnp.where(low, outs[0][0], outs[1][0]).astype(BF)
        inv_ref[rows, :] = jnp.where(lane == head, outs[0][1], jnp.where(lane == head + 1, outs[1][1], inv_ref[rows, :]))


def attend(packed):
    n, w = packed.shape
    d = w // 3
    hp = d // PAIR

    def cols(off):
        return pl.BlockSpec((n, PAIR), lambda h: (0, h + off))

    return pl.pallas_call(
        functools.partial(attend_kernel, tq=128),
        grid=(hp,),
        in_specs=[cols(0), cols(hp), cols(2 * hp)],
        out_specs=[cols(0), pl.BlockSpec((n, PAIR), lambda h: (0, 0)), pl.BlockSpec((2, n, n), lambda h: (h, 0, 0))],
        out_shape=[shape((n, d)), shape((n, PAIR), F32), shape((2 * hp, n, n))],
        scratch_shapes=[pltpu.VMEM((n, 2 * PAIR), BF)],
        compiler_params=params(40),
        cost_estimate=pl.CostEstimate(flops=16 * n * n * d, bytes_accessed=4 * n * n * hp, transcendentals=0),
        name="attend",
    )(packed, packed, packed)


WHOLE = pl.BlockSpec(memory_space=pltpu.VMEM)
FAR = pl.BlockSpec(memory_space=pltpu.HBM)


def transpose_rows(block, out, cols):
    t = block.T
    d = t.shape[0]
    half = d // PIECES // 2
    for h in range(2):
        for v in range(PIECES):
            at = (2 * v + h) * half
            to = (h * PIECES + v) * half
            out[to : to + half, cols] = t[at : at + half]


def core_rows(ref, which):
    half = ref.shape[0] // 2
    return ref[pl.ds(pl.multiple_of(which * half, half), half), :]


def piece_blocks(g, ref, first):
    rows = g.shape[0] // PIECES
    for k in range(g.shape[1] // 128):
        at = (first + k) * rows
        ref[:, at : at + rows, :] = g[:, k * 128 : (k + 1) * 128].reshape(PIECES, rows, 128)


def middle_of(x_ref, mix_ref, wo_ref, vec_ref, rows):
    return x_ref[rows, :].astype(F32) + dot(mix_ref[rows, :], wo_ref[...], NN) + line(vec_ref, "ob")


def hidden_kernel(c_ref, *refs, i, head, tm, sub):
    refs = list(refs)
    take = lambda k: [refs.pop(0) for _ in range(k)]
    if head:
        x_ref, mix_ref, wo_ref, vec_ref = take(4)
    else:
        sec_ref, sec_t, up_t, o_in, ds_in = take(5)
    up_ref, w1_ref, w2_ref, b1_ref, gk_ref, gs_ref, db1_ref, o_ref, ds_ref = take(9)
    if head:
        sec_ref, sec_t, up_t = take(3)
    act, dh = take(2)
    n, d = up_ref.shape
    wide = act.shape[1]

    def shares(first, last):
        return [slice((v * CHUNKS + i) * 128, (v * CHUNKS + i + 1) * 128) for v in range(first // 128, last // 128)]

    def columns(first, last):
        return jnp.concatenate([w1_ref[:, at] for at in shares(first, last)], axis=1)

    def lines(first, last):
        return jnp.concatenate([w2_ref[at, :] for at in shares(first, last)], axis=0)

    if head:
        for t in range(n // 256):
            rows = slice(t * 256, (t + 1) * 256)
            spread, r = stats(middle_of(x_ref, mix_ref, wo_ref, vec_ref, rows))
            sec = (spread * r * line(vec_ref, "mg") + line(vec_ref, "ms")).astype(BF)
            sec_ref[rows, :] = sec
            transpose_rows(sec, sec_t, rows)
            up_t[:, rows] = up_ref[rows, :].T
    db1_ref[...] = jnp.zeros_like(db1_ref)
    for first in range(0, wide, sub):
        cols = slice(first, first + sub)
        bias = jnp.concatenate([b1_ref[v * CHUNKS + i : v * CHUNKS + i + 1, :] for v in range(first // 128, (first + sub) // 128)], axis=1)

        def tile(t, _):
            rows = pl.ds(pl.multiple_of(t * tm, tm), tm)
            h = dot(sec_ref[rows, :], columns(first, first + sub), NN) + bias
            da = dot(up_ref[rows, :], lines(first, first + sub), NT)
            cdf, pdf = normal(h)
            act[rows, cols] = (h * cdf).astype(BF)
            dhv = da * (cdf + h * pdf)
            dh[rows, cols] = dhv.astype(BF)
            db1_ref[:, cols] += jnp.sum(dhv, axis=0, keepdims=True)
            return 0

        lax.fori_loop(0, n // tm, tile, 0)
    base = PIECES * (d // PIECES // 2)
    c = c_ref[0]
    for ref, mine in ((gs_ref, 1 - c), (gk_ref, c)):
        piece_blocks(dot(core_rows(sec_t, mine), dh[...], NN).astype(BF), ref, 0)
        g = dot(core_rows(up_t, mine), act[...], NN).astype(BF)
        for k in range(wide // 128):
            ref[k, base:, :] = g[:, k * 128 : (k + 1) * 128]

    def gather(t, _):
        rows = pl.ds(pl.multiple_of(t * tm, tm), tm)
        o = dot(act[rows, :], lines(0, wide), NN)
        o_ref[rows, :] = o if head else o_in[rows, :] + o
        ds = dot(dh[rows, :], columns(0, wide), NT)
        ds_ref[rows, :] = ds if head else ds_in[rows, :] + ds
        return 0

    lax.fori_loop(0, n // tm, gather, 0)


def hidden_part(core, head, carried, up, w1, w2, b1, i, tm=512, sub=512):
    n, d = up.shape
    wide = 128 * PIECES
    assert wide * CHUNKS == w1.shape[1]
    g = (PIECES, PIECES * (d // PIECES // 2) + d // 2, 128)
    args = list(head) if head else list(carried)
    made = [shape(g), shape(g), shape((1, wide), F32), shape((n, d), F32), shape((n, d), F32)]
    if head:
        made += [shape((n, d)), shape((d, n)), shape((d, n))]
    return pl.pallas_call(
        functools.partial(hidden_kernel, i=i, head=bool(head), tm=tm, sub=sub),
        in_specs=[pl.BlockSpec(memory_space=pltpu.SMEM)] + [WHOLE] * (len(args) + 4),
        out_specs=[WHOLE] * len(made),
        out_shape=made,
        input_output_aliases={} if head else {4: 3, 5: 4},
        scratch_shapes=[pltpu.VMEM((n, wide), BF), pltpu.VMEM((n, wide), BF)],
        compiler_params=params(10),
        cost_estimate=pl.CostEstimate(flops=24 * n * d * wide, bytes_accessed=8 * d * wide, transcendentals=0),
        name="hidden",
    )(core, *args, up, w1, w2, b1)


def outer_kernel(c_ref, x_ref, up_ref, mix_ref, li_ref, wo_ref, vec_ref, o_ref, ds_ref, out_ref, dbr_ref, do_ref, gk_ref, gs_ref, sums_ref, mix_t, *, tm):
    n, d = x_ref.shape
    sums = None
    lanes = lax.broadcasted_iota(jnp.int32, (PAIR, d), 1) // HEAD_DIM
    spread_heads = (lanes == lax.broadcasted_iota(jnp.int32, (PAIR, d), 0)).astype(BF)
    for t in range(n // tm):
        rows = slice(t * tm, (t + 1) * tm)
        m = middle_of(x_ref, mix_ref, wo_ref, vec_ref, rows)
        spread, r = stats(m)
        nv = spread * r
        up = up_ref[rows, :].astype(F32)
        transpose_rows(mix_ref[rows, :], mix_t, rows)
        dy = ds_ref[rows, :]
        dyg = dy * line(vec_ref, "mg")
        dm = up + r * (dyg - jnp.mean(dyg, axis=-1, keepdims=True) - nv * jnp.mean(dyg * nv, axis=-1, keepdims=True))
        db = dm.astype(BF)
        dbr_ref[rows, :] = db
        out_ref[rows, :] = (m + o_ref[rows, :] + line(vec_ref, "rb")).astype(BF)
        li = li_ref[rows, :]
        coarse = li.astype(BF)
        fine = (li - coarse.astype(F32)).astype(BF)
        scale = dot(coarse, spread_heads, NN) + dot(fine, spread_heads, NN)
        do_ref[rows, :] = (dot(db, wo_ref[...], NT) * scale).astype(BF)
        part = [jnp.sum(v, axis=0, keepdims=True) for v in (db.astype(F32), dy * nv, dy, up)]
        sums = part if sums is None else [a + b for a, b in zip(sums, part)]
    sums_ref[...] = jnp.concatenate(sums + [jnp.zeros((4, d), F32)], axis=0)
    for ref, mine in ((gs_ref, 1 - c_ref[0]), (gk_ref, c_ref[0])):
        piece_blocks(dot(core_rows(mix_t, mine), dbr_ref[...], NN).astype(BF), ref, 0)


def outer(core, x, up, mix, li, wo, vec, o, ds, tm=256):
    n, d = x.shape
    g = (PIECES, d // 128 * (d // PIECES // 2), 128)
    return pl.pallas_call(
        functools.partial(outer_kernel, tm=tm),
        in_specs=[pl.BlockSpec(memory_space=pltpu.SMEM)] + [WHOLE] * 8,
        out_specs=[WHOLE] * 6,
        out_shape=[shape((n, d))] * 3 + [shape(g), shape(g), shape((8, d), F32)],
        scratch_shapes=[pltpu.VMEM((d, n), BF)],
        compiler_params=params(8),
        cost_estimate=pl.CostEstimate(flops=24 * n * d * d, bytes_accessed=20 * n * d, transcendentals=0),
        name="outer",
    )(core, x, up, mix, li, wo, vec, o, ds)


def by_piece(g):
    rows = g.shape[0] // PIECES
    return [g[:, i : i + 128].reshape(PIECES, rows, 128) for i in range(0, g.shape[1], 128)]


def reflect_kernel(c_ref, q_ref, k_ref, v_ref, o_ref, do_ref, p_ref, ft_ref, dq_ref, dk_ref, dv_ref, gk_ref, gs_ref, ds_ref, *, tq):
    n = k_ref.shape[0]
    low = lax.broadcasted_iota(jnp.int32, (tq, PAIR), 1) < HEAD_DIM
    q_t = q_ref[...].T
    do_t = do_ref[...].T
    scale = HEAD_DIM**-0.5
    dks, dvs = [], []
    for a in range(2):
        for t in range(n // tq):
            rows = pl.ds(t * tq, tq)
            do = do_ref[rows, :]
            zero = jnp.zeros_like(do)
            doa = jnp.where(low, do, zero) if a == 0 else jnp.where(low, zero, do)
            delta = jnp.sum(doa.astype(F32) * o_ref[rows, :].astype(F32), axis=-1, keepdims=True)
            dp = dot(doa, v_ref[...], NT)
            ds = (p_ref[a, rows, :].astype(F32) * (dp - delta)).astype(BF)
            ds_ref[rows, :] = ds
            dq = (dot(ds, k_ref[...], NN) * scale).astype(BF)
            dq_ref[rows, :] = dq if a == 0 else jnp.where(low, dq_ref[rows, :], dq)
        part = slice(HEAD_DIM * a, HEAD_DIM * (a + 1))
        dvs.append(dot(do_t[part], p_ref[a], NN))
        dks.append(dot(q_t[part], ds_ref[...], NN) * scale)
    dv = jnp.concatenate(dvs, axis=0).astype(BF).T
    dk = jnp.concatenate(dks, axis=0).astype(BF).T
    dv_ref[...] = dv
    dk_ref[...] = dk
    g = dot(ft_ref[...], jnp.concatenate([dq_ref[...], dk, dv], axis=1), NN).astype(BF)
    per = g.shape[0] // PIECES
    h = pl.program_id(0)
    for step, ref in enumerate((gs_ref, gk_ref)):

        @pl.when(h == step)
        def _():
            for i, block in enumerate(by_piece(g)):
                ref[:, i * per : (i + 1) * per, :] = block


def reflect(core, packed, o, do, p, first_t, start):
    n, w = packed.shape
    d = w // 3
    hp = d // PAIR

    def which(h, c):
        return (h + 1 - c[0]) % 2

    def cols(off):
        return pl.BlockSpec((n, PAIR), lambda h, c: (0, which(h, c) + off))

    g = (PIECES, 3 * (d // PIECES), 128)
    piece = pl.BlockSpec(g, lambda h, c: (0, 0, 0), pipeline_mode=pl.Buffered(1))
    return pl.pallas_call(
        functools.partial(reflect_kernel, tq=256),
        grid_spec=pltpu.PrefetchScalarGridSpec(
            num_scalar_prefetch=1,
            grid=(2,),
            in_specs=[
                cols(start), cols(start + hp), cols(start + 2 * hp), cols(start), cols(start),
                pl.BlockSpec((2, n, n), lambda h, c: (which(h, c) + start, 0, 0)),
                pl.BlockSpec((d, n), lambda h, c: (0, 0), pipeline_mode=pl.Buffered(1)),
            ],
            out_specs=[cols(0)] * 3 + [piece] * 2,
            scratch_shapes=[pltpu.VMEM((n, n), BF)],
        ),
        out_shape=[shape((n, 2 * PAIR))] * 3 + [shape(g)] * 2,
        compiler_params=params(27),
        cost_estimate=pl.CostEstimate(flops=160 * n * n * PAIR, bytes_accessed=8 * n * n, transcendentals=0),
        name="reflect",
    )(core, packed, packed, packed, o, do, p, first_t)


SMALL = 16


def back_kernel(*refs, chunks):
    x_ref, dbr_ref, w_ref, vec_in, mid_ref = refs[:5]
    db1 = refs[5 : 5 + CHUNKS]
    parts = refs[5 + CHUNKS : 5 + CHUNKS + 3 * chunks]
    tg_ref, small_ref, sums = refs[5 + CHUNKS + 3 * chunks :]

    @pl.when(pl.program_id(0) == 0)
    def _():
        sums[...] = jnp.zeros_like(sums)

    d = x_ref.shape[1]
    cw = d // chunks
    dy = None
    for i in range(3 * chunks):
        which, chunk = i % 3, i // 3
        at = which * d + chunk * cw
        part = dot(parts[i][...], w_ref[:, at : at + cw], NT)
        dy = part if dy is None else dy + part
        row = {0: 2, 2: 3}.get(which)
        if row is not None:
            sums[row : row + 1, chunk * cw : (chunk + 1) * cw] += jnp.sum(parts[i][...].astype(F32), axis=0, keepdims=True)
    spread, r = stats(x_ref[...].astype(F32))
    nv = spread * r
    dyg = dy * line(vec_in, "ag")
    dx = r * (dyg - jnp.mean(dyg, axis=-1, keepdims=True) - nv * jnp.mean(dyg * nv, axis=-1, keepdims=True))
    tg_ref[...] = (dbr_ref[...].astype(F32) + dx).astype(BF)
    sums[0:1, :] += jnp.sum(dy * nv, axis=0, keepdims=True)
    sums[1:2, :] += jnp.sum(dy, axis=0, keepdims=True)

    @pl.when(pl.program_id(0) == pl.num_programs(0) - 1)
    def _():
        per = d // PIECES
        sums[4:8, :] = mid_ref[0:4, :]
        rows = sums[...]
        for v in range(PIECES):
            vectors = jnp.concatenate([rows[:, v * per : (v + 1) * per], jnp.zeros((8, 128 - per), F32)], axis=1)
            biases = [b[:, v * 128 : (v + 1) * 128] for b in db1]
            piece = jnp.concatenate([vectors] + biases + [jnp.zeros((SMALL - 8 - CHUNKS, 128), F32)], axis=0)
            small_ref[v * SMALL : (v + 1) * SMALL, :] = piece.astype(BF)


def project_back(x, dbr, w, vec, mids, db1, parts):
    n, d = x.shape
    tm = 256
    row = pl.BlockSpec((tm, d), lambda i: (i, 0))

    def full(*s):
        return pl.BlockSpec(s, lambda i: (0, 0), pipeline_mode=pl.Buffered(1))

    chunks = len(parts) // 3
    return pl.pallas_call(
        functools.partial(back_kernel, chunks=chunks),
        grid=(n // tm,),
        in_specs=[row, row, full(d, 3 * d), full(*vec.shape), full(*mids.shape)]
        + [full(*b.shape) for b in db1]
        + [pl.BlockSpec((tm, d // chunks), lambda i: (i, 0))] * (3 * chunks),
        out_specs=[row, full(PIECES * SMALL, 128)],
        out_shape=[shape((n, d)), shape((PIECES * SMALL, 128))],
        scratch_shapes=[pltpu.VMEM((8, d), F32)],
        compiler_params=params(24),
        cost_estimate=pl.CostEstimate(flops=12 * n * d * d, bytes_accessed=16 * n * d, transcendentals=0),
        name="project_back",
    )(x, dbr, w, vec, mids, *db1, *parts)


def exchange(x, axis, by):
    count = lax.axis_size(axis)
    return lax.ppermute(x, axis, [(i, i ^ by) for i in range(count)])


def to_core(g):
    return exchange(g, "seq", 1)


def pick(x, index, axis=0):
    return lax.dynamic_index_in_dim(x, index, axis, keepdims=False)


def after(x, *others):
    return lax.optimization_barrier((x,) + others)[0]


class Part:
    def __init__(self, held, received, rows):
        self.held = (held.reshape(-1, 128), 0)
        self.received = (received.reshape(-1, 128), 0)
        self.rows = rows
        self.open = [0, 1, 2]

    def count(self):
        return self.rows << len(self.open)


def slot_kernel(ids_ref, *refs, items, inputs):
    ins, outs = refs[:inputs], refs[inputs:]

    def read(term, at, count):
        ref, offset = term
        return ins[ref][pl.ds(at + offset, count), :].astype(F32)

    step = 16
    for kind, *rest in items:
        if kind == "split":
            held, received, groups, size, bit, (send, to), keep = rest
            mine = ids_ref[bit]
            for a in range(groups):
                own = pl.multiple_of((2 * a + mine) * size, step)
                other = pl.multiple_of((2 * a + 1 - mine) * size, step)
                outs[send][to + a * size : to + (a + 1) * size, :] = (read(held, other, size) + read(received, other, size)).astype(BF)
                outs[keep][a * size : (a + 1) * size, :] = (read(held, own, size) + read(received, own, size)).astype(BF)
        elif kind == "sum":
            held, received, size, (send, to) = rest
            outs[send][to : to + size, :] = (read(held, 0, size) + read(received, 0, size)).astype(BF)
        else:
            first, second, size, bit, (send, to), keep = rest
            for mine in (0, 1):

                @pl.when(ids_ref[bit] == mine)
                def _():
                    own, other = (first, second) if mine == 0 else (second, first)
                    outs[send][to : to + size, :] = (read(other[0], 0, size) + read(other[1], 0, size)).astype(BF)
                    outs[keep][...] = (read(own[0], 0, size) + read(own[1], 0, size)).astype(BF)


def slot(ids, exchanges, *tokens):
    arrays, items, sizes, moves = [], [], [], []

    def use(term):
        for i, a in enumerate(arrays):
            if a is term[0]:
                return i, term[1]
        arrays.append(term[0])
        return len(arrays) - 1, term[1]

    for stage, parts in exchanges:
        send, to = len(sizes), 0
        sizes.append(0)
        placed = []
        if stage == "pick":
            one, two = parts
            size = one.count()
            items.append(("pick", (use(one.held), use(one.received)), (use(two.held), use(two.received)), size, 1, (send, 0), len(sizes)))
            placed.append((one, len(sizes), 0, 0))
            sizes.append(size)
            to = size
        else:
            for p in parts:
                held, received = use(p.held), use(p.received)
                if stage == "x":
                    items.append(("sum", held, received, p.count(), (send, to)))
                    placed.append((p, send, to, to))
                    to += p.count()
                    continue
                if stage == "half":
                    groups, bit = 1 << len(p.open), 1
                else:
                    groups, bit = 1 << (len(p.open) - 1 - p.open.index(stage)), 2 + stage
                size = p.count() // (2 * groups)
                items.append(("split", held, received, groups, size, bit, (send, to), len(sizes)))
                placed.append((p, len(sizes), 0, to))
                sizes.append(groups * size)
                to += groups * size
                if stage == "half":
                    p.rows //= 2
                else:
                    p.open.remove(stage)
        sizes[send] = to
        moves.append((stage, send, placed))

    if tokens:
        arrays = list(lax.optimization_barrier(tuple(arrays) + tokens)[: len(arrays)])
    whole = pl.BlockSpec(memory_space=pltpu.VMEM)
    outs = pl.pallas_call(
        functools.partial(slot_kernel, items=items, inputs=len(arrays)),
        in_specs=[pl.BlockSpec(memory_space=pltpu.SMEM)] + [whole] * len(arrays),
        out_specs=[whole] * len(sizes),
        out_shape=[shape((size, 128)) for size in sizes],
        compiler_params=params(2),
        cost_estimate=pl.CostEstimate(flops=0, bytes_accessed=512 * sum(sizes), transcendentals=0),
        name="slot",
    )(ids, *arrays)
    unit = lax.axis_size("vol") // PIECES
    sent, received = [], []
    for stage, send, placed in moves:
        if stage in ("half", "pick", "x"):
            got = exchange(outs[send], "seq", 2)
        else:
            got = exchange(outs[send], "vol", unit << stage)
        sent.append(outs[send])
        received.append(got)
        for p, keep, at, to in placed:
            p.held = (outs[keep], at)
            p.received = (got, to)
    return sent, received


def home_kernel(ids_ref, live_ref, *refs, mask):
    out_ref = refs[-1]
    for k, ref in enumerate(refs[:-1]):

        @pl.when(pl.program_id(0) == k)
        def _():
            value = ref[...].astype(F32)
            if mask:
                value = value * live_ref[ids_ref[5] ^ k]
            out_ref[...] = value.astype(out_ref.dtype)


def send_home(ids, live, own, others, slices, dtype, mask):
    rows, d = others[0].shape
    return pl.pallas_call(
        functools.partial(home_kernel, mask=mask),
        grid_spec=pltpu.PrefetchScalarGridSpec(
            num_scalar_prefetch=2,
            grid=(slices,),
            in_specs=[pl.BlockSpec((rows, d), lambda k, i, l: (0, 0), pipeline_mode=pl.Buffered(1))] * slices,
            out_specs=pl.BlockSpec((None, rows, d), lambda k, i, l: (k ^ i[5], 0, 0)),
        ),
        out_shape=shape((slices, rows, d), dtype),
        compiler_params=params(8),
        cost_estimate=pl.CostEstimate(flops=0, bytes_accessed=6 * slices * rows * d, transcendentals=0),
        name="home",
    )(ids, live, own, *others)


def assemble_ff_kernel(ids_ref, *refs, per, sizes):
    terms, middle = refs[:4], refs[4:8]
    expand_ref, reduce_ref = refs[8:]
    c = ids_ref[0]

    def first_layer(i, core, value):
        size = per // 2
        for k in range(PIECES):
            at = (k * CHUNKS + i) * 128
            expand_ref[pl.ds(pl.multiple_of(core * size, size), size), at : at + 128] = value[k * size : (k + 1) * size, :]

    def second_layer(i, core, value):
        d = value.shape[0]
        reduce_ref[i * 128 : (i + 1) * 128, pl.ds(pl.multiple_of(core * d, 128), d)] = value.T

    half = per // 2 * PIECES
    for core, (own, partner), (one_b, two_b) in ((c, terms[:2], middle[:2]), (1 - c, terms[2:], middle[2:])):
        for x in (0, 1):

            @pl.when(ids_ref[1] == x)
            def _():
                one, two = (own, partner) if x == 0 else (partner, own)
                first_layer(0, core, one[: sizes[0], :].astype(F32))
                second_layer(0, core, two[: sizes[0], :].astype(F32))

        value = one_b[...].astype(F32) + two_b[...].astype(F32)
        first_layer(1, core, value[:half])
        second_layer(1, core, value[half:])
        rows = slice(sizes[0], sizes[0] + sizes[1])
        value = own[rows, :].astype(F32) + partner[rows, :].astype(F32)
        first_layer(2, core, value[:half])
        second_layer(2, core, value[half:])


def assemble_end_kernel(ids_ref, *refs, per, size):
    terms = refs[:4]
    output_ref, input_ref, vector_ref = refs[4:]
    c = ids_ref[0]
    d = PIECES * per

    def output_part(core, value):
        part = per // 2
        for k in range(d // 128):
            rows = pl.ds(pl.multiple_of(core * part, part), part)
            output_ref[rows, k * 128 : (k + 1) * 128] = value[k * part : (k + 1) * part, :]

    def pair_part(i, core, value):
        for k in range(3):
            at = pl.multiple_of(k * d + (2 * i + core) * 128, 128)
            input_ref[:, pl.ds(at, 128)] = value[k * per : (k + 1) * per, :]

    for core, (own, partner) in ((c, terms[:2]), (1 - c, terms[2:])):
        for i in (1, 2):
            rows = slice((i - 1) * size, i * size)
            pair_part(i, core, own[rows, :].astype(F32) + partner[rows, :].astype(F32))
        for x in (0, 1):

            @pl.when(ids_ref[1] == x)
            def _():
                one, two = (own, partner) if x == 0 else (partner, own)
                output_part(core, one[2 * size : 3 * size, :].astype(F32))
                pair_part(0, core, two[2 * size : 3 * size, :].astype(F32))

    vector_ref[...] = terms[0][3 * size :, :].astype(F32) + terms[1][3 * size :, :].astype(F32)


def assemble(kernel, ids, per, arrays, outs, name):
    whole = pl.BlockSpec(memory_space=pltpu.VMEM)
    return pl.pallas_call(
        functools.partial(kernel, per=per),
        in_specs=[pl.BlockSpec(memory_space=pltpu.SMEM)] + [whole] * len(arrays),
        out_specs=[whole] * len(outs),
        out_shape=[shape(o, F32) for o in outs],
        compiler_params=params(8),
        name=name,
    )(ids, *arrays)


def on_device(
    volume_slices, volume_owner, tokens, cotangent, attend_gain, attend_shift, input_weight, query_bias, value_bias,
    output_weight, output_bias, mixer_gain, mixer_shift, expand_weight, expand_bias, reduce_weight, reduce_bias,
):
    slices, rows, d = tokens.shape
    ff = expand_weight.shape[1]
    nv = lax.axis_size("vol")
    peers = lax.axis_size("seq")
    me = lax.axis_index("seq")
    core_id = me % 2
    x_id = (me // 2) % 2
    core = core_id.astype(jnp.int32).reshape(1)
    n = rows * peers
    vol = lax.axis_index("vol")
    unit = nv // PIECES
    ids = jnp.stack([core_id, x_id, (vol // unit) % 2, (vol // (2 * unit)) % 2, (vol // (4 * unit)) % 2, me]).astype(jnp.int32)

    def from_peers(x, ks):
        parts = [pick(x, me ^ k) for k in ks]
        return [p if k == 0 else exchange(p, "seq", k) for p, k in zip(parts, ks)]

    far_parts = from_peers(tokens, (3, 2))
    near_parts = from_peers(tokens, (0, 1))
    zero = jnp.zeros((d,), BF)
    vec = jnp.concatenate(
        [attend_gain, attend_shift, query_bias, zero, value_bias, output_bias, mixer_gain, mixer_shift, reduce_bias] + [zero] * 7
    ).astype(F32).reshape(16, d)
    wide = ff // CHUNKS
    lanes = wide // PIECES
    b1 = expand_bias.astype(F32).reshape(ff // 128, 128)
    load = jnp.sum(jnp.where(volume_owner == lax.axis_index("vol"), volume_slices, 0))
    live = (jnp.arange(slices) < load).astype(BF)

    made = project_in(jnp.concatenate(near_parts), 0, n, None, vec, input_weight)
    far = jnp.concatenate([after(far_parts[1], made[2], b1, live), far_parts[0]])
    x, first_t, packed = project_in(far, 2 * rows, n, made, vec, input_weight)
    upstream = jnp.concatenate(from_peers(after(cotangent, far_parts[0], made[2]) * live[:, None, None], (0, 1, 2, 3)))

    mixed, inverse, weights = attend(packed)

    db1 = []

    def hidden(token, head, carried, i):
        gk, gs, b, *made = hidden_part(token, head, carried, upstream, expand_weight, reduce_weight, b1, i)
        db1.append(b)
        return gk, gs, made

    Y, Z1, Z2 = 0, 1, 2
    piece_rows = d // 2 + d // 2
    pair_rows = 3 * (d // PIECES)
    k0, s0, (o, ds, *kept) = hidden(core, (x, mixed, output_weight, vec), None, 0)
    r0 = to_core(s0)
    k1, s1, (o, ds) = hidden(after(core, s0), None, (*kept, o, ds), 1)
    r1 = to_core(s1)
    ga = Part(k0, r0, piece_rows)
    sent, _ = slot(ids, [("half", [ga])], s1)
    k2, s2, (o, ds) = hidden(after(core, s1, *sent), None, (*kept, o, ds), 2)
    r2 = to_core(s2)
    gb = Part(k1, r1, piece_rows)
    sent, _ = slot(ids, [(Z1, [gb])], s2)
    out, d_branch, d_mixed, k3, s3, sums_mid = outer(
        after(core, s2, *sent), x, upstream, mixed, inverse, output_weight, vec, o, ds
    )
    r3 = to_core(s3)

    def homeward(a):
        blocks = [a[k * rows : (k + 1) * rows] for k in range(1, peers)]
        return blocks, [exchange(b, "seq", k + 1) for k, b in enumerate(blocks)]

    out_sent, outs = homeward(out)
    gc = Part(k2, r2, piece_rows)
    sent, got = slot(ids, [(Y, [gc])], s3)
    parts = []

    def reflect_part(token, i):
        dq, dk, dv, gk, gs = reflect(token, packed, mixed, d_mixed, weights, first_t, 2 * i)
        parts.extend([dq, dk, dv])
        return gk, gs

    p0, q0 = reflect_part(after(core, s3, *sent, *out_sent), 0)
    t0 = to_core(q0)
    wait_c = got[0]
    sent, _ = slot(ids, [(Y, [ga]), (Z2, [gb])], q0)
    p1, q1 = reflect_part(after(core, q0, wait_c, *sent, *outs), 1)
    t1 = to_core(q1)
    gd, gd2 = Part(k3, r3, pair_rows), Part(p0, t0, pair_rows)
    sent, _ = slot(ids, [(Z1, [ga, gc]), ("pick", [gd, gd2])], q1)
    p2, q2 = reflect_part(after(core, q1, *sent), 2)
    t2 = to_core(q2)
    ge1 = Part(p1, t1, pair_rows)
    sent, late_got = slot(ids, [(Y, [ge1, gd]), (Z2, [ga, gc])], q2)
    d_tokens, small = project_back(after(x, *sent), d_branch, input_weight, vec, sums_mid, db1, parts)

    tg_sent, tgs = homeward(d_tokens)
    ge2 = Part(p2, t2, pair_rows)
    gv = Part(small, to_core(small), SMALL)
    sent1, got1 = slot(ids, [(Y, [ge2, gv]), (Z1, [ge1, gd])], small, *tg_sent, late_got[1])
    block_out = send_home(ids, live, out, [after(o, *sent1) for o in outs], slices, BF, True)
    sent2, got2 = slot(ids, [(Z1, [ge2, gv]), (Z2, [ge1, gd]), (Y, [gb]), ("x", [ga, gc])], *got1, block_out, *tgs[1:])
    per = d // PIECES
    spare = [1 << i for i in range(unit.bit_length() - 1)]
    tgs = [after(t, *sent2) for t in tgs]
    tokens_grad = send_home(ids, live, d_tokens, tgs, slices, F32, False)
    sent3, got3 = slot(ids, [(Z2, [ge2, gv]), ("x", [gb])], *got2[:3], tokens_grad)
    ff_terms = [after(a, *sent3) for a in (sent2[3], got2[3])]
    ff_terms += [to_core(a) for a in ff_terms]
    sent4, got4 = slot(ids, [("x", [ge1, ge2, gd, gv])], got3[0], *ff_terms[2:])
    gb_terms = [after(a, *sent4) for a in (sent3[1], got3[1])]
    gb_terms += [to_core(a) for a in gb_terms]
    expand_grad, reduce_grad = assemble(
        functools.partial(assemble_ff_kernel, sizes=[ga.count(), gc.count()]), ids, per, ff_terms + gb_terms, [(per, ff), (ff // PIECES, d)], "assemble_ff"
    )
    ends = [sent4[0], after(got4[0], expand_grad)]
    ends += [to_core(a) for a in ends]
    output_grad, input_grad, vectors = assemble(
        functools.partial(assemble_end_kernel, size=pair_rows), ids, per, ends, [(per, d), (per, 3 * d), (SMALL, 128)], "assemble_end"
    )
    bias_rows = vectors[8 : 8 + CHUNKS]
    vectors = vectors[:8, :per]
    if unit > 1:
        sub = vol % unit

        def add_rest(a):
            for by in spare:
                a = a + exchange(a, "vol", by)
            return a

        def cut(a, axis):
            size = a.shape[axis] // unit
            return lax.dynamic_slice_in_dim(add_rest(a), sub * size, size, axis)

        expand_grad, reduce_grad, output_grad, input_grad = [cut(a, 0) for a in (expand_grad, reduce_grad, output_grad, input_grad)]
        expand_bias_grad = cut(bias_rows.reshape(-1), 0)
        vectors = cut(vectors, 1)
    else:
        expand_bias_grad = bias_rows.reshape(-1)
    return (
        block_out, tokens_grad, vectors[0], vectors[1], input_grad, vectors[2], vectors[3], output_grad, vectors[4],
        vectors[5], vectors[6], expand_grad, expand_bias_grad, reduce_grad, vectors[7],
    )


def solution(mesh):
    rows = P("vol", "seq", None)
    return jax.shard_map(
        on_device,
        mesh=mesh,
        in_specs=(P(), P(), rows, rows) + (P(),) * 13,
        out_specs=(rows, rows, P("vol"), P("vol"), P("vol", None), P("vol"), P("vol"), P("vol", None), P("vol"), P("vol"),
                   P("vol"), P("vol", None), P("vol"), P("vol", None), P("vol")),
        check_vma=False,
    )
```

```python
import functools

import jax
import jax.numpy as jnp
from jax import lax
from jax.experimental import pallas as pl
from jax.experimental.pallas import tpu as pltpu
from jax.sharding import PartitionSpec as P

HEAD_DIM = 64
PAIR = 2 * HEAD_DIM
LOG2E = 1.4426950408889634
PIECES = 8
CHUNKS = 3
ROW = {n: i for i, n in enumerate(("ag", "ash", "qb", "zero", "vb", "ob", "mg", "ms", "rb"))}
BF = jnp.bfloat16
F32 = jnp.float32
NN = (((1,), (0,)), ((), ()))
NT = (((1,), (1,)), ((), ()))

def dot(a, b, dims):
    return lax.dot_general(a, b, dims, preferred_element_type=F32)


def params(mib=24):
    return pltpu.CompilerParams(vmem_limit_bytes=mib << 20)


def line(ref, name):
    return ref[ROW[name] : ROW[name] + 1, :]


def shape(dims, dtype=BF):
    return jax.ShapeDtypeStruct(dims, dtype)


def normal(h):
    return 0.5 + 0.5 * lax.erf(h * 0.5**0.5), jnp.exp2(h * h * (-0.5 * LOG2E)) * 0.3989422804014327


def stats(v):
    spread = v - jnp.mean(v, axis=-1, keepdims=True)
    return spread, lax.rsqrt(jnp.mean(spread * spread, axis=-1, keepdims=True) + 1e-6)


def in_kernel(x_ref, vec_ref, w_ref, *rest):
    x_out, first_t, packed = rest[-3:]
    x = x_ref[...]
    d = x.shape[1]
    spread, r = stats(x.astype(F32))
    f = (spread * r * line(vec_ref, "ag") + line(vec_ref, "ash")).astype(BF)
    x_out[...] = x
    for i, bias in enumerate(("qb", "zero", "vb")):
        packed[:, i * d : (i + 1) * d] = (dot(f, w_ref[:, i * d : (i + 1) * d], NN) + line(vec_ref, bias)).astype(BF)
    first_t[...] = f.T


def project_in(part, offset, total, before, vec, weight):
    rows, d = part.shape
    wide = weight.shape[1]
    tm = 256
    first_block = offset // tm

    def full(a):
        return pl.BlockSpec(a.shape, lambda i: (0, 0), pipeline_mode=pl.Buffered(1))

    in_specs = [pl.BlockSpec((tm, d), lambda i: (i, 0)), full(vec), full(weight)]
    args = [part, vec, weight]
    aliases = {}
    if before is not None:
        aliases = {3: 0, 4: 1, 5: 2}
        in_specs += [pl.BlockSpec(memory_space=pl.ANY)] * 3
        args += list(before)
    return pl.pallas_call(
        in_kernel,
        grid=(rows // tm,),
        in_specs=in_specs,
        out_specs=[
            pl.BlockSpec((tm, d), lambda i: (i + first_block, 0)),
            pl.BlockSpec((d, tm), lambda i: (0, i + first_block)),
            pl.BlockSpec((tm, wide), lambda i: (i + first_block, 0)),
        ],
        out_shape=[shape((total, d)), shape((d, total)), shape((total, wide))],
        input_output_aliases=aliases,
        compiler_params=params(24),
        cost_estimate=pl.CostEstimate(flops=6 * rows * d * wide, bytes_accessed=2 * (d * wide + rows * (wide + 3 * d)), transcendentals=0),
        name="project_in",
    )(*args)


def attend_kernel(q_ref, k_ref, v_ref, o_ref, inv_ref, p_ref, vx_ref, *, tq):
    n = k_ref.shape[0]
    head = 2 * pl.program_id(0)
    lane = lax.broadcasted_iota(jnp.int32, (tq, PAIR), 1)
    vx_ref[:, :PAIR] = v_ref[...]
    vx_ref[:, PAIR:] = jnp.ones((n, PAIR), BF)
    low = lax.broadcasted_iota(jnp.int32, (tq, PAIR), 1) < HEAD_DIM
    for t in range(n // tq):
        rows = pl.ds(t * tq, tq)
        q = q_ref[rows, :]
        zero = jnp.zeros_like(q)
        outs = []
        for a in range(2):
            qa = jnp.where(low, q, zero) if a == 0 else jnp.where(low, zero, q)
            s = dot(qa, k_ref[...], NT)
            top = jnp.max(s, axis=-1, keepdims=True)
            p = jnp.exp2((s - top) * (LOG2E * HEAD_DIM**-0.5)).astype(BF)
            p_ref[a, rows, :] = p
            both = dot(p, vx_ref[...], NN)
            inv = 1.0 / both[:, PAIR:]
            outs.append((both[:, :PAIR] * inv, inv))
        o_ref[rows, :] = jnp.where(low, outs[0][0], outs[1][0]).astype(BF)
        inv_ref[rows, :] = jnp.where(lane == head, outs[0][1], jnp.where(lane == head + 1, outs[1][1], inv_ref[rows, :]))


def attend(packed):
    n, w = packed.shape
    d = w // 3
    hp = d // PAIR

    def cols(off):
        return pl.BlockSpec((n, PAIR), lambda h: (0, h + off))

    return pl.pallas_call(
        functools.partial(attend_kernel, tq=128),
        grid=(hp,),
        in_specs=[cols(0), cols(hp), cols(2 * hp)],
        out_specs=[cols(0), pl.BlockSpec((n, PAIR), lambda h: (0, 0)), pl.BlockSpec((2, n, n), lambda h: (h, 0, 0))],
        out_shape=[shape((n, d)), shape((n, PAIR), F32), shape((2 * hp, n, n))],
        scratch_shapes=[pltpu.VMEM((n, 2 * PAIR), BF)],
        compiler_params=params(40),
        cost_estimate=pl.CostEstimate(flops=16 * n * n * d, bytes_accessed=4 * n * n * hp, transcendentals=0),
        name="attend",
    )(packed, packed, packed)


WHOLE = pl.BlockSpec(memory_space=pltpu.VMEM)
FAR = pl.BlockSpec(memory_space=pltpu.HBM)


def transpose_rows(block, out, cols):
    t = block.T
    d = t.shape[0]
    half = d // PIECES // 2
    for h in range(2):
        for v in range(PIECES):
            at = (2 * v + h) * half
            to = (h * PIECES + v) * half
            out[to : to + half, cols] = t[at : at + half]


def core_rows(ref, which):
    half = ref.shape[0] // 2
    return ref[pl.ds(pl.multiple_of(which * half, half), half), :]


def piece_blocks(g, ref, first):
    rows = g.shape[0] // PIECES
    for k in range(g.shape[1] // 128):
        at = (first + k) * rows
        ref[:, at : at + rows, :] = g[:, k * 128 : (k + 1) * 128].reshape(PIECES, rows, 128)


def middle_of(x_ref, mix_ref, wo_ref, vec_ref, rows):
    return x_ref[rows, :].astype(F32) + dot(mix_ref[rows, :], wo_ref[...], NN) + line(vec_ref, "ob")


def hidden_kernel(c_ref, *refs, i, head, tm, sub):
    refs = list(refs)
    take = lambda k: [refs.pop(0) for _ in range(k)]
    if head:
        x_ref, mix_ref, wo_ref, vec_ref = take(4)
    else:
        sec_ref, sec_t, up_t, o_in, ds_in = take(5)
    up_ref, w1_ref, w2_ref, b1_ref, gk_ref, gs_ref, db1_ref, o_ref, ds_ref = take(9)
    if head:
        sec_ref, sec_t, up_t = take(3)
    act, dh = take(2)
    n, d = up_ref.shape
    wide = act.shape[1]

    def shares(first, last):
        return [slice((v * CHUNKS + i) * 128, (v * CHUNKS + i + 1) * 128) for v in range(first // 128, last // 128)]

    def columns(first, last):
        return jnp.concatenate([w1_ref[:, at] for at in shares(first, last)], axis=1)

    def lines(first, last):
        return jnp.concatenate([w2_ref[at, :] for at in shares(first, last)], axis=0)

    if head:
        for t in range(n // 256):
            rows = slice(t * 256, (t + 1) * 256)
            spread, r = stats(middle_of(x_ref, mix_ref, wo_ref, vec_ref, rows))
            sec = (spread * r * line(vec_ref, "mg") + line(vec_ref, "ms")).astype(BF)
            sec_ref[rows, :] = sec
            transpose_rows(sec, sec_t, rows)
            up_t[:, rows] = up_ref[rows, :].T
    db1_ref[...] = jnp.zeros_like(db1_ref)
    for first in range(0, wide, sub):
        cols = slice(first, first + sub)
        bias = jnp.concatenate([b1_ref[v * CHUNKS + i : v * CHUNKS + i + 1, :] for v in range(first // 128, (first + sub) // 128)], axis=1)

        def tile(t, _):
            rows = pl.ds(pl.multiple_of(t * tm, tm), tm)
            h = dot(sec_ref[rows, :], columns(first, first + sub), NN) + bias
            da = dot(up_ref[rows, :], lines(first, first + sub), NT)
            cdf, pdf = normal(h)
            act[rows, cols] = (h * cdf).astype(BF)
            dhv = da * (cdf + h * pdf)
            dh[rows, cols] = dhv.astype(BF)
            db1_ref[:, cols] += jnp.sum(dhv, axis=0, keepdims=True)
            return 0

        lax.fori_loop(0, n // tm, tile, 0)
    base = PIECES * (d // PIECES // 2)
    c = c_ref[0]
    for ref, mine in ((gs_ref, 1 - c), (gk_ref, c)):
        piece_blocks(dot(core_rows(sec_t, mine), dh[...], NN).astype(BF), ref, 0)
        g = dot(core_rows(up_t, mine), act[...], NN).astype(BF)
        for k in range(wide // 128):
            ref[k, base:, :] = g[:, k * 128 : (k + 1) * 128]

    def gather(t, _):
        rows = pl.ds(pl.multiple_of(t * tm, tm), tm)
        o = dot(act[rows, :], lines(0, wide), NN)
        o_ref[rows, :] = o if head else o_in[rows, :] + o
        ds = dot(dh[rows, :], columns(0, wide), NT)
        ds_ref[rows, :] = ds if head else ds_in[rows, :] + ds
        return 0

    lax.fori_loop(0, n // tm, gather, 0)


def hidden_part(core, head, carried, up, w1, w2, b1, i, tm=512, sub=512):
    n, d = up.shape
    wide = 128 * PIECES
    assert wide * CHUNKS == w1.shape[1]
    g = (PIECES, PIECES * (d // PIECES // 2) + d // 2, 128)
    args = list(head) if head else list(carried)
    made = [shape(g), shape(g), shape((1, wide), F32), shape((n, d), F32), shape((n, d), F32)]
    if head:
        made += [shape((n, d)), shape((d, n)), shape((d, n))]
    return pl.pallas_call(
        functools.partial(hidden_kernel, i=i, head=bool(head), tm=tm, sub=sub),
        in_specs=[pl.BlockSpec(memory_space=pltpu.SMEM)] + [WHOLE] * (len(args) + 4),
        out_specs=[WHOLE] * len(made),
        out_shape=made,
        input_output_aliases={} if head else {4: 3, 5: 4},
        scratch_shapes=[pltpu.VMEM((n, wide), BF), pltpu.VMEM((n, wide), BF)],
        compiler_params=params(10),
        cost_estimate=pl.CostEstimate(flops=24 * n * d * wide, bytes_accessed=8 * d * wide, transcendentals=0),
        name="hidden",
    )(core, *args, up, w1, w2, b1)


def outer_kernel(c_ref, x_ref, up_ref, mix_ref, li_ref, wo_ref, vec_ref, o_ref, ds_ref, out_ref, dbr_ref, do_ref, gk_ref, gs_ref, sums_ref, mix_t, *, tm):
    n, d = x_ref.shape
    sums = None
    lanes = lax.broadcasted_iota(jnp.int32, (PAIR, d), 1) // HEAD_DIM
    spread_heads = (lanes == lax.broadcasted_iota(jnp.int32, (PAIR, d), 0)).astype(BF)
    for t in range(n // tm):
        rows = slice(t * tm, (t + 1) * tm)
        m = middle_of(x_ref, mix_ref, wo_ref, vec_ref, rows)
        spread, r = stats(m)
        nv = spread * r
        up = up_ref[rows, :].astype(F32)
        transpose_rows(mix_ref[rows, :], mix_t, rows)
        dy = ds_ref[rows, :]
        dyg = dy * line(vec_ref, "mg")
        dm = up + r * (dyg - jnp.mean(dyg, axis=-1, keepdims=True) - nv * jnp.mean(dyg * nv, axis=-1, keepdims=True))
        db = dm.astype(BF)
        dbr_ref[rows, :] = db
        out_ref[rows, :] = (m + o_ref[rows, :] + line(vec_ref, "rb")).astype(BF)
        li = li_ref[rows, :]
        coarse = li.astype(BF)
        fine = (li - coarse.astype(F32)).astype(BF)
        scale = dot(coarse, spread_heads, NN) + dot(fine, spread_heads, NN)
        do_ref[rows, :] = (dot(db, wo_ref[...], NT) * scale).astype(BF)
        part = [jnp.sum(v, axis=0, keepdims=True) for v in (db.astype(F32), dy * nv, dy, up)]
        sums = part if sums is None else [a + b for a, b in zip(sums, part)]
    sums_ref[...] = jnp.concatenate(sums + [jnp.zeros((4, d), F32)], axis=0)
    for ref, mine in ((gs_ref, 1 - c_ref[0]), (gk_ref, c_ref[0])):
        piece_blocks(dot(core_rows(mix_t, mine), dbr_ref[...], NN).astype(BF), ref, 0)


def outer(core, x, up, mix, li, wo, vec, o, ds, tm=256):
    n, d = x.shape
    g = (PIECES, d // 128 * (d // PIECES // 2), 128)
    return pl.pallas_call(
        functools.partial(outer_kernel, tm=tm),
        in_specs=[pl.BlockSpec(memory_space=pltpu.SMEM)] + [WHOLE] * 8,
        out_specs=[WHOLE] * 6,
        out_shape=[shape((n, d))] * 3 + [shape(g), shape(g), shape((8, d), F32)],
        scratch_shapes=[pltpu.VMEM((d, n), BF)],
        compiler_params=params(8),
        cost_estimate=pl.CostEstimate(flops=24 * n * d * d, bytes_accessed=20 * n * d, transcendentals=0),
        name="outer",
    )(core, x, up, mix, li, wo, vec, o, ds)


def by_piece(g):
    rows = g.shape[0] // PIECES
    return [g[:, i : i + 128].reshape(PIECES, rows, 128) for i in range(0, g.shape[1], 128)]


def reflect_kernel(c_ref, q_ref, k_ref, v_ref, o_ref, do_ref, p_ref, ft_ref, dq_ref, dk_ref, dv_ref, gk_ref, gs_ref, ds_ref, *, tq):
    n = k_ref.shape[0]
    low = lax.broadcasted_iota(jnp.int32, (tq, PAIR), 1) < HEAD_DIM
    q_t = q_ref[...].T
    do_t = do_ref[...].T
    scale = HEAD_DIM**-0.5
    dks, dvs = [], []
    for a in range(2):
        for t in range(n // tq):
            rows = pl.ds(t * tq, tq)
            do = do_ref[rows, :]
            zero = jnp.zeros_like(do)
            doa = jnp.where(low, do, zero) if a == 0 else jnp.where(low, zero, do)
            delta = jnp.sum(doa.astype(F32) * o_ref[rows, :].astype(F32), axis=-1, keepdims=True)
            dp = dot(doa, v_ref[...], NT)
            ds = (p_ref[a, rows, :].astype(F32) * (dp - delta)).astype(BF)
            ds_ref[rows, :] = ds
            dq = (dot(ds, k_ref[...], NN) * scale).astype(BF)
            dq_ref[rows, :] = dq if a == 0 else jnp.where(low, dq_ref[rows, :], dq)
        part = slice(HEAD_DIM * a, HEAD_DIM * (a + 1))
        dvs.append(dot(do_t[part], p_ref[a], NN))
        dks.append(dot(q_t[part], ds_ref[...], NN) * scale)
    dv = jnp.concatenate(dvs, axis=0).astype(BF).T
    dk = jnp.concatenate(dks, axis=0).astype(BF).T
    dv_ref[...] = dv
    dk_ref[...] = dk
    g = dot(ft_ref[...], jnp.concatenate([dq_ref[...], dk, dv], axis=1), NN).astype(BF)
    per = g.shape[0] // PIECES
    h = pl.program_id(0)
    for step, ref in enumerate((gs_ref, gk_ref)):

        @pl.when(h == step)
        def _():
            for i, block in enumerate(by_piece(g)):
                ref[:, i * per : (i + 1) * per, :] = block


def reflect(core, packed, o, do, p, first_t, start):
    n, w = packed.shape
    d = w // 3
    hp = d // PAIR

    def which(h, c):
        return (h + 1 - c[0]) % 2

    def cols(off):
        return pl.BlockSpec((n, PAIR), lambda h, c: (0, which(h, c) + off))

    g = (PIECES, 3 * (d // PIECES), 128)
    piece = pl.BlockSpec(g, lambda h, c: (0, 0, 0), pipeline_mode=pl.Buffered(1))
    return pl.pallas_call(
        functools.partial(reflect_kernel, tq=256),
        grid_spec=pltpu.PrefetchScalarGridSpec(
            num_scalar_prefetch=1,
            grid=(2,),
            in_specs=[
                cols(start), cols(start + hp), cols(start + 2 * hp), cols(start), cols(start),
                pl.BlockSpec((2, n, n), lambda h, c: (which(h, c) + start, 0, 0)),
                pl.BlockSpec((d, n), lambda h, c: (0, 0), pipeline_mode=pl.Buffered(1)),
            ],
            out_specs=[cols(0)] * 3 + [piece] * 2,
            scratch_shapes=[pltpu.VMEM((n, n), BF)],
        ),
        out_shape=[shape((n, 2 * PAIR))] * 3 + [shape(g)] * 2,
        compiler_params=params(27),
        cost_estimate=pl.CostEstimate(flops=160 * n * n * PAIR, bytes_accessed=8 * n * n, transcendentals=0),
        name="reflect",
    )(core, packed, packed, packed, o, do, p, first_t)


SMALL = 16


def back_kernel(*refs, chunks):
    x_ref, dbr_ref, w_ref, vec_in, mid_ref = refs[:5]
    db1 = refs[5 : 5 + CHUNKS]
    parts = refs[5 + CHUNKS : 5 + CHUNKS + 3 * chunks]
    tg_ref, small_ref, sums = refs[5 + CHUNKS + 3 * chunks :]

    @pl.when(pl.program_id(0) == 0)
    def _():
        sums[...] = jnp.zeros_like(sums)

    d = x_ref.shape[1]
    cw = d // chunks
    dy = None
    for i in range(3 * chunks):
        which, chunk = i % 3, i // 3
        at = which * d + chunk * cw
        part = dot(parts[i][...], w_ref[:, at : at + cw], NT)
        dy = part if dy is None else dy + part
        row = {0: 2, 2: 3}.get(which)
        if row is not None:
            sums[row : row + 1, chunk * cw : (chunk + 1) * cw] += jnp.sum(parts[i][...].astype(F32), axis=0, keepdims=True)
    spread, r = stats(x_ref[...].astype(F32))
    nv = spread * r
    dyg = dy * line(vec_in, "ag")
    dx = r * (dyg - jnp.mean(dyg, axis=-1, keepdims=True) - nv * jnp.mean(dyg * nv, axis=-1, keepdims=True))
    tg_ref[...] = (dbr_ref[...].astype(F32) + dx).astype(BF)
    sums[0:1, :] += jnp.sum(dy * nv, axis=0, keepdims=True)
    sums[1:2, :] += jnp.sum(dy, axis=0, keepdims=True)

    @pl.when(pl.program_id(0) == pl.num_programs(0) - 1)
    def _():
        per = d // PIECES
        sums[4:8, :] = mid_ref[0:4, :]
        rows = sums[...]
        for v in range(PIECES):
            vectors = jnp.concatenate([rows[:, v * per : (v + 1) * per], jnp.zeros((8, 128 - per), F32)], axis=1)
            biases = [b[:, v * 128 : (v + 1) * 128] for b in db1]
            piece = jnp.concatenate([vectors] + biases + [jnp.zeros((SMALL - 8 - CHUNKS, 128), F32)], axis=0)
            small_ref[v * SMALL : (v + 1) * SMALL, :] = piece.astype(BF)


def project_back(x, dbr, w, vec, mids, db1, parts):
    n, d = x.shape
    tm = 256
    row = pl.BlockSpec((tm, d), lambda i: (i, 0))

    def full(*s):
        return pl.BlockSpec(s, lambda i: (0, 0), pipeline_mode=pl.Buffered(1))

    chunks = len(parts) // 3
    return pl.pallas_call(
        functools.partial(back_kernel, chunks=chunks),
        grid=(n // tm,),
        in_specs=[row, row, full(d, 3 * d), full(*vec.shape), full(*mids.shape)]
        + [full(*b.shape) for b in db1]
        + [pl.BlockSpec((tm, d // chunks), lambda i: (i, 0))] * (3 * chunks),
        out_specs=[row, full(PIECES * SMALL, 128)],
        out_shape=[shape((n, d)), shape((PIECES * SMALL, 128))],
        scratch_shapes=[pltpu.VMEM((8, d), F32)],
        compiler_params=params(24),
        cost_estimate=pl.CostEstimate(flops=12 * n * d * d, bytes_accessed=16 * n * d, transcendentals=0),
        name="project_back",
    )(x, dbr, w, vec, mids, *db1, *parts)


def exchange(x, axis, by):
    count = lax.axis_size(axis)
    return lax.ppermute(x, axis, [(i, i ^ by) for i in range(count)])


def to_core(g):
    return exchange(g, "seq", 1)


def pick(x, index, axis=0):
    return lax.dynamic_index_in_dim(x, index, axis, keepdims=False)


def after(x, *others):
    return lax.optimization_barrier((x,) + others)[0]


class Part:
    def __init__(self, held, received, rows):
        self.held = (held.reshape(-1, 128), 0)
        self.received = (received.reshape(-1, 128), 0)
        self.rows = rows
        self.open = [0, 1, 2]

    def count(self):
        return self.rows << len(self.open)


def slot_kernel(ids_ref, *refs, items, inputs):
    ins, outs = refs[:inputs], refs[inputs:]

    def read(term, at, count):
        ref, offset = term
        return ins[ref][pl.ds(at + offset, count), :].astype(F32)

    step = 16
    for kind, *rest in items:
        if kind == "split":
            held, received, groups, size, bit, (send, to), keep = rest
            mine = ids_ref[bit]
            for a in range(groups):
                own = pl.multiple_of((2 * a + mine) * size, step)
                other = pl.multiple_of((2 * a + 1 - mine) * size, step)
                outs[send][to + a * size : to + (a + 1) * size, :] = (read(held, other, size) + read(received, other, size)).astype(BF)
                outs[keep][a * size : (a + 1) * size, :] = (read(held, own, size) + read(received, own, size)).astype(BF)
        elif kind == "sum":
            held, received, size, (send, to) = rest
            outs[send][to : to + size, :] = (read(held, 0, size) + read(received, 0, size)).astype(BF)
        else:
            first, second, size, bit, (send, to), keep = rest
            for mine in (0, 1):

                @pl.when(ids_ref[bit] == mine)
                def _():
                    own, other = (first, second) if mine == 0 else (second, first)
                    outs[send][to : to + size, :] = (read(other[0], 0, size) + read(other[1], 0, size)).astype(BF)
                    outs[keep][...] = (read(own[0], 0, size) + read(own[1], 0, size)).astype(BF)


def slot(ids, exchanges, *tokens):
    arrays, items, sizes, moves = [], [], [], []

    def use(term):
        for i, a in enumerate(arrays):
            if a is term[0]:
                return i, term[1]
        arrays.append(term[0])
        return len(arrays) - 1, term[1]

    for stage, parts in exchanges:
        send, to = len(sizes), 0
        sizes.append(0)
        placed = []
        if stage == "pick":
            one, two = parts
            size = one.count()
            items.append(("pick", (use(one.held), use(one.received)), (use(two.held), use(two.received)), size, 1, (send, 0), len(sizes)))
            placed.append((one, len(sizes), 0, 0))
            sizes.append(size)
            to = size
        else:
            for p in parts:
                held, received = use(p.held), use(p.received)
                if stage == "x":
                    items.append(("sum", held, received, p.count(), (send, to)))
                    placed.append((p, send, to, to))
                    to += p.count()
                    continue
                if stage == "half":
                    groups, bit = 1 << len(p.open), 1
                else:
                    groups, bit = 1 << (len(p.open) - 1 - p.open.index(stage)), 2 + stage
                size = p.count() // (2 * groups)
                items.append(("split", held, received, groups, size, bit, (send, to), len(sizes)))
                placed.append((p, len(sizes), 0, to))
                sizes.append(groups * size)
                to += groups * size
                if stage == "half":
                    p.rows //= 2
                else:
                    p.open.remove(stage)
        sizes[send] = to
        moves.append((stage, send, placed))

    if tokens:
        arrays = list(lax.optimization_barrier(tuple(arrays) + tokens)[: len(arrays)])
    whole = pl.BlockSpec(memory_space=pltpu.VMEM)
    outs = pl.pallas_call(
        functools.partial(slot_kernel, items=items, inputs=len(arrays)),
        in_specs=[pl.BlockSpec(memory_space=pltpu.SMEM)] + [whole] * len(arrays),
        out_specs=[whole] * len(sizes),
        out_shape=[shape((size, 128)) for size in sizes],
        compiler_params=params(2),
        cost_estimate=pl.CostEstimate(flops=0, bytes_accessed=512 * sum(sizes), transcendentals=0),
        name="slot",
    )(ids, *arrays)
    unit = lax.axis_size("vol") // PIECES
    sent, received = [], []
    for stage, send, placed in moves:
        if stage in ("half", "pick", "x"):
            got = exchange(outs[send], "seq", 2)
        else:
            got = exchange(outs[send], "vol", unit << stage)
        sent.append(outs[send])
        received.append(got)
        for p, keep, at, to in placed:
            p.held = (outs[keep], at)
            p.received = (got, to)
    return sent, received


def home_kernel(ids_ref, live_ref, *refs, mask):
    out_ref = refs[-1]
    for k, ref in enumerate(refs[:-1]):

        @pl.when(pl.program_id(0) == k)
        def _():
            value = ref[...].astype(F32)
            if mask:
                value = value * live_ref[ids_ref[5] ^ k]
            out_ref[...] = value.astype(out_ref.dtype)


def send_home(ids, live, own, others, slices, dtype, mask):
    rows, d = others[0].shape
    return pl.pallas_call(
        functools.partial(home_kernel, mask=mask),
        grid_spec=pltpu.PrefetchScalarGridSpec(
            num_scalar_prefetch=2,
            grid=(slices,),
            in_specs=[pl.BlockSpec((rows, d), lambda k, i, l: (0, 0), pipeline_mode=pl.Buffered(1))] * slices,
            out_specs=pl.BlockSpec((None, rows, d), lambda k, i, l: (k ^ i[5], 0, 0)),
        ),
        out_shape=shape((slices, rows, d), dtype),
        compiler_params=params(8),
        cost_estimate=pl.CostEstimate(flops=0, bytes_accessed=6 * slices * rows * d, transcendentals=0),
        name="home",
    )(ids, live, own, *others)


def assemble_ff_kernel(ids_ref, *refs, per, sizes):
    terms = refs[:4]
    expand_ref, reduce_ref = refs[4:]
    c = ids_ref[0]

    def first_layer(i, core, value):
        size = per // 2
        for k in range(PIECES):
            at = (k * CHUNKS + i) * 128
            expand_ref[pl.ds(pl.multiple_of(core * size, size), size), at : at + 128] = value[k * size : (k + 1) * size, :]

    def second_layer(i, core, value):
        d = value.shape[0]
        reduce_ref[i * 128 : (i + 1) * 128, pl.ds(pl.multiple_of(core * d, 128), d)] = value.T

    half = per // 2 * PIECES
    for core, (own, partner) in ((c, terms[:2]), (1 - c, terms[2:])):
        for x in (0, 1):

            @pl.when(ids_ref[1] == x)
            def _():
                one, two = (own, partner) if x == 0 else (partner, own)
                first_layer(0, core, one[: sizes[0], :].astype(F32))
                second_layer(0, core, two[: sizes[0], :].astype(F32))

        at = sizes[0]
        for i in (1, 2):
            rows = slice(at, at + sizes[i])
            value = own[rows, :].astype(F32) + partner[rows, :].astype(F32)
            first_layer(i, core, value[:half])
            second_layer(i, core, value[half:])
            at += sizes[i]


def assemble_end_kernel(ids_ref, *refs, per, size):
    terms = refs[:4]
    output_ref, input_ref, vector_ref = refs[4:]
    c = ids_ref[0]
    d = PIECES * per

    def output_part(core, value):
        part = per // 2
        for k in range(d // 128):
            rows = pl.ds(pl.multiple_of(core * part, part), part)
            output_ref[rows, k * 128 : (k + 1) * 128] = value[k * part : (k + 1) * part, :]

    def pair_part(i, core, value):
        for k in range(3):
            at = pl.multiple_of(k * d + (2 * i + core) * 128, 128)
            input_ref[:, pl.ds(at, 128)] = value[k * per : (k + 1) * per, :]

    for core, (own, partner) in ((c, terms[:2]), (1 - c, terms[2:])):
        for i in (1, 2):
            rows = slice((i - 1) * size, i * size)
            pair_part(i, core, own[rows, :].astype(F32) + partner[rows, :].astype(F32))
        for x in (0, 1):

            @pl.when(ids_ref[1] == x)
            def _():
                one, two = (own, partner) if x == 0 else (partner, own)
                output_part(core, one[2 * size : 3 * size, :].astype(F32))
                pair_part(0, core, two[2 * size : 3 * size, :].astype(F32))

    vector_ref[...] = terms[0][3 * size :, :].astype(F32) + terms[1][3 * size :, :].astype(F32)


def assemble(kernel, ids, per, arrays, outs, name):
    whole = pl.BlockSpec(memory_space=pltpu.VMEM)
    return pl.pallas_call(
        functools.partial(kernel, per=per),
        in_specs=[pl.BlockSpec(memory_space=pltpu.SMEM)] + [whole] * len(arrays),
        out_specs=[whole] * len(outs),
        out_shape=[shape(o, F32) for o in outs],
        compiler_params=params(8),
        name=name,
    )(ids, *arrays)


def on_device(
    volume_slices, volume_owner, tokens, cotangent, attend_gain, attend_shift, input_weight, query_bias, value_bias,
    output_weight, output_bias, mixer_gain, mixer_shift, expand_weight, expand_bias, reduce_weight, reduce_bias,
):
    slices, rows, d = tokens.shape
    ff = expand_weight.shape[1]
    nv = lax.axis_size("vol")
    peers = lax.axis_size("seq")
    me = lax.axis_index("seq")
    core_id = me % 2
    x_id = (me // 2) % 2
    core = core_id.astype(jnp.int32).reshape(1)
    n = rows * peers
    vol = lax.axis_index("vol")
    unit = nv // PIECES
    ids = jnp.stack([core_id, x_id, (vol // unit) % 2, (vol // (2 * unit)) % 2, (vol // (4 * unit)) % 2, me]).astype(jnp.int32)

    def from_peers(x, ks):
        parts = [pick(x, me ^ k) for k in ks]
        return [p if k == 0 else exchange(p, "seq", k) for p, k in zip(parts, ks)]

    far_parts = from_peers(tokens, (3, 2))
    near_parts = from_peers(tokens, (0, 1))
    zero = jnp.zeros((d,), BF)
    vec = jnp.concatenate(
        [attend_gain, attend_shift, query_bias, zero, value_bias, output_bias, mixer_gain, mixer_shift, reduce_bias] + [zero] * 7
    ).astype(F32).reshape(16, d)
    wide = ff // CHUNKS
    lanes = wide // PIECES
    b1 = expand_bias.astype(F32).reshape(ff // 128, 128)
    load = jnp.sum(jnp.where(volume_owner == lax.axis_index("vol"), volume_slices, 0))
    live = (jnp.arange(slices) < load).astype(BF)

    made = project_in(jnp.concatenate(near_parts), 0, n, None, vec, input_weight)
    far = jnp.concatenate([after(far_parts[1], made[2], b1, live), far_parts[0]])
    x, first_t, packed = project_in(far, 2 * rows, n, made, vec, input_weight)
    upstream = jnp.concatenate(from_peers(after(cotangent, far_parts[0], made[2]) * live[:, None, None], (0, 1, 2, 3)))

    mixed, inverse, weights = attend(packed)

    db1 = []

    def hidden(token, head, carried, i):
        gk, gs, b, *made = hidden_part(token, head, carried, upstream, expand_weight, reduce_weight, b1, i)
        db1.append(b)
        return gk, gs, made

    Y, Z1, Z2 = 0, 1, 2
    piece_rows = d // 2 + d // 2
    pair_rows = 3 * (d // PIECES)
    k0, s0, (o, ds, *kept) = hidden(core, (x, mixed, output_weight, vec), None, 0)
    r0 = to_core(s0)
    k1, s1, (o, ds) = hidden(after(core, s0), None, (*kept, o, ds), 1)
    r1 = to_core(s1)
    ga = Part(k0, r0, piece_rows)
    sent, _ = slot(ids, [("half", [ga])], s1)
    k2, s2, (o, ds) = hidden(after(core, s1, *sent), None, (*kept, o, ds), 2)
    r2 = to_core(s2)
    gb = Part(k1, r1, piece_rows)
    sent, _ = slot(ids, [(Z1, [gb])], s2)
    out, d_branch, d_mixed, k3, s3, sums_mid = outer(
        after(core, s2, *sent), x, upstream, mixed, inverse, output_weight, vec, o, ds
    )
    r3 = to_core(s3)

    def homeward(a):
        blocks = [a[k * rows : (k + 1) * rows] for k in range(1, peers)]
        return blocks, [exchange(b, "seq", k + 1) for k, b in enumerate(blocks)]

    out_sent, outs = homeward(out)
    gc = Part(k2, r2, piece_rows)
    sent, got = slot(ids, [(Y, [gc])], s3)
    parts = []

    def reflect_part(token, i):
        dq, dk, dv, gk, gs = reflect(token, packed, mixed, d_mixed, weights, first_t, 2 * i)
        parts.extend([dq, dk, dv])
        return gk, gs

    p0, q0 = reflect_part(after(core, s3, *sent, *out_sent), 0)
    t0 = to_core(q0)
    wait_c = got[0]
    sent, _ = slot(ids, [(Y, [ga]), (Z2, [gb])], q0)
    p1, q1 = reflect_part(after(core, q0, wait_c, *sent, *outs), 1)
    t1 = to_core(q1)
    gd, gd2 = Part(k3, r3, pair_rows), Part(p0, t0, pair_rows)
    sent, _ = slot(ids, [(Z1, [ga, gc]), ("pick", [gd, gd2])], q1)
    p2, q2 = reflect_part(after(core, q1, *sent), 2)
    t2 = to_core(q2)
    ge1 = Part(p1, t1, pair_rows)
    sent, late_got = slot(ids, [(Y, [ge1, gd]), (Z2, [ga, gc])], q2)
    d_tokens, small = project_back(after(x, *sent), d_branch, input_weight, vec, sums_mid, db1, parts)

    tg_sent, tgs = homeward(d_tokens)
    ge2 = Part(p2, t2, pair_rows)
    gv = Part(small, to_core(small), SMALL)
    sent1, got1 = slot(ids, [(Y, [ge2, gv]), (Z1, [ge1, gd])], small, *tg_sent, late_got[1])
    block_out = send_home(ids, live, out, [after(o, *sent1) for o in outs], slices, BF, True)
    sent2, got2 = slot(ids, [(Z1, [ge2, gv]), (Z2, [ge1, gd]), (Y, [gb])], *got1, block_out, *tgs[1:])
    per = d // PIECES
    spare = [1 << i for i in range(unit.bit_length() - 1)]
    tgs = [after(t, *sent2) for t in tgs]
    tokens_grad = send_home(ids, live, d_tokens, tgs, slices, F32, False)
    sent3, got3 = slot(ids, [(Z2, [ge2, gv]), ("x", [ga, gb, gc])], *got2, tokens_grad)
    sent4, got4 = slot(ids, [("x", [ge1, ge2, gd, gv])], got3[0])
    ff_terms = [after(a, *sent4) for a in (sent3[-1], got3[-1])]
    ff_terms += [to_core(a) for a in ff_terms]
    expand_grad, reduce_grad = assemble(
        functools.partial(assemble_ff_kernel, sizes=[p.count() for p in (ga, gb, gc)]), ids, per, ff_terms, [(per, ff), (ff // PIECES, d)], "assemble_ff"
    )
    ends = [sent4[0], after(got4[0], expand_grad)]
    ends += [to_core(a) for a in ends]
    output_grad, input_grad, vectors = assemble(
        functools.partial(assemble_end_kernel, size=pair_rows), ids, per, ends, [(per, d), (per, 3 * d), (SMALL, 128)], "assemble_end"
    )
    bias_rows = vectors[8 : 8 + CHUNKS]
    vectors = vectors[:8, :per]
    if unit > 1:
        sub = vol % unit

        def add_rest(a):
            for by in spare:
                a = a + exchange(a, "vol", by)
            return a

        def cut(a, axis):
            size = a.shape[axis] // unit
            return lax.dynamic_slice_in_dim(add_rest(a), sub * size, size, axis)

        expand_grad, reduce_grad, output_grad, input_grad = [cut(a, 0) for a in (expand_grad, reduce_grad, output_grad, input_grad)]
        expand_bias_grad = cut(bias_rows.reshape(-1), 0)
        vectors = cut(vectors, 1)
    else:
        expand_bias_grad = bias_rows.reshape(-1)
    return (
        block_out, tokens_grad, vectors[0], vectors[1], input_grad, vectors[2], vectors[3], output_grad, vectors[4],
        vectors[5], vectors[6], expand_grad, expand_bias_grad, reduce_grad, vectors[7],
    )


def solution(mesh):
    rows = P("vol", "seq", None)
    return jax.shard_map(
        on_device,
        mesh=mesh,
        in_specs=(P(), P(), rows, rows) + (P(),) * 13,
        out_specs=(rows, rows, P("vol"), P("vol"), P("vol", None), P("vol"), P("vol"), P("vol", None), P("vol"), P("vol"),
                   P("vol"), P("vol", None), P("vol"), P("vol", None), P("vol")),
        check_vma=False,
    )
```

```python
import functools

import jax
import jax.numpy as jnp
from jax import lax
from jax.experimental import pallas as pl
from jax.experimental.pallas import tpu as pltpu
from jax.sharding import PartitionSpec as P

HEAD_DIM = 64
PAIR = 2 * HEAD_DIM
LOG2E = 1.4426950408889634
PIECES = 8
CHUNKS = 3
ROW = {n: i for i, n in enumerate(("ag", "ash", "qb", "zero", "vb", "ob", "mg", "ms", "rb"))}
BF = jnp.bfloat16
F32 = jnp.float32
NN = (((1,), (0,)), ((), ()))
NT = (((1,), (1,)), ((), ()))

def dot(a, b, dims):
    return lax.dot_general(a, b, dims, preferred_element_type=F32)


def params(mib=24):
    return pltpu.CompilerParams(vmem_limit_bytes=mib << 20)


def line(ref, name):
    return ref[ROW[name] : ROW[name] + 1, :]


def shape(dims, dtype=BF):
    return jax.ShapeDtypeStruct(dims, dtype)


def normal(h):
    return 0.5 + 0.5 * lax.erf(h * 0.5**0.5), jnp.exp2(h * h * (-0.5 * LOG2E)) * 0.3989422804014327


def stats(v):
    spread = v - jnp.mean(v, axis=-1, keepdims=True)
    return spread, lax.rsqrt(jnp.mean(spread * spread, axis=-1, keepdims=True) + 1e-6)


def in_kernel(x_ref, vec_ref, w_ref, *rest):
    x_out, first_t, packed = rest[-3:]
    x = x_ref[...]
    d = x.shape[1]
    spread, r = stats(x.astype(F32))
    f = (spread * r * line(vec_ref, "ag") + line(vec_ref, "ash")).astype(BF)
    x_out[...] = x
    for i, bias in enumerate(("qb", "zero", "vb")):
        packed[:, i * d : (i + 1) * d] = (dot(f, w_ref[:, i * d : (i + 1) * d], NN) + line(vec_ref, bias)).astype(BF)
    first_t[...] = f.T


def project_in(part, offset, total, before, vec, weight):
    rows, d = part.shape
    wide = weight.shape[1]
    tm = 256
    first_block = offset // tm

    def full(a):
        return pl.BlockSpec(a.shape, lambda i: (0, 0), pipeline_mode=pl.Buffered(1))

    in_specs = [pl.BlockSpec((tm, d), lambda i: (i, 0)), full(vec), full(weight)]
    args = [part, vec, weight]
    aliases = {}
    if before is not None:
        aliases = {3: 0, 4: 1, 5: 2}
        in_specs += [pl.BlockSpec(memory_space=pl.ANY)] * 3
        args += list(before)
    return pl.pallas_call(
        in_kernel,
        grid=(rows // tm,),
        in_specs=in_specs,
        out_specs=[
            pl.BlockSpec((tm, d), lambda i: (i + first_block, 0)),
            pl.BlockSpec((d, tm), lambda i: (0, i + first_block)),
            pl.BlockSpec((tm, wide), lambda i: (i + first_block, 0)),
        ],
        out_shape=[shape((total, d)), shape((d, total)), shape((total, wide))],
        input_output_aliases=aliases,
        compiler_params=params(24),
        cost_estimate=pl.CostEstimate(flops=6 * rows * d * wide, bytes_accessed=2 * (d * wide + rows * (wide + 3 * d)), transcendentals=0),
        name="project_in",
    )(*args)


def attend_kernel(q_ref, k_ref, v_ref, o_ref, inv_ref, p_ref, vx_ref, *, tq):
    n = k_ref.shape[0]
    head = 2 * pl.program_id(0)
    lane = lax.broadcasted_iota(jnp.int32, (tq, PAIR), 1)
    vx_ref[:, :PAIR] = v_ref[...]
    vx_ref[:, PAIR:] = jnp.ones((n, PAIR), BF)
    low = lax.broadcasted_iota(jnp.int32, (tq, PAIR), 1) < HEAD_DIM
    for t in range(n // tq):
        rows = pl.ds(t * tq, tq)
        q = q_ref[rows, :]
        zero = jnp.zeros_like(q)
        outs = []
        for a in range(2):
            qa = jnp.where(low, q, zero) if a == 0 else jnp.where(low, zero, q)
            s = dot(qa, k_ref[...], NT)
            top = jnp.max(s, axis=-1, keepdims=True)
            p = jnp.exp2((s - top) * (LOG2E * HEAD_DIM**-0.5)).astype(BF)
            p_ref[a, rows, :] = p
            both = dot(p, vx_ref[...], NN)
            inv = 1.0 / both[:, PAIR:]
            outs.append((both[:, :PAIR] * inv, inv))
        o_ref[rows, :] = jnp.where(low, outs[0][0], outs[1][0]).astype(BF)
        inv_ref[rows, :] = jnp.where(lane == head, outs[0][1], jnp.where(lane == head + 1, outs[1][1], inv_ref[rows, :]))


def attend(packed):
    n, w = packed.shape
    d = w // 3
    hp = d // PAIR

    def cols(off):
        return pl.BlockSpec((n, PAIR), lambda h: (0, h + off))

    return pl.pallas_call(
        functools.partial(attend_kernel, tq=128),
        grid=(hp,),
        in_specs=[cols(0), cols(hp), cols(2 * hp)],
        out_specs=[cols(0), pl.BlockSpec((n, PAIR), lambda h: (0, 0)), pl.BlockSpec((2, n, n), lambda h: (h, 0, 0))],
        out_shape=[shape((n, d)), shape((n, PAIR), F32), shape((2 * hp, n, n))],
        scratch_shapes=[pltpu.VMEM((n, 2 * PAIR), BF)],
        compiler_params=params(40),
        cost_estimate=pl.CostEstimate(flops=16 * n * n * d, bytes_accessed=4 * n * n * hp, transcendentals=0),
        name="attend",
    )(packed, packed, packed)


WHOLE = pl.BlockSpec(memory_space=pltpu.VMEM)
FAR = pl.BlockSpec(memory_space=pltpu.HBM)


def transpose_rows(block, out, cols):
    t = block.T
    d = t.shape[0]
    half = d // PIECES // 2
    for h in range(2):
        for v in range(PIECES):
            at = (2 * v + h) * half
            to = (h * PIECES + v) * half
            out[to : to + half, cols] = t[at : at + half]


def core_rows(ref, which):
    half = ref.shape[0] // 2
    return ref[pl.ds(pl.multiple_of(which * half, half), half), :]


def piece_blocks(g, ref, first):
    rows = g.shape[0] // PIECES
    for k in range(g.shape[1] // 128):
        at = (first + k) * rows
        ref[:, at : at + rows, :] = g[:, k * 128 : (k + 1) * 128].reshape(PIECES, rows, 128)


def middle_of(x_ref, mix_ref, wo_ref, vec_ref, rows):
    return x_ref[rows, :].astype(F32) + dot(mix_ref[rows, :], wo_ref[...], NN) + line(vec_ref, "ob")


def hidden_kernel(c_ref, *refs, i, head, tm, sub):
    refs = list(refs)
    take = lambda k: [refs.pop(0) for _ in range(k)]
    if head:
        x_ref, mix_ref, wo_ref, vec_ref = take(4)
    else:
        sec_ref, sec_t, up_t, o_in, ds_in = take(5)
    up_ref, w1_ref, w2_ref, b1_ref, gk_ref, gs_ref, db1_ref, o_ref, ds_ref = take(9)
    if head:
        sec_ref, sec_t, up_t = take(3)
    act, dh = take(2)
    n, d = up_ref.shape
    wide = act.shape[1]

    def shares(first, last):
        return [slice((v * CHUNKS + i) * 128, (v * CHUNKS + i + 1) * 128) for v in range(first // 128, last // 128)]

    def columns(first, last):
        return jnp.concatenate([w1_ref[:, at] for at in shares(first, last)], axis=1)

    def lines(first, last):
        return jnp.concatenate([w2_ref[at, :] for at in shares(first, last)], axis=0)

    if head:
        for t in range(n // 256):
            rows = slice(t * 256, (t + 1) * 256)
            spread, r = stats(middle_of(x_ref, mix_ref, wo_ref, vec_ref, rows))
            sec = (spread * r * line(vec_ref, "mg") + line(vec_ref, "ms")).astype(BF)
            sec_ref[rows, :] = sec
            transpose_rows(sec, sec_t, rows)
            up_t[:, rows] = up_ref[rows, :].T
    db1_ref[...] = jnp.zeros_like(db1_ref)
    for first in range(0, wide, sub):
        cols = slice(first, first + sub)
        bias = jnp.concatenate([b1_ref[v * CHUNKS + i : v * CHUNKS + i + 1, :] for v in range(first // 128, (first + sub) // 128)], axis=1)

        def tile(t, _):
            rows = pl.ds(pl.multiple_of(t * tm, tm), tm)
            h = dot(sec_ref[rows, :], columns(first, first + sub), NN) + bias
            da = dot(up_ref[rows, :], lines(first, first + sub), NT)
            cdf, pdf = normal(h)
            act[rows, cols] = (h * cdf).astype(BF)
            dhv = da * (cdf + h * pdf)
            dh[rows, cols] = dhv.astype(BF)
            db1_ref[:, cols] += jnp.sum(dhv, axis=0, keepdims=True)
            return 0

        lax.fori_loop(0, n // tm, tile, 0)
    base = PIECES * (d // PIECES // 2)
    c = c_ref[0]
    for ref, mine in ((gs_ref, 1 - c), (gk_ref, c)):
        piece_blocks(dot(core_rows(sec_t, mine), dh[...], NN).astype(BF), ref, 0)
        g = dot(core_rows(up_t, mine), act[...], NN).astype(BF)
        for k in range(wide // 128):
            ref[k, base:, :] = g[:, k * 128 : (k + 1) * 128]

    def gather(t, _):
        rows = pl.ds(pl.multiple_of(t * tm, tm), tm)
        o = dot(act[rows, :], lines(0, wide), NN)
        o_ref[rows, :] = o if head else o_in[rows, :] + o
        ds = dot(dh[rows, :], columns(0, wide), NT)
        ds_ref[rows, :] = ds if head else ds_in[rows, :] + ds
        return 0

    lax.fori_loop(0, n // tm, gather, 0)


def hidden_part(core, head, carried, up, w1, w2, b1, i, tm=512, sub=512):
    n, d = up.shape
    wide = 128 * PIECES
    assert wide * CHUNKS == w1.shape[1]
    g = (PIECES, PIECES * (d // PIECES // 2) + d // 2, 128)
    args = list(head) if head else list(carried)
    made = [shape(g), shape(g), shape((1, wide), F32), shape((n, d), F32), shape((n, d), F32)]
    if head:
        made += [shape((n, d)), shape((d, n)), shape((d, n))]
    return pl.pallas_call(
        functools.partial(hidden_kernel, i=i, head=bool(head), tm=tm, sub=sub),
        in_specs=[pl.BlockSpec(memory_space=pltpu.SMEM)] + [WHOLE] * (len(args) + 4),
        out_specs=[WHOLE] * len(made),
        out_shape=made,
        input_output_aliases={} if head else {4: 3, 5: 4},
        scratch_shapes=[pltpu.VMEM((n, wide), BF), pltpu.VMEM((n, wide), BF)],
        compiler_params=params(10),
        cost_estimate=pl.CostEstimate(flops=24 * n * d * wide, bytes_accessed=8 * d * wide, transcendentals=0),
        name="hidden",
    )(core, *args, up, w1, w2, b1)


def outer_kernel(c_ref, x_ref, up_ref, mix_ref, li_ref, wo_ref, vec_ref, o_ref, ds_ref, out_ref, dbr_ref, do_ref, gk_ref, gs_ref, sums_ref, mix_t, *, tm):
    n, d = x_ref.shape
    sums = None
    lanes = lax.broadcasted_iota(jnp.int32, (PAIR, d), 1) // HEAD_DIM
    spread_heads = (lanes == lax.broadcasted_iota(jnp.int32, (PAIR, d), 0)).astype(BF)
    for t in range(n // tm):
        rows = slice(t * tm, (t + 1) * tm)
        m = middle_of(x_ref, mix_ref, wo_ref, vec_ref, rows)
        spread, r = stats(m)
        nv = spread * r
        up = up_ref[rows, :].astype(F32)
        transpose_rows(mix_ref[rows, :], mix_t, rows)
        dy = ds_ref[rows, :]
        dyg = dy * line(vec_ref, "mg")
        dm = up + r * (dyg - jnp.mean(dyg, axis=-1, keepdims=True) - nv * jnp.mean(dyg * nv, axis=-1, keepdims=True))
        db = dm.astype(BF)
        dbr_ref[rows, :] = db
        out_ref[rows, :] = (m + o_ref[rows, :] + line(vec_ref, "rb")).astype(BF)
        li = li_ref[rows, :]
        coarse = li.astype(BF)
        fine = (li - coarse.astype(F32)).astype(BF)
        scale = dot(coarse, spread_heads, NN) + dot(fine, spread_heads, NN)
        do_ref[rows, :] = (dot(db, wo_ref[...], NT) * scale).astype(BF)
        part = [jnp.sum(v, axis=0, keepdims=True) for v in (db.astype(F32), dy * nv, dy, up)]
        sums = part if sums is None else [a + b for a, b in zip(sums, part)]
    sums_ref[...] = jnp.concatenate(sums + [jnp.zeros((4, d), F32)], axis=0)
    for ref, mine in ((gs_ref, 1 - c_ref[0]), (gk_ref, c_ref[0])):
        piece_blocks(dot(core_rows(mix_t, mine), dbr_ref[...], NN).astype(BF), ref, 0)


def outer(core, x, up, mix, li, wo, vec, o, ds, tm=256):
    n, d = x.shape
    g = (PIECES, d // 128 * (d // PIECES // 2), 128)
    return pl.pallas_call(
        functools.partial(outer_kernel, tm=tm),
        in_specs=[pl.BlockSpec(memory_space=pltpu.SMEM)] + [WHOLE] * 8,
        out_specs=[WHOLE] * 6,
        out_shape=[shape((n, d))] * 3 + [shape(g), shape(g), shape((8, d), F32)],
        scratch_shapes=[pltpu.VMEM((d, n), BF)],
        compiler_params=params(8),
        cost_estimate=pl.CostEstimate(flops=24 * n * d * d, bytes_accessed=20 * n * d, transcendentals=0),
        name="outer",
    )(core, x, up, mix, li, wo, vec, o, ds)


def by_piece(g):
    rows = g.shape[0] // PIECES
    return [g[:, i : i + 128].reshape(PIECES, rows, 128) for i in range(0, g.shape[1], 128)]


def reflect_kernel(c_ref, q_ref, k_ref, v_ref, o_ref, do_ref, p_ref, ft_ref, dq_ref, dk_ref, dv_ref, gk_ref, gs_ref, ds_ref, *, tq):
    n = k_ref.shape[0]
    low = lax.broadcasted_iota(jnp.int32, (tq, PAIR), 1) < HEAD_DIM
    q_t = q_ref[...].T
    do_t = do_ref[...].T
    scale = HEAD_DIM**-0.5
    dks, dvs = [], []
    for a in range(2):
        for t in range(n // tq):
            rows = pl.ds(t * tq, tq)
            do = do_ref[rows, :]
            zero = jnp.zeros_like(do)
            doa = jnp.where(low, do, zero) if a == 0 else jnp.where(low, zero, do)
            delta = jnp.sum(doa.astype(F32) * o_ref[rows, :].astype(F32), axis=-1, keepdims=True)
            dp = dot(doa, v_ref[...], NT)
            ds = (p_ref[a, rows, :].astype(F32) * (dp - delta)).astype(BF)
            ds_ref[rows, :] = ds
            dq = (dot(ds, k_ref[...], NN) * scale).astype(BF)
            dq_ref[rows, :] = dq if a == 0 else jnp.where(low, dq_ref[rows, :], dq)
        part = slice(HEAD_DIM * a, HEAD_DIM * (a + 1))
        dvs.append(dot(do_t[part], p_ref[a], NN))
        dks.append(dot(q_t[part], ds_ref[...], NN) * scale)
    dv = jnp.concatenate(dvs, axis=0).astype(BF).T
    dk = jnp.concatenate(dks, axis=0).astype(BF).T
    dv_ref[...] = dv
    dk_ref[...] = dk
    g = dot(ft_ref[...], jnp.concatenate([dq_ref[...], dk, dv], axis=1), NN).astype(BF)
    per = g.shape[0] // PIECES
    h = pl.program_id(0)
    for step, ref in enumerate((gs_ref, gk_ref)):

        @pl.when(h == step)
        def _():
            for i, block in enumerate(by_piece(g)):
                ref[:, i * per : (i + 1) * per, :] = block


def reflect(core, packed, o, do, p, first_t, start):
    n, w = packed.shape
    d = w // 3
    hp = d // PAIR

    def which(h, c):
        return (h + 1 - c[0]) % 2

    def cols(off):
        return pl.BlockSpec((n, PAIR), lambda h, c: (0, which(h, c) + off))

    g = (PIECES, 3 * (d // PIECES), 128)
    piece = pl.BlockSpec(g, lambda h, c: (0, 0, 0), pipeline_mode=pl.Buffered(1))
    return pl.pallas_call(
        functools.partial(reflect_kernel, tq=256),
        grid_spec=pltpu.PrefetchScalarGridSpec(
            num_scalar_prefetch=1,
            grid=(2,),
            in_specs=[
                cols(start), cols(start + hp), cols(start + 2 * hp), cols(start), cols(start),
                pl.BlockSpec((2, n, n), lambda h, c: (which(h, c) + start, 0, 0)),
                pl.BlockSpec((d, n), lambda h, c: (0, 0), pipeline_mode=pl.Buffered(1)),
            ],
            out_specs=[cols(0)] * 3 + [piece] * 2,
            scratch_shapes=[pltpu.VMEM((n, n), BF)],
        ),
        out_shape=[shape((n, 2 * PAIR))] * 3 + [shape(g)] * 2,
        compiler_params=params(27),
        cost_estimate=pl.CostEstimate(flops=160 * n * n * PAIR, bytes_accessed=8 * n * n, transcendentals=0),
        name="reflect",
    )(core, packed, packed, packed, o, do, p, first_t)


SMALL = 16


def back_kernel(*refs, chunks):
    x_ref, dbr_ref, w_ref, vec_in, mid_ref = refs[:5]
    db1 = refs[5 : 5 + CHUNKS]
    parts = refs[5 + CHUNKS : 5 + CHUNKS + 3 * chunks]
    tg_ref, small_ref, sums = refs[5 + CHUNKS + 3 * chunks :]

    @pl.when(pl.program_id(0) == 0)
    def _():
        sums[...] = jnp.zeros_like(sums)

    d = x_ref.shape[1]
    cw = d // chunks
    dy = None
    for i in range(3 * chunks):
        which, chunk = i % 3, i // 3
        at = which * d + chunk * cw
        part = dot(parts[i][...], w_ref[:, at : at + cw], NT)
        dy = part if dy is None else dy + part
        row = {0: 2, 2: 3}.get(which)
        if row is not None:
            sums[row : row + 1, chunk * cw : (chunk + 1) * cw] += jnp.sum(parts[i][...].astype(F32), axis=0, keepdims=True)
    spread, r = stats(x_ref[...].astype(F32))
    nv = spread * r
    dyg = dy * line(vec_in, "ag")
    dx = r * (dyg - jnp.mean(dyg, axis=-1, keepdims=True) - nv * jnp.mean(dyg * nv, axis=-1, keepdims=True))
    tg_ref[...] = (dbr_ref[...].astype(F32) + dx).astype(BF)
    sums[0:1, :] += jnp.sum(dy * nv, axis=0, keepdims=True)
    sums[1:2, :] += jnp.sum(dy, axis=0, keepdims=True)

    @pl.when(pl.program_id(0) == pl.num_programs(0) - 1)
    def _():
        per = d // PIECES
        sums[4:8, :] = mid_ref[0:4, :]
        rows = sums[...]
        for v in range(PIECES):
            vectors = jnp.concatenate([rows[:, v * per : (v + 1) * per], jnp.zeros((8, 128 - per), F32)], axis=1)
            biases = [b[:, v * 128 : (v + 1) * 128] for b in db1]
            piece = jnp.concatenate([vectors] + biases + [jnp.zeros((SMALL - 8 - CHUNKS, 128), F32)], axis=0)
            small_ref[v * SMALL : (v + 1) * SMALL, :] = piece.astype(BF)


def project_back(x, dbr, w, vec, mids, db1, parts):
    n, d = x.shape
    tm = 256
    row = pl.BlockSpec((tm, d), lambda i: (i, 0))

    def full(*s):
        return pl.BlockSpec(s, lambda i: (0, 0), pipeline_mode=pl.Buffered(1))

    chunks = len(parts) // 3
    return pl.pallas_call(
        functools.partial(back_kernel, chunks=chunks),
        grid=(n // tm,),
        in_specs=[row, row, full(d, 3 * d), full(*vec.shape), full(*mids.shape)]
        + [full(*b.shape) for b in db1]
        + [pl.BlockSpec((tm, d // chunks), lambda i: (i, 0))] * (3 * chunks),
        out_specs=[row, full(PIECES * SMALL, 128)],
        out_shape=[shape((n, d)), shape((PIECES * SMALL, 128))],
        scratch_shapes=[pltpu.VMEM((8, d), F32)],
        compiler_params=params(24),
        cost_estimate=pl.CostEstimate(flops=12 * n * d * d, bytes_accessed=16 * n * d, transcendentals=0),
        name="project_back",
    )(x, dbr, w, vec, mids, *db1, *parts)


def exchange(x, axis, by):
    count = lax.axis_size(axis)
    return lax.ppermute(x, axis, [(i, i ^ by) for i in range(count)])


def to_core(g):
    return exchange(g, "seq", 1)


def pick(x, index, axis=0):
    return lax.dynamic_index_in_dim(x, index, axis, keepdims=False)


def after(x, *others):
    return lax.optimization_barrier((x,) + others)[0]


class Part:
    def __init__(self, held, received, rows):
        self.held = (held.reshape(-1, 128), 0)
        self.received = (received.reshape(-1, 128), 0)
        self.rows = rows
        self.open = [0, 1, 2]

    def count(self):
        return self.rows << len(self.open)


def slot_kernel(ids_ref, *refs, items, inputs):
    ins, outs = refs[:inputs], refs[inputs:]

    def read(term, at, count):
        ref, offset = term
        return ins[ref][pl.ds(at + offset, count), :].astype(F32)

    step = 16
    for kind, *rest in items:
        if kind == "split":
            held, received, groups, size, bit, (send, to), keep = rest
            mine = ids_ref[bit]
            for a in range(groups):
                own = pl.multiple_of((2 * a + mine) * size, step)
                other = pl.multiple_of((2 * a + 1 - mine) * size, step)
                outs[send][to + a * size : to + (a + 1) * size, :] = (read(held, other, size) + read(received, other, size)).astype(BF)
                outs[keep][a * size : (a + 1) * size, :] = (read(held, own, size) + read(received, own, size)).astype(BF)
        elif kind == "sum":
            held, received, size, (send, to) = rest
            outs[send][to : to + size, :] = (read(held, 0, size) + read(received, 0, size)).astype(BF)
        else:
            first, second, size, bit, (send, to), keep = rest
            for mine in (0, 1):

                @pl.when(ids_ref[bit] == mine)
                def _():
                    own, other = (first, second) if mine == 0 else (second, first)
                    outs[send][to : to + size, :] = (read(other[0], 0, size) + read(other[1], 0, size)).astype(BF)
                    outs[keep][...] = (read(own[0], 0, size) + read(own[1], 0, size)).astype(BF)


def slot(ids, exchanges, *tokens):
    arrays, items, sizes, moves = [], [], [], []

    def use(term):
        for i, a in enumerate(arrays):
            if a is term[0]:
                return i, term[1]
        arrays.append(term[0])
        return len(arrays) - 1, term[1]

    for stage, parts in exchanges:
        send, to = len(sizes), 0
        sizes.append(0)
        placed = []
        if stage == "pick":
            one, two = parts
            size = one.count()
            items.append(("pick", (use(one.held), use(one.received)), (use(two.held), use(two.received)), size, 1, (send, 0), len(sizes)))
            placed.append((one, len(sizes), 0, 0))
            sizes.append(size)
            to = size
        else:
            for p in parts:
                held, received = use(p.held), use(p.received)
                if stage == "x":
                    items.append(("sum", held, received, p.count(), (send, to)))
                    placed.append((p, send, to, to))
                    to += p.count()
                    continue
                if stage == "half":
                    groups, bit = 1 << len(p.open), 1
                else:
                    groups, bit = 1 << (len(p.open) - 1 - p.open.index(stage)), 2 + stage
                size = p.count() // (2 * groups)
                items.append(("split", held, received, groups, size, bit, (send, to), len(sizes)))
                placed.append((p, len(sizes), 0, to))
                sizes.append(groups * size)
                to += groups * size
                if stage == "half":
                    p.rows //= 2
                else:
                    p.open.remove(stage)
        sizes[send] = to
        moves.append((stage, send, placed))

    if tokens:
        arrays = list(lax.optimization_barrier(tuple(arrays) + tokens)[: len(arrays)])
    whole = pl.BlockSpec(memory_space=pltpu.VMEM)
    outs = pl.pallas_call(
        functools.partial(slot_kernel, items=items, inputs=len(arrays)),
        in_specs=[pl.BlockSpec(memory_space=pltpu.SMEM)] + [whole] * len(arrays),
        out_specs=[whole] * len(sizes),
        out_shape=[shape((size, 128)) for size in sizes],
        compiler_params=params(2),
        cost_estimate=pl.CostEstimate(flops=0, bytes_accessed=512 * sum(sizes), transcendentals=0),
        name="slot",
    )(ids, *arrays)
    unit = lax.axis_size("vol") // PIECES
    sent, received = [], []
    for stage, send, placed in moves:
        if stage in ("half", "pick", "x"):
            got = exchange(outs[send], "seq", 2)
        else:
            got = exchange(outs[send], "vol", unit << stage)
        sent.append(outs[send])
        received.append(got)
        for p, keep, at, to in placed:
            p.held = (outs[keep], at)
            p.received = (got, to)
    return sent, received


def home_kernel(ids_ref, live_ref, *refs, mask):
    out_ref = refs[-1]
    for k, ref in enumerate(refs[:-1]):

        @pl.when(pl.program_id(0) == k)
        def _():
            value = ref[...].astype(F32)
            if mask:
                value = value * live_ref[ids_ref[5] ^ k]
            out_ref[...] = value.astype(out_ref.dtype)


def send_home(ids, live, own, others, slices, dtype, mask):
    rows, d = others[0].shape
    return pl.pallas_call(
        functools.partial(home_kernel, mask=mask),
        grid_spec=pltpu.PrefetchScalarGridSpec(
            num_scalar_prefetch=2,
            grid=(slices,),
            in_specs=[pl.BlockSpec((rows, d), lambda k, i, l: (0, 0), pipeline_mode=pl.Buffered(1))] * slices,
            out_specs=pl.BlockSpec((None, rows, d), lambda k, i, l: (k ^ i[5], 0, 0)),
        ),
        out_shape=shape((slices, rows, d), dtype),
        compiler_params=params(8),
        cost_estimate=pl.CostEstimate(flops=0, bytes_accessed=6 * slices * rows * d, transcendentals=0),
        name="home",
    )(ids, live, own, *others)


def assemble_ff_kernel(ids_ref, *refs, per, sizes):
    terms = refs[:4]
    expand_ref, reduce_ref = refs[4:]
    c = ids_ref[0]

    def first_layer(i, core, value):
        size = per // 2
        for k in range(PIECES):
            at = (k * CHUNKS + i) * 128
            expand_ref[pl.ds(pl.multiple_of(core * size, size), size), at : at + 128] = value[k * size : (k + 1) * size, :]

    def second_layer(i, core, value):
        d = value.shape[0]
        reduce_ref[i * 128 : (i + 1) * 128, pl.ds(pl.multiple_of(core * d, 128), d)] = value.T

    half = per // 2 * PIECES
    for core, (own, partner) in ((c, terms[:2]), (1 - c, terms[2:])):
        for x in (0, 1):

            @pl.when(ids_ref[1] == x)
            def _():
                one, two = (own, partner) if x == 0 else (partner, own)
                first_layer(0, core, one[: sizes[0], :].astype(F32))
                second_layer(0, core, two[: sizes[0], :].astype(F32))

        at = sizes[0]
        for i in (1, 2):
            rows = slice(at, at + sizes[i])
            value = own[rows, :].astype(F32) + partner[rows, :].astype(F32)
            first_layer(i, core, value[:half])
            second_layer(i, core, value[half:])
            at += sizes[i]


def assemble_end_kernel(ids_ref, *refs, per, size):
    terms = refs[:4]
    output_ref, input_ref, vector_ref = refs[4:]
    c = ids_ref[0]
    d = PIECES * per

    def output_part(core, value):
        part = per // 2
        for k in range(d // 128):
            rows = pl.ds(pl.multiple_of(core * part, part), part)
            output_ref[rows, k * 128 : (k + 1) * 128] = value[k * part : (k + 1) * part, :]

    def pair_part(i, core, value):
        for k in range(3):
            at = pl.multiple_of(k * d + (2 * i + core) * 128, 128)
            input_ref[:, pl.ds(at, 128)] = value[k * per : (k + 1) * per, :]

    for core, (own, partner) in ((c, terms[:2]), (1 - c, terms[2:])):
        for i in (1, 2):
            rows = slice((i - 1) * size, i * size)
            pair_part(i, core, own[rows, :].astype(F32) + partner[rows, :].astype(F32))
        for x in (0, 1):

            @pl.when(ids_ref[1] == x)
            def _():
                one, two = (own, partner) if x == 0 else (partner, own)
                output_part(core, one[2 * size : 3 * size, :].astype(F32))
                pair_part(0, core, two[2 * size : 3 * size, :].astype(F32))

    vector_ref[...] = terms[0][3 * size :, :].astype(F32) + terms[1][3 * size :, :].astype(F32)


def assemble(kernel, ids, per, arrays, outs, name):
    whole = pl.BlockSpec(memory_space=pltpu.VMEM)
    return pl.pallas_call(
        functools.partial(kernel, per=per),
        in_specs=[pl.BlockSpec(memory_space=pltpu.SMEM)] + [whole] * len(arrays),
        out_specs=[whole] * len(outs),
        out_shape=[shape(o, F32) for o in outs],
        compiler_params=params(8),
        name=name,
    )(ids, *arrays)


def on_device(
    volume_slices, volume_owner, tokens, cotangent, attend_gain, attend_shift, input_weight, query_bias, value_bias,
    output_weight, output_bias, mixer_gain, mixer_shift, expand_weight, expand_bias, reduce_weight, reduce_bias,
):
    slices, rows, d = tokens.shape
    ff = expand_weight.shape[1]
    nv = lax.axis_size("vol")
    peers = lax.axis_size("seq")
    me = lax.axis_index("seq")
    core_id = me % 2
    x_id = (me // 2) % 2
    core = core_id.astype(jnp.int32).reshape(1)
    n = rows * peers
    vol = lax.axis_index("vol")
    unit = nv // PIECES
    ids = jnp.stack([core_id, x_id, (vol // unit) % 2, (vol // (2 * unit)) % 2, (vol // (4 * unit)) % 2, me]).astype(jnp.int32)

    def from_peers(x, ks):
        parts = [pick(x, me ^ k) for k in ks]
        return [p if k == 0 else exchange(p, "seq", k) for p, k in zip(parts, ks)]

    far_parts = from_peers(tokens, (3, 2))
    near_parts = from_peers(tokens, (0, 1))
    zero = jnp.zeros((d,), BF)
    vec = jnp.concatenate(
        [attend_gain, attend_shift, query_bias, zero, value_bias, output_bias, mixer_gain, mixer_shift, reduce_bias] + [zero] * 7
    ).astype(F32).reshape(16, d)
    wide = ff // CHUNKS
    lanes = wide // PIECES
    b1 = expand_bias.astype(F32).reshape(ff // 128, 128)
    load = jnp.sum(jnp.where(volume_owner == lax.axis_index("vol"), volume_slices, 0))
    live = (jnp.arange(slices) < load).astype(BF)

    made = project_in(jnp.concatenate(near_parts), 0, n, None, vec, input_weight)
    far = jnp.concatenate([after(far_parts[1], made[2], b1, live), far_parts[0]])
    x, first_t, packed = project_in(far, 2 * rows, n, made, vec, input_weight)
    upstream = jnp.concatenate(from_peers(after(cotangent, far_parts[0], made[2]) * live[:, None, None], (0, 1, 2, 3)))

    mixed, inverse, weights = attend(packed)

    db1 = []

    def hidden(token, head, carried, i):
        gk, gs, b, *made = hidden_part(token, head, carried, upstream, expand_weight, reduce_weight, b1, i)
        db1.append(b)
        return gk, gs, made

    Y, Z1, Z2 = 0, 1, 2
    piece_rows = d // 2 + d // 2
    pair_rows = 3 * (d // PIECES)
    k0, s0, (o, ds, *kept) = hidden(core, (x, mixed, output_weight, vec), None, 0)
    r0 = to_core(s0)
    k1, s1, (o, ds) = hidden(after(core, s0), None, (*kept, o, ds), 1)
    r1 = to_core(s1)
    ga = Part(k0, r0, piece_rows)
    sent, _ = slot(ids, [("half", [ga])], s1)
    k2, s2, (o, ds) = hidden(after(core, s1, *sent), None, (*kept, o, ds), 2)
    r2 = to_core(s2)
    gb = Part(k1, r1, piece_rows)
    sent, _ = slot(ids, [(Z1, [gb])], s2)
    out, d_branch, d_mixed, k3, s3, sums_mid = outer(
        after(core, s2, *sent), x, upstream, mixed, inverse, output_weight, vec, o, ds
    )
    r3 = to_core(s3)

    def homeward(a):
        blocks = [a[k * rows : (k + 1) * rows] for k in range(1, peers)]
        return blocks, [exchange(b, "seq", k + 1) for k, b in enumerate(blocks)]

    out_sent, outs = homeward(out)
    gc = Part(k2, r2, piece_rows)
    sent, got = slot(ids, [(Y, [gc])], s3)
    parts = []

    def reflect_part(token, i):
        dq, dk, dv, gk, gs = reflect(token, packed, mixed, d_mixed, weights, first_t, 2 * i)
        parts.extend([dq, dk, dv])
        return gk, gs

    p0, q0 = reflect_part(after(core, s3, *sent, *out_sent), 0)
    t0 = to_core(q0)
    wait_c = got[0]
    sent, _ = slot(ids, [(Y, [ga]), (Z2, [gb])], q0)
    p1, q1 = reflect_part(after(core, q0, wait_c, *sent, *outs), 1)
    t1 = to_core(q1)
    gd, gd2 = Part(k3, r3, pair_rows), Part(p0, t0, pair_rows)
    sent, _ = slot(ids, [(Z1, [ga, gc]), ("pick", [gd, gd2])], q1)
    p2, q2 = reflect_part(after(core, q1, *sent), 2)
    t2 = to_core(q2)
    ge1 = Part(p1, t1, pair_rows)
    sent, late_got = slot(ids, [(Y, [ge1, gd]), (Z2, [ga, gc])], q2)
    d_tokens, small = project_back(after(x, *sent), d_branch, input_weight, vec, sums_mid, db1, parts)

    tg_sent, tgs = homeward(d_tokens)
    ge2 = Part(p2, t2, pair_rows)
    gv = Part(small, to_core(small), SMALL)
    sent1, got1 = slot(ids, [(Y, [ge2, gv]), (Z1, [ge1, gd])], small, *tg_sent, late_got[1])
    block_out = send_home(ids, live, out, [after(o, *sent1) for o in outs], slices, BF, True)
    sent2, got2 = slot(ids, [(Z1, [ge2, gv]), (Z2, [ge1, gd]), (Y, [gb])], *got1, block_out, tgs[1])
    per = d // PIECES
    spare = [1 << i for i in range(unit.bit_length() - 1)]
    sent3, got3 = slot(ids, [(Z2, [ge2, gv]), ("x", [ga, gb, gc])], *got2)
    tgs = [after(t, *sent3) for t in tgs]
    tokens_grad = send_home(ids, live, d_tokens, tgs, slices, F32, False)
    sent4, got4 = slot(ids, [("x", [ge1, ge2, gd, gv])], got3[0], tokens_grad)
    ff_terms = [after(a, *sent4) for a in (sent3[-1], got3[-1])]
    ff_terms += [to_core(a) for a in ff_terms]
    expand_grad, reduce_grad = assemble(
        functools.partial(assemble_ff_kernel, sizes=[p.count() for p in (ga, gb, gc)]), ids, per, ff_terms, [(per, ff), (ff // PIECES, d)], "assemble_ff"
    )
    ends = [sent4[0], got4[0]]
    ends += [to_core(a) for a in ends]
    output_grad, input_grad, vectors = assemble(
        functools.partial(assemble_end_kernel, size=pair_rows), ids, per, ends, [(per, d), (per, 3 * d), (SMALL, 128)], "assemble_end"
    )
    bias_rows = vectors[8 : 8 + CHUNKS]
    vectors = vectors[:8, :per]
    if unit > 1:
        sub = vol % unit

        def add_rest(a):
            for by in spare:
                a = a + exchange(a, "vol", by)
            return a

        def cut(a, axis):
            size = a.shape[axis] // unit
            return lax.dynamic_slice_in_dim(add_rest(a), sub * size, size, axis)

        expand_grad, reduce_grad, output_grad, input_grad = [cut(a, 0) for a in (expand_grad, reduce_grad, output_grad, input_grad)]
        expand_bias_grad = cut(bias_rows.reshape(-1), 0)
        vectors = cut(vectors, 1)
    else:
        expand_bias_grad = bias_rows.reshape(-1)
    return (
        block_out, tokens_grad, vectors[0], vectors[1], input_grad, vectors[2], vectors[3], output_grad, vectors[4],
        vectors[5], vectors[6], expand_grad, expand_bias_grad, reduce_grad, vectors[7],
    )


def solution(mesh):
    rows = P("vol", "seq", None)
    return jax.shard_map(
        on_device,
        mesh=mesh,
        in_specs=(P(), P(), rows, rows) + (P(),) * 13,
        out_specs=(rows, rows, P("vol"), P("vol"), P("vol", None), P("vol"), P("vol"), P("vol", None), P("vol"), P("vol"),
                   P("vol"), P("vol", None), P("vol"), P("vol", None), P("vol")),
        check_vma=False,
    )
```
